32 devices in a mesh: wide: 8 (over z, x), narrow: 4 (over y, core).
Axes of the slice: x: 2, y: 2, z: 4, core: 2. Of those that a mesh axis runs over, the one named last changes fastest.
Arguments:
- inputs: bfloat16 [12288, 768], P(('wide', 'narrow')), may hold values from -6 to 6
- lengths: int32 [32], P(('wide', 'narrow')), may hold values from 1 to 384, 9216 in all
- triple_weight: bfloat16 [768, 2304], P(('wide', 'narrow')), may hold values from -0.21875 to 0.21875
- triple_bias: bfloat16 [2304], P(('wide', 'narrow')), may hold values from -1.796875 to 1.796875
- mix_weight: bfloat16 [768, 768], P(('wide', 'narrow')), may hold values from -1.75 to 1.75
- mix_bias: bfloat16 [768], P(('wide', 'narrow')), may hold values from -1.796875 to 1.796875
- first_gain: bfloat16 [768], P(('wide', 'narrow')), may hold values from 0.25 to 1.75
- first_shift: bfloat16 [768], P(('wide', 'narrow')), may hold values from -1.796875 to 1.796875
- up_weight: bfloat16 [768, 3072], P('wide', 'narrow'), may hold values from -0.21875 to 0.21875
- up_bias: bfloat16 [3072], P('narrow'), may hold values from -1.796875 to 1.796875
- down_weight: bfloat16 [3072, 768], P('narrow', 'wide'), may hold values from -0.109375 to 0.109375
- down_bias: bfloat16 [768], P('wide'), may hold values from -1.796875 to 1.796875
- second_gain: bfloat16 [768], P(('wide', 'narrow')), may hold values from 0.25 to 1.75
- second_shift: bfloat16 [768], P(('wide', 'narrow')), may hold values from -1.796875 to 1.796875
- cotangent: bfloat16 [12288, 768], P(('wide', 'narrow')), may hold values from -6 to 6
Outputs:
- outputs: bfloat16 [12288, 768], P(('wide', 'narrow'))
- input_grad: bfloat16 [12288, 768], P(('wide', 'narrow'))
- triple_weight_grad: float32 [768, 2304], P(('wide', 'narrow'))
- triple_bias_grad: float32 [2304], P(('wide', 'narrow'))
- mix_weight_grad: float32 [768, 768], P(('wide', 'narrow'))
- mix_bias_grad: float32 [768], P(('wide', 'narrow'))
- first_gain_grad: float32 [768], P(('wide', 'narrow'))
- first_shift_grad: float32 [768], P(('wide', 'narrow'))
- up_weight_grad: float32 [768, 3072], P('wide', 'narrow')
- up_bias_grad: float32 [3072], P('narrow')
- down_weight_grad: float32 [3072, 768], P('narrow', 'wide')
- down_bias_grad: float32 [768], P('wide')
- second_gain_grad: float32 [768], P(('wide', 'narrow'))
- second_shift_grad: float32 [768], P(('wide', 'narrow'))
The draws below stay inside these ranges and needn't reach their ends.
Inputs may be any that keep to these rules, and one draw needn't show every extreme that they name: `lengths`: entry b is the number of live tokens of the sequence in row block b; the rest of the block is padding. Some sequence fills its block.
All inputs are finite; a program needn't handle non-finite values.
Results may differ from the reference program's by a relative error of at most 0.017.
Values may be sent and summed in bfloat16 or wider, within the bound.
No kernel may reach another device: no remote copies, remote signals or barrier semaphores. Data moves between devices by JAX's collectives and lax.ppermute only.
A program may use at most 128 MiB of HBM per device.

```python
import math
import jax
import jax.numpy as jnp
import numpy as np
from jax import lax

D = 768
H = 12
HD = 64
FF = 3072
SEQ = 384
TOKENS = 12288
DEVICES = 32


def spiked(entries, stream_key, source, target, blocks, factor):
    owner, partner = [(jnp.arange(entries.shape[dim]) // (entries.shape[dim] // blocks)).reshape([-1 if axis == dim else 1 for axis in range(entries.ndim)]) for dim in (source, target)]
    chosen = jax.random.permutation(stream_key, blocks)[partner]
    strong = (owner == chosen) | (owner == (partner + blocks // 2) % blocks)
    return jnp.where(strong, factor * entries, entries)


def block_levels(own_key, shape, split, least, top_value):
    level = 1.0
    for axis_at, parts in split:
        draws = jax.random.uniform(jax.random.fold_in(jax.random.fold_in(own_key, 6), axis_at), (parts,), jnp.float32, least / len(split), top_value / len(split))
        level = level * jnp.repeat(jnp.exp(draws), shape[axis_at] // parts).reshape((-1,) + (1,) * (len(shape) - 1 - axis_at))
    return level


def profile(count, total, limit, slope):
    loads = [(1 << 20) // math.isqrt(grade ** slope) + 1 for grade in range(2, count + 1)]
    rest, holding = total - limit - (count - 1), [1] * (count - 1)
    while rest > 0:
        free = [i for i in range(count - 1) if holding[i] < limit]
        whole, budget = sum([loads[i] for i in free]), rest
        for i in free:
            more = min(limit - holding[i], max(1, budget * loads[i] // whole), rest)
            holding[i] = holding[i] + more
            rest = rest - more
    return np.array([limit] + holding)


def ragged(rng, number_of, total, reach, skew):
    if number_of == 2:
        one = jax.random.randint(rng, (), max(1, total - reach), min(reach, total - 1) + 1)
        return jnp.stack([one, total - one])
    sizes = jnp.asarray(profile(number_of, total, reach, skew), jnp.int32)
    twos = (number_of - 1) // 2
    giver, receiver = sizes[1:1 + 2 * twos:2], sizes[2:2 + 2 * twos:2]
    margin = jnp.minimum(giver - 1, reach - receiver)
    shifted = jax.random.randint(jax.random.fold_in(rng, 1), (twos,), 0, 1 << 20) % (margin + 1)
    sizes = sizes.at[1:1 + 2 * twos:2].set(giver - shifted).at[2:2 + 2 * twos:2].set(receiver + shifted)
    return sizes[jax.random.permutation(jax.random.fold_in(rng, 2), number_of)]


def normal_values(stream_key, shape, spread, reach, pieces=(), kind=jnp.bfloat16):
    array = spread * jax.random.normal(stream_key, shape, jnp.float32)
    if pieces:
        array = array * block_levels(stream_key, shape, pieces, -0.22, 0.18)
    return jnp.clip(array, -reach, reach).astype(kind)


def noise_with(own_key, extent, scale, most, cuts, heavy, kind=jnp.bfloat16):
    values = scale * jax.random.normal(own_key, extent, jnp.float32)
    if cuts:
        values = values * block_levels(own_key, extent, cuts, -0.22, 0.18)
    return jnp.clip(spiked(values, jax.random.fold_in(own_key, 3), *heavy), -most, most).astype(kind)


def setup_inputs(seed: int = 0) -> dict:
    splits = jax.random.split(jax.random.key(seed), 16)
    return {
        "inputs": normal_values(splits[0], (TOKENS, D), 1.0, 6.0, ((0, 32),)),
        "lengths": ragged(splits[1], DEVICES, DEVICES * SEQ * 3 // 4, SEQ, 0).astype(jnp.int32),
        "triple_weight": normal_values(splits[2], (D, 3 * D), D ** -0.5, 0.21875, ((0, 32),)),
        "triple_bias": normal_values(splits[3], (3 * D,), 0.3, 1.796875, ((0, 32),)),
        "mix_weight": normal_values(splits[4], (D, D), (D // 64) ** -0.5, 1.75, ((0, 32),)),
        "mix_bias": normal_values(splits[5], (D,), 0.3, 1.796875, ((0, 32),)),
        "first_gain": jnp.clip(1.0 + 0.15 * jax.random.normal(splits[6], (D,), jnp.float32), 0.25, 1.75).astype(jnp.bfloat16),
        "first_shift": normal_values(splits[7], (D,), 0.3, 1.796875, ((0, 32),)),
        "up_weight": normal_values(splits[8], (D, FF), D ** -0.5, 0.21875, ((0, 8), (1, 4))),
        "up_bias": normal_values(splits[9], (FF,), 0.3, 1.796875, ((0, 4),)),
        "down_weight": normal_values(splits[10], (FF, D), FF ** -0.5, 0.109375, ((0, 4), (1, 8))),
        "down_bias": normal_values(splits[11], (D,), 0.3, 1.796875, ((0, 8),)),
        "second_gain": jnp.clip(1.0 + 0.15 * jax.random.normal(splits[12], (D,), jnp.float32), 0.25, 1.75).astype(jnp.bfloat16),
        "second_shift": normal_values(splits[13], (D,), 0.3, 1.796875, ((0, 32),)),
        "cotangent": noise_with(splits[14], (TOKENS, D), 1.0, 6.0, ((0, 32),), (0, 1, 32, 2.75)),
    }


@jax.custom_vjp
def low(v):
    return lax.optimization_barrier(v.astype(jnp.bfloat16)).astype(jnp.float32)

@jax.custom_vjp
def low_back(v):
    return v

def low_keep(v):
    return (low(v), None)

def low_pass(kept, grad):
    return (grad,)

def back_keep(v):
    return (v, None)

def back_low(kept, grad):
    return (low(grad),)
low.defvjp(low_keep, low_pass)
low_back.defvjp(back_keep, back_low)
EPSILON = 1e-06
HIGHEST = lax.Precision.HIGHEST

def tables(token_rows, width, head):
    position = jnp.arange(token_rows, dtype=jnp.float32)
    column = jnp.arange(width, dtype=jnp.int32)
    pair_index = (column % head // 2).astype(jnp.float32)
    frequency = jnp.exp(pair_index * (-2.0 / head) * math.log(10000.0))
    angle = position[:, None] * frequency[None, :]
    parity = (column % 2).astype(jnp.float32) * 2.0 - 1.0
    return (jnp.cos(angle), jnp.sin(angle) * parity[None, :])

def swapped(values):
    shape = values.shape
    paired = values.reshape(shape[:-1] + (shape[-1] // 2, 2))
    return paired[..., ::-1].reshape(shape)

def rotate(values, cosine, sine):
    return values * cosine + swapped(values) * sine

def normalize(values, gain, shift):
    mean_row = lax.optimization_barrier(jnp.mean(values, -1, keepdims=True))
    centred = values - mean_row
    inverse = lax.rsqrt(lax.optimization_barrier(jnp.mean(centred * centred, -1, keepdims=True)) + EPSILON)
    return centred * inverse * gain + shift

def attend(item):
    query, key, value, length = item
    scores = low_back(jnp.einsum('qhd,khd->hqk', query, key, precision=HIGHEST) * (1.0 / math.sqrt(HD)))
    valid = jnp.arange(SEQ, dtype=jnp.int32) < length
    scores = jnp.where(valid[None, None, :], scores, -1e+30)
    weights = jax.nn.softmax(scores, axis=-1)
    return jnp.einsum('hqk,khd->qhd', low(weights), value, precision=HIGHEST)

def layer(params, inputs, length_block, cosine, sine):
    triple_weight, triple_bias, mix_weight, mix_bias, first_gain, first_shift, up_weight, up_bias, down_weight, down_bias, second_gain, second_shift = params
    groups = inputs.shape[0]
    triple = low_back(jnp.einsum('gsd,de->gse', inputs, triple_weight, precision=HIGHEST) + triple_bias)
    query = low(rotate(triple[..., :D], cosine, sine))
    key = low(rotate(triple[..., D:2 * D], cosine, sine))
    value = low(triple[..., 2 * D:])
    head_shape = (groups, SEQ, H, HD)
    context = lax.map(jax.checkpoint(attend), (query.reshape(head_shape), key.reshape(head_shape), value.reshape(head_shape), length_block))
    context = low(low_back(context.reshape(groups, SEQ, D)))
    branch = low_back(jnp.einsum('gsd,de->gse', context, mix_weight, precision=HIGHEST) + mix_bias)
    first = normalize(inputs + branch, first_gain, first_shift)
    upward = low_back(jnp.einsum('gsd,df->gsf', low(first), up_weight, precision=HIGHEST) + up_bias)
    active = low(jax.nn.gelu(upward, approximate=False))
    downward = low_back(jnp.einsum('gsf,fd->gsd', active, down_weight, precision=HIGHEST) + down_bias)
    return normalize(first + downward, second_gain, second_shift)

def reference(inputs, lengths, triple_weight, triple_bias, mix_weight, mix_bias, first_gain, first_shift, up_weight, up_bias, down_weight, down_bias, second_gain, second_shift, cotangent):
    params = tuple((item.astype(jnp.float32) for item in (triple_weight, triple_bias, mix_weight, mix_bias, first_gain, first_shift, up_weight, up_bias, down_weight, down_bias, second_gain, second_shift)))
    cosine, sine = tables(SEQ, D, HD)
    sequences = TOKENS // SEQ
    per_step = math.gcd(sequences, max(1, 4096 // SEQ))
    step_count = sequences // per_step
    grouped_shape = (step_count, per_step, SEQ, D)
    input_blocks = inputs.astype(jnp.float32).reshape(grouped_shape)
    cotangent_blocks = cotangent.astype(jnp.float32).reshape(grouped_shape)
    length_blocks = lengths.astype(jnp.int32).reshape(step_count, per_step)

    def one_step(totals, item):
        input_block, cotangent_block, length_block = item

        def apply(params_in, values_in):
            return layer(params_in, values_in, length_block, cosine, sine)
        result, pull_back = jax.vjp(apply, params, input_block)
        grad_params, grad_block = pull_back(cotangent_block)
        totals = tuple((left + right for left, right in zip(totals, grad_params)))
        return (totals, (result, grad_block))
    zeros = tuple((jnp.zeros_like(item) for item in params))
    totals, (results, grads) = lax.scan(one_step, zeros, (input_blocks, cotangent_blocks, length_blocks))
    outputs = results.reshape(TOKENS, D).astype(jnp.bfloat16)
    input_grad = grads.reshape(TOKENS, D).astype(jnp.bfloat16)
    return (outputs, input_grad, totals[0], totals[1], totals[2], totals[3], totals[4], totals[5], totals[6], totals[7], totals[8], totals[9], totals[10], totals[11])
```

```python
import functools
import math

import jax
import jax.numpy as jnp
from jax import lax
from jax.experimental import pallas as pl
from jax.experimental.pallas import tpu as pltpu
from jax.sharding import PartitionSpec as P

H = 12
HD = 64


EPSILON = 1e-06


def tables(token_rows, width, head):
    position = jnp.arange(token_rows, dtype=jnp.float32)
    column = jnp.arange(width, dtype=jnp.int32)
    pair_index = (column % head // 2).astype(jnp.float32)
    frequency = jnp.exp(pair_index * (-2.0 / head) * math.log(10000.0))
    angle = position[:, None] * frequency[None, :]
    parity = (column % 2).astype(jnp.float32) * 2.0 - 1.0
    return (jnp.cos(angle), jnp.sin(angle) * parity[None, :])


def swapped(values):
    shape = values.shape
    paired = values.reshape(shape[:-1] + (shape[-1] // 2, 2))
    return paired[..., ::-1].reshape(shape)


def rotate(values, cosine, sine):
    return values * cosine + swapped(values) * sine


def unrotate(grad, cosine, sine):
    return grad * cosine + swapped(grad * sine)


def normalize_forward(values, gain, shift):
    mean_row = jnp.mean(values, -1, keepdims=True)
    centred = values - mean_row
    inverse = lax.rsqrt(jnp.mean(centred * centred, -1, keepdims=True) + EPSILON)
    unit = centred * inverse
    return (unit * gain + shift, unit, inverse)


def normalize_backward(grad, unit, inverse, gain):
    scaled = grad * gain
    inner = (
        scaled
        - jnp.mean(scaled, -1, keepdims=True)
        - unit * jnp.mean(scaled * unit, -1, keepdims=True)
    )
    return (inner * inverse, jnp.sum(grad * unit, 0), jnp.sum(grad, 0))


def gelu_exact(values):
    return jax.nn.gelu(values, approximate=False)


def gelu_backward(upward, grad_active):
    unused, pull_back = jax.vjp(gelu_exact, upward)
    return pull_back(grad_active)[0]


def softmax_block(query_block, key, valid, scale):
    scores = (
        jnp.einsum("qhd,khd->hqk", query_block, key, preferred_element_type=jnp.float32) * scale
    )
    scores = jnp.where(valid[None, None, :], scores, -1e30)
    return jax.nn.softmax(scores, axis=-1)


def attention_forward(query, key, value, valid, scale):
    token_rows = query.shape[0]
    block = min(512, token_rows)
    weights_block = softmax_block(query, key, valid, scale)
    context = jnp.einsum(
        "hqk,khd->qhd",
        weights_block.astype(jnp.bfloat16),
        value,
        preferred_element_type=jnp.float32,
    )
    pieces = context.reshape(block, -1).astype(jnp.bfloat16)
    return pieces


def attention_backward(query, key, value, grad_context, valid, scale):
    weights_block = softmax_block(query, key, valid, scale)
    grad_weights = jnp.einsum(
        "qhd,khd->hqk", grad_context, value, preferred_element_type=jnp.float32
    )
    inner = weights_block * (
        grad_weights - jnp.sum(weights_block * grad_weights, -1, keepdims=True)
    )
    inner_low = inner.astype(jnp.bfloat16)
    query_pieces = (
        jnp.einsum("hqk,khd->qhd", inner_low, key, preferred_element_type=jnp.float32) * scale
    )
    grad_key = (
        jnp.einsum("hqk,qhd->khd", inner_low, query, preferred_element_type=jnp.float32) * scale
    )
    grad_value = jnp.einsum(
        "hqk,qhd->khd",
        weights_block.astype(jnp.bfloat16),
        grad_context,
        preferred_element_type=jnp.float32,
    )
    return (query_pieces, grad_key, grad_value)


def body(
    inputs,
    lengths,
    triple_weight,
    triple_bias,
    mix_weight,
    mix_bias,
    first_gain,
    first_shift,
    up_weight,
    up_bias,
    down_weight,
    down_bias,
    second_gain,
    second_shift,
    cotangent,
):
    token_rows, width = inputs.shape
    scale = 1.0 / math.sqrt(HD)
    head_shape = (token_rows, H, HD)
    (
        triple_full,
        mix_full,
        triple_bias_full,
        mix_bias_full,
        gain_one,
        shift_one,
        gain_two,
        shift_two,
    ) = (
        lax.all_gather(triple_weight, ("wide", "narrow"), axis=0, tiled=True),
        lax.all_gather(mix_weight, ("wide", "narrow"), axis=0, tiled=True),
        lax.all_gather(triple_bias, ("wide", "narrow"), axis=0, tiled=True),
        lax.all_gather(mix_bias, ("wide", "narrow"), axis=0, tiled=True),
        lax.all_gather(first_gain, ("wide", "narrow"), axis=0, tiled=True),
        lax.all_gather(first_shift, ("wide", "narrow"), axis=0, tiled=True),
        lax.all_gather(second_gain, ("wide", "narrow"), axis=0, tiled=True),
        lax.all_gather(second_shift, ("wide", "narrow"), axis=0, tiled=True),
    )
    up_rows, down_columns, down_bias_full = (
        lax.all_gather(up_weight, "wide", axis=0, tiled=True),
        lax.all_gather(down_weight, "wide", axis=1, tiled=True),
        lax.all_gather(down_bias, "wide", axis=0, tiled=True),
    )
    gain_one = gain_one.astype(jnp.float32)
    gain_two = gain_two.astype(jnp.float32)
    cosine, sine = tables(token_rows, width, HD)
    valid = jnp.arange(token_rows, dtype=jnp.int32) < lengths[0]
    triple = jnp.dot(
        inputs, triple_full, preferred_element_type=jnp.float32
    ) + triple_bias_full.astype(jnp.float32)
    query = rotate(triple[:, :width], cosine, sine).astype(jnp.bfloat16).reshape(head_shape)
    key = (
        rotate(triple[:, width : 2 * width], cosine, sine).astype(jnp.bfloat16).reshape(head_shape)
    )
    value = triple[:, 2 * width :].astype(jnp.bfloat16).reshape(head_shape)
    context = attention_forward(query, key, value, valid, scale)
    branch = jnp.dot(context, mix_full, preferred_element_type=jnp.float32) + mix_bias_full.astype(
        jnp.float32
    )
    first, first_unit, first_inverse = normalize_forward(
        inputs.astype(jnp.float32) + branch, gain_one, shift_one.astype(jnp.float32)
    )
    first_low = first.astype(jnp.bfloat16)
    gathered = lax.all_gather(first_low, "narrow", axis=0, tiled=True)
    upward = jnp.dot(gathered, up_rows, preferred_element_type=jnp.float32) + up_bias.astype(
        jnp.float32
    )
    active = gelu_exact(upward).astype(jnp.bfloat16)
    downward = lax.psum_scatter(
        jnp.dot(active, down_columns, preferred_element_type=jnp.float32).astype(jnp.bfloat16),
        "narrow",
        scatter_dimension=0,
        tiled=True,
    ).astype(jnp.float32)
    downward = downward + down_bias_full.astype(jnp.float32)
    result, second_unit, second_inverse = normalize_forward(
        first + downward, gain_two, shift_two.astype(jnp.float32)
    )
    outputs = result.astype(jnp.bfloat16)
    grad_second, second_gain_grad, second_shift_grad = normalize_backward(
        cotangent.astype(jnp.float32), second_unit, second_inverse, gain_two
    )
    grad_down = grad_second.astype(jnp.bfloat16)
    grad_gathered = lax.all_gather(grad_down, "narrow", axis=0, tiled=True)
    grad_active = jnp.dot(grad_gathered, down_columns.T, preferred_element_type=jnp.float32)
    grad_up = gelu_backward(upward, grad_active).astype(jnp.bfloat16)
    grad_feed = lax.psum_scatter(
        jnp.dot(grad_up, up_rows.T, preferred_element_type=jnp.float32).astype(jnp.bfloat16),
        "narrow",
        scatter_dimension=0,
        tiled=True,
    ).astype(jnp.float32)
    up_part = jnp.dot(gathered.T, grad_up, preferred_element_type=jnp.float32)
    down_part = jnp.dot(active.T, grad_gathered, preferred_element_type=jnp.float32)
    down_bias_part = jnp.sum(grad_gathered, 0, dtype=jnp.float32)
    up_weight_grad, down_weight_grad, down_bias_grad = (
        lax.psum_scatter(
            up_part.astype(jnp.bfloat16), "wide", scatter_dimension=0, tiled=True
        ).astype(jnp.float32),
        lax.psum_scatter(
            down_part.astype(jnp.bfloat16), "wide", scatter_dimension=1, tiled=True
        ).astype(jnp.float32),
        lax.psum_scatter(
            down_bias_part.astype(jnp.bfloat16), "wide", scatter_dimension=0, tiled=True
        ).astype(jnp.float32),
    )
    up_bias_grad = lax.psum(jnp.sum(grad_up, 0, dtype=jnp.float32), "wide")
    grad_first = grad_second + grad_feed
    grad_middle, first_gain_grad, first_shift_grad = normalize_backward(
        grad_first, first_unit, first_inverse, gain_one
    )
    grad_branch = grad_middle.astype(jnp.bfloat16)
    mix_weight_grad = jnp.dot(context.T, grad_branch, preferred_element_type=jnp.float32)
    mix_bias_grad = jnp.sum(grad_branch, 0, dtype=jnp.float32)
    triple_back, mix_back = (
        lax.all_gather(triple_weight, ("wide", "narrow"), axis=0, tiled=True),
        lax.all_gather(mix_weight, ("wide", "narrow"), axis=0, tiled=True),
    )
    grad_context = (
        jnp.dot(grad_branch, mix_back.T, preferred_element_type=jnp.float32)
        .astype(jnp.bfloat16)
        .reshape(head_shape)
    )
    grad_query, grad_key, grad_value = attention_backward(
        query, key, value, grad_context, valid, scale
    )
    grad_triple = jnp.concatenate(
        [
            unrotate(grad_query.reshape(token_rows, width), cosine, sine),
            unrotate(grad_key.reshape(token_rows, width), cosine, sine),
            grad_value.reshape(token_rows, width),
        ],
        1,
    ).astype(jnp.bfloat16)
    triple_local = jnp.dot(inputs.T, grad_triple, preferred_element_type=jnp.float32)
    triple_bias_local = jnp.sum(grad_triple, 0, dtype=jnp.float32)
    grad_inputs = grad_middle + jnp.dot(
        grad_triple, triple_back.T, preferred_element_type=jnp.float32
    )
    summed = (
        lax.psum_scatter(triple_local, ("wide", "narrow"), scatter_dimension=0, tiled=True),
        lax.psum_scatter(mix_weight_grad, ("wide", "narrow"), scatter_dimension=0, tiled=True),
        lax.psum_scatter(triple_bias_local, ("wide", "narrow"), scatter_dimension=0, tiled=True),
        lax.psum_scatter(mix_bias_grad, ("wide", "narrow"), scatter_dimension=0, tiled=True),
        lax.psum_scatter(first_gain_grad, ("wide", "narrow"), scatter_dimension=0, tiled=True),
        lax.psum_scatter(first_shift_grad, ("wide", "narrow"), scatter_dimension=0, tiled=True),
        lax.psum_scatter(second_gain_grad, ("wide", "narrow"), scatter_dimension=0, tiled=True),
        lax.psum_scatter(second_shift_grad, ("wide", "narrow"), scatter_dimension=0, tiled=True),
    )
    return (
        outputs,
        grad_inputs.astype(jnp.bfloat16),
        summed[0],
        summed[2],
        summed[1],
        summed[3],
        summed[4],
        summed[5],
        up_weight_grad,
        up_bias_grad,
        down_weight_grad,
        down_bias_grad,
        summed[6],
        summed[7],
    )


VMEM = pltpu.VMEM
SMEM = pltpu.SMEM
BF = jnp.bfloat16
F32 = jnp.float32
AXES = ("wide", "narrow")
WHOLE = pl.BlockSpec(memory_space=VMEM)
SCALARS = pl.BlockSpec(memory_space=SMEM)
LEFT = pl.BlockSpec(memory_space=pl.ANY)


def nn(a, b):
    return lax.dot_general(a, b, (((1,), (0,)), ((), ())), preferred_element_type=F32)


def nt(a, b):
    return lax.dot_general(a, b, (((1,), (1,)), ((), ())), preferred_element_type=F32)


def tn(a, b):
    return lax.dot_general(a, b, (((0,), (0,)), ((), ())), preferred_element_type=F32)


def shape(dims, dtype=BF):
    return jax.ShapeDtypeStruct(dims, dtype)


def call(kernel, outs, specs, scratch, operands, flops, megabytes, out_specs=None):
    moved = sum(math.prod(o.shape) * o.dtype.itemsize for o in operands)
    return pl.pallas_call(
        kernel,
        out_shape=outs,
        in_specs=specs,
        out_specs=[WHOLE] * len(outs) if out_specs is None else out_specs,
        scratch_shapes=scratch,
        compiler_params=pltpu.CompilerParams(vmem_limit_bytes=megabytes << 20),
        cost_estimate=pl.CostEstimate(
            flops=int(flops), bytes_accessed=int(moved), transcendentals=0
        ),
    )(*operands)


def drain(ref, sem):
    pltpu.make_async_copy(ref, ref, sem).wait()


class Plan:
    def __init__(self, wide, narrow):
        self.wide, self.narrow = wide, narrow
        self.devices = wide * narrow
        x, y = narrow, narrow // 2
        high, bit = [], wide // 2 * narrow
        while bit > x:
            high.append(bit)
            bit //= 2
        self.high = len(high)
        self.orders = (high + [x, y], high + [y, x])
        self.bits = len(self.orders[0])
        self.slots = 1 << self.bits

    def lead(self, core, slot):
        mask = 0
        for k, bit in enumerate(self.orders[core]):
            if slot >> k & 1:
                mask ^= bit
        return mask

    def send(self, value, slot):
        pairs = [(i, i ^ self.lead(i & 1, slot)) for i in range(self.devices)]
        return lax.ppermute(value, AXES, pairs)

    def swap(self, value):
        return lax.ppermute(value, AXES, [(i, i ^ 1) for i in range(self.devices)])

    def chips(self, index):
        leads = [
            jnp.array([self.lead(core, r) >> 1 for r in range(self.slots)], jnp.int32)
            for core in (0, 1)
        ]
        core, chip = index & 1, index >> 1
        own = jnp.where(core == 0, leads[0], leads[1]) ^ chip
        other = jnp.where(core == 0, leads[1], leads[0]) ^ chip
        return own, other

    def gather(self, piece):
        count = 1 << self.high
        near = jnp.concatenate([piece] + [self.send(piece, m) for m in range(1, count)], 0)
        low = jnp.concatenate([near, self.send(near, count)], 0)
        high = self.send(low, 2 * count)
        return low, high, self.swap(low), self.swap(high)

    def scatter(self, low, high):
        count = 1 << self.high
        came = self.send(high, 2 * count)

        def add(part):
            return (low[part].astype(F32) + came[part].astype(F32)).astype(BF)

        away = add(slice(count, 2 * count))
        stay = add(slice(0, count))
        came_next = self.send(away, count)
        parts = [
            (stay[k].astype(F32) + came_next[k].astype(F32)).astype(BF) for k in range(count)
        ]
        total = parts[0].astype(F32)
        for k in range(1, count):
            total = total + self.send(parts[k], k).astype(F32)
        return total

    def total(self, value):
        for k in range(self.bits):
            value = value + self.send(value, 1 << k)
        return value + self.swap(value)


def table_base(plan):
    return {"own": 0, "other": plan.slots, "core": 2 * plan.slots, "live": 2 * plan.slots + 1}


def mean(v):
    return jnp.mean(v, -1, keepdims=True)


def swap_lanes(v):
    lane = lax.broadcasted_iota(jnp.int32, v.shape, 1)
    return jnp.where(lane % 2 == 0, pltpu.roll(v, v.shape[1] - 1, 1), pltpu.roll(v, 1, 1))


def first_half(rows):
    return lax.broadcasted_iota(jnp.int32, (rows, 2 * HD), 1) < HD


def fetch_attention(plan, table, pieces, triple, mix, sems, rows, columns):
    base = table_base(plan)
    core = table[base["core"]]
    half_slots = plan.slots // 2
    third = columns // 3
    for h in (0, 1):
        for r in range(plan.slots):
            chip = table[base["own" if h == 0 else "other"] + r]
            piece = pieces[2 * h + r // half_slots].at[r % half_slots]
            if triple is not None:
                pltpu.make_async_copy(
                    piece.at[pl.ds(0, rows)],
                    triple.at[h, pl.ds(pl.multiple_of(chip * rows, 16), rows)],
                    sems.at[0, h],
                ).start()
            if mix is not None:
                for b in range(3):
                    pltpu.make_async_copy(
                        piece.at[pl.ds(rows, rows // 3), pl.ds(b * third, third)],
                        mix.at[
                            core ^ h,
                            pl.ds(pl.multiple_of(chip * rows + b * (rows // 3), 16), rows // 3),
                        ],
                        sems.at[1, h],
                    ).start()


def fetch_hidden(plan, table, pieces, weight, sems, rows, columns):
    base = table_base(plan)
    half_slots = plan.slots // 2
    across = plan.narrow // 2
    for h in (0, 1):
        for r in range(plan.slots):
            chip = table[base["own" if h == 0 else "other"] + r]
            down, over = chip // across, chip % across
            pltpu.make_async_copy(
                pieces[2 * h + r // half_slots].at[r % half_slots],
                weight.at[
                    h,
                    pl.ds(pl.multiple_of(down * rows, 16), rows),
                    pl.ds(pl.multiple_of(over * columns, 128), columns),
                ],
                sems.at[h],
            ).start()


def attention_kernel(plan, rows, table, x_ref, a, b, c, d, cos_ref, sin_ref, bias_ref, vec_ref,
                     own_ref, other_ref, p_own_ref, p_other_ref, context_ref, unit_ref, inv_ref,
                     low_ref, triple, mix, sems):
    base = table_base(plan)
    core, live = table[base["core"]], table[base["live"]]
    tokens, width = x_ref.shape
    half = width // 2
    fetch_attention(plan, table, (a, b, c, d), triple, mix, sems, rows, 3 * half)
    x = x_ref[...]
    cos, sin = cos_ref[...], sin_ref[...]
    left = first_half(tokens)
    valid = lax.broadcasted_iota(jnp.int32, (1, tokens), 1) < live
    scale = jnp.asarray(1.0 / math.sqrt(HD), BF)
    for h, (keep, probs) in enumerate(((own_ref, p_own_ref), (other_ref, p_other_ref))):
        drain(triple.at[h], sems.at[0, h])
        canonical = core ^ h
        bias = bias_ref[canonical]
        for q in range(half // 128):
            at = [slice(g * half + 128 * q, g * half + 128 * q + 128) for g in range(3)]
            out = [nn(x, triple[h, :, s]) + bias[:, s] for s in at]
            query, key = [(v * cos + swap_lanes(v) * sin).astype(BF) for v in out[:2]]
            value = out[2].astype(BF)
            for s, v in zip(at, (query, key, value)):
                keep[:, s] = v
            context = []
            for e in (0, 1):
                mine = left if e == 0 else ~left
                masked = jnp.where(mine, query, jnp.zeros_like(query)) * scale
                score = jnp.where(valid, nt(masked, key), -1e30)
                power = jnp.exp(score - jnp.max(score, -1, keepdims=True))
                prob = power * (1.0 / jnp.sum(power, -1, keepdims=True))
                prob = prob.astype(BF)
                probs[2 * q + e] = prob
                context.append(nn(prob, value))
            context_ref[:, pl.ds(pl.multiple_of(canonical * half + 128 * q, 128), 128)] = (
                jnp.where(left, context[0], context[1]).astype(BF)
            )
    for h in (0, 1):
        drain(mix.at[core ^ h], sems.at[1, h])
    context = context_ref[...]
    branch = jnp.concatenate([nn(context, mix[0]), nn(context, mix[1])], 1)
    summed = x.astype(F32) + (branch + vec_ref[0:1, :])
    centred = summed - mean(summed)
    inverse = lax.rsqrt(mean(centred * centred) + EPSILON)
    unit = centred * inverse
    unit_ref[...] = unit
    inv_ref[...] = jnp.broadcast_to(inverse, inv_ref.shape)
    low_ref[...] = (unit * vec_ref[1:2, :] + vec_ref[2:3, :]).astype(BF)


def up_kernel(plan, rows, columns, table, low_ref, a, b, c, d, bias_ref,
              own_ref, other_ref, slope_own_ref, slope_other_ref, weight, sems):
    fetch_hidden(plan, table, (a, b, c, d), weight, sems, rows, columns)
    core = table[table_base(plan)["core"]]
    low = low_ref[...]
    step = 256
    for h, (out, slope) in enumerate(((own_ref, slope_own_ref), (other_ref, slope_other_ref))):
        drain(weight.at[h], sems.at[h])
        bias = bias_ref[core ^ h]
        for k in range(out.shape[1] // step):
            s = slice(k * step, (k + 1) * step)
            up = nn(low, weight[h, :, s]) + bias[:, s]
            share = 0.5 * (1.0 + lax.erf(up * math.sqrt(0.5)))
            out[:, s] = (up * share).astype(BF)
            slope[:, s] = (
                share + up * jnp.exp(-0.5 * up * up) * (1.0 / math.sqrt(2.0 * math.pi))
            ).astype(BF)


def down_kernel(plan, rows, columns, table, act_own, act_other, a, b, c, d, unit_ref, cot_ref,
                vec_ref, out_ref, grad_ref, grad_low_ref, sums_ref, weight, sems):
    fetch_hidden(plan, table, (a, b, c, d), weight, sems, rows, columns)
    first = unit_ref[...] * vec_ref[1:2, :] + vec_ref[2:3, :]
    cot = cot_ref[...].astype(F32)
    scaled = cot * vec_ref[3:4, :]
    scaled_mean = mean(scaled)
    sums_ref[1:2, :] = jnp.sum(cot, 0, keepdims=True)
    drain(weight.at[0], sems.at[0])
    total = nt(act_own[...], weight[0])
    drain(weight.at[1], sems.at[1])
    total = total + nt(act_other[...], weight[1])
    summed = first + (total + vec_ref[5:6, :])
    centred = summed - mean(summed)
    inverse = lax.rsqrt(mean(centred * centred) + EPSILON)
    unit = centred * inverse
    grad = inverse * (scaled - scaled_mean - unit * mean(scaled * unit))
    grad_ref[...] = grad
    low = grad.astype(BF)
    grad_low_ref[...] = low
    sums_ref[0:1, :] = jnp.sum(cot * unit, 0, keepdims=True)
    sums_ref[2:3, :] = jnp.sum(low.astype(F32), 0, keepdims=True)
    out_ref[...] = (unit * vec_ref[3:4, :] + vec_ref[4:5, :]).astype(BF)


def grad_up_kernel(plan, rows, columns, table, low_ref, a, b, c, d, slope_own, slope_other,
                   own_ref, other_ref, sums_ref, weight, sems):
    fetch_hidden(plan, table, (a, b, c, d), weight, sems, rows, columns)
    low = low_ref[...]
    step = 256
    for h, (slope, out) in reversed(
        list(enumerate(((slope_own, own_ref), (slope_other, other_ref))))
    ):
        drain(weight.at[h], sems.at[h])
        for k in range(out.shape[1] // step):
            s = slice(k * step, (k + 1) * step)
            grad = (nn(low, weight[h, :, s]) * slope[:, s].astype(F32)).astype(BF)
            out[:, s] = grad
            sums_ref[h : h + 1, s] = jnp.sum(grad.astype(F32), 0, keepdims=True)


def hidden_grad_kernel(plan, rows, columns, table, left_own, left_other, right_own, right_other,
                       low_ref, high_ref, block, sems):
    base = table_base(plan)
    across, half_slots = plan.narrow // 2, plan.slots // 2
    a, b = left_own[...], left_other[...]
    for y in range(across):
        s = slice(y * columns, (y + 1) * columns)
        tile = tn(a, right_own[:, s]) + tn(b, right_other[:, s])
        block[:, y] = tile.astype(BF).reshape(plan.wide, rows, columns)
    for r in reversed(range(plan.slots)):
        chip = table[base["own"] + r]
        out = (low_ref, high_ref)[r // half_slots]
        pltpu.make_async_copy(
            block.at[chip // across, chip % across], out.at[r % half_slots], sems.at[r // half_slots]
        ).start()
    drain(high_ref, sems.at[1])
    drain(low_ref, sems.at[0])


def first_grad_kernel(plan, rows, columns, arows, table, gu_own, gu_other, a, b, c, d, e, f, g, k,
                      grad_ref, unit_ref, inv_ref, vec_ref, middle_ref, low_ref, context_ref,
                      sums_ref, weight, sems, mix, mix_sems):
    fetch_hidden(plan, table, (a, b, c, d), weight, sems, rows, columns)
    width = unit_ref.shape[1]
    fetch_attention(plan, table, (e, f, g, k), None, mix, mix_sems, arows, width // 2 * 3)
    core = table[table_base(plan)["core"]]
    drain(weight.at[0], sems.at[0])
    total = nt(gu_own[...], weight[0])
    drain(weight.at[1], sems.at[1])
    total = total + nt(gu_other[...], weight[1])
    grad = grad_ref[...] + total
    unit = unit_ref[...]
    scaled = grad * vec_ref[1:2, :]
    middle = inv_ref[:, 0:1] * (scaled - mean(scaled) - unit * mean(scaled * unit))
    low = middle.astype(BF)
    middle_ref[...] = middle
    low_ref[...] = low
    sums_ref[0:1, :] = jnp.sum(grad * unit, 0, keepdims=True)
    sums_ref[1:2, :] = jnp.sum(grad, 0, keepdims=True)
    sums_ref[2:3, :] = jnp.sum(low.astype(F32), 0, keepdims=True)
    for h in (0, 1):
        drain(mix.at[core ^ h], mix_sems.at[1, h])
    half = width // 2
    context_ref[...] = (nt(low[:, :half], mix[0]) + nt(low[:, half:], mix[1])).astype(BF)


def attention_grad_kernel(plan, h, table, keep_ref, probs_ref, grad_ref, cos_ref, sin_ref,
                          out_ref, sums_ref):
    core = table[table_base(plan)["core"]]
    tokens, width = grad_ref.shape
    half = width // 2
    cos, sin = cos_ref[...], sin_ref[...]
    left = first_half(tokens)
    scale = 1.0 / math.sqrt(HD)
    for q in range(half // 128):
        at = [slice(g * half + 128 * q, g * half + 128 * q + 128) for g in range(3)]
        query, key, value = [keep_ref[:, s] for s in at]
        came = grad_ref[:, pl.ds(pl.multiple_of((core ^ h) * half + 128 * q, 128), 128)]
        parts = []
        for e in (0, 1):
            mine = left if e == 0 else ~left
            low = probs_ref[2 * q + e]
            prob = low.astype(F32)
            grad = nt(jnp.where(mine, came, jnp.zeros_like(came)), value)
            score = prob * (grad - jnp.sum(prob * grad, -1, keepdims=True))
            score = score.astype(BF)
            parts.append((nn(score, key), tn(score, query), tn(low, came)))
        grads = [jnp.where(left, u, v) for u, v in zip(*parts)]
        grads = [(g * scale) * cos + swap_lanes((g * scale) * sin) for g in grads[:2]] + grads[2:]
        for s, g in zip(at, grads):
            g = g.astype(BF)
            out_ref[:, s] = g
            sums_ref[:, s] = jnp.sum(g.astype(F32), 0, keepdims=True)


def attention_weight_kernel(plan, rows, table, xt_ref, g_own, g_other, ct_ref, b_own, b_other,
                            low_ref, high_ref, block, mixed, sems):
    base = table_base(plan)
    half_slots = plan.slots // 2
    tokens, columns = g_own.shape
    third = columns // 3
    block[...] = (
        (nn(xt_ref[:, :tokens], g_own[...]) + nn(xt_ref[:, tokens:], g_other[...]))
        .astype(BF)
        .reshape(block.shape)
    )
    mixed[...] = (
        (nn(ct_ref[:, :tokens], b_own[...]) + nn(ct_ref[:, tokens:], b_other[...]))
        .astype(BF)
        .reshape(mixed.shape)
    )
    for r in reversed(range(plan.slots)):
        chip = table[base["own"] + r]
        out, at = (low_ref, high_ref)[r // half_slots], r % half_slots
        sem = sems.at[r // half_slots]
        pltpu.make_async_copy(block.at[chip], out.at[at, pl.ds(0, rows)], sem).start()
        for b in range(3):
            pltpu.make_async_copy(
                mixed.at[chip, b],
                out.at[at, pl.ds(rows, rows // 3), pl.ds(b * third, third)],
                sem,
            ).start()
    drain(high_ref, sems.at[1])
    drain(low_ref, sems.at[0])


def input_grad_kernel(plan, rows, table, middle_ref, g_own, g_other, a, b, c, d, out_ref,
                      triple, sems):
    width = middle_ref.shape[1]
    fetch_attention(plan, table, (a, b, c, d), triple, None, sems, rows, width // 2 * 3)
    drain(triple.at[0], sems.at[0, 0])
    total = nt(g_own[...], triple[0])
    drain(triple.at[1], sems.at[0, 1])
    total = total + nt(g_other[...], triple[1])
    out_ref[...] = (middle_ref[...] + total).astype(BF)


def half_tables(tokens):
    position = jnp.arange(tokens, dtype=F32)
    column = jnp.arange(2 * HD, dtype=jnp.int32)
    pair = (column % HD // 2).astype(F32)
    angle = position[:, None] * jnp.exp(pair * (-2.0 / HD) * math.log(10000.0))[None, :]
    parity = (column % 2).astype(F32) * 2.0 - 1.0
    return jnp.cos(angle), jnp.sin(angle) * parity[None, :]


def fast_body(
    plan,
    inputs,
    lengths,
    triple_weight,
    triple_bias,
    mix_weight,
    mix_bias,
    first_gain,
    first_shift,
    up_weight,
    up_bias,
    down_weight,
    down_bias,
    second_gain,
    second_shift,
    cotangent,
):
    tokens, width = inputs.shape
    half = width // 2
    devices, wide, narrow = plan.devices, plan.wide, plan.narrow
    index = lax.axis_index(AXES)
    core = index & 1
    of_wide, of_narrow = lax.axis_index("wide"), lax.axis_index("narrow")
    own_chips, other_chips = plan.chips(index)
    table = jnp.concatenate([own_chips, other_chips, core[None], lengths]).astype(jnp.int32)
    hidden = up_weight.shape[1]
    tile_rows = up_weight.shape[0]
    piece = triple_weight.shape[0]
    rows = 2 * piece
    slots, half_slots = plan.slots, plan.slots // 2

    def by_core(pair):
        mine = jnp.where(core == 0, pair[0], pair[1])
        theirs = jnp.where(core == 0, pair[1], pair[0])
        return mine, theirs

    def in_order(mine, theirs, axis):
        return jnp.where(
            core == 0,
            jnp.concatenate([mine, theirs], axis),
            jnp.concatenate([theirs, mine], axis),
        )

    columns = triple_weight.reshape(piece, 3, 2, half).transpose(2, 0, 1, 3)
    columns = columns.reshape(2, piece, 3 * half)
    joined = jnp.concatenate(
        [columns, mix_weight.reshape(piece, 2, half).transpose(1, 0, 2)], 2
    )
    mine, theirs = by_core(joined)
    chip_rows = in_order(mine, plan.swap(theirs), 0)
    mix_part = chip_rows[:, 3 * half :].reshape(3, rows // 3, half)
    mix_part = mix_part.transpose(1, 0, 2).reshape(rows // 3, 3 * half)
    payload = jnp.concatenate([chip_rows[:, : 3 * half], mix_part], 0)[None]
    attention = plan.gather(payload)
    ups = plan.gather(up_weight[None])
    downs = plan.gather(down_weight.T[None])

    up_share, down_share = hidden // wide, down_bias.shape[0] // narrow
    shares = jnp.concatenate(
        [
            triple_bias,
            mix_bias,
            first_gain,
            first_shift,
            second_gain,
            second_shift,
            lax.dynamic_slice(up_bias, (of_wide * up_share,), (up_share,)),
            lax.dynamic_slice(down_bias, (of_narrow * down_share,), (down_share,)),
        ]
    )
    size = shares.shape[0]
    padded = -(-size // 128) * 128
    shares = jnp.pad(shares, (0, padded - size))
    rows_at = jnp.arange(devices, dtype=jnp.int32)[:, None] == index
    vectors = plan.total(jnp.where(rows_at, shares[None, :], jnp.zeros_like(shares)[None, :]))
    vectors = vectors.astype(F32)
    at, found = 0, []
    for count in (3 * piece, piece, piece, piece, piece, piece, up_share, down_share):
        found.append(vectors[:, at : at + count])
        at += count
    bias_halves = found[0].reshape(3, 2, half).transpose(1, 0, 2).reshape(2, 1, 3 * half)
    up_halves = found[6].reshape(wide, narrow // 2, 2, up_share).transpose(2, 1, 0, 3)
    up_halves = up_halves.reshape(2, 1, hidden * narrow // 2)
    vecs = jnp.stack([v.reshape(width) for v in found[1:6] + found[7:8]])
    vecs = jnp.pad(vecs, ((0, 2), (0, 0)))
    cos, sin = half_tables(tokens)
    inputs_t = jnp.concatenate([inputs.T, plan.swap(inputs).T], 1)

    flops = 2.0 * tokens * width * width
    hidden_half = hidden * narrow // 2
    own, other, p_own, p_other, context, unit, inv, low = call(
        functools.partial(attention_kernel, plan, rows),
        [
            shape((tokens, 3 * half)),
            shape((tokens, 3 * half)),
            shape((half // HD, tokens, tokens)),
            shape((half // HD, tokens, tokens)),
            shape((tokens, width)),
            shape((tokens, width), F32),
            shape((tokens, 128), F32),
            shape((tokens, width)),
        ],
        [SCALARS, WHOLE] + [LEFT] * 4 + [WHOLE] * 4,
        [
            VMEM((2, width, 3 * half), BF),
            VMEM((2, width, half), BF),
            pltpu.SemaphoreType.DMA((2, 2)),
        ],
        (table, inputs, *attention, cos, sin, bias_halves, vecs),
        8 * flops,
        48,
    )
    hidden_scratch = [
        VMEM((2, width, hidden_half), BF),
        pltpu.SemaphoreType.DMA((2,)),
    ]
    act_own, act_other, slope_own, slope_other = call(
        functools.partial(up_kernel, plan, tile_rows, hidden),
        [shape((tokens, hidden_half))] * 4,
        [SCALARS, WHOLE] + [LEFT] * 4 + [WHOLE],
        hidden_scratch,
        (table, low, *ups, up_halves),
        8 * flops,
        48,
    )
    context_came, low_came, act_came = plan.swap(context), plan.swap(low), plan.swap(act_other)
    outputs, grad_second, grad_down, sums_second = call(
        functools.partial(down_kernel, plan, tile_rows, hidden),
        [
            shape((tokens, width)),
            shape((tokens, width), F32),
            shape((tokens, width)),
            shape((3, width), F32),
        ],
        [SCALARS, WHOLE, WHOLE] + [LEFT] * 4 + [WHOLE] * 3,
        hidden_scratch,
        (table, act_own, act_other, *downs, unit, cotangent, vecs),
        4 * flops,
        48,
    )
    grad_down_came = plan.swap(grad_down)
    gu_own, gu_other, sums_up = call(
        functools.partial(grad_up_kernel, plan, tile_rows, hidden),
        [shape((tokens, hidden_half))] * 2 + [shape((2, hidden_half), F32)],
        [SCALARS, WHOLE] + [LEFT] * 4 + [WHOLE] * 2,
        hidden_scratch,
        (table, grad_down, *downs, slope_own, slope_other),
        4 * flops,
        48,
    )
    gu_came = plan.swap(gu_other)

    def hidden_grad(left, left_came, right, right_came):
        return call(
            functools.partial(hidden_grad_kernel, plan, tile_rows, hidden),
            [shape((half_slots, tile_rows, hidden))] * 2,
            [SCALARS] + [WHOLE] * 4,
            [VMEM((wide, narrow // 2, tile_rows, hidden), BF), pltpu.SemaphoreType.DMA((2,))],
            (table, left, left_came, right, right_came),
            4 * flops,
            48,
            [LEFT] * 2,
        )

    down_total = plan.scatter(*hidden_grad(grad_down, grad_down_came, act_own, act_came))
    grad_middle, grad_branch, grad_context, sums_first = call(
        functools.partial(first_grad_kernel, plan, tile_rows, hidden, rows),
        [
            shape((tokens, width), F32),
            shape((tokens, width)),
            shape((tokens, width)),
            shape((3, width), F32),
        ],
        [SCALARS, WHOLE, WHOLE] + [LEFT] * 8 + [WHOLE] * 4,
        hidden_scratch
        + [VMEM((2, width, half), BF), pltpu.SemaphoreType.DMA((2, 2))],
        (table, gu_own, gu_other, *ups, *attention, grad_second, unit, inv, vecs),
        5 * flops,
        48,
    )
    branch_mine, branch_theirs = by_core((grad_branch[:, :half], grad_branch[:, half:]))
    branch_came = plan.swap(branch_theirs)
    up_total = plan.scatter(*hidden_grad(low, low_came, gu_own, gu_came))
    context_t = jnp.concatenate([context.T, context_came.T], 1)

    def attention_grad(h, keep, probs):
        return call(
            functools.partial(attention_grad_kernel, plan, h),
            [shape((tokens, 3 * half)), shape((1, 3 * half), F32)],
            [SCALARS] + [WHOLE] * 5,
            [],
            (table, keep, probs, grad_context, cos, sin),
            2 * flops,
            48,
        )

    gt_other, bias_other = attention_grad(1, other, p_other)
    gt_came = plan.swap(gt_other)
    gt_own, bias_own = attention_grad(0, own, p_own)
    packed = call(
        functools.partial(attention_weight_kernel, plan, rows),
        [shape((half_slots, rows + rows // 3, 3 * half))] * 2,
        [SCALARS] + [WHOLE] * 6,
        [
            VMEM((slots, rows, 3 * half), BF),
            VMEM((slots, 3, rows // 3, half), BF),
            pltpu.SemaphoreType.DMA((2,)),
        ],
        (table, inputs_t, gt_own, gt_came, context_t, branch_mine, branch_came),
        4 * flops,
        48,
        [LEFT] * 2,
    )
    attention_total = plan.scatter(*packed)
    (input_grad,) = call(
        functools.partial(input_grad_kernel, plan, rows),
        [shape((tokens, width))],
        [SCALARS, WHOLE, WHOLE, WHOLE] + [LEFT] * 4,
        [VMEM((2, width, 3 * half), BF), pltpu.SemaphoreType.DMA((2, 2))],
        (table, grad_middle, gt_own, gt_other, *attention),
        3 * flops,
        48,
    )

    bias_grad = in_order(bias_own, bias_other, 0).reshape(2, 3, half).transpose(1, 0, 2)
    up_grad = jnp.where(core == 0, sums_up, sums_up[::-1])
    up_grad = up_grad.reshape(2, narrow // 2, hidden).transpose(1, 0, 2)
    flat = jnp.concatenate(
        [
            bias_grad.reshape(-1),
            sums_first[2],
            sums_first[0],
            sums_first[1],
            up_grad.reshape(-1),
            sums_second[2],
            sums_second[0],
            sums_second[1],
        ]
    )
    flat = plan.total(flat.reshape(-1, 128)).reshape(-1)
    places = [0]
    for count in (3 * width, width, width, width, hidden * narrow, width, width):
        places.append(places[-1] + count)

    def share(which, at, count):
        return lax.dynamic_slice(flat, (places[which] + at * count,), (count,))

    mix_rows = attention_total[rows:].reshape(rows // 3, 3, half).transpose(1, 0, 2)
    chip_grads = jnp.concatenate([attention_total[:rows], mix_rows.reshape(rows, half)], 1)
    mine, theirs = by_core((chip_grads[:piece], chip_grads[piece:]))
    came = plan.swap(theirs)
    pair = in_order(mine[None], came[None], 0)
    triple_grad = pair[:, :, : 3 * half].reshape(2, piece, 3, half).transpose(1, 2, 0, 3)
    mix_grad = pair[:, :, 3 * half :].transpose(1, 0, 2)
    return (
        outputs,
        input_grad,
        triple_grad.reshape(piece, 3 * width),
        share(0, index, 3 * piece),
        mix_grad.reshape(piece, width),
        share(1, index, piece),
        share(2, index, piece),
        share(3, index, piece),
        up_total,
        share(4, of_narrow, hidden),
        down_total.T,
        share(5, of_wide, down_bias.shape[0]),
        share(6, index, piece),
        share(7, index, piece),
    )


def fits(plan_shape, width, hidden):
    wide, narrow = plan_shape
    powers = all(n >= 4 and n & (n - 1) == 0 for n in (wide, narrow)) and narrow == 4
    return (
        powers
        and width % (wide * 16) == 0
        and width % (wide * narrow // 2 * 48) == 0
        and hidden % (narrow * 128) == 0
        and width % 768 == 0
    )


def solution(mesh):
    placed = (
        P(("wide", "narrow"), None),
        P(("wide", "narrow")),
        P(("wide", "narrow"), None),
        P(("wide", "narrow")),
        P(("wide", "narrow"), None),
        P(("wide", "narrow")),
        P(("wide", "narrow")),
        P(("wide", "narrow")),
        P("wide", "narrow"),
        P("narrow"),
        P("narrow", "wide"),
        P("wide"),
        P(("wide", "narrow")),
        P(("wide", "narrow")),
        P(("wide", "narrow"), None),
    )
    wide, narrow = mesh.shape["wide"], mesh.shape["narrow"]

    def layer(*arrays):
        rows, hidden = arrays[8].shape
        if fits((wide, narrow), rows * wide, hidden * narrow):
            return fast_body(Plan(wide, narrow), *arrays)
        return body(*arrays)

    return jax.shard_map(
        layer,
        mesh=mesh,
        in_specs=placed,
        out_specs=(
            P(("wide", "narrow"), None),
            P(("wide", "narrow"), None),
            P(("wide", "narrow"), None),
            P(("wide", "narrow")),
            P(("wide", "narrow"), None),
            P(("wide", "narrow")),
            P(("wide", "narrow")),
            P(("wide", "narrow")),
            P("wide", "narrow"),
            P("narrow"),
            P("narrow", "wide"),
            P("wide"),
            P(("wide", "narrow")),
            P(("wide", "narrow")),
        ),
        check_vma=False,
    )
```

```python
import functools
import math

import jax
import jax.numpy as jnp
import numpy as np
from jax import lax
from jax.experimental import pallas as pl
from jax.experimental.pallas import tpu as pltpu
from jax.sharding import PartitionSpec as P

H = 12
HD = 64


EPSILON = 1e-06


def tables(token_rows, width, head):
    position = jnp.arange(token_rows, dtype=jnp.float32)
    column = jnp.arange(width, dtype=jnp.int32)
    pair_index = (column % head // 2).astype(jnp.float32)
    frequency = jnp.exp(pair_index * (-2.0 / head) * math.log(10000.0))
    angle = position[:, None] * frequency[None, :]
    parity = (column % 2).astype(jnp.float32) * 2.0 - 1.0
    return (jnp.cos(angle), jnp.sin(angle) * parity[None, :])


def swapped(values):
    shape = values.shape
    paired = values.reshape(shape[:-1] + (shape[-1] // 2, 2))
    return paired[..., ::-1].reshape(shape)


def rotate(values, cosine, sine):
    return values * cosine + swapped(values) * sine


def unrotate(grad, cosine, sine):
    return grad * cosine + swapped(grad * sine)


def normalize_forward(values, gain, shift):
    mean_row = jnp.mean(values, -1, keepdims=True)
    centred = values - mean_row
    inverse = lax.rsqrt(jnp.mean(centred * centred, -1, keepdims=True) + EPSILON)
    unit = centred * inverse
    return (unit * gain + shift, unit, inverse)


def normalize_backward(grad, unit, inverse, gain):
    scaled = grad * gain
    inner = (
        scaled
        - jnp.mean(scaled, -1, keepdims=True)
        - unit * jnp.mean(scaled * unit, -1, keepdims=True)
    )
    return (inner * inverse, jnp.sum(grad * unit, 0), jnp.sum(grad, 0))


def gelu_exact(values):
    return jax.nn.gelu(values, approximate=False)


def gelu_backward(upward, grad_active):
    unused, pull_back = jax.vjp(gelu_exact, upward)
    return pull_back(grad_active)[0]


def softmax_block(query_block, key, valid, scale):
    scores = (
        jnp.einsum("qhd,khd->hqk", query_block, key, preferred_element_type=jnp.float32) * scale
    )
    scores = jnp.where(valid[None, None, :], scores, -1e30)
    return jax.nn.softmax(scores, axis=-1)


def attention_forward(query, key, value, valid, scale):
    token_rows = query.shape[0]
    block = min(512, token_rows)
    weights_block = softmax_block(query, key, valid, scale)
    context = jnp.einsum(
        "hqk,khd->qhd",
        weights_block.astype(jnp.bfloat16),
        value,
        preferred_element_type=jnp.float32,
    )
    pieces = context.reshape(block, -1).astype(jnp.bfloat16)
    return pieces


def attention_backward(query, key, value, grad_context, valid, scale):
    weights_block = softmax_block(query, key, valid, scale)
    grad_weights = jnp.einsum(
        "qhd,khd->hqk", grad_context, value, preferred_element_type=jnp.float32
    )
    inner = weights_block * (
        grad_weights - jnp.sum(weights_block * grad_weights, -1, keepdims=True)
    )
    inner_low = inner.astype(jnp.bfloat16)
    query_pieces = (
        jnp.einsum("hqk,khd->qhd", inner_low, key, preferred_element_type=jnp.float32) * scale
    )
    grad_key = (
        jnp.einsum("hqk,qhd->khd", inner_low, query, preferred_element_type=jnp.float32) * scale
    )
    grad_value = jnp.einsum(
        "hqk,qhd->khd",
        weights_block.astype(jnp.bfloat16),
        grad_context,
        preferred_element_type=jnp.float32,
    )
    return (query_pieces, grad_key, grad_value)


def body(
    inputs,
    lengths,
    triple_weight,
    triple_bias,
    mix_weight,
    mix_bias,
    first_gain,
    first_shift,
    up_weight,
    up_bias,
    down_weight,
    down_bias,
    second_gain,
    second_shift,
    cotangent,
):
    token_rows, width = inputs.shape
    scale = 1.0 / math.sqrt(HD)
    head_shape = (token_rows, H, HD)
    (
        triple_full,
        mix_full,
        triple_bias_full,
        mix_bias_full,
        gain_one,
        shift_one,
        gain_two,
        shift_two,
    ) = (
        lax.all_gather(triple_weight, ("wide", "narrow"), axis=0, tiled=True),
        lax.all_gather(mix_weight, ("wide", "narrow"), axis=0, tiled=True),
        lax.all_gather(triple_bias, ("wide", "narrow"), axis=0, tiled=True),
        lax.all_gather(mix_bias, ("wide", "narrow"), axis=0, tiled=True),
        lax.all_gather(first_gain, ("wide", "narrow"), axis=0, tiled=True),
        lax.all_gather(first_shift, ("wide", "narrow"), axis=0, tiled=True),
        lax.all_gather(second_gain, ("wide", "narrow"), axis=0, tiled=True),
        lax.all_gather(second_shift, ("wide", "narrow"), axis=0, tiled=True),
    )
    up_rows, down_columns, down_bias_full = (
        lax.all_gather(up_weight, "wide", axis=0, tiled=True),
        lax.all_gather(down_weight, "wide", axis=1, tiled=True),
        lax.all_gather(down_bias, "wide", axis=0, tiled=True),
    )
    gain_one = gain_one.astype(jnp.float32)
    gain_two = gain_two.astype(jnp.float32)
    cosine, sine = tables(token_rows, width, HD)
    valid = jnp.arange(token_rows, dtype=jnp.int32) < lengths[0]
    triple = jnp.dot(
        inputs, triple_full, preferred_element_type=jnp.float32
    ) + triple_bias_full.astype(jnp.float32)
    query = rotate(triple[:, :width], cosine, sine).astype(jnp.bfloat16).reshape(head_shape)
    key = (
        rotate(triple[:, width : 2 * width], cosine, sine).astype(jnp.bfloat16).reshape(head_shape)
    )
    value = triple[:, 2 * width :].astype(jnp.bfloat16).reshape(head_shape)
    context = attention_forward(query, key, value, valid, scale)
    branch = jnp.dot(context, mix_full, preferred_element_type=jnp.float32) + mix_bias_full.astype(
        jnp.float32
    )
    first, first_unit, first_inverse = normalize_forward(
        inputs.astype(jnp.float32) + branch, gain_one, shift_one.astype(jnp.float32)
    )
    first_low = first.astype(jnp.bfloat16)
    gathered = lax.all_gather(first_low, "narrow", axis=0, tiled=True)
    upward = jnp.dot(gathered, up_rows, preferred_element_type=jnp.float32) + up_bias.astype(
        jnp.float32
    )
    active = gelu_exact(upward).astype(jnp.bfloat16)
    downward = lax.psum_scatter(
        jnp.dot(active, down_columns, preferred_element_type=jnp.float32).astype(jnp.bfloat16),
        "narrow",
        scatter_dimension=0,
        tiled=True,
    ).astype(jnp.float32)
    downward = downward + down_bias_full.astype(jnp.float32)
    result, second_unit, second_inverse = normalize_forward(
        first + downward, gain_two, shift_two.astype(jnp.float32)
    )
    outputs = result.astype(jnp.bfloat16)
    grad_second, second_gain_grad, second_shift_grad = normalize_backward(
        cotangent.astype(jnp.float32), second_unit, second_inverse, gain_two
    )
    grad_down = grad_second.astype(jnp.bfloat16)
    grad_gathered = lax.all_gather(grad_down, "narrow", axis=0, tiled=True)
    grad_active = jnp.dot(grad_gathered, down_columns.T, preferred_element_type=jnp.float32)
    grad_up = gelu_backward(upward, grad_active).astype(jnp.bfloat16)
    grad_feed = lax.psum_scatter(
        jnp.dot(grad_up, up_rows.T, preferred_element_type=jnp.float32).astype(jnp.bfloat16),
        "narrow",
        scatter_dimension=0,
        tiled=True,
    ).astype(jnp.float32)
    up_part = jnp.dot(gathered.T, grad_up, preferred_element_type=jnp.float32)
    down_part = jnp.dot(active.T, grad_gathered, preferred_element_type=jnp.float32)
    down_bias_part = jnp.sum(grad_gathered, 0, dtype=jnp.float32)
    up_weight_grad, down_weight_grad, down_bias_grad = (
        lax.psum_scatter(
            up_part.astype(jnp.bfloat16), "wide", scatter_dimension=0, tiled=True
        ).astype(jnp.float32),
        lax.psum_scatter(
            down_part.astype(jnp.bfloat16), "wide", scatter_dimension=1, tiled=True
        ).astype(jnp.float32),
        lax.psum_scatter(
            down_bias_part.astype(jnp.bfloat16), "wide", scatter_dimension=0, tiled=True
        ).astype(jnp.float32),
    )
    up_bias_grad = lax.psum(jnp.sum(grad_up, 0, dtype=jnp.float32), "wide")
    grad_first = grad_second + grad_feed
    grad_middle, first_gain_grad, first_shift_grad = normalize_backward(
        grad_first, first_unit, first_inverse, gain_one
    )
    grad_branch = grad_middle.astype(jnp.bfloat16)
    mix_weight_grad = jnp.dot(context.T, grad_branch, preferred_element_type=jnp.float32)
    mix_bias_grad = jnp.sum(grad_branch, 0, dtype=jnp.float32)
    triple_back, mix_back = (
        lax.all_gather(triple_weight, ("wide", "narrow"), axis=0, tiled=True),
        lax.all_gather(mix_weight, ("wide", "narrow"), axis=0, tiled=True),
    )
    grad_context = (
        jnp.dot(grad_branch, mix_back.T, preferred_element_type=jnp.float32)
        .astype(jnp.bfloat16)
        .reshape(head_shape)
    )
    grad_query, grad_key, grad_value = attention_backward(
        query, key, value, grad_context, valid, scale
    )
    grad_triple = jnp.concatenate(
        [
            unrotate(grad_query.reshape(token_rows, width), cosine, sine),
            unrotate(grad_key.reshape(token_rows, width), cosine, sine),
            grad_value.reshape(token_rows, width),
        ],
        1,
    ).astype(jnp.bfloat16)
    triple_local = jnp.dot(inputs.T, grad_triple, preferred_element_type=jnp.float32)
    triple_bias_local = jnp.sum(grad_triple, 0, dtype=jnp.float32)
    grad_inputs = grad_middle + jnp.dot(
        grad_triple, triple_back.T, preferred_element_type=jnp.float32
    )
    summed = (
        lax.psum_scatter(triple_local, ("wide", "narrow"), scatter_dimension=0, tiled=True),
        lax.psum_scatter(mix_weight_grad, ("wide", "narrow"), scatter_dimension=0, tiled=True),
        lax.psum_scatter(triple_bias_local, ("wide", "narrow"), scatter_dimension=0, tiled=True),
        lax.psum_scatter(mix_bias_grad, ("wide", "narrow"), scatter_dimension=0, tiled=True),
        lax.psum_scatter(first_gain_grad, ("wide", "narrow"), scatter_dimension=0, tiled=True),
        lax.psum_scatter(first_shift_grad, ("wide", "narrow"), scatter_dimension=0, tiled=True),
        lax.psum_scatter(second_gain_grad, ("wide", "narrow"), scatter_dimension=0, tiled=True),
        lax.psum_scatter(second_shift_grad, ("wide", "narrow"), scatter_dimension=0, tiled=True),
    )
    return (
        outputs,
        grad_inputs.astype(jnp.bfloat16),
        summed[0],
        summed[2],
        summed[1],
        summed[3],
        summed[4],
        summed[5],
        up_weight_grad,
        up_bias_grad,
        down_weight_grad,
        down_bias_grad,
        summed[6],
        summed[7],
    )


VMEM = pltpu.VMEM
SMEM = pltpu.SMEM
BF = jnp.bfloat16
F32 = jnp.float32
AXES = ("wide", "narrow")
WHOLE = pl.BlockSpec(memory_space=VMEM)
SCALARS = pl.BlockSpec(memory_space=SMEM)
LEFT = pl.BlockSpec(memory_space=pltpu.HBM)


def nn(a, b):
    return lax.dot_general(a, b, (((1,), (0,)), ((), ())), preferred_element_type=F32)


def nt(a, b):
    return lax.dot_general(a, b, (((1,), (1,)), ((), ())), preferred_element_type=F32)


def tn(a, b):
    return lax.dot_general(a, b, (((0,), (0,)), ((), ())), preferred_element_type=F32)


def shape(dims, dtype=BF):
    return jax.ShapeDtypeStruct(dims, dtype)


class Load:
    def __init__(self, source, held, sem):
        self.copy = pltpu.make_async_copy(source, held, sem)
        self.held, self.waited = held, False
        self.shape = held.shape
        self.copy.start()

    def __call__(self):
        if not self.waited:
            self.copy.wait()
            self.waited = True
        return self.held


def call(kernel, outs, operands, kinds, scratch, flops, megabytes, out_specs=None):
    specs = {"s": SCALARS, "v": WHOLE, "h": LEFT, "l": LEFT}
    loads = [k for k, kind in enumerate(kinds) if kind == "l"]
    held = [VMEM(operands[k].shape, operands[k].dtype) for k in loads]
    assert len(kinds) == len(operands)

    def whole(*refs):
        refs = list(refs)
        count = len(loads)
        if count:
            sems = refs.pop()
            buffers, refs = refs[-count:], refs[:-count]
            for n, k in enumerate(loads):
                refs[k] = Load(refs[k], buffers[n], sems.at[n])
        kernel(*refs)
        for k in loads:
            refs[k]()

    return pl.pallas_call(
        whole,
        out_shape=outs,
        in_specs=[specs[kind] for kind in kinds],
        out_specs=[WHOLE] * len(outs) if out_specs is None else out_specs,
        scratch_shapes=list(scratch)
        + held
        + ([pltpu.SemaphoreType.DMA((len(loads),))] if loads else []),
        compiler_params=pltpu.CompilerParams(vmem_limit_bytes=megabytes << 20),
        cost_estimate=pl.CostEstimate(
            flops=int(flops), bytes_accessed=1, transcendentals=0
        ),
    )(*operands)


def drain(ref, sem):
    pltpu.make_async_copy(ref, ref, sem).wait()


class Plan:
    def __init__(self, wide, narrow):
        self.wide, self.narrow = wide, narrow
        self.devices = wide * narrow
        x, y = narrow, narrow // 2
        self.last, self.first = (y, x), (x, y)
        self.far = wide // 2
        self.line = self.devices // self.far
        self.slots = 4 * self.far

    def over(self, core, slot):
        mask = self.first[core] if slot // self.far & 1 else 0
        return mask ^ (self.last[core] if slot // self.far & 2 else 0)

    def chips(self, device):
        core = device & 1
        return [
            (device ^ (r % self.far * self.line) ^ self.over(c, r)) >> 1
            for c in (core, core ^ 1)
            for r in range(self.slots)
        ]

    def table(self, index, live):
        chips = np.array([self.chips(i) for i in range(self.devices)], np.int32)
        mine = lax.dynamic_slice(jnp.asarray(chips), (index, 0), (1, chips.shape[1]))[0]
        return jnp.concatenate([mine, (index & 1)[None].astype(jnp.int32), live])

    def own(self, table, slot):
        return table[slot]

    def other(self, table, slot):
        return table[self.slots + slot]

    def core(self, table):
        return table[2 * self.slots]

    def live(self, table):
        return table[2 * self.slots + 1]

    def permute(self, value, masks):
        return lax.ppermute(value, AXES, [(i, i ^ masks[i & 1]) for i in range(self.devices)])

    def swap(self, value):
        return self.permute(value, (1, 1))

    def lines(self):
        return [[i + self.line * k for k in range(self.far)] for i in range(self.line)]

    def gather_far(self, value):
        masks = [(m * self.line, m * self.line) for m in range(1, self.far)]
        return [value] + [self.permute(value, m) for m in masks]

    def send_far(self, parts):
        masks = [(m * self.line, m * self.line) for m in range(1, self.far)]
        return [self.permute(v, m) for v, m in zip(parts[1:], masks)]


def added(low, came):
    return (low.astype(F32) + came.astype(F32)).astype(BF)


def halves(low, came):
    count = low.shape[0] // 2
    return added(low[:count], came[:count]), added(low[count:], came[count:])


def together(*lists):
    flat = list(lax.optimization_barrier(tuple(v for values in lists for v in values)))
    return [[flat.pop(0) for _ in values] for values in lists]


def after_all(values, *others):
    return lax.optimization_barrier(tuple(values) + others)[: len(values)]


def after(value, *others):
    return lax.optimization_barrier((value,) + others)[0] if others else value


def mean(v):
    return jnp.mean(v, -1, keepdims=True)


def swap_lanes(v):
    lane = lax.broadcasted_iota(jnp.int32, v.shape, 1)
    return jnp.where(lane % 2 == 0, pltpu.roll(v, v.shape[1] - 1, 1), pltpu.roll(v, 1, 1))


def first_half(rows):
    return lax.broadcasted_iota(jnp.int32, (rows, 2 * HD), 1) < HD


def fetch_attention(plan, table, h, pieces, triple, mix, sems, rows):
    core = plan.core(table)
    half_slots = plan.slots // 2
    third = rows // 3
    columns = pieces[2].shape[2]
    for r in range(plan.slots):
        chip = (plan.own, plan.other)[h](table, r)
        side, at = divmod(r, half_slots)
        first, second = pieces[side].at[at], pieces[2 + side].at[at]
        if triple is not None:
            pltpu.make_async_copy(
                first.at[:, pl.ds(0, columns)],
                triple.at[pl.ds(pl.multiple_of(chip * rows, 16), 2 * third)],
                sems.at[0],
            ).start()
            pltpu.make_async_copy(
                second.at[pl.ds(0, third)],
                triple.at[pl.ds(pl.multiple_of(chip * rows + 2 * third, 16), third)],
                sems.at[0],
            ).start()
        if mix is not None:
            for b in range(3):
                pltpu.make_async_copy(
                    second.at[pl.ds(third, third), pl.ds(b * columns // 3, columns // 3)],
                    mix.at[core ^ h, pl.ds(pl.multiple_of(chip * rows + b * third, 16), third)],
                    sems.at[h],
                ).start()


def fetch_hidden(plan, table, pieces, weight, sems, rows, columns):
    half_slots = plan.slots // 2
    across = plan.narrow // 2
    for h in (0, 1):
        for r in range(plan.slots):
            chip = (plan.own, plan.other)[h](table, r)
            down, over = chip // across, chip % across
            pltpu.make_async_copy(
                pieces[2 * h + r // half_slots].at[r % half_slots],
                weight.at[
                    h,
                    pl.ds(pl.multiple_of(down * rows, 16), rows),
                    pl.ds(pl.multiple_of(over * columns, 128), columns),
                ],
                sems.at[h],
            ).start()


TRIPLE, MIX, GAIN1, SHIFT1, GAIN2, SHIFT2, UP = 0, 3, 4, 5, 6, 7, 8
TABLE_ROWS = 16
SHARE = 128


def split_kernel(plan, index_ref, triple_ref, mix_ref, tb_ref, mb_ref, g1_ref, s1_ref, g2_ref,
                 s2_ref, ub_ref, db_ref, mine_ref, share_ref, theirs_ref, spread):
    index = index_ref[0]
    core = index % 2
    of_wide, of_narrow = index // plan.narrow, index % plan.narrow
    triple, mix = triple_ref(), mix_ref()
    width = mix.shape[1]
    half = width // 2
    for out, h in ((mine_ref, core), (theirs_ref, core ^ 1)):
        for g in range(3):
            at = pl.multiple_of(g * width + h * half, 128)
            out[:, g * half : (g + 1) * half] = triple[:, pl.ds(at, half)]
        out[:, 3 * half : 4 * half] = mix[:, pl.ds(pl.multiple_of(h * half, 128), half)]

    spread[...] = jnp.zeros_like(spread)
    for row, ref in ((TRIPLE, tb_ref), (MIX, mb_ref), (GAIN1, g1_ref), (SHIFT1, s1_ref),
                     (GAIN2, g2_ref), (SHIFT2, s2_ref)):
        spread[row : row + 1, : ref.shape[1]] = ref()[...].astype(F32)
    for row, ref, which, parts in (
        (UP, ub_ref, of_wide, plan.wide),
        (UP + plan.narrow, db_ref, of_narrow, plan.narrow),
    ):
        count = ref.shape[1] // parts
        values = ref()[...].astype(F32)
        mine = jnp.zeros((1, count), F32)
        for k in range(parts):
            mine = jnp.where(which == k, values[:, k * count : (k + 1) * count], mine)
        spread[row : row + 1, :count] = mine
    share = spread[...].astype(BF)
    share_ref[...] = share
    theirs_ref[:TABLE_ROWS, 4 * half :] = share


def join_kernel(plan, table, mine_ref, share_ref, came_ref, first_ref, second_ref):
    core = plan.core(table)
    half = mine_ref.shape[1] // 4
    mine, came = mine_ref[...].astype(F32), came_ref[:, : 4 * half].astype(F32)
    both = jnp.concatenate(
        [jnp.where(core == 0, mine, came), jnp.where(core == 0, came, mine)], 0
    ).astype(BF)
    third = both.shape[0] // 3
    first_ref[0, :, : 3 * half] = both[: 2 * third, : 3 * half]
    second_ref[0, :third, :] = both[2 * third :, : 3 * half]
    for b in range(3):
        second_ref[0, third:, b * half : (b + 1) * half] = (
            both[b * third : (b + 1) * third, 3 * half :]
        )
    share, other = share_ref[...], came_ref[:TABLE_ROWS, 4 * half :]
    first_ref[0, :TABLE_ROWS, 3 * half :] = jnp.where(core == 0, share, other)
    first_ref[0, TABLE_ROWS:, 3 * half :] = jnp.where(core == 0, other, share)


def vectors_kernel(plan, share, table, low_ref, high_ref, out_ref, held, triple, plain, up, down,
                   sem):
    half_slots = plan.slots // 2
    columns = low_ref.shape[2] - SHARE
    for r in range(plan.slots):
        pltpu.make_async_copy(
            (low_ref, high_ref)[r // half_slots].at[r % half_slots, :, pl.ds(columns, SHARE)],
            held.at[plan.own(table, r)],
            sem.at[0],
        ).start()
    for ref in (triple, plain, up, down):
        ref[...] = jnp.zeros_like(ref)
    drain(held, sem.at[0])
    width = out_ref.shape[1]
    part = width // plan.wide

    def put(ref, rows, at):
        block, lane = divmod(at, SHARE)
        s = slice(block * SHARE, (block + 2) * SHARE)
        ref[..., s] = ref[..., s] + (pltpu.roll(rows, lane, 1) if lane else rows)

    for device in range(plan.devices):
        of_wide, of_narrow = divmod(device, plan.narrow)
        rows = held[device // 2].astype(F32)[device % 2 * TABLE_ROWS :][:TABLE_ROWS]
        rows = jnp.concatenate([rows, jnp.zeros_like(rows)], 1)
        put(triple, rows[:8], 3 * share * device)
        put(plain, rows[:8], share * device)
        put(up.at[of_narrow], rows[8:], part * of_wide)
        put(down, rows[8:], share * device)
    out_ref[...] = jnp.zeros_like(out_ref)
    for g in range(3):
        out_ref[TRIPLE + g : TRIPLE + g + 1, :] = triple[0:1, g * width : (g + 1) * width]
    out_ref[MIX:UP, :] = plain[MIX:UP, :width]
    for n in range(plan.narrow):
        out_ref[UP + n : UP + n + 1, :] = up[n, 0:1, :width]
    row = UP + plan.narrow
    out_ref[row : row + 1, :] = down[row - 8 : row - 7, :width]


def pack_vectors(plan, core, width, bias_own, bias_other, first_ref, second_ref, up_ref, out_ref):
    out_ref[...] = jnp.zeros_like(out_ref)
    half = width // 2
    for h, ref in ((0, bias_own), (1, bias_other)):
        at = pl.ds(pl.multiple_of((core ^ h) * half, 128), half)
        for g in range(3):
            out_ref[TRIPLE + g : TRIPLE + g + 1, at] = ref[:, g * half : (g + 1) * half]
    out_ref[MIX : MIX + 1, :width] = first_ref[2:3, :]
    out_ref[GAIN1 : GAIN1 + 2, :width] = first_ref[0:2, :]
    out_ref[GAIN2 : GAIN2 + 2, :width] = second_ref[0:2, :]
    for h in (0, 1):
        for y in range(plan.narrow // 2):
            row = up_ref[h : h + 1, y * width : (y + 1) * width]
            out_ref[pl.ds(UP + 2 * y + (core ^ h), 1), :width] = row
    out_ref[UP + plan.narrow : UP + plan.narrow + 1, :width] = second_ref[2:3, :]


def attention_kernel(plan, rows, h, table, x_ref, a, b, c, d, cos_ref, sin_ref, vec_ref,
                     keep_ref, probs_ref, context_ref, triple, sems):
    core, live = plan.core(table), plan.live(table)
    tokens, width = x_ref.shape
    half = width // 2
    fetch_attention(plan, table, h, (a, b, c, d), triple, None, sems, rows)
    x = x_ref()[...]
    cos, sin = cos_ref[...], sin_ref[...]
    left = first_half(tokens)
    valid = lax.broadcasted_iota(jnp.int32, (1, tokens), 1) < live
    scale = jnp.asarray(1.0 / math.sqrt(HD), BF)
    drain(triple, sems.at[0])
    for q in range(half // 128):
        at = [slice(g * half + 128 * q, g * half + 128 * q + 128) for g in range(3)]
        here = pl.ds(pl.multiple_of((core ^ h) * half + 128 * q, 128), 128)
        out = [
            nn(x, triple[:, s]) + vec_ref[TRIPLE + g : TRIPLE + g + 1, here]
            for g, s in enumerate(at)
        ]
        query, key = [(v * cos + swap_lanes(v) * sin).astype(BF) for v in out[:2]]
        value = out[2].astype(BF)
        for s, v in zip(at, (query, key, value)):
            keep_ref[:, s] = v
        context = []
        for e in (0, 1):
            mine = left if e == 0 else ~left
            masked = jnp.where(mine, query, jnp.zeros_like(query)) * scale
            score = jnp.where(valid, nt(masked, key), -1e30)
            power = jnp.exp(score - jnp.max(score, -1, keepdims=True))
            prob = power * (1.0 / jnp.sum(power, -1, keepdims=True))
            prob = prob.astype(BF)
            probs_ref[2 * q + e] = prob
            context.append(nn(prob, value))
        context_ref[:, 128 * q : 128 * q + 128] = (
            jnp.where(left, context[0], context[1]).astype(BF)
        )


def mix_kernel(plan, rows, table, x_ref, context_own, context_other, a, b, c, d, e, f, g, k,
               vec_ref, unit_ref, inv_ref, low_ref, mix, sems):
    core = plan.core(table)
    half = context_own.shape[1]
    for h, pieces in ((0, (a, b, c, d)), (1, (e, f, g, k))):
        fetch_attention(plan, table, h, pieces, None, mix, sems, rows)
    for h in (0, 1):
        drain(mix.at[core ^ h], sems.at[h])
    sides = []
    for side in (0, 1):
        total = 0.0
        for h, context in ((0, context_own), (1, context_other)):
            at = pl.ds(pl.multiple_of((core ^ h) * half, 128), half)
            total = total + nn(context[...], mix[side, at, :])
        sides.append(total)
    branch = jnp.concatenate(sides, 1)
    summed = x_ref()[...].astype(F32) + (branch + vec_ref[MIX : MIX + 1, :])
    centred = summed - mean(summed)
    inverse = lax.rsqrt(mean(centred * centred) + EPSILON)
    unit = centred * inverse
    unit_ref[...] = unit
    inv_ref[...] = jnp.broadcast_to(inverse, inv_ref.shape)
    low_ref[...] = (
        unit * vec_ref[GAIN1 : GAIN1 + 1, :] + vec_ref[SHIFT1 : SHIFT1 + 1, :]
    ).astype(BF)


def up_kernel(plan, rows, columns, table, low_ref, a, b, c, d, vec_ref,
              own_ref, other_ref, slope_own_ref, slope_other_ref, weight, sems):
    fetch_hidden(plan, table, (a, b, c, d), weight, sems, rows, columns)
    core = plan.core(table)
    low = low_ref[...]
    step = 256
    for h, (out, slope) in enumerate(((own_ref, slope_own_ref), (other_ref, slope_other_ref))):
        drain(weight.at[h], sems.at[h])
        for k in range(out.shape[1] // step):
            s = slice(k * step, (k + 1) * step)
            y, at = divmod(k * step, columns)
            row = vec_ref[pl.ds(UP + 2 * y + (core ^ h), 1), at : at + step]
            up = nn(low, weight[h, :, s]) + row
            share = 0.5 * (1.0 + lax.erf(up * math.sqrt(0.5)))
            out[:, s] = (up * share).astype(BF)
            slope[:, s] = (
                share + up * jnp.exp(-0.5 * up * up) * (1.0 / math.sqrt(2.0 * math.pi))
            ).astype(BF)


def down_kernel(plan, rows, columns, table, act_own, act_other, a, b, c, d, unit_ref,
                cot_ref, vec_ref, out_ref, grad_ref, grad_low_ref, sums_ref, weight, sems):
    fetch_hidden(plan, table, (a, b, c, d), weight, sems, rows, columns)
    first = (
        unit_ref()[...] * vec_ref[GAIN1 : GAIN1 + 1, :] + vec_ref[SHIFT1 : SHIFT1 + 1, :]
    )
    cot = cot_ref()[...].astype(F32)
    scaled = cot * vec_ref[GAIN2 : GAIN2 + 1, :]
    scaled_mean = mean(scaled)
    sums_ref[1:2, :] = jnp.sum(cot, 0, keepdims=True)
    drain(weight.at[0], sems.at[0])
    total = nt(act_own[...], weight[0])
    drain(weight.at[1], sems.at[1])
    total = total + nt(act_other[...], weight[1])
    bias = vec_ref[UP + plan.narrow : UP + plan.narrow + 1, :]
    summed = first + (total + bias)
    centred = summed - mean(summed)
    inverse = lax.rsqrt(mean(centred * centred) + EPSILON)
    unit = centred * inverse
    grad = inverse * (scaled - scaled_mean - unit * mean(scaled * unit))
    grad_ref[...] = grad
    low = grad.astype(BF)
    grad_low_ref[...] = low
    sums_ref[0:1, :] = jnp.sum(cot * unit, 0, keepdims=True)
    sums_ref[2:3, :] = jnp.sum(low.astype(F32), 0, keepdims=True)
    out_ref[...] = (
        unit * vec_ref[GAIN2 : GAIN2 + 1, :] + vec_ref[SHIFT2 : SHIFT2 + 1, :]
    ).astype(BF)


def grad_up_kernel(plan, rows, columns, table, low_ref, a, b, c, d, slope_own, slope_other,
                   own_ref, other_ref, sums_ref, weight, sems):
    fetch_hidden(plan, table, (a, b, c, d), weight, sems, rows, columns)
    low = low_ref[...]
    step = 256
    for h, slope, out in ((1, slope_other, other_ref), (0, slope_own, own_ref)):
        drain(weight.at[h], sems.at[h])
        slope = slope
        for k in range(out.shape[1] // step):
            s = slice(k * step, (k + 1) * step)
            grad = (nn(low, weight[h, :, s]) * slope[:, s].astype(F32)).astype(BF)
            out[:, s] = grad
            sums_ref[h : h + 1, s] = jnp.sum(grad.astype(F32), 0, keepdims=True)


def hidden_grad_kernel(plan, rows, columns, table, left_own, left_other, right_own,
                       right_other, low_ref, high_ref, block, sems):
    across, half_slots = plan.narrow // 2, plan.slots // 2
    a, b = left_own[...], left_other[...]
    for y in range(across):
        s = slice(y * columns, (y + 1) * columns)
        tile = tn(a, right_own[:, s]) + tn(b, right_other[:, s])
        block[:, y] = tile.astype(BF).reshape(plan.wide, rows, columns)
    for r in reversed(range(plan.slots)):
        chip = plan.own(table, r)
        out = (low_ref, high_ref)[r // half_slots]
        pltpu.make_async_copy(
            block.at[chip // across, chip % across], out.at[r % half_slots], sems.at[r // half_slots]
        ).start()
    drain(high_ref, sems.at[1])
    drain(low_ref, sems.at[0])


def first_grad_kernel(plan, rows, columns, arows, table, gu_own, gu_other, a, b, c, d,
                      e, f, g, k, l, m, n, o, grad_ref, unit_ref, inv_ref, vec_ref, middle_ref,
                      mine_ref, theirs_ref, context_ref, sums_ref, weight, sems, mix, mix_sems,
                      low_ref):
    fetch_hidden(plan, table, (a, b, c, d), weight, sems, rows, columns)
    width = unit_ref.shape[1]
    half = width // 2
    for h, pieces in ((0, (e, f, g, k)), (1, (l, m, n, o))):
        fetch_attention(plan, table, h, pieces, None, mix, mix_sems, arows)
    core = plan.core(table)
    drain(weight.at[0], sems.at[0])
    total = nt(gu_own[...], weight[0])
    drain(weight.at[1], sems.at[1])
    total = total + nt(gu_other[...], weight[1])
    grad = grad_ref()[...] + total
    unit = unit_ref()[...]
    scaled = grad * vec_ref[GAIN1 : GAIN1 + 1, :]
    middle = inv_ref()[:, 0:1] * (scaled - mean(scaled) - unit * mean(scaled * unit))
    low = middle.astype(BF)
    middle_ref[...] = middle
    low_ref[...] = low
    mine_ref[...] = low_ref[:, pl.ds(pl.multiple_of(core * half, 128), half)]
    theirs_ref[...] = low_ref[:, pl.ds(pl.multiple_of((core ^ 1) * half, 128), half)]
    sums_ref[0:1, :] = jnp.sum(grad * unit, 0, keepdims=True)
    sums_ref[1:2, :] = jnp.sum(grad, 0, keepdims=True)
    sums_ref[2:3, :] = jnp.sum(low.astype(F32), 0, keepdims=True)
    for h in (0, 1):
        drain(mix.at[core ^ h], mix_sems.at[h])
    context_ref[...] = (nt(low[:, :half], mix[0]) + nt(low[:, half:], mix[1])).astype(BF)


def attention_grad_kernel(plan, h, table, keep_ref, probs_ref, grad_ref, cos_ref, sin_ref,
                          out_ref, sums_ref):
    core = plan.core(table)
    tokens, width = grad_ref.shape
    half = width // 2
    cos, sin = cos_ref[...], sin_ref[...]
    left = first_half(tokens)
    scale = 1.0 / math.sqrt(HD)
    keep, grads_in, probs = keep_ref(), grad_ref, probs_ref()
    for q in range(half // 128):
        at = [slice(g * half + 128 * q, g * half + 128 * q + 128) for g in range(3)]
        query, key, value = [keep[:, s] for s in at]
        came = grads_in[:, pl.ds(pl.multiple_of((core ^ h) * half + 128 * q, 128), 128)]
        parts = []
        for e in (0, 1):
            mine = left if e == 0 else ~left
            low = probs[2 * q + e]
            prob = low.astype(F32)
            grad = nt(jnp.where(mine, came, jnp.zeros_like(came)), value)
            score = prob * (grad - jnp.sum(prob * grad, -1, keepdims=True))
            score = score.astype(BF)
            parts.append((nn(score, key), tn(score, query), tn(low, came)))
        grads = [jnp.where(left, u, v) for u, v in zip(*parts)]
        grads = [(g * scale) * cos + swap_lanes((g * scale) * sin) for g in grads[:2]] + grads[2:]
        for s, g in zip(at, grads):
            g = g.astype(BF)
            out_ref[:, s] = g
            sums_ref[:, s] = jnp.sum(g.astype(F32), 0, keepdims=True)


def attention_weight_kernel(plan, rows, table, x_own, x_other, g_own, g_other, c_own, c_other,
                            c_came_own, c_came_other, b_own, b_other, bias_own, bias_other,
                            first_ref, second_ref, up_ref, low_ref, high_ref, block, mixed, sums,
                            low_sums, sems):
    core = plan.core(table)
    half_slots = plan.slots // 2
    tokens, columns = g_own.shape
    third = columns // 3
    height = rows + rows // 3
    pack_vectors(
        plan, core, x_own.shape[1], bias_own, bias_other, first_ref, second_ref, up_ref, sums
    )
    low_sums[...] = sums[...].astype(BF)
    for ref, sem in ((high_ref, sems.at[1]), (low_ref, sems.at[0])):
        pltpu.make_async_copy(
            low_sums, ref.at[pl.ds(half_slots * height, TABLE_ROWS)], sem
        ).start()
    block[...] = (
        (tn(x_own[...], g_own[...]) + tn(x_other[...], g_other[...]))
        .astype(BF)
        .reshape(block.shape)
    )
    for h, mine, came in ((0, c_own, c_came_other), (1, c_other, c_came_own)):
        mixed[pl.ds((core ^ h) * half_slots, half_slots)] = (
            (tn(mine[...], b_own[...]) + tn(came[...], b_other[...]))
            .astype(BF)
            .reshape((half_slots,) + mixed.shape[1:])
        )
    for r in reversed(range(plan.slots)):
        chip = plan.own(table, r)
        out, at = (low_ref, high_ref)[r // half_slots], r % half_slots * height
        sem = sems.at[r // half_slots]
        pltpu.make_async_copy(block.at[chip], out.at[pl.ds(at, rows)], sem).start()
        for b in range(3):
            pltpu.make_async_copy(
                mixed.at[chip, b],
                out.at[pl.ds(at + rows, rows // 3), pl.ds(b * third, third)],
                sem,
            ).start()
    drain(high_ref, sems.at[1])
    drain(low_ref, sems.at[0])


def input_grad_kernel(plan, rows, table, middle_ref, g_own, g_other, a, b, c, d, e, f, g, k,
                      out_ref, triple, sems):
    for h, pieces in ((0, (a, b, c, d)), (1, (e, f, g, k))):
        fetch_attention(plan, table, h, pieces, triple.at[h], None, sems.at[h], rows)
    drain(triple.at[0], sems.at[0, 0])
    total = nt(g_own[...], triple[0])
    drain(triple.at[1], sems.at[1, 0])
    total = total + nt(g_other[...], triple[1])
    out_ref[...] = (middle_ref[...] + total).astype(BF)


def half_tables(tokens):
    position = jnp.arange(tokens, dtype=F32)
    column = jnp.arange(2 * HD, dtype=jnp.int32)
    pair = (column % HD // 2).astype(F32)
    angle = position[:, None] * jnp.exp(pair * (-2.0 / HD) * math.log(10000.0))[None, :]
    parity = (column % 2).astype(F32) * 2.0 - 1.0
    return jnp.cos(angle), jnp.sin(angle) * parity[None, :]


def fast_body(
    plan,
    inputs,
    lengths,
    triple_weight,
    triple_bias,
    mix_weight,
    mix_bias,
    first_gain,
    first_shift,
    up_weight,
    up_bias,
    down_weight,
    down_bias,
    second_gain,
    second_shift,
    cotangent,
):
    tokens, width = inputs.shape
    half = width // 2
    wide, narrow = plan.wide, plan.narrow
    index = lax.axis_index(AXES)
    core = index & 1
    of_wide, of_narrow = lax.axis_index("wide"), lax.axis_index("narrow")
    table = plan.table(index, lengths)
    hidden = up_weight.shape[1]
    tile_rows = up_weight.shape[0]
    piece = triple_weight.shape[0]
    rows = 2 * piece
    third = rows // 3
    half_slots = plan.slots // 2
    flops = 2.0 * tokens * width * width
    hidden_half = hidden * narrow // 2

    def by_core(pair):
        mine = jnp.where(core == 0, pair[0], pair[1])
        theirs = jnp.where(core == 0, pair[1], pair[0])
        return mine, theirs

    def in_order(mine, theirs, axis):
        return jnp.where(
            core == 0,
            jnp.concatenate([mine, theirs], axis),
            jnp.concatenate([theirs, mine], axis),
        )

    row = functools.partial(jnp.reshape, shape=(1, -1))
    mine, share, theirs = call(
        functools.partial(split_kernel, plan),
        [
            shape((piece, 4 * half)),
            shape((TABLE_ROWS, SHARE)),
            shape((piece, 4 * half + SHARE)),
        ],
        (
            index.astype(jnp.int32)[None],
            triple_weight,
            mix_weight,
            row(triple_bias),
            row(mix_bias),
            row(first_gain),
            row(first_shift),
            row(second_gain),
            row(second_shift),
            row(up_bias),
            row(down_bias),
        ),
        "s" + 10 * "l",
        [VMEM((TABLE_ROWS, SHARE), F32)],
        0,
        60,
    )
    first, second = call(
        functools.partial(join_kernel, plan),
        [shape((1, 2 * third, 3 * half + SHARE)), shape((1, 2 * third, 3 * half))],
        (table, mine, share, plan.swap(theirs)),
        "svvv",
        [],
        0,
        16,
    )
    cat = functools.partial(jnp.concatenate, axis=0)
    cos, sin = half_tables(tokens)
    first = cat(plan.gather_far(first))
    came = plan.permute(first, plan.first)
    second = plan.gather_far(after(second, first))
    came, *second = after_all((came, *second))
    first, second = cat((first, came)), cat(second)
    first = (first, plan.permute(first, plan.last))
    came = plan.permute(second, plan.first)
    up = plan.gather_far(after(up_weight[None], second))
    first, (came, cos, sin), up = together(first, (came, cos, sin), up)
    second, up = cat((second, came)), cat(up)
    second = (second, plan.permute(second, plan.last))
    came = plan.permute(up, plan.first)
    down = plan.gather_far(after(down_weight.T[None], up))
    att_own, (came, up), down = together((*first, *second), (came, up), down)
    down, up = cat(down), cat((up, came))
    down_came = plan.permute(down, plan.first)
    ups = (up, plan.permute(up, plan.last))
    att_other = [plan.swap(v) for v in att_own]
    (vecs,) = call(
        functools.partial(vectors_kernel, plan, piece),
        [shape((TABLE_ROWS, width), F32)],
        (table, *att_own[:2]),
        "shh",
        [
            VMEM((plan.slots, 2 * third, SHARE), BF),
            VMEM((8, 3 * width + 2 * SHARE), F32),
            VMEM((8, width + 2 * SHARE), F32),
            VMEM((narrow, 8, width + 2 * SHARE), F32),
            VMEM((8, width + 2 * SHARE), F32),
            pltpu.SemaphoreType.DMA((1,)),
        ],
        0,
        32,
    )

    def attend(h, pieces, gate=()):
        return call(
            functools.partial(attention_kernel, plan, rows, h),
            [
                shape((tokens, 3 * half)),
                shape((half // HD, tokens, tokens)),
                shape((tokens, half)),
            ],
            (after(table, *gate), inputs, *pieces, cos, sin, vecs),
            "slhhhhvvv",
            [VMEM((width, 3 * half), BF), pltpu.SemaphoreType.DMA((1,))],
            1,
            24,
        )

    own, p_own, context_own = attend(0, att_own, (up,))
    down = cat(after_all((down, down_came), context_own))
    downs = (down, plan.permute(down, plan.last))
    other, p_other, context_other = attend(1, att_other, (down,))
    ups = after_all(ups, context_other)
    ups = (*ups, plan.swap(ups[0]), plan.swap(ups[1]))
    unit, inv, low = call(
        functools.partial(mix_kernel, plan, rows),
        [shape((tokens, width), F32), shape((tokens, 128), F32), shape((tokens, width))],
        (table, inputs, context_own, context_other, *att_own, *att_other, vecs),
        "slvvhhhhhhhhv",
        [VMEM((2, width, half), BF), pltpu.SemaphoreType.DMA((2,))],
        1,
        24,
    )
    hidden_scratch = [
        VMEM((2, width, hidden_half), BF),
        pltpu.SemaphoreType.DMA((2,)),
    ]
    act_own, act_other, slope_own, slope_other = call(
        functools.partial(up_kernel, plan, tile_rows, hidden),
        [shape((tokens, hidden_half))] * 4,
        (table, low, *ups, vecs),
        "svhhhhv",
        hidden_scratch,
        1,
        24,
    )
    downs = after_all(downs, act_own)
    downs = (*downs, plan.swap(downs[0]), plan.swap(downs[1]))
    inputs_came, low_came, act_came = plan.swap(inputs), plan.swap(low), plan.swap(act_other)
    context_came = plan.swap(context_own), plan.swap(context_other)
    outputs, grad_second, grad_down, sums_second = call(
        functools.partial(down_kernel, plan, tile_rows, hidden),
        [
            shape((tokens, width)),
            shape((tokens, width), F32),
            shape((tokens, width)),
            shape((3, width), F32),
        ],
        (table, act_own, act_other, *downs, unit, cotangent, vecs),
        "svvhhhhllv",
        hidden_scratch,
        1,
        24,
    )
    grad_down_came = plan.swap(grad_down)
    gu_own, gu_other, sums_up = call(
        functools.partial(grad_up_kernel, plan, tile_rows, hidden),
        [shape((tokens, hidden_half))] * 2 + [shape((2, hidden_half), F32)],
        (table, grad_down, *downs, slope_own, slope_other),
        "svhhhhvv",
        hidden_scratch,
        1,
        24,
    )
    gu_came = plan.swap(gu_other)

    def hidden_grad(left, left_came, right, right_came, gate):
        return call(
            functools.partial(hidden_grad_kernel, plan, tile_rows, hidden),
            [shape((half_slots, tile_rows, hidden))] * 2,
            (after(table, *gate), left, left_came, right, right_came),
            "svvvv",
            [VMEM((wide, narrow // 2, tile_rows, hidden), BF), pltpu.SemaphoreType.DMA((2,))],
            1,
            24,
            [LEFT] * 2,
        )

    down_low, down_high = hidden_grad(grad_down, grad_down_came, act_own, act_came, (sums_up,))
    down_came = plan.permute(down_high, plan.last)
    up_low, up_high = hidden_grad(low, low_came, gu_own, gu_came, (down_low,))
    up_came = plan.permute(up_high, plan.last)
    grad_middle, branch_mine, branch_theirs, grad_context, sums_first = call(
        functools.partial(first_grad_kernel, plan, tile_rows, hidden, rows),
        [
            shape((tokens, width), F32),
            shape((tokens, half)),
            shape((tokens, half)),
            shape((tokens, width)),
            shape((3, width), F32),
        ],
        (
            after(table, up_low),
            gu_own,
            gu_other,
            *ups,
            *att_own,
            *att_other,
            grad_second,
            unit,
            inv,
            vecs,
        ),
        "svvhhhhhhhhhhhhlllv",
        hidden_scratch
        + [
            VMEM((2, width, half), BF),
            pltpu.SemaphoreType.DMA((2,)),
            VMEM((tokens, width), BF),
        ],
        1,
        24,
    )
    branch_came = plan.swap(branch_theirs)

    def attention_grad(h, keep, probs, gate=()):
        return call(
            functools.partial(attention_grad_kernel, plan, h),
            [shape((tokens, 3 * half)), shape((1, 3 * half), F32)],
            (after(table, *gate), keep, probs, grad_context, cos, sin),
            "sllvvv",
            [],
            1,
            24,
        )

    gt_other, bias_other = attention_grad(1, other, p_other)
    gt_came = plan.swap(gt_other)
    down_stay, down_away = halves(*after_all((down_low, down_came), bias_other))
    down_came = plan.permute(down_away, plan.first)
    gt_own, bias_own = attention_grad(0, own, p_own, (down_away,))
    up_stay, up_away = halves(*after_all((up_low, up_came), bias_own))
    up_came = plan.permute(up_away, plan.first)
    height = rows + third
    packed_low, packed_high = call(
        functools.partial(attention_weight_kernel, plan, rows),
        [shape((half_slots * height + TABLE_ROWS, 3 * half))] * 2,
        (
            after(table, up_away),
            inputs,
            inputs_came,
            gt_own,
            gt_came,
            context_own,
            context_other,
            *context_came,
            branch_mine,
            branch_came,
            bias_own,
            bias_other,
            sums_first,
            sums_second,
            sums_up,
        ),
        "s" + 15 * "v",
        [
            VMEM((plan.slots, rows, 3 * half), BF),
            VMEM((plan.slots, 3, third, half), BF),
            VMEM((TABLE_ROWS, 3 * half), F32),
            VMEM((TABLE_ROWS, 3 * half), BF),
            pltpu.SemaphoreType.DMA((2,)),
        ],
        80 * flops,
        24,
        [LEFT] * 2,
    )
    packed_came = plan.permute(packed_high, plan.last)
    down_stay, down_came, up_stay, up_came = after_all(
        (down_stay, down_came, up_stay, up_came), packed_low
    )
    near = [
        jnp.stack([added(down_stay[k], down_came[k]), added(up_stay[k], up_came[k])])
        for k in range(plan.far)
    ]
    near_came = plan.send_far(near)
    (input_grad,) = call(
        functools.partial(input_grad_kernel, plan, rows),
        [shape((tokens, width))],
        (after(table, near[0]), grad_middle, gt_own, gt_other, *att_own, *att_other),
        "svvvhhhhhhhh",
        [VMEM((2, width, 3 * half), BF), pltpu.SemaphoreType.DMA((2, 1))],
        80 * flops,
        40,
    )
    packed_low, packed_came = after_all((packed_low, packed_came), input_grad)
    cut, end = half_slots // 2 * height, half_slots * height
    sums = added(packed_low[end:], packed_came[end:])
    packed_stay = added(packed_low[:cut], packed_came[:cut])
    packed_away = cat([added(packed_low[cut:end], packed_came[cut:end]), sums])
    packed_came = plan.permute(packed_away, plan.first)
    (packed_came,) = after_all((packed_came,), *near_came)
    total = sum([v.astype(F32) for v in near_came], near[0].astype(F32))
    down_total, up_total = total[0], total[1]
    sums = added(sums, packed_came[cut:])
    parts = [
        cat(
            [
                added(packed_stay[k * height :][:height], packed_came[k * height :][:height]),
                sums,
            ]
        )
        for k in range(plan.far)
    ]
    attention_total = sum([v.astype(F32) for v in plan.send_far(parts)], parts[0].astype(F32))
    sums = attention_total[height:, :width]
    flat = (sums + plan.swap(sums)).reshape(-1)

    def share_of(row, at, count):
        return lax.dynamic_slice(flat, (row * width + at * count,), (count,))

    mix_rows = attention_total[rows:height].reshape(rows // 3, 3, half).transpose(1, 0, 2)
    chip_grads = jnp.concatenate([attention_total[:rows], mix_rows.reshape(rows, half)], 1)
    mine, theirs = by_core((chip_grads[:piece], chip_grads[piece:]))
    came = plan.swap(theirs)
    pair = in_order(mine[None], came[None], 0)
    triple_grad = pair[:, :, : 3 * half].reshape(2, piece, 3, half).transpose(1, 2, 0, 3)
    mix_grad = pair[:, :, 3 * half :].transpose(1, 0, 2)
    return (
        outputs,
        input_grad,
        triple_grad.reshape(piece, 3 * width),
        share_of(TRIPLE, index, 3 * piece),
        mix_grad.reshape(piece, width),
        share_of(MIX, index, piece),
        share_of(GAIN1, index, piece),
        share_of(SHIFT1, index, piece),
        up_total,
        share_of(UP, of_narrow, hidden),
        down_total.T,
        share_of(UP + narrow, of_wide, down_bias.shape[0]),
        share_of(GAIN2, index, piece),
        share_of(SHIFT2, index, piece),
    )


def fits(plan_shape, width, hidden):
    wide, narrow = plan_shape
    powers = all(n >= 4 and n & (n - 1) == 0 for n in (wide, narrow)) and narrow == 4
    return (
        powers
        and width % (wide * 16) == 0
        and width % (wide * narrow // 2 * 48) == 0
        and hidden % (narrow * 128) == 0
        and width % 768 == 0
    )


def solution(mesh):
    placed = (
        P(("wide", "narrow"), None),
        P(("wide", "narrow")),
        P(("wide", "narrow"), None),
        P(("wide", "narrow")),
        P(("wide", "narrow"), None),
        P(("wide", "narrow")),
        P(("wide", "narrow")),
        P(("wide", "narrow")),
        P("wide", "narrow"),
        P("narrow"),
        P("narrow", "wide"),
        P("wide"),
        P(("wide", "narrow")),
        P(("wide", "narrow")),
        P(("wide", "narrow"), None),
    )
    wide, narrow = mesh.shape["wide"], mesh.shape["narrow"]

    def layer(*arrays):
        rows, hidden = arrays[8].shape
        if fits((wide, narrow), rows * wide, hidden * narrow):
            return fast_body(Plan(wide, narrow), *arrays)
        return body(*arrays)

    return jax.shard_map(
        layer,
        mesh=mesh,
        in_specs=placed,
        out_specs=(
            P(("wide", "narrow"), None),
            P(("wide", "narrow"), None),
            P(("wide", "narrow"), None),
            P(("wide", "narrow")),
            P(("wide", "narrow"), None),
            P(("wide", "narrow")),
            P(("wide", "narrow")),
            P(("wide", "narrow")),
            P("wide", "narrow"),
            P("narrow"),
            P("narrow", "wide"),
            P("wide"),
            P(("wide", "narrow")),
            P(("wide", "narrow")),
        ),
        check_vma=False,
    )
```

```python
import functools
import math

import jax
import jax.numpy as jnp
import numpy as np
from jax import lax
from jax.experimental import pallas as pl
from jax.experimental.pallas import tpu as pltpu
from jax.sharding import PartitionSpec as P

H = 12
HD = 64


EPSILON = 1e-06


def tables(token_rows, width, head):
    position = jnp.arange(token_rows, dtype=jnp.float32)
    column = jnp.arange(width, dtype=jnp.int32)
    pair_index = (column % head // 2).astype(jnp.float32)
    frequency = jnp.exp(pair_index * (-2.0 / head) * math.log(10000.0))
    angle = position[:, None] * frequency[None, :]
    parity = (column % 2).astype(jnp.float32) * 2.0 - 1.0
    return (jnp.cos(angle), jnp.sin(angle) * parity[None, :])


def swapped(values):
    shape = values.shape
    paired = values.reshape(shape[:-1] + (shape[-1] // 2, 2))
    return paired[..., ::-1].reshape(shape)


def rotate(values, cosine, sine):
    return values * cosine + swapped(values) * sine


def unrotate(grad, cosine, sine):
    return grad * cosine + swapped(grad * sine)


def normalize_forward(values, gain, shift):
    mean_row = jnp.mean(values, -1, keepdims=True)
    centred = values - mean_row
    inverse = lax.rsqrt(jnp.mean(centred * centred, -1, keepdims=True) + EPSILON)
    unit = centred * inverse
    return (unit * gain + shift, unit, inverse)


def normalize_backward(grad, unit, inverse, gain):
    scaled = grad * gain
    inner = (
        scaled
        - jnp.mean(scaled, -1, keepdims=True)
        - unit * jnp.mean(scaled * unit, -1, keepdims=True)
    )
    return (inner * inverse, jnp.sum(grad * unit, 0), jnp.sum(grad, 0))


def gelu_exact(values):
    return jax.nn.gelu(values, approximate=False)


def gelu_backward(upward, grad_active):
    unused, pull_back = jax.vjp(gelu_exact, upward)
    return pull_back(grad_active)[0]


def softmax_block(query_block, key, valid, scale):
    scores = (
        jnp.einsum("qhd,khd->hqk", query_block, key, preferred_element_type=jnp.float32) * scale
    )
    scores = jnp.where(valid[None, None, :], scores, -1e30)
    return jax.nn.softmax(scores, axis=-1)


def attention_forward(query, key, value, valid, scale):
    token_rows = query.shape[0]
    block = min(512, token_rows)
    weights_block = softmax_block(query, key, valid, scale)
    context = jnp.einsum(
        "hqk,khd->qhd",
        weights_block.astype(jnp.bfloat16),
        value,
        preferred_element_type=jnp.float32,
    )
    pieces = context.reshape(block, -1).astype(jnp.bfloat16)
    return pieces


def attention_backward(query, key, value, grad_context, valid, scale):
    weights_block = softmax_block(query, key, valid, scale)
    grad_weights = jnp.einsum(
        "qhd,khd->hqk", grad_context, value, preferred_element_type=jnp.float32
    )
    inner = weights_block * (
        grad_weights - jnp.sum(weights_block * grad_weights, -1, keepdims=True)
    )
    inner_low = inner.astype(jnp.bfloat16)
    query_pieces = (
        jnp.einsum("hqk,khd->qhd", inner_low, key, preferred_element_type=jnp.float32) * scale
    )
    grad_key = (
        jnp.einsum("hqk,qhd->khd", inner_low, query, preferred_element_type=jnp.float32) * scale
    )
    grad_value = jnp.einsum(
        "hqk,qhd->khd",
        weights_block.astype(jnp.bfloat16),
        grad_context,
        preferred_element_type=jnp.float32,
    )
    return (query_pieces, grad_key, grad_value)


def body(
    inputs,
    lengths,
    triple_weight,
    triple_bias,
    mix_weight,
    mix_bias,
    first_gain,
    first_shift,
    up_weight,
    up_bias,
    down_weight,
    down_bias,
    second_gain,
    second_shift,
    cotangent,
):
    token_rows, width = inputs.shape
    scale = 1.0 / math.sqrt(HD)
    head_shape = (token_rows, H, HD)
    (
        triple_full,
        mix_full,
        triple_bias_full,
        mix_bias_full,
        gain_one,
        shift_one,
        gain_two,
        shift_two,
    ) = (
        lax.all_gather(triple_weight, ("wide", "narrow"), axis=0, tiled=True),
        lax.all_gather(mix_weight, ("wide", "narrow"), axis=0, tiled=True),
        lax.all_gather(triple_bias, ("wide", "narrow"), axis=0, tiled=True),
        lax.all_gather(mix_bias, ("wide", "narrow"), axis=0, tiled=True),
        lax.all_gather(first_gain, ("wide", "narrow"), axis=0, tiled=True),
        lax.all_gather(first_shift, ("wide", "narrow"), axis=0, tiled=True),
        lax.all_gather(second_gain, ("wide", "narrow"), axis=0, tiled=True),
        lax.all_gather(second_shift, ("wide", "narrow"), axis=0, tiled=True),
    )
    up_rows, down_columns, down_bias_full = (
        lax.all_gather(up_weight, "wide", axis=0, tiled=True),
        lax.all_gather(down_weight, "wide", axis=1, tiled=True),
        lax.all_gather(down_bias, "wide", axis=0, tiled=True),
    )
    gain_one = gain_one.astype(jnp.float32)
    gain_two = gain_two.astype(jnp.float32)
    cosine, sine = tables(token_rows, width, HD)
    valid = jnp.arange(token_rows, dtype=jnp.int32) < lengths[0]
    triple = jnp.dot(
        inputs, triple_full, preferred_element_type=jnp.float32
    ) + triple_bias_full.astype(jnp.float32)
    query = rotate(triple[:, :width], cosine, sine).astype(jnp.bfloat16).reshape(head_shape)
    key = (
        rotate(triple[:, width : 2 * width], cosine, sine).astype(jnp.bfloat16).reshape(head_shape)
    )
    value = triple[:, 2 * width :].astype(jnp.bfloat16).reshape(head_shape)
    context = attention_forward(query, key, value, valid, scale)
    branch = jnp.dot(context, mix_full, preferred_element_type=jnp.float32) + mix_bias_full.astype(
        jnp.float32
    )
    first, first_unit, first_inverse = normalize_forward(
        inputs.astype(jnp.float32) + branch, gain_one, shift_one.astype(jnp.float32)
    )
    first_low = first.astype(jnp.bfloat16)
    gathered = lax.all_gather(first_low, "narrow", axis=0, tiled=True)
    upward = jnp.dot(gathered, up_rows, preferred_element_type=jnp.float32) + up_bias.astype(
        jnp.float32
    )
    active = gelu_exact(upward).astype(jnp.bfloat16)
    downward = lax.psum_scatter(
        jnp.dot(active, down_columns, preferred_element_type=jnp.float32).astype(jnp.bfloat16),
        "narrow",
        scatter_dimension=0,
        tiled=True,
    ).astype(jnp.float32)
    downward = downward + down_bias_full.astype(jnp.float32)
    result, second_unit, second_inverse = normalize_forward(
        first + downward, gain_two, shift_two.astype(jnp.float32)
    )
    outputs = result.astype(jnp.bfloat16)
    grad_second, second_gain_grad, second_shift_grad = normalize_backward(
        cotangent.astype(jnp.float32), second_unit, second_inverse, gain_two
    )
    grad_down = grad_second.astype(jnp.bfloat16)
    grad_gathered = lax.all_gather(grad_down, "narrow", axis=0, tiled=True)
    grad_active = jnp.dot(grad_gathered, down_columns.T, preferred_element_type=jnp.float32)
    grad_up = gelu_backward(upward, grad_active).astype(jnp.bfloat16)
    grad_feed = lax.psum_scatter(
        jnp.dot(grad_up, up_rows.T, preferred_element_type=jnp.float32).astype(jnp.bfloat16),
        "narrow",
        scatter_dimension=0,
        tiled=True,
    ).astype(jnp.float32)
    up_part = jnp.dot(gathered.T, grad_up, preferred_element_type=jnp.float32)
    down_part = jnp.dot(active.T, grad_gathered, preferred_element_type=jnp.float32)
    down_bias_part = jnp.sum(grad_gathered, 0, dtype=jnp.float32)
    up_weight_grad, down_weight_grad, down_bias_grad = (
        lax.psum_scatter(
            up_part.astype(jnp.bfloat16), "wide", scatter_dimension=0, tiled=True
        ).astype(jnp.float32),
        lax.psum_scatter(
            down_part.astype(jnp.bfloat16), "wide", scatter_dimension=1, tiled=True
        ).astype(jnp.float32),
        lax.psum_scatter(
            down_bias_part.astype(jnp.bfloat16), "wide", scatter_dimension=0, tiled=True
        ).astype(jnp.float32),
    )
    up_bias_grad = lax.psum(jnp.sum(grad_up, 0, dtype=jnp.float32), "wide")
    grad_first = grad_second + grad_feed
    grad_middle, first_gain_grad, first_shift_grad = normalize_backward(
        grad_first, first_unit, first_inverse, gain_one
    )
    grad_branch = grad_middle.astype(jnp.bfloat16)
    mix_weight_grad = jnp.dot(context.T, grad_branch, preferred_element_type=jnp.float32)
    mix_bias_grad = jnp.sum(grad_branch, 0, dtype=jnp.float32)
    triple_back, mix_back = (
        lax.all_gather(triple_weight, ("wide", "narrow"), axis=0, tiled=True),
        lax.all_gather(mix_weight, ("wide", "narrow"), axis=0, tiled=True),
    )
    grad_context = (
        jnp.dot(grad_branch, mix_back.T, preferred_element_type=jnp.float32)
        .astype(jnp.bfloat16)
        .reshape(head_shape)
    )
    grad_query, grad_key, grad_value = attention_backward(
        query, key, value, grad_context, valid, scale
    )
    grad_triple = jnp.concatenate(
        [
            unrotate(grad_query.reshape(token_rows, width), cosine, sine),
            unrotate(grad_key.reshape(token_rows, width), cosine, sine),
            grad_value.reshape(token_rows, width),
        ],
        1,
    ).astype(jnp.bfloat16)
    triple_local = jnp.dot(inputs.T, grad_triple, preferred_element_type=jnp.float32)
    triple_bias_local = jnp.sum(grad_triple, 0, dtype=jnp.float32)
    grad_inputs = grad_middle + jnp.dot(
        grad_triple, triple_back.T, preferred_element_type=jnp.float32
    )
    summed = (
        lax.psum_scatter(triple_local, ("wide", "narrow"), scatter_dimension=0, tiled=True),
        lax.psum_scatter(mix_weight_grad, ("wide", "narrow"), scatter_dimension=0, tiled=True),
        lax.psum_scatter(triple_bias_local, ("wide", "narrow"), scatter_dimension=0, tiled=True),
        lax.psum_scatter(mix_bias_grad, ("wide", "narrow"), scatter_dimension=0, tiled=True),
        lax.psum_scatter(first_gain_grad, ("wide", "narrow"), scatter_dimension=0, tiled=True),
        lax.psum_scatter(first_shift_grad, ("wide", "narrow"), scatter_dimension=0, tiled=True),
        lax.psum_scatter(second_gain_grad, ("wide", "narrow"), scatter_dimension=0, tiled=True),
        lax.psum_scatter(second_shift_grad, ("wide", "narrow"), scatter_dimension=0, tiled=True),
    )
    return (
        outputs,
        grad_inputs.astype(jnp.bfloat16),
        summed[0],
        summed[2],
        summed[1],
        summed[3],
        summed[4],
        summed[5],
        up_weight_grad,
        up_bias_grad,
        down_weight_grad,
        down_bias_grad,
        summed[6],
        summed[7],
    )


VMEM = pltpu.VMEM
SMEM = pltpu.SMEM
BF = jnp.bfloat16
F32 = jnp.float32
AXES = ("wide", "narrow")
WHOLE = pl.BlockSpec(memory_space=VMEM)
SCALARS = pl.BlockSpec(memory_space=SMEM)
LEFT = pl.BlockSpec(memory_space=pltpu.HBM)


def nn(a, b):
    return lax.dot_general(a, b, (((1,), (0,)), ((), ())), preferred_element_type=F32)


def nt(a, b):
    return lax.dot_general(a, b, (((1,), (1,)), ((), ())), preferred_element_type=F32)


def tn(a, b):
    return lax.dot_general(a, b, (((0,), (0,)), ((), ())), preferred_element_type=F32)


def shape(dims, dtype=BF):
    return jax.ShapeDtypeStruct(dims, dtype)


class Load:
    def __init__(self, source, held, sem):
        self.copy = pltpu.make_async_copy(source, held, sem)
        self.held, self.waited = held, False
        self.shape = held.shape
        self.copy.start()

    def __call__(self):
        if not self.waited:
            self.copy.wait()
            self.waited = True
        return self.held


def call(kernel, outs, operands, kinds, scratch, flops, megabytes, out_specs=None):
    specs = {"s": SCALARS, "v": WHOLE, "h": LEFT, "l": LEFT}
    loads = [k for k, kind in enumerate(kinds) if kind == "l"]
    held = [VMEM(operands[k].shape, operands[k].dtype) for k in loads]
    assert len(kinds) == len(operands)

    def whole(*refs):
        refs = list(refs)
        count = len(loads)
        if count:
            sems = refs.pop()
            buffers, refs = refs[-count:], refs[:-count]
            for n, k in enumerate(loads):
                refs[k] = Load(refs[k], buffers[n], sems.at[n])
        kernel(*refs)
        for k in loads:
            refs[k]()

    return pl.pallas_call(
        whole,
        out_shape=outs,
        in_specs=[specs[kind] for kind in kinds],
        out_specs=[WHOLE] * len(outs) if out_specs is None else out_specs,
        scratch_shapes=list(scratch)
        + held
        + ([pltpu.SemaphoreType.DMA((len(loads),))] if loads else []),
        compiler_params=pltpu.CompilerParams(vmem_limit_bytes=megabytes << 20),
        cost_estimate=pl.CostEstimate(
            flops=int(flops), bytes_accessed=1, transcendentals=0
        ),
    )(*operands)


def drain(ref, sem):
    pltpu.make_async_copy(ref, ref, sem).wait()


class Plan:
    def __init__(self, wide, narrow):
        self.wide, self.narrow = wide, narrow
        self.devices = wide * narrow
        x, y = narrow, narrow // 2
        self.first, self.last = (x, y), (y, x)
        self.far = wide // 2
        line = self.devices // self.far
        along = [(line << k, line << k) for k in reversed(range(self.far.bit_length() - 1))]
        self.far_first = (*along, self.first, self.last)
        self.far_second = (self.first, *along, self.last)
        self.routes = (self.far_first, self.far_second)
        self.slots = 1 << len(self.far_first)

    def lead(self, route, slot):
        masks = [0, 0]
        for k, pair in enumerate(route):
            if slot >> k & 1:
                masks = [mask ^ bit for mask, bit in zip(masks, pair)]
        return masks

    def chips(self, device):
        core = device & 1
        return [
            (device ^ self.lead(route, r)[c]) >> 1
            for route in self.routes
            for c in (core, core ^ 1)
            for r in range(self.slots)
        ]

    def table(self, index, live):
        chips = np.array([self.chips(i) for i in range(self.devices)], np.int32)
        mine = lax.dynamic_slice(jnp.asarray(chips), (index, 0), (1, chips.shape[1]))[0]
        return jnp.concatenate([mine, (index & 1)[None].astype(jnp.int32), live])

    def chip(self, table, route, h, slot):
        return table[(2 * self.routes.index(route) + h) * self.slots + slot]

    def core(self, table):
        return table[2 * len(self.routes) * self.slots]

    def live(self, table):
        return table[2 * len(self.routes) * self.slots + 1]

    def permute(self, value, masks):
        return lax.ppermute(value, AXES, [(i, i ^ masks[i & 1]) for i in range(self.devices)])

    def swap(self, value):
        return self.permute(value, (1, 1))

    def send(self, value, route, slot):
        return self.permute(value, self.lead(route, slot))

    def gather_far(self, value):
        return [value] + [self.send(value, self.far_first, m) for m in range(1, self.far)]

    def send_far(self, parts):
        return [self.send(v, self.far_first, m) for m, v in enumerate(parts) if m]


def added(low, came):
    return (low.astype(F32) + came.astype(F32)).astype(BF)


def halves(low, came):
    count = low.shape[0] // 2
    return added(low[:count], came[:count]), added(low[count:], came[count:])


def together(*lists):
    flat = list(lax.optimization_barrier(tuple(v for values in lists for v in values)))
    return [[flat.pop(0) for _ in values] for values in lists]


def after_all(values, *others):
    return lax.optimization_barrier(tuple(values) + others)[: len(values)]


def after(value, *others):
    return lax.optimization_barrier((value,) + others)[0] if others else value


def mean(v):
    return jnp.mean(v, -1, keepdims=True)


def swap_lanes(v):
    lane = lax.broadcasted_iota(jnp.int32, v.shape, 1)
    return jnp.where(lane % 2 == 0, pltpu.roll(v, v.shape[1] - 1, 1), pltpu.roll(v, 1, 1))


def first_half(rows):
    return lax.broadcasted_iota(jnp.int32, (rows, 2 * HD), 1) < HD


def place_attention(plan, table, h, pieces, triple, mix, rows):
    core = plan.core(table)
    half_slots = plan.slots // 2
    third = rows // 3
    columns = pieces[2].shape[2]
    width = columns // 3
    for r in range(plan.slots):
        chip = plan.chip(table, plan.far_first, h, r)
        side, at = divmod(r, half_slots)
        first, second = pieces[side], pieces[2 + side]
        if triple is not None:
            top = pl.ds(pl.multiple_of(chip * rows, 16), 2 * third)
            triple[top, :] = first[at, :, :columns]
            rest = pl.ds(pl.multiple_of(chip * rows + 2 * third, 16), third)
            triple[rest, :] = second[at, :third, :]
        if mix is not None:
            for b in range(3):
                here = pl.ds(pl.multiple_of(chip * rows + b * third, 16), third)
                mix[core ^ h, here, :] = second[at, third:, b * width : (b + 1) * width]


def place_hidden(plan, route, table, h, pieces, weight, rows, columns):
    half_slots = plan.slots // 2
    across = plan.narrow // 2
    for r in range(plan.slots):
        chip = plan.chip(table, route, h, r)
        down = pl.ds(pl.multiple_of(chip // across * rows, 16), rows)
        over = pl.ds(pl.multiple_of(chip % across * columns, 128), columns)
        weight[down, over] = pieces[r // half_slots][r % half_slots]


TRIPLE, MIX, GAIN1, SHIFT1, GAIN2, SHIFT2, UP = 0, 3, 4, 5, 6, 7, 8
TABLE_ROWS = 16
SHARE = 128


def split_kernel(plan, index_ref, triple_ref, mix_ref, tb_ref, mb_ref, g1_ref, s1_ref, g2_ref,
                 s2_ref, ub_ref, db_ref, mine_ref, share_ref, theirs_ref, spread):
    index = index_ref[0]
    core = index % 2
    of_wide, of_narrow = index // plan.narrow, index % plan.narrow
    triple, mix = triple_ref(), mix_ref()
    width = mix.shape[1]
    half = width // 2
    for out, h in ((mine_ref, core), (theirs_ref, core ^ 1)):
        for g in range(3):
            at = pl.multiple_of(g * width + h * half, 128)
            out[:, g * half : (g + 1) * half] = triple[:, pl.ds(at, half)]
        out[:, 3 * half : 4 * half] = mix[:, pl.ds(pl.multiple_of(h * half, 128), half)]

    spread[...] = jnp.zeros_like(spread)
    for row, ref in ((TRIPLE, tb_ref), (MIX, mb_ref), (GAIN1, g1_ref), (SHIFT1, s1_ref),
                     (GAIN2, g2_ref), (SHIFT2, s2_ref)):
        spread[row : row + 1, : ref.shape[1]] = ref()[...].astype(F32)
    for row, ref, which, parts in (
        (UP, ub_ref, of_wide, plan.wide),
        (UP + plan.narrow, db_ref, of_narrow, plan.narrow),
    ):
        count = ref.shape[1] // parts
        values = ref()[...].astype(F32)
        mine = jnp.zeros((1, count), F32)
        for k in range(parts):
            mine = jnp.where(which == k, values[:, k * count : (k + 1) * count], mine)
        spread[row : row + 1, :count] = mine
    share = spread[...].astype(BF)
    share_ref[...] = share
    theirs_ref[:TABLE_ROWS, 4 * half :] = share


def join_kernel(plan, table, mine_ref, share_ref, came_ref, first_ref, second_ref):
    core = plan.core(table)
    half = mine_ref.shape[1] // 4
    mine, came = mine_ref[...].astype(F32), came_ref[:, : 4 * half].astype(F32)
    both = jnp.concatenate(
        [jnp.where(core == 0, mine, came), jnp.where(core == 0, came, mine)], 0
    ).astype(BF)
    third = both.shape[0] // 3
    first_ref[0, :, : 3 * half] = both[: 2 * third, : 3 * half]
    second_ref[0, :third, :] = both[2 * third :, : 3 * half]
    for b in range(3):
        second_ref[0, third:, b * half : (b + 1) * half] = (
            both[b * third : (b + 1) * third, 3 * half :]
        )
    share, other = share_ref[...], came_ref[:TABLE_ROWS, 4 * half :]
    first_ref[0, :TABLE_ROWS, 3 * half :] = jnp.where(core == 0, share, other)
    first_ref[0, TABLE_ROWS:, 3 * half :] = jnp.where(core == 0, other, share)


def vectors_kernel(plan, share, table, low_ref, high_ref, out_ref, held, triple, plain, up, down):
    half_slots = plan.slots // 2
    columns = low_ref.shape[2] - SHARE
    for r in range(plan.slots):
        piece = (low_ref, high_ref)[r // half_slots]
        held[plan.chip(table, plan.far_first, 0, r)] = piece[r % half_slots, :, columns:]
    for ref in (triple, plain, up, down):
        ref[...] = jnp.zeros_like(ref)
    width = out_ref.shape[1]
    part = width // plan.wide

    def put(ref, rows, at):
        block, lane = divmod(at, SHARE)
        s = slice(block * SHARE, (block + 2) * SHARE)
        ref[..., s] = ref[..., s] + (pltpu.roll(rows, lane, 1) if lane else rows)

    for device in range(plan.devices):
        of_wide, of_narrow = divmod(device, plan.narrow)
        rows = held[device // 2].astype(F32)[device % 2 * TABLE_ROWS :][:TABLE_ROWS]
        rows = jnp.concatenate([rows, jnp.zeros_like(rows)], 1)
        put(triple, rows[:8], 3 * share * device)
        put(plain, rows[:8], share * device)
        put(up.at[of_narrow], rows[8:], part * of_wide)
        put(down, rows[8:], share * device)
    out_ref[...] = jnp.zeros_like(out_ref)
    for g in range(3):
        out_ref[TRIPLE + g : TRIPLE + g + 1, :] = triple[0:1, g * width : (g + 1) * width]
    out_ref[MIX:UP, :] = plain[MIX:UP, :width]
    for n in range(plan.narrow):
        out_ref[UP + n : UP + n + 1, :] = up[n, 0:1, :width]
    row = UP + plan.narrow
    out_ref[row : row + 1, :] = down[row - 8 : row - 7, :width]


def pack_vectors(plan, core, width, bias_own, bias_other, first_ref, second_ref, up_ref, out_ref):
    out_ref[...] = jnp.zeros_like(out_ref)
    half = width // 2
    for h, ref in ((0, bias_own), (1, bias_other)):
        at = pl.ds(pl.multiple_of((core ^ h) * half, 128), half)
        for g in range(3):
            out_ref[TRIPLE + g : TRIPLE + g + 1, at] = ref[:, g * half : (g + 1) * half]
    out_ref[MIX : MIX + 1, :width] = first_ref[2:3, :]
    out_ref[GAIN1 : GAIN1 + 2, :width] = first_ref[0:2, :]
    out_ref[GAIN2 : GAIN2 + 2, :width] = second_ref[0:2, :]
    for h in (0, 1):
        for y in range(plan.narrow // 2):
            row = up_ref[h : h + 1, y * width : (y + 1) * width]
            out_ref[pl.ds(UP + 2 * y + (core ^ h), 1), :width] = row
    out_ref[UP + plan.narrow : UP + plan.narrow + 1, :width] = second_ref[2:3, :]


def attention_kernel(plan, rows, h, table, x_ref, a, b, c, d, cos_ref, sin_ref, vec_ref,
                     keep_ref, probs_ref, context_ref, triple):
    core, live = plan.core(table), plan.live(table)
    tokens, width = x_ref.shape
    half = width // 2
    place_attention(plan, table, h, (a, b, c, d), triple, None, rows)
    x = x_ref[...]
    cos, sin = cos_ref[...], sin_ref[...]
    left = first_half(tokens)
    valid = lax.broadcasted_iota(jnp.int32, (1, tokens), 1) < live
    scale = jnp.asarray(1.0 / math.sqrt(HD), BF)
    for q in range(half // 128):
        at = [slice(g * half + 128 * q, g * half + 128 * q + 128) for g in range(3)]
        here = pl.ds(pl.multiple_of((core ^ h) * half + 128 * q, 128), 128)
        out = [
            nn(x, triple[:, s]) + vec_ref[TRIPLE + g : TRIPLE + g + 1, here]
            for g, s in enumerate(at)
        ]
        query, key = [(v * cos + swap_lanes(v) * sin).astype(BF) for v in out[:2]]
        value = out[2].astype(BF)
        for s, v in zip(at, (query, key, value)):
            keep_ref[:, s] = v
        context = []
        for e in (0, 1):
            mine = left if e == 0 else ~left
            masked = jnp.where(mine, query, jnp.zeros_like(query)) * scale
            score = jnp.where(valid, nt(masked, key), -1e30)
            power = jnp.exp(score - jnp.max(score, -1, keepdims=True))
            prob = power * (1.0 / jnp.sum(power, -1, keepdims=True))
            prob = prob.astype(BF)
            probs_ref[2 * q + e] = prob
            context.append(nn(prob, value))
        context_ref[:, 128 * q : 128 * q + 128] = (
            jnp.where(left, context[0], context[1]).astype(BF)
        )


def mix_kernel(plan, rows, table, x_ref, context_own, context_other, a, b, c, d, e, f, g, k,
               vec_ref, unit_ref, inv_ref, low_ref, mix):
    core = plan.core(table)
    half = context_own.shape[1]
    for h, pieces in ((0, (a, b, c, d)), (1, (e, f, g, k))):
        place_attention(plan, table, h, pieces, None, mix, rows)
    sides = []
    for side in (0, 1):
        total = 0.0
        for h, context in ((0, context_own), (1, context_other)):
            at = pl.ds(pl.multiple_of((core ^ h) * half, 128), half)
            total = total + nn(context[...], mix[side, at, :])
        sides.append(total)
    branch = jnp.concatenate(sides, 1)
    summed = x_ref[...].astype(F32) + (branch + vec_ref[MIX : MIX + 1, :])
    centred = summed - mean(summed)
    inverse = lax.rsqrt(mean(centred * centred) + EPSILON)
    unit = centred * inverse
    unit_ref[...] = unit
    inv_ref[...] = jnp.broadcast_to(inverse, inv_ref.shape)
    low_ref[...] = (
        unit * vec_ref[GAIN1 : GAIN1 + 1, :] + vec_ref[SHIFT1 : SHIFT1 + 1, :]
    ).astype(BF)


def up_kernel(plan, route, rows, columns, table, low_ref, a, b, c, d, vec_ref,
              own_ref, other_ref, slope_own_ref, slope_other_ref, weight):
    core = plan.core(table)
    low = low_ref[...]
    step = 256
    for h, (out, slope) in enumerate(((own_ref, slope_own_ref), (other_ref, slope_other_ref))):
        place_hidden(plan, route, table, h, ((a, b), (c, d))[h], weight.at[h], rows, columns)
        for k in range(out.shape[1] // step):
            s = slice(k * step, (k + 1) * step)
            y, at = divmod(k * step, columns)
            row = vec_ref[pl.ds(UP + 2 * y + (core ^ h), 1), at : at + step]
            up = nn(low, weight[h, :, s]) + row
            share = 0.5 * (1.0 + lax.erf(up * math.sqrt(0.5)))
            out[:, s] = (up * share).astype(BF)
            slope[:, s] = (
                share + up * jnp.exp(-0.5 * up * up) * (1.0 / math.sqrt(2.0 * math.pi))
            ).astype(BF)


def down_own_kernel(plan, route, rows, columns, table, act, a, b, out_ref, weight):
    place_hidden(plan, route, table, 0, (a, b), weight, rows, columns)
    out_ref[...] = nt(act[...], weight[...])


def down_kernel(plan, route, rows, columns, table, part_ref, act, a, b, unit_ref,
                cot_ref, vec_ref, out_ref, grad_ref, grad_low_ref, sums_ref, weight):
    place_hidden(plan, route, table, 1, (a, b), weight, rows, columns)
    first = (
        unit_ref[...] * vec_ref[GAIN1 : GAIN1 + 1, :] + vec_ref[SHIFT1 : SHIFT1 + 1, :]
    )
    cot = cot_ref[...].astype(F32)
    scaled = cot * vec_ref[GAIN2 : GAIN2 + 1, :]
    scaled_mean = mean(scaled)
    sums_ref[1:2, :] = jnp.sum(cot, 0, keepdims=True)
    total = part_ref[...] + nt(act[...], weight[...])
    bias = vec_ref[UP + plan.narrow : UP + plan.narrow + 1, :]
    summed = first + (total + bias)
    centred = summed - mean(summed)
    inverse = lax.rsqrt(mean(centred * centred) + EPSILON)
    unit = centred * inverse
    grad = inverse * (scaled - scaled_mean - unit * mean(scaled * unit))
    grad_ref[...] = grad
    low = grad.astype(BF)
    grad_low_ref[...] = low
    sums_ref[0:1, :] = jnp.sum(cot * unit, 0, keepdims=True)
    sums_ref[2:3, :] = jnp.sum(low.astype(F32), 0, keepdims=True)
    out_ref[...] = (
        unit * vec_ref[GAIN2 : GAIN2 + 1, :] + vec_ref[SHIFT2 : SHIFT2 + 1, :]
    ).astype(BF)


def grad_up_kernel(plan, route, rows, columns, table, low_ref, a, b, c, d, slope_own, slope_other,
                   own_ref, other_ref, sums_ref, weight):
    low = low_ref[...]
    step = 256
    for h, slope, out in ((1, slope_other, other_ref), (0, slope_own, own_ref)):
        place_hidden(plan, route, table, h, ((a, b), (c, d))[h], weight.at[h], rows, columns)
        for k in range(out.shape[1] // step):
            s = slice(k * step, (k + 1) * step)
            grad = (nn(low, weight[h, :, s]) * slope[:, s].astype(F32)).astype(BF)
            out[:, s] = grad
            sums_ref[h : h + 1, s] = jnp.sum(grad.astype(F32), 0, keepdims=True)


def hidden_grad_kernel(plan, route, rows, columns, table, left_own, left_other, right_own,
                       right_other, low_ref, high_ref, block):
    across, half_slots = plan.narrow // 2, plan.slots // 2
    a, b = left_own[...], left_other[...]
    for y in range(across):
        s = slice(y * columns, (y + 1) * columns)
        tile = tn(a, right_own[:, s]) + tn(b, right_other[:, s])
        block[:, y] = tile.astype(BF).reshape(plan.wide, rows, columns)
    for r in reversed(range(plan.slots)):
        chip = plan.chip(table, route, 0, r)
        out = (low_ref, high_ref)[r // half_slots]
        out[r % half_slots] = block[chip // across, chip % across]


def first_grad_kernel(plan, route, rows, columns, arows, table, gu_own, gu_other, a, b, c, d,
                      e, f, g, k, l, m, n, o, grad_ref, unit_ref, inv_ref, vec_ref, middle_ref,
                      mine_ref, theirs_ref, context_ref, sums_ref, weight, mix, low_ref):
    for h in (0, 1):
        place_hidden(plan, route, table, h, ((a, b), (c, d))[h], weight.at[h], rows, columns)
    width = unit_ref.shape[1]
    half = width // 2
    for h, pieces in ((0, (e, f, g, k)), (1, (l, m, n, o))):
        place_attention(plan, table, h, pieces, None, mix, arows)
    core = plan.core(table)
    total = nt(gu_own[...], weight[0])
    total = total + nt(gu_other[...], weight[1])
    grad = grad_ref[...] + total
    unit = unit_ref[...]
    scaled = grad * vec_ref[GAIN1 : GAIN1 + 1, :]
    middle = inv_ref[:, 0:1] * (scaled - mean(scaled) - unit * mean(scaled * unit))
    low = middle.astype(BF)
    middle_ref[...] = middle
    low_ref[...] = low
    mine_ref[...] = low_ref[:, pl.ds(pl.multiple_of(core * half, 128), half)]
    theirs_ref[...] = low_ref[:, pl.ds(pl.multiple_of((core ^ 1) * half, 128), half)]
    sums_ref[0:1, :] = jnp.sum(grad * unit, 0, keepdims=True)
    sums_ref[1:2, :] = jnp.sum(grad, 0, keepdims=True)
    sums_ref[2:3, :] = jnp.sum(low.astype(F32), 0, keepdims=True)
    context_ref[...] = (nt(low[:, :half], mix[0]) + nt(low[:, half:], mix[1])).astype(BF)


def attention_grad_kernel(plan, h, table, keep_ref, probs_ref, grad_ref, cos_ref, sin_ref,
                          out_ref, sums_ref):
    core = plan.core(table)
    tokens, width = grad_ref.shape
    half = width // 2
    cos, sin = cos_ref[...], sin_ref[...]
    left = first_half(tokens)
    scale = 1.0 / math.sqrt(HD)
    keep, grads_in, probs = keep_ref, grad_ref, probs_ref
    for q in range(half // 128):
        at = [slice(g * half + 128 * q, g * half + 128 * q + 128) for g in range(3)]
        query, key, value = [keep[:, s] for s in at]
        came = grads_in[:, pl.ds(pl.multiple_of((core ^ h) * half + 128 * q, 128), 128)]
        parts = []
        for e in (0, 1):
            mine = left if e == 0 else ~left
            low = probs[2 * q + e]
            prob = low.astype(F32)
            grad = nt(jnp.where(mine, came, jnp.zeros_like(came)), value)
            score = prob * (grad - jnp.sum(prob * grad, -1, keepdims=True))
            score = score.astype(BF)
            parts.append((nn(score, key), tn(score, query), tn(low, came)))
        grads = [jnp.where(left, u, v) for u, v in zip(*parts)]
        grads = [(g * scale) * cos + swap_lanes((g * scale) * sin) for g in grads[:2]] + grads[2:]
        for s, g in zip(at, grads):
            g = g.astype(BF)
            out_ref[:, s] = g
            sums_ref[:, s] = jnp.sum(g.astype(F32), 0, keepdims=True)


def attention_weight_kernel(plan, rows, table, x_own, x_other, g_own, g_other, c_own, c_other,
                            c_came_own, c_came_other, b_own, b_other, bias_own, bias_other,
                            first_ref, second_ref, up_ref, low_ref, high_ref, block, mixed, sums):
    core = plan.core(table)
    half_slots = plan.slots // 2
    tokens, columns = g_own.shape
    third = columns // 3
    height = rows + rows // 3
    pack_vectors(
        plan, core, x_own.shape[1], bias_own, bias_other, first_ref, second_ref, up_ref, sums
    )
    for ref in (high_ref, low_ref):
        ref[half_slots * height :, :] = sums[...].astype(BF)
    block[...] = (
        (tn(x_own[...], g_own[...]) + tn(x_other[...], g_other[...]))
        .astype(BF)
        .reshape(block.shape)
    )
    for h, mine, came in ((0, c_own, c_came_other), (1, c_other, c_came_own)):
        mixed[pl.ds((core ^ h) * half_slots, half_slots)] = (
            (tn(mine[...], b_own[...]) + tn(came[...], b_other[...]))
            .astype(BF)
            .reshape((half_slots,) + mixed.shape[1:])
        )
    for r in reversed(range(plan.slots)):
        chip = plan.chip(table, plan.far_first, 0, r)
        out, at = (low_ref, high_ref)[r // half_slots], r % half_slots * height
        out[at : at + rows, :] = block[chip]
        for b in range(3):
            out[at + rows : at + height, b * third : (b + 1) * third] = mixed[chip, b]


def input_grad_kernel(plan, rows, table, middle_ref, g_own, g_other, a, b, c, d, e, f, g, k,
                      out_ref, triple):
    for h, pieces in ((0, (a, b, c, d)), (1, (e, f, g, k))):
        place_attention(plan, table, h, pieces, triple.at[h], None, rows)
    total = nt(g_own[...], triple[0])
    total = total + nt(g_other[...], triple[1])
    out_ref[...] = (middle_ref[...] + total).astype(BF)


def half_tables(tokens):
    position = jnp.arange(tokens, dtype=F32)
    column = jnp.arange(2 * HD, dtype=jnp.int32)
    pair = (column % HD // 2).astype(F32)
    angle = position[:, None] * jnp.exp(pair * (-2.0 / HD) * math.log(10000.0))[None, :]
    parity = (column % 2).astype(F32) * 2.0 - 1.0
    return jnp.cos(angle), jnp.sin(angle) * parity[None, :]


def fast_body(
    plan,
    inputs,
    lengths,
    triple_weight,
    triple_bias,
    mix_weight,
    mix_bias,
    first_gain,
    first_shift,
    up_weight,
    up_bias,
    down_weight,
    down_bias,
    second_gain,
    second_shift,
    cotangent,
):
    tokens, width = inputs.shape
    half = width // 2
    wide, narrow = plan.wide, plan.narrow
    index = lax.axis_index(AXES)
    core = index & 1
    of_wide, of_narrow = lax.axis_index("wide"), lax.axis_index("narrow")
    table = plan.table(index, lengths)
    hidden = up_weight.shape[1]
    tile_rows = up_weight.shape[0]
    piece = triple_weight.shape[0]
    rows = 2 * piece
    third = rows // 3
    half_slots = plan.slots // 2
    far_first, far_second = plan.far_first, plan.far_second
    flops = 2.0 * tokens * width * width
    hidden_half = hidden * narrow // 2

    def by_core(pair):
        mine = jnp.where(core == 0, pair[0], pair[1])
        theirs = jnp.where(core == 0, pair[1], pair[0])
        return mine, theirs

    def in_order(mine, theirs, axis):
        return jnp.where(
            core == 0,
            jnp.concatenate([mine, theirs], axis),
            jnp.concatenate([theirs, mine], axis),
        )

    row = functools.partial(jnp.reshape, shape=(1, -1))
    mine, share, theirs = call(
        functools.partial(split_kernel, plan),
        [
            shape((piece, 4 * half)),
            shape((TABLE_ROWS, SHARE)),
            shape((piece, 4 * half + SHARE)),
        ],
        (
            index.astype(jnp.int32)[None],
            triple_weight,
            mix_weight,
            row(triple_bias),
            row(mix_bias),
            row(first_gain),
            row(first_shift),
            row(second_gain),
            row(second_shift),
            row(up_bias),
            row(down_bias),
        ),
        "s" + 10 * "l",
        [VMEM((TABLE_ROWS, SHARE), F32)],
        0,
        60,
    )
    first, second = call(
        functools.partial(join_kernel, plan),
        [shape((1, 2 * third, 3 * half + SHARE)), shape((1, 2 * third, 3 * half))],
        (table, mine, share, plan.swap(theirs)),
        "svvv",
        [],
        0,
        16,
    )
    cat = functools.partial(jnp.concatenate, axis=0)
    cos, sin = half_tables(tokens)
    inputs_came = plan.swap(after(inputs, first))
    down = after(down_weight.T[None], first)
    down_came = plan.send(down, far_second, 1)
    first = plan.gather_far(first)
    first, (down, down_came, inputs_came) = together(first, (down, down_came, inputs_came))
    first, down = cat(first), cat((down, down_came))
    first_came = plan.permute(first, plan.first)
    second = plan.gather_far(after(second, first))
    up = after(up_weight[None], first)
    up_came = plan.send(up, far_first, 1)
    first, first_came = after_all((first, first_came))
    first = cat((first, first_came))
    first_came = plan.permute(first, plan.last)
    second = cat(after_all(second, first))
    second_came = plan.permute(second, plan.first)
    up = cat(after_all((up, up_came), second))
    up_came = plan.send(up, far_first, 2)
    down = after(down, up)
    down_came = plan.send(down, far_second, 2)
    second, second_came = after_all((second, second_came), up)
    second = cat((second, second_came))
    first, first_came = after_all((first, first_came), second)
    second_came = plan.permute(second, plan.last)
    up = cat(after_all((up, up_came), first_came))
    up_came = plan.permute(up, plan.first)
    down = cat(after_all((down, down_came), up))
    down_came = plan.send(down, far_second, 4)
    second, second_came, cos, sin = after_all((second, second_came, cos, sin), down)
    att_own = [first, first_came, second, second_came]
    att_other = [plan.swap(v) for v in att_own]
    (vecs,) = call(
        functools.partial(vectors_kernel, plan, piece),
        [shape((TABLE_ROWS, width), F32)],
        (table, *att_own[:2]),
        "svv",
        [
            VMEM((plan.slots, 2 * third, SHARE), BF),
            VMEM((8, 3 * width + 2 * SHARE), F32),
            VMEM((8, width + 2 * SHARE), F32),
            VMEM((narrow, 8, width + 2 * SHARE), F32),
            VMEM((8, width + 2 * SHARE), F32),
        ],
        0,
        32,
    )

    def attend(h, pieces, gate=()):
        return call(
            functools.partial(attention_kernel, plan, rows, h),
            [
                shape((tokens, 3 * half)),
                shape((half // HD, tokens, tokens)),
                shape((tokens, half)),
            ],
            (after(table, *gate), inputs, *pieces, cos, sin, vecs),
            "s" + 8 * "v",
            [VMEM((width, 3 * half), BF)],
            80 * flops,
            24,
        )

    own, p_own, context_own = attend(0, att_own, (second_came, *att_other[:2]))
    up = cat(after_all((up, up_came), context_own))
    ups = (up, plan.permute(up, plan.last))
    down = cat(after_all((down, down_came), up))
    downs = (down, plan.permute(down, plan.last))
    other, p_other, context_other = attend(1, att_other, (down,))
    unit, inv, low = call(
        functools.partial(mix_kernel, plan, rows),
        [shape((tokens, width), F32), shape((tokens, 128), F32), shape((tokens, width))],
        (table, inputs, context_own, context_other, *att_own, *att_other, vecs),
        "s" + 12 * "v",
        [VMEM((2, width, half), BF)],
        1,
        24,
    )
    hidden_scratch = [VMEM((2, width, hidden_half), BF)]
    ups = after_all(ups, low)
    ups = (*ups, plan.swap(ups[0]), plan.swap(ups[1]))
    downs = (*downs, plan.swap(downs[0]))
    context_came = plan.swap(context_own), plan.swap(context_other)
    act_own, act_other, slope_own, slope_other = call(
        functools.partial(up_kernel, plan, far_first, tile_rows, hidden),
        [shape((tokens, hidden_half))] * 4,
        (after(table, *context_came, downs[2]), low, *ups, vecs),
        "s" + 6 * "v",
        hidden_scratch,
        1,
        24,
    )
    downs = after_all(downs, act_own)
    downs = (*downs, plan.swap(downs[1]))
    low_came, act_came = plan.swap(low), plan.swap(act_other)
    half_scratch = [VMEM((width, hidden_half), BF)]
    (downward,) = call(
        functools.partial(down_own_kernel, plan, far_second, tile_rows, hidden),
        [shape((tokens, width), F32)],
        (table, act_own, *downs[:2]),
        "svvv",
        half_scratch,
        80 * flops,
        24,
    )
    outputs, grad_second, grad_down, sums_second = call(
        functools.partial(down_kernel, plan, far_second, tile_rows, hidden),
        [
            shape((tokens, width)),
            shape((tokens, width), F32),
            shape((tokens, width)),
            shape((3, width), F32),
        ],
        (table, downward, act_other, *downs[2:], unit, cotangent, vecs),
        "s" + 7 * "v",
        half_scratch,
        1,
        24,
    )
    grad_down_came = plan.swap(grad_down)
    gu_own, gu_other, sums_up = call(
        functools.partial(grad_up_kernel, plan, far_second, tile_rows, hidden),
        [shape((tokens, hidden_half))] * 2 + [shape((2, hidden_half), F32)],
        (table, grad_down, *downs, slope_own, slope_other),
        "s" + 7 * "v",
        hidden_scratch,
        1,
        24,
    )
    gu_came = plan.swap(gu_other)

    def hidden_grad(route, left, left_came, right, right_came, cost, gate):
        return call(
            functools.partial(hidden_grad_kernel, plan, route, tile_rows, hidden),
            [shape((half_slots, tile_rows, hidden))] * 2,
            (after(table, *gate), left, left_came, right, right_came),
            "svvvv",
            [VMEM((wide, narrow // 2, tile_rows, hidden), BF)],
            cost,
            24,
        )

    down_low, down_high = hidden_grad(
        far_second, grad_down, grad_down_came, act_own, act_came, 80 * flops, (sums_up,)
    )
    down_came = plan.permute(down_high, plan.last)
    up_low, up_high = hidden_grad(far_first, low, low_came, gu_own, gu_came, 1, (down_low,))
    up_came = plan.permute(up_high, plan.last)
    grad_middle, branch_mine, branch_theirs, grad_context, sums_first = call(
        functools.partial(first_grad_kernel, plan, far_first, tile_rows, hidden, rows),
        [
            shape((tokens, width), F32),
            shape((tokens, half)),
            shape((tokens, half)),
            shape((tokens, width)),
            shape((3, width), F32),
        ],
        (
            after(table, up_low),
            gu_own,
            gu_other,
            *ups,
            *att_own,
            *att_other,
            grad_second,
            unit,
            inv,
            vecs,
        ),
        "s" + 18 * "v",
        hidden_scratch
        + [VMEM((2, width, half), BF), VMEM((tokens, width), BF)],
        1,
        24,
    )
    branch_came = plan.swap(branch_theirs)

    def attention_grad(h, keep, probs, gate=()):
        return call(
            functools.partial(attention_grad_kernel, plan, h),
            [shape((tokens, 3 * half)), shape((1, 3 * half), F32)],
            (after(table, *gate), keep, probs, grad_context, cos, sin),
            "svvvvv",
            [],
            1,
            24,
        )

    gt_other, bias_other = attention_grad(1, other, p_other, (act_came,))
    gt_came = plan.swap(gt_other)
    down_stay, down_away = halves(*after_all((down_low, down_came), bias_other))
    down_came = plan.send(down_away, far_second, 4)
    gt_own, bias_own = attention_grad(0, own, p_own, (down_away,))
    up_stay, up_away = halves(*after_all((up_low, up_came), bias_own))
    up_came = plan.permute(up_away, plan.first)
    height = rows + third
    packed_low, packed_high = call(
        functools.partial(attention_weight_kernel, plan, rows),
        [shape((half_slots * height + TABLE_ROWS, 3 * half))] * 2,
        (
            after(table, up_away),
            inputs,
            inputs_came,
            gt_own,
            gt_came,
            context_own,
            context_other,
            *context_came,
            branch_mine,
            branch_came,
            bias_own,
            bias_other,
            sums_first,
            sums_second,
            sums_up,
        ),
        "s" + 15 * "v",
        [
            VMEM((plan.slots, rows, 3 * half), BF),
            VMEM((plan.slots, 3, third, half), BF),
            VMEM((TABLE_ROWS, 3 * half), F32),
        ],
        80 * flops,
        24,
    )
    packed_came = plan.permute(packed_high, plan.last)
    down_stay, down_away = halves(*after_all((down_stay, down_came), packed_low))
    down_came = plan.send(down_away, far_second, 2)
    up_stay, up_away = halves(*after_all((up_stay, up_came), down_away))
    up_came = plan.send(up_away, far_first, 2)
    (input_grad,) = call(
        functools.partial(input_grad_kernel, plan, rows),
        [shape((tokens, width))],
        (after(table, up_away), grad_middle, gt_own, gt_other, *att_own, *att_other),
        "s" + 11 * "v",
        [VMEM((2, width, 3 * half), BF)],
        80 * flops,
        24,
    )
    packed_low, packed_came = after_all((packed_low, packed_came), input_grad)
    cut, end = half_slots // 2 * height, half_slots * height
    sums = added(packed_low[end:], packed_came[end:])
    packed_stay = added(packed_low[:cut], packed_came[:cut])
    packed_away = cat([added(packed_low[cut:end], packed_came[cut:end]), sums])
    packed_came = plan.permute(packed_away, plan.first)
    down_stay, down_came, up_stay, up_came = after_all(
        (down_stay, down_came, up_stay, up_came), packed_away
    )
    down_stay, down_away = halves(down_stay, down_came)
    down_came = plan.send(down_away, far_second, 1)
    up_stay, up_away = halves(up_stay, up_came)
    up_came = plan.send(up_away, far_first, 1)
    (packed_came,) = after_all((packed_came,), down_away, up_away)
    sums = added(sums, packed_came[cut:])
    parts = [
        cat(
            [
                added(packed_stay[k * height :][:height], packed_came[k * height :][:height]),
                sums,
            ]
        )
        for k in range(plan.far)
    ]
    down_stay, down_came, up_stay, up_came = after_all(
        (down_stay, down_came, up_stay, up_came), parts[1]
    )
    down_total = down_stay[0].astype(F32) + down_came[0].astype(F32)
    up_total = up_stay[0].astype(F32) + up_came[0].astype(F32)
    attention_total = sum([v.astype(F32) for v in plan.send_far(parts)], parts[0].astype(F32))
    sums = attention_total[height:, :width]
    flat = (sums + plan.swap(sums)).reshape(-1)

    def share_of(row, at, count):
        return lax.dynamic_slice(flat, (row * width + at * count,), (count,))

    mix_rows = attention_total[rows:height].reshape(rows // 3, 3, half).transpose(1, 0, 2)
    chip_grads = jnp.concatenate([attention_total[:rows], mix_rows.reshape(rows, half)], 1)
    mine, theirs = by_core((chip_grads[:piece], chip_grads[piece:]))
    came = plan.swap(theirs)
    pair = in_order(mine[None], came[None], 0)
    triple_grad = pair[:, :, : 3 * half].reshape(2, piece, 3, half).transpose(1, 2, 0, 3)
    mix_grad = pair[:, :, 3 * half :].transpose(1, 0, 2)
    return (
        outputs,
        input_grad,
        triple_grad.reshape(piece, 3 * width),
        share_of(TRIPLE, index, 3 * piece),
        mix_grad.reshape(piece, width),
        share_of(MIX, index, piece),
        share_of(GAIN1, index, piece),
        share_of(SHIFT1, index, piece),
        up_total,
        share_of(UP, of_narrow, hidden),
        down_total.T,
        share_of(UP + narrow, of_wide, down_bias.shape[0]),
        share_of(GAIN2, index, piece),
        share_of(SHIFT2, index, piece),
    )


def fits(plan_shape, width, hidden):
    wide, narrow = plan_shape
    powers = all(n >= 4 and n & (n - 1) == 0 for n in (wide, narrow)) and narrow == 4
    return (
        powers
        and width % (wide * 16) == 0
        and width % (wide * narrow // 2 * 48) == 0
        and hidden % (narrow * 128) == 0
        and width % 768 == 0
    )


def solution(mesh):
    placed = (
        P(("wide", "narrow"), None),
        P(("wide", "narrow")),
        P(("wide", "narrow"), None),
        P(("wide", "narrow")),
        P(("wide", "narrow"), None),
        P(("wide", "narrow")),
        P(("wide", "narrow")),
        P(("wide", "narrow")),
        P("wide", "narrow"),
        P("narrow"),
        P("narrow", "wide"),
        P("wide"),
        P(("wide", "narrow")),
        P(("wide", "narrow")),
        P(("wide", "narrow"), None),
    )
    wide, narrow = mesh.shape["wide"], mesh.shape["narrow"]

    def layer(*arrays):
        rows, hidden = arrays[8].shape
        if fits((wide, narrow), rows * wide, hidden * narrow):
            return fast_body(Plan(wide, narrow), *arrays)
        return body(*arrays)

    return jax.shard_map(
        layer,
        mesh=mesh,
        in_specs=placed,
        out_specs=(
            P(("wide", "narrow"), None),
            P(("wide", "narrow"), None),
            P(("wide", "narrow"), None),
            P(("wide", "narrow")),
            P(("wide", "narrow"), None),
            P(("wide", "narrow")),
            P(("wide", "narrow")),
            P(("wide", "narrow")),
            P("wide", "narrow"),
            P("narrow"),
            P("narrow", "wide"),
            P("wide"),
            P(("wide", "narrow")),
            P(("wide", "narrow")),
        ),
        check_vma=False,
    )
```

```python
import functools
import math

import jax
import jax.numpy as jnp
import numpy as np
from jax import lax
from jax.experimental import pallas as pl
from jax.experimental.pallas import tpu as pltpu
from jax.sharding import PartitionSpec as P

H = 12
HD = 64


EPSILON = 1e-06


def tables(token_rows, width, head):
    position = jnp.arange(token_rows, dtype=jnp.float32)
    column = jnp.arange(width, dtype=jnp.int32)
    pair_index = (column % head // 2).astype(jnp.float32)
    frequency = jnp.exp(pair_index * (-2.0 / head) * math.log(10000.0))
    angle = position[:, None] * frequency[None, :]
    parity = (column % 2).astype(jnp.float32) * 2.0 - 1.0
    return (jnp.cos(angle), jnp.sin(angle) * parity[None, :])


def swapped(values):
    shape = values.shape
    paired = values.reshape(shape[:-1] + (shape[-1] // 2, 2))
    return paired[..., ::-1].reshape(shape)


def rotate(values, cosine, sine):
    return values * cosine + swapped(values) * sine


def unrotate(grad, cosine, sine):
    return grad * cosine + swapped(grad * sine)


def normalize_forward(values, gain, shift):
    mean_row = jnp.mean(values, -1, keepdims=True)
    centred = values - mean_row
    inverse = lax.rsqrt(jnp.mean(centred * centred, -1, keepdims=True) + EPSILON)
    unit = centred * inverse
    return (unit * gain + shift, unit, inverse)


def normalize_backward(grad, unit, inverse, gain):
    scaled = grad * gain
    inner = (
        scaled
        - jnp.mean(scaled, -1, keepdims=True)
        - unit * jnp.mean(scaled * unit, -1, keepdims=True)
    )
    return (inner * inverse, jnp.sum(grad * unit, 0), jnp.sum(grad, 0))


def gelu_exact(values):
    return jax.nn.gelu(values, approximate=False)


def gelu_backward(upward, grad_active):
    unused, pull_back = jax.vjp(gelu_exact, upward)
    return pull_back(grad_active)[0]


def softmax_block(query_block, key, valid, scale):
    scores = (
        jnp.einsum("qhd,khd->hqk", query_block, key, preferred_element_type=jnp.float32) * scale
    )
    scores = jnp.where(valid[None, None, :], scores, -1e30)
    return jax.nn.softmax(scores, axis=-1)


def attention_forward(query, key, value, valid, scale):
    token_rows = query.shape[0]
    block = min(512, token_rows)
    weights_block = softmax_block(query, key, valid, scale)
    context = jnp.einsum(
        "hqk,khd->qhd",
        weights_block.astype(jnp.bfloat16),
        value,
        preferred_element_type=jnp.float32,
    )
    pieces = context.reshape(block, -1).astype(jnp.bfloat16)
    return pieces


def attention_backward(query, key, value, grad_context, valid, scale):
    weights_block = softmax_block(query, key, valid, scale)
    grad_weights = jnp.einsum(
        "qhd,khd->hqk", grad_context, value, preferred_element_type=jnp.float32
    )
    inner = weights_block * (
        grad_weights - jnp.sum(weights_block * grad_weights, -1, keepdims=True)
    )
    inner_low = inner.astype(jnp.bfloat16)
    query_pieces = (
        jnp.einsum("hqk,khd->qhd", inner_low, key, preferred_element_type=jnp.float32) * scale
    )
    grad_key = (
        jnp.einsum("hqk,qhd->khd", inner_low, query, preferred_element_type=jnp.float32) * scale
    )
    grad_value = jnp.einsum(
        "hqk,qhd->khd",
        weights_block.astype(jnp.bfloat16),
        grad_context,
        preferred_element_type=jnp.float32,
    )
    return (query_pieces, grad_key, grad_value)


def body(
    inputs,
    lengths,
    triple_weight,
    triple_bias,
    mix_weight,
    mix_bias,
    first_gain,
    first_shift,
    up_weight,
    up_bias,
    down_weight,
    down_bias,
    second_gain,
    second_shift,
    cotangent,
):
    token_rows, width = inputs.shape
    scale = 1.0 / math.sqrt(HD)
    head_shape = (token_rows, H, HD)
    (
        triple_full,
        mix_full,
        triple_bias_full,
        mix_bias_full,
        gain_one,
        shift_one,
        gain_two,
        shift_two,
    ) = (
        lax.all_gather(triple_weight, ("wide", "narrow"), axis=0, tiled=True),
        lax.all_gather(mix_weight, ("wide", "narrow"), axis=0, tiled=True),
        lax.all_gather(triple_bias, ("wide", "narrow"), axis=0, tiled=True),
        lax.all_gather(mix_bias, ("wide", "narrow"), axis=0, tiled=True),
        lax.all_gather(first_gain, ("wide", "narrow"), axis=0, tiled=True),
        lax.all_gather(first_shift, ("wide", "narrow"), axis=0, tiled=True),
        lax.all_gather(second_gain, ("wide", "narrow"), axis=0, tiled=True),
        lax.all_gather(second_shift, ("wide", "narrow"), axis=0, tiled=True),
    )
    up_rows, down_columns, down_bias_full = (
        lax.all_gather(up_weight, "wide", axis=0, tiled=True),
        lax.all_gather(down_weight, "wide", axis=1, tiled=True),
        lax.all_gather(down_bias, "wide", axis=0, tiled=True),
    )
    gain_one = gain_one.astype(jnp.float32)
    gain_two = gain_two.astype(jnp.float32)
    cosine, sine = tables(token_rows, width, HD)
    valid = jnp.arange(token_rows, dtype=jnp.int32) < lengths[0]
    triple = jnp.dot(
        inputs, triple_full, preferred_element_type=jnp.float32
    ) + triple_bias_full.astype(jnp.float32)
    query = rotate(triple[:, :width], cosine, sine).astype(jnp.bfloat16).reshape(head_shape)
    key = (
        rotate(triple[:, width : 2 * width], cosine, sine).astype(jnp.bfloat16).reshape(head_shape)
    )
    value = triple[:, 2 * width :].astype(jnp.bfloat16).reshape(head_shape)
    context = attention_forward(query, key, value, valid, scale)
    branch = jnp.dot(context, mix_full, preferred_element_type=jnp.float32) + mix_bias_full.astype(
        jnp.float32
    )
    first, first_unit, first_inverse = normalize_forward(
        inputs.astype(jnp.float32) + branch, gain_one, shift_one.astype(jnp.float32)
    )
    first_low = first.astype(jnp.bfloat16)
    gathered = lax.all_gather(first_low, "narrow", axis=0, tiled=True)
    upward = jnp.dot(gathered, up_rows, preferred_element_type=jnp.float32) + up_bias.astype(
        jnp.float32
    )
    active = gelu_exact(upward).astype(jnp.bfloat16)
    downward = lax.psum_scatter(
        jnp.dot(active, down_columns, preferred_element_type=jnp.float32).astype(jnp.bfloat16),
        "narrow",
        scatter_dimension=0,
        tiled=True,
    ).astype(jnp.float32)
    downward = downward + down_bias_full.astype(jnp.float32)
    result, second_unit, second_inverse = normalize_forward(
        first + downward, gain_two, shift_two.astype(jnp.float32)
    )
    outputs = result.astype(jnp.bfloat16)
    grad_second, second_gain_grad, second_shift_grad = normalize_backward(
        cotangent.astype(jnp.float32), second_unit, second_inverse, gain_two
    )
    grad_down = grad_second.astype(jnp.bfloat16)
    grad_gathered = lax.all_gather(grad_down, "narrow", axis=0, tiled=True)
    grad_active = jnp.dot(grad_gathered, down_columns.T, preferred_element_type=jnp.float32)
    grad_up = gelu_backward(upward, grad_active).astype(jnp.bfloat16)
    grad_feed = lax.psum_scatter(
        jnp.dot(grad_up, up_rows.T, preferred_element_type=jnp.float32).astype(jnp.bfloat16),
        "narrow",
        scatter_dimension=0,
        tiled=True,
    ).astype(jnp.float32)
    up_part = jnp.dot(gathered.T, grad_up, preferred_element_type=jnp.float32)
    down_part = jnp.dot(active.T, grad_gathered, preferred_element_type=jnp.float32)
    down_bias_part = jnp.sum(grad_gathered, 0, dtype=jnp.float32)
    up_weight_grad, down_weight_grad, down_bias_grad = (
        lax.psum_scatter(
            up_part.astype(jnp.bfloat16), "wide", scatter_dimension=0, tiled=True
        ).astype(jnp.float32),
        lax.psum_scatter(
            down_part.astype(jnp.bfloat16), "wide", scatter_dimension=1, tiled=True
        ).astype(jnp.float32),
        lax.psum_scatter(
            down_bias_part.astype(jnp.bfloat16), "wide", scatter_dimension=0, tiled=True
        ).astype(jnp.float32),
    )
    up_bias_grad = lax.psum(jnp.sum(grad_up, 0, dtype=jnp.float32), "wide")
    grad_first = grad_second + grad_feed
    grad_middle, first_gain_grad, first_shift_grad = normalize_backward(
        grad_first, first_unit, first_inverse, gain_one
    )
    grad_branch = grad_middle.astype(jnp.bfloat16)
    mix_weight_grad = jnp.dot(context.T, grad_branch, preferred_element_type=jnp.float32)
    mix_bias_grad = jnp.sum(grad_branch, 0, dtype=jnp.float32)
    triple_back, mix_back = (
        lax.all_gather(triple_weight, ("wide", "narrow"), axis=0, tiled=True),
        lax.all_gather(mix_weight, ("wide", "narrow"), axis=0, tiled=True),
    )
    grad_context = (
        jnp.dot(grad_branch, mix_back.T, preferred_element_type=jnp.float32)
        .astype(jnp.bfloat16)
        .reshape(head_shape)
    )
    grad_query, grad_key, grad_value = attention_backward(
        query, key, value, grad_context, valid, scale
    )
    grad_triple = jnp.concatenate(
        [
            unrotate(grad_query.reshape(token_rows, width), cosine, sine),
            unrotate(grad_key.reshape(token_rows, width), cosine, sine),
            grad_value.reshape(token_rows, width),
        ],
        1,
    ).astype(jnp.bfloat16)
    triple_local = jnp.dot(inputs.T, grad_triple, preferred_element_type=jnp.float32)
    triple_bias_local = jnp.sum(grad_triple, 0, dtype=jnp.float32)
    grad_inputs = grad_middle + jnp.dot(
        grad_triple, triple_back.T, preferred_element_type=jnp.float32
    )
    summed = (
        lax.psum_scatter(triple_local, ("wide", "narrow"), scatter_dimension=0, tiled=True),
        lax.psum_scatter(mix_weight_grad, ("wide", "narrow"), scatter_dimension=0, tiled=True),
        lax.psum_scatter(triple_bias_local, ("wide", "narrow"), scatter_dimension=0, tiled=True),
        lax.psum_scatter(mix_bias_grad, ("wide", "narrow"), scatter_dimension=0, tiled=True),
        lax.psum_scatter(first_gain_grad, ("wide", "narrow"), scatter_dimension=0, tiled=True),
        lax.psum_scatter(first_shift_grad, ("wide", "narrow"), scatter_dimension=0, tiled=True),
        lax.psum_scatter(second_gain_grad, ("wide", "narrow"), scatter_dimension=0, tiled=True),
        lax.psum_scatter(second_shift_grad, ("wide", "narrow"), scatter_dimension=0, tiled=True),
    )
    return (
        outputs,
        grad_inputs.astype(jnp.bfloat16),
        summed[0],
        summed[2],
        summed[1],
        summed[3],
        summed[4],
        summed[5],
        up_weight_grad,
        up_bias_grad,
        down_weight_grad,
        down_bias_grad,
        summed[6],
        summed[7],
    )


VMEM = pltpu.VMEM
SMEM = pltpu.SMEM
BF = jnp.bfloat16
F32 = jnp.float32
AXES = ("wide", "narrow")
WHOLE = pl.BlockSpec(memory_space=VMEM)
SCALARS = pl.BlockSpec(memory_space=SMEM)
LEFT = pl.BlockSpec(memory_space=pltpu.HBM)


def nn(a, b):
    return lax.dot_general(a, b, (((1,), (0,)), ((), ())), preferred_element_type=F32)


def nt(a, b):
    return lax.dot_general(a, b, (((1,), (1,)), ((), ())), preferred_element_type=F32)


def tn(a, b):
    return lax.dot_general(a, b, (((0,), (0,)), ((), ())), preferred_element_type=F32)


def shape(dims, dtype=BF):
    return jax.ShapeDtypeStruct(dims, dtype)


class Load:
    def __init__(self, source, held, sem):
        self.copy = pltpu.make_async_copy(source, held, sem)
        self.held, self.waited = held, False
        self.shape = held.shape
        self.copy.start()

    def __call__(self):
        if not self.waited:
            self.copy.wait()
            self.waited = True
        return self.held


def call(kernel, outs, operands, kinds, scratch, flops, megabytes, out_specs=None):
    specs = {"s": SCALARS, "v": WHOLE, "h": LEFT, "l": LEFT}
    loads = [k for k, kind in enumerate(kinds) if kind == "l"]
    held = [VMEM(operands[k].shape, operands[k].dtype) for k in loads]
    assert len(kinds) == len(operands)

    def whole(*refs):
        refs = list(refs)
        count = len(loads)
        if count:
            sems = refs.pop()
            buffers, refs = refs[-count:], refs[:-count]
            for n, k in enumerate(loads):
                refs[k] = Load(refs[k], buffers[n], sems.at[n])
        kernel(*refs)
        for k in loads:
            refs[k]()

    return pl.pallas_call(
        whole,
        out_shape=outs,
        in_specs=[specs[kind] for kind in kinds],
        out_specs=[WHOLE] * len(outs) if out_specs is None else out_specs,
        scratch_shapes=list(scratch)
        + held
        + ([pltpu.SemaphoreType.DMA((len(loads),))] if loads else []),
        compiler_params=pltpu.CompilerParams(vmem_limit_bytes=megabytes << 20),
        cost_estimate=pl.CostEstimate(
            flops=int(flops), bytes_accessed=1, transcendentals=0
        ),
    )(*operands)


def drain(ref, sem):
    pltpu.make_async_copy(ref, ref, sem).wait()


class Plan:
    def __init__(self, wide, narrow):
        self.wide, self.narrow = wide, narrow
        self.devices = wide * narrow
        x, y = narrow, narrow // 2
        self.first, self.last = (x, y), (y, x)
        self.far = wide // 2
        line = self.devices // self.far
        along = [(line << k, line << k) for k in reversed(range(self.far.bit_length() - 1))]
        self.far_first = (*along, self.first, self.last)
        self.far_second = (self.first, *along, self.last)
        self.routes = (self.far_first, self.far_second)
        self.slots = 1 << len(self.far_first)

    def lead(self, route, slot):
        masks = [0, 0]
        for k, pair in enumerate(route):
            if slot >> k & 1:
                masks = [mask ^ bit for mask, bit in zip(masks, pair)]
        return masks

    def chips(self, device):
        core = device & 1
        return [
            (device ^ self.lead(route, r)[c]) >> 1
            for route in self.routes
            for c in (core, core ^ 1)
            for r in range(self.slots)
        ]

    def table(self, index, live):
        chips = np.array([self.chips(i) for i in range(self.devices)], np.int32)
        mine = lax.dynamic_slice(jnp.asarray(chips), (index, 0), (1, chips.shape[1]))[0]
        return jnp.concatenate([mine, (index & 1)[None].astype(jnp.int32), live])

    def chip(self, table, route, h, slot):
        return table[(2 * self.routes.index(route) + h) * self.slots + slot]

    def core(self, table):
        return table[2 * len(self.routes) * self.slots]

    def live(self, table):
        return table[2 * len(self.routes) * self.slots + 1]

    def permute(self, value, masks):
        return lax.ppermute(value, AXES, [(i, i ^ masks[i & 1]) for i in range(self.devices)])

    def swap(self, value):
        return self.permute(value, (1, 1))

    def send(self, value, route, slot):
        return self.permute(value, self.lead(route, slot))

    def gather_far(self, value):
        return [value] + [self.send(value, self.far_first, m) for m in range(1, self.far)]

    def send_far(self, parts):
        return [self.send(v, self.far_first, m) for m, v in enumerate(parts) if m]


def added(*values):
    return sum([v.astype(F32) for v in values[1:]], values[0].astype(F32)).astype(BF)


def halves(*values):
    count = values[0].shape[0] // 2
    return added(*(v[:count] for v in values)), added(*(v[count:] for v in values))


def together(*lists):
    flat = list(lax.optimization_barrier(tuple(v for values in lists for v in values)))
    return [[flat.pop(0) for _ in values] for values in lists]


def after_all(values, *others):
    return lax.optimization_barrier(tuple(values) + others)[: len(values)]


def after(value, *others):
    return lax.optimization_barrier((value,) + others)[0] if others else value


def mean(v):
    return jnp.mean(v, -1, keepdims=True)


def swap_lanes(v):
    lane = lax.broadcasted_iota(jnp.int32, v.shape, 1)
    return jnp.where(lane % 2 == 0, pltpu.roll(v, v.shape[1] - 1, 1), pltpu.roll(v, 1, 1))


def first_half(rows):
    return lax.broadcasted_iota(jnp.int32, (rows, 2 * HD), 1) < HD


def place_attention(plan, table, h, pieces, triple, mix, rows):
    core = plan.core(table)
    half_slots = plan.slots // 2
    third = rows // 3
    columns = pieces[0].shape[2]
    width = columns // 3
    for r in range(plan.slots):
        chip = plan.chip(table, plan.far_first, h, r)
        side, at = divmod(r, half_slots)
        first, second = pieces[side], pieces[2 + side]
        if triple is not None:
            top = pl.ds(pl.multiple_of(chip * rows, 16), 2 * third)
            triple[top, :] = first[at]
            rest = pl.ds(pl.multiple_of(chip * rows + 2 * third, 16), third)
            triple[rest, :] = second[at, :third, :columns]
        if mix is not None:
            for b in range(3):
                here = pl.ds(pl.multiple_of(chip * rows + b * third, 16), third)
                mix[core ^ h, here, :] = second[at, third:, b * width : (b + 1) * width]


def place_hidden(plan, route, table, h, pieces, weight, rows, columns):
    across = plan.narrow // 2
    slots = [(piece, k) for piece in pieces for k in range(piece.shape[0])]
    for r, (piece, k) in enumerate(slots):
        chip = plan.chip(table, route, h, r)
        down = pl.ds(pl.multiple_of(chip // across * rows, 16), rows)
        over = pl.ds(pl.multiple_of(chip % across * columns, 128), columns)
        weight[down, over] = piece[k]


TRIPLE, MIX, GAIN1, SHIFT1, GAIN2, SHIFT2, UP = 0, 3, 4, 5, 6, 7, 8
TABLE_ROWS = 16
SHARE = 128


def split_kernel(index_ref, triple_ref, mix_ref, mine_ref, theirs_ref):
    core = index_ref[0] % 2
    width = mix_ref.shape[1]
    half = width // 2
    for out, h in ((mine_ref, core), (theirs_ref, core ^ 1)):
        for g in range(3):
            at = pl.multiple_of(g * width + h * half, 128)
            out[:, g * half : (g + 1) * half] = triple_ref[:, pl.ds(at, half)]
        out[:, 3 * half :] = mix_ref[:, pl.ds(pl.multiple_of(h * half, 128), half)]


def join_kernel(index_ref, mine_ref, came_ref, first_ref, rest_ref):
    core = index_ref[0] % 2
    half = mine_ref.shape[1] // 4
    mine, came = mine_ref[...].astype(F32), came_ref[...].astype(F32)
    both = jnp.concatenate(
        [jnp.where(core == 0, mine, came), jnp.where(core == 0, came, mine)], 0
    ).astype(BF)
    third = both.shape[0] // 3
    first_ref[0] = both[: 2 * third, : 3 * half]
    rest_ref[:third, :] = both[2 * third :, : 3 * half]
    for b in range(3):
        rest_ref[third:, b * half : (b + 1) * half] = both[b * third : (b + 1) * third, 3 * half :]


def spread_kernel(plan, index_ref, tb_ref, mb_ref, g1_ref, s1_ref, g2_ref, s2_ref, ub_ref, db_ref,
                  share_ref, spread):
    of_narrow = index_ref[0] % plan.narrow
    spread[...] = jnp.zeros_like(spread)
    for row, ref in ((TRIPLE, tb_ref), (MIX, mb_ref), (GAIN1, g1_ref), (SHIFT1, s1_ref),
                     (GAIN2, g2_ref), (SHIFT2, s2_ref), (UP, ub_ref)):
        spread[row : row + 1, : ref.shape[1]] = ref()[...].astype(F32)
    count = db_ref.shape[1] // plan.narrow
    values = db_ref()[...].astype(F32)
    mine = values[:, :count]
    for k in range(1, plan.narrow):
        mine = jnp.where(of_narrow == k, values[:, k * count : (k + 1) * count], mine)
    spread[UP + plan.narrow : UP + plan.narrow + 1, :count] = mine
    share_ref[...] = spread[...].astype(BF)


def beside_kernel(index_ref, rest_ref, share_ref, came_ref, out_ref):
    core = index_ref[0] % 2
    columns = rest_ref.shape[1]
    share, came = share_ref[...], came_ref[...]
    out_ref[0, :, :columns] = rest_ref[...]
    out_ref[0, :TABLE_ROWS, columns:] = jnp.where(core == 0, share, came)
    out_ref[0, TABLE_ROWS:, columns:] = jnp.where(core == 0, came, share)


def vectors_kernel(plan, share, table, low_ref, high_ref, out_ref, held, triple, plain, up, down):
    half_slots = plan.slots // 2
    columns = low_ref.shape[2] - SHARE
    for r in range(plan.slots):
        piece = (low_ref, high_ref)[r // half_slots]
        held[plan.chip(table, plan.far_first, 0, r)] = piece[r % half_slots, :, columns:]
    for ref in (triple, plain, up, down):
        ref[...] = jnp.zeros_like(ref)
    width = out_ref.shape[1]
    part = width // plan.wide

    def put(ref, rows, at):
        block, lane = divmod(at, SHARE)
        s = slice(block * SHARE, (block + 2) * SHARE)
        ref[..., s] = ref[..., s] + (pltpu.roll(rows, lane, 1) if lane else rows)

    for device in range(plan.devices):
        of_wide, of_narrow = divmod(device, plan.narrow)
        rows = held[device // 2].astype(F32)[device % 2 * TABLE_ROWS :][:TABLE_ROWS]
        rows = jnp.concatenate([rows, jnp.zeros_like(rows)], 1)
        put(triple, rows[:8], 3 * share * device)
        put(plain, rows[:8], share * device)
        put(up.at[of_narrow], rows[8:], part * of_wide)
        put(down, rows[8:], share * device)
    out_ref[...] = jnp.zeros_like(out_ref)
    for g in range(3):
        out_ref[TRIPLE + g : TRIPLE + g + 1, :] = triple[0:1, g * width : (g + 1) * width]
    out_ref[MIX:UP, :] = plain[MIX:UP, :width]
    for n in range(plan.narrow):
        out_ref[UP + n : UP + n + 1, :] = up[n, 0:1, :width]
    row = UP + plan.narrow
    out_ref[row : row + 1, :] = down[row - 8 : row - 7, :width]


def pack_vectors(plan, core, width, bias_own, bias_other, first_ref, second_ref, up_ref, out_ref):
    out_ref[...] = jnp.zeros_like(out_ref)
    half = width // 2
    for h, ref in ((0, bias_own), (1, bias_other)):
        at = pl.ds(pl.multiple_of((core ^ h) * half, 128), half)
        for g in range(3):
            out_ref[TRIPLE + g : TRIPLE + g + 1, at] = ref[:, g * half : (g + 1) * half]
    out_ref[MIX : MIX + 1, :width] = first_ref[2:3, :]
    out_ref[GAIN1 : GAIN1 + 2, :width] = first_ref[0:2, :]
    out_ref[GAIN2 : GAIN2 + 2, :width] = second_ref[0:2, :]
    for h in (0, 1):
        for y in range(plan.narrow // 2):
            row = up_ref[h : h + 1, y * width : (y + 1) * width]
            out_ref[pl.ds(UP + 2 * y + (core ^ h), 1), :width] = row
    out_ref[UP + plan.narrow : UP + plan.narrow + 1, :width] = second_ref[2:3, :]


def attention_kernel(plan, rows, h, table, x_ref, a, b, c, d, cos_ref, sin_ref, vec_ref,
                     keep_ref, probs_ref, context_ref, triple):
    core, live = plan.core(table), plan.live(table)
    tokens, width = x_ref.shape
    half = width // 2
    place_attention(plan, table, h, (a, b, c, d), triple, None, rows)
    x = x_ref[...]
    cos, sin = cos_ref[...], sin_ref[...]
    left = first_half(tokens)
    valid = lax.broadcasted_iota(jnp.int32, (1, tokens), 1) < live
    scale = jnp.asarray(1.0 / math.sqrt(HD), BF)
    for q in range(half // 128):
        at = [slice(g * half + 128 * q, g * half + 128 * q + 128) for g in range(3)]
        here = pl.ds(pl.multiple_of((core ^ h) * half + 128 * q, 128), 128)
        out = [
            nn(x, triple[:, s]) + vec_ref[TRIPLE + g : TRIPLE + g + 1, here]
            for g, s in enumerate(at)
        ]
        query, key = [(v * cos + swap_lanes(v) * sin).astype(BF) for v in out[:2]]
        value = out[2].astype(BF)
        for s, v in zip(at, (query, key, value)):
            keep_ref[:, s] = v
        context = []
        for e in (0, 1):
            mine = left if e == 0 else ~left
            masked = jnp.where(mine, query, jnp.zeros_like(query)) * scale
            score = jnp.where(valid, nt(masked, key), -1e30)
            power = jnp.exp(score - jnp.max(score, -1, keepdims=True))
            prob = power * (1.0 / jnp.sum(power, -1, keepdims=True))
            prob = prob.astype(BF)
            probs_ref[2 * q + e] = prob
            context.append(nn(prob, value))
        context_ref[:, 128 * q : 128 * q + 128] = (
            jnp.where(left, context[0], context[1]).astype(BF)
        )


def mix_kernel(plan, rows, table, x_ref, context_own, context_other, a, b, c, d, e, f, g, k,
               vec_ref, unit_ref, inv_ref, low_ref, mix):
    core = plan.core(table)
    half = context_own.shape[1]
    for h, pieces in ((0, (a, b, c, d)), (1, (e, f, g, k))):
        place_attention(plan, table, h, pieces, None, mix, rows)
    sides = []
    for side in (0, 1):
        total = 0.0
        for h, context in ((0, context_own), (1, context_other)):
            at = pl.ds(pl.multiple_of((core ^ h) * half, 128), half)
            total = total + nn(context[...], mix[side, at, :])
        sides.append(total)
    branch = jnp.concatenate(sides, 1)
    summed = x_ref[...].astype(F32) + (branch + vec_ref[MIX : MIX + 1, :])
    centred = summed - mean(summed)
    inverse = lax.rsqrt(mean(centred * centred) + EPSILON)
    unit = centred * inverse
    unit_ref[...] = unit
    inv_ref[...] = jnp.broadcast_to(inverse, inv_ref.shape)
    low_ref[...] = (
        unit * vec_ref[GAIN1 : GAIN1 + 1, :] + vec_ref[SHIFT1 : SHIFT1 + 1, :]
    ).astype(BF)


def up_kernel(plan, route, rows, columns, table, low_ref, a, b, c, d, e, f, g, k, vec_ref,
              own_ref, other_ref, slope_own_ref, slope_other_ref, weight):
    core = plan.core(table)
    low = low_ref[...]
    step = 256
    for h, (out, slope) in enumerate(((own_ref, slope_own_ref), (other_ref, slope_other_ref))):
        place_hidden(plan, route, table, h, ((a, b, c, d), (e, f, g, k))[h], weight.at[h], rows, columns)
        for n in range(out.shape[1] // step):
            s = slice(n * step, (n + 1) * step)
            y, at = divmod(n * step, columns)
            row = vec_ref[pl.ds(UP + 2 * y + (core ^ h), 1), at : at + step]
            up = nn(low, weight[h, :, s]) + row
            share = 0.5 * (1.0 + lax.erf(up * math.sqrt(0.5)))
            out[:, s] = (up * share).astype(BF)
            slope[:, s] = (
                share + up * jnp.exp(-0.5 * up * up) * (1.0 / math.sqrt(2.0 * math.pi))
            ).astype(BF)


def down_own_kernel(plan, route, rows, columns, table, act, a, b, out_ref, weight):
    place_hidden(plan, route, table, 0, (a, b), weight, rows, columns)
    out_ref[...] = nt(act[...], weight[...])


def down_kernel(plan, route, rows, columns, table, part_ref, act, a, b, unit_ref,
                cot_ref, vec_ref, out_ref, grad_ref, grad_low_ref, sums_ref, weight):
    place_hidden(plan, route, table, 1, (a, b), weight, rows, columns)
    first = (
        unit_ref[...] * vec_ref[GAIN1 : GAIN1 + 1, :] + vec_ref[SHIFT1 : SHIFT1 + 1, :]
    )
    cot = cot_ref[...].astype(F32)
    scaled = cot * vec_ref[GAIN2 : GAIN2 + 1, :]
    scaled_mean = mean(scaled)
    sums_ref[1:2, :] = jnp.sum(cot, 0, keepdims=True)
    total = part_ref[...] + nt(act[...], weight[...])
    bias = vec_ref[UP + plan.narrow : UP + plan.narrow + 1, :]
    summed = first + (total + bias)
    centred = summed - mean(summed)
    inverse = lax.rsqrt(mean(centred * centred) + EPSILON)
    unit = centred * inverse
    grad = inverse * (scaled - scaled_mean - unit * mean(scaled * unit))
    grad_ref[...] = grad
    low = grad.astype(BF)
    grad_low_ref[...] = low
    sums_ref[0:1, :] = jnp.sum(cot * unit, 0, keepdims=True)
    sums_ref[2:3, :] = jnp.sum(low.astype(F32), 0, keepdims=True)
    out_ref[...] = (
        unit * vec_ref[GAIN2 : GAIN2 + 1, :] + vec_ref[SHIFT2 : SHIFT2 + 1, :]
    ).astype(BF)


def grad_up_kernel(plan, route, rows, columns, table, low_ref, a, b, c, d, slope_own,
                   slope_other, own_ref, other_ref, sums_ref, weight):
    low = low_ref[...]
    step = 256
    for h, slope, out in ((1, slope_other, other_ref), (0, slope_own, own_ref)):
        place_hidden(plan, route, table, h, ((a, b), (c, d))[h], weight.at[h], rows, columns)
        for n in range(out.shape[1] // step):
            s = slice(n * step, (n + 1) * step)
            grad = (nn(low, weight[h, :, s]) * slope[:, s].astype(F32)).astype(BF)
            out[:, s] = grad
            sums_ref[h : h + 1, s] = jnp.sum(grad.astype(F32), 0, keepdims=True)


def hidden_grad_kernel(plan, route, rows, columns, table, left_own, left_other, right_own,
                       right_other, low_ref, high_ref, block):
    across, half_slots = plan.narrow // 2, plan.slots // 2
    a, b = left_own[...], left_other[...]
    for y in range(across):
        s = slice(y * columns, (y + 1) * columns)
        tile = tn(a, right_own[:, s]) + tn(b, right_other[:, s])
        block[:, y] = tile.astype(BF).reshape(plan.wide, rows, columns)
    for r in reversed(range(plan.slots)):
        chip = plan.chip(table, route, 0, r)
        out = (low_ref, high_ref)[r // half_slots]
        out[r % half_slots] = block[chip // across, chip % across]


def first_grad_kernel(plan, route, rows, columns, arows, table, gu_own, gu_other, a, b, c, d,
                      e, f, g, k, p, q, r, s, l, m, n, o, grad_ref, unit_ref, inv_ref, vec_ref, middle_ref,
                      mine_ref, theirs_ref, context_ref, sums_ref, weight, mix, low_ref):
    for h in (0, 1):
        place_hidden(plan, route, table, h, ((a, b, c, d), (e, f, g, k))[h], weight.at[h], rows, columns)
    width = unit_ref.shape[1]
    half = width // 2
    for h, pieces in ((0, (p, q, r, s)), (1, (l, m, n, o))):
        place_attention(plan, table, h, pieces, None, mix, arows)
    core = plan.core(table)
    total = nt(gu_own[...], weight[0])
    total = total + nt(gu_other[...], weight[1])
    grad = grad_ref[...] + total
    unit = unit_ref[...]
    scaled = grad * vec_ref[GAIN1 : GAIN1 + 1, :]
    middle = inv_ref[:, 0:1] * (scaled - mean(scaled) - unit * mean(scaled * unit))
    low = middle.astype(BF)
    middle_ref[...] = middle
    low_ref[...] = low
    mine_ref[...] = low_ref[:, pl.ds(pl.multiple_of(core * half, 128), half)]
    theirs_ref[...] = low_ref[:, pl.ds(pl.multiple_of((core ^ 1) * half, 128), half)]
    sums_ref[0:1, :] = jnp.sum(grad * unit, 0, keepdims=True)
    sums_ref[1:2, :] = jnp.sum(grad, 0, keepdims=True)
    sums_ref[2:3, :] = jnp.sum(low.astype(F32), 0, keepdims=True)
    context_ref[...] = (nt(low[:, :half], mix[0]) + nt(low[:, half:], mix[1])).astype(BF)


def attention_grad_kernel(plan, h, table, keep_ref, probs_ref, grad_ref, cos_ref, sin_ref,
                          out_ref, sums_ref):
    core = plan.core(table)
    tokens, width = grad_ref.shape
    half = width // 2
    cos, sin = cos_ref[...], sin_ref[...]
    left = first_half(tokens)
    scale = 1.0 / math.sqrt(HD)
    keep, grads_in, probs = keep_ref, grad_ref, probs_ref
    for q in range(half // 128):
        at = [slice(g * half + 128 * q, g * half + 128 * q + 128) for g in range(3)]
        query, key, value = [keep[:, s] for s in at]
        came = grads_in[:, pl.ds(pl.multiple_of((core ^ h) * half + 128 * q, 128), 128)]
        parts = []
        for e in (0, 1):
            mine = left if e == 0 else ~left
            low = probs[2 * q + e]
            prob = low.astype(F32)
            grad = nt(jnp.where(mine, came, jnp.zeros_like(came)), value)
            score = prob * (grad - jnp.sum(prob * grad, -1, keepdims=True))
            score = score.astype(BF)
            parts.append((nn(score, key), tn(score, query), tn(low, came)))
        grads = [jnp.where(left, u, v) for u, v in zip(*parts)]
        grads = [(g * scale) * cos + swap_lanes((g * scale) * sin) for g in grads[:2]] + grads[2:]
        for s, g in zip(at, grads):
            g = g.astype(BF)
            out_ref[:, s] = g
            sums_ref[:, s] = jnp.sum(g.astype(F32), 0, keepdims=True)


def attention_weight_kernel(plan, rows, table, x_own, x_other, g_own, g_other, c_own, c_other,
                            c_came_own, c_came_other, b_own, b_other, bias_own, bias_other,
                            first_ref, second_ref, up_ref, low_ref, high_ref, block, mixed, sums):
    core = plan.core(table)
    half_slots = plan.slots // 2
    tokens, columns = g_own.shape
    third = columns // 3
    height = rows + rows // 3
    pack_vectors(
        plan, core, x_own.shape[1], bias_own, bias_other, first_ref, second_ref, up_ref, sums
    )
    for ref in (high_ref, low_ref):
        ref[half_slots * height :, :] = sums[...].astype(BF)
    block[...] = (
        (tn(x_own[...], g_own[...]) + tn(x_other[...], g_other[...]))
        .astype(BF)
        .reshape(block.shape)
    )
    for h, mine, came in ((0, c_own, c_came_other), (1, c_other, c_came_own)):
        mixed[pl.ds((core ^ h) * half_slots, half_slots)] = (
            (tn(mine[...], b_own[...]) + tn(came[...], b_other[...]))
            .astype(BF)
            .reshape((half_slots,) + mixed.shape[1:])
        )
    for r in reversed(range(plan.slots)):
        chip = plan.chip(table, plan.far_first, 0, r)
        out, at = (low_ref, high_ref)[r // half_slots], r % half_slots * height
        out[at : at + rows, :] = block[chip]
        for b in range(3):
            out[at + rows : at + height, b * third : (b + 1) * third] = mixed[chip, b]


def input_grad_kernel(plan, rows, table, middle_ref, g_own, g_other, a, b, c, d, e, f, g, k,
                      out_ref, triple):
    for h, pieces in ((0, (a, b, c, d)), (1, (e, f, g, k))):
        place_attention(plan, table, h, pieces, triple.at[h], None, rows)
    total = nt(g_own[...], triple[0])
    total = total + nt(g_other[...], triple[1])
    out_ref[...] = (middle_ref[...] + total).astype(BF)


def total_kernel(plan, rows, table, a, b, c, d, mine_ref, theirs_ref, both):
    core = plan.core(table)
    total = sum([ref[...].astype(F32) for ref in (b, c, d)], a[...].astype(F32))
    third, half = rows // 3, total.shape[1] // 3
    width = 2 * half
    both[:, : 3 * half] = total[:rows]
    for k in range(3):
        both[k * third : (k + 1) * third, 3 * half :] = (
            total[rows : rows + third, k * half : (k + 1) * half]
        )
    piece = rows // 2
    mine_ref[:piece, :] = both[pl.ds(pl.multiple_of(core * piece, 8), piece), :]
    theirs_ref[:piece, :] = both[pl.ds(pl.multiple_of((core ^ 1) * piece, 8), piece), :]
    for ref in (mine_ref, theirs_ref):
        ref[piece:, :width] = total[rows + third :, :width]


def share_kernel(plan, table, index_ref, mine_ref, came_ref, triple_ref, mix_ref, tb_ref, mb_ref,
                 g1_ref, s1_ref, ub_ref, db_ref, g2_ref, s2_ref):
    core, index = plan.core(table), index_ref[0]
    piece, width = mix_ref.shape
    half = width // 2
    for ref, h in ((mine_ref, core), (came_ref, core ^ 1)):
        for g in range(3):
            at = pl.ds(pl.multiple_of(g * width + h * half, 128), half)
            triple_ref[:, at] = ref[:piece, g * half : (g + 1) * half]
        mix_ref[:, pl.ds(pl.multiple_of(h * half, 128), half)] = ref[:piece, 3 * half : 4 * half]
    sums = mine_ref[piece:, :width] + came_ref[piece:, :width]
    biases = jnp.concatenate([sums[g : g + 1, :] for g in range(3)], 1)
    biases = jnp.broadcast_to(biases, (8, 3 * width))
    tb_ref[...] = pltpu.roll(biases, (3 * width - index * 3 * piece) % (3 * width), 1)[
        0:1, : 3 * piece
    ]
    rolled = pltpu.roll(sums[:8], (width - index * piece) % width, 1)
    for row, ref in ((MIX, mb_ref), (GAIN1, g1_ref), (SHIFT1, s1_ref), (GAIN2, g2_ref),
                     (SHIFT2, s2_ref)):
        ref[...] = rolled[row : row + 1, :piece]
    of_wide, of_narrow = index // plan.narrow, index % plan.narrow
    mine = sums[UP : UP + 1, :]
    for n in range(1, plan.narrow):
        mine = jnp.where(of_narrow == n, sums[UP + n : UP + n + 1, :], mine)
    ub_ref[...] = mine
    count = db_ref.shape[1]
    rolled = pltpu.roll(sums[8:], (width - of_wide * count) % width, 1)
    row = UP + plan.narrow - 8
    db_ref[...] = rolled[row : row + 1, :count]


def half_tables(tokens):
    position = jnp.arange(tokens, dtype=F32)
    column = jnp.arange(2 * HD, dtype=jnp.int32)
    pair = (column % HD // 2).astype(F32)
    angle = position[:, None] * jnp.exp(pair * (-2.0 / HD) * math.log(10000.0))[None, :]
    parity = (column % 2).astype(F32) * 2.0 - 1.0
    return jnp.cos(angle), jnp.sin(angle) * parity[None, :]


def fast_body(
    plan,
    inputs,
    lengths,
    triple_weight,
    triple_bias,
    mix_weight,
    mix_bias,
    first_gain,
    first_shift,
    up_weight,
    up_bias,
    down_weight,
    down_bias,
    second_gain,
    second_shift,
    cotangent,
):
    tokens, width = inputs.shape
    half = width // 2
    wide, narrow = plan.wide, plan.narrow
    index = lax.axis_index(AXES)
    core = index & 1
    of_wide = lax.axis_index("wide")
    table = plan.table(index, lengths)
    hidden = up_weight.shape[1]
    tile_rows = up_weight.shape[0]
    piece = triple_weight.shape[0]
    rows = 2 * piece
    third = rows // 3
    half_slots = plan.slots // 2
    far_first, far_second = plan.far_first, plan.far_second
    flops = 2.0 * tokens * width * width
    hidden_half = hidden * narrow // 2

    place = index.astype(jnp.int32)[None]
    mine, theirs = call(
        split_kernel,
        [shape((piece, 4 * half))] * 2,
        (place, triple_weight, mix_weight),
        "svv",
        [],
        0,
        16,
    )
    first, rest = call(
        join_kernel,
        [shape((1, 2 * third, 3 * half)), shape((2 * third, 3 * half))],
        (place, mine, plan.swap(theirs)),
        "svv",
        [],
        0,
        16,
    )
    row = functools.partial(jnp.reshape, shape=(1, -1))
    up_share = lax.dynamic_slice(up_bias, (of_wide * (hidden // wide),), (hidden // wide,))
    (share,) = call(
        functools.partial(spread_kernel, plan),
        [shape((TABLE_ROWS, SHARE))],
        (
            after(place, first),
            row(triple_bias),
            row(mix_bias),
            row(first_gain),
            row(first_shift),
            row(second_gain),
            row(second_shift),
            row(up_share),
            row(down_bias),
        ),
        "s" + 8 * "l",
        [VMEM((TABLE_ROWS, SHARE), F32)],
        0,
        60,
    )
    (second,) = call(
        beside_kernel,
        [shape((1, 2 * third, 3 * half + SHARE))],
        (place, rest, share, plan.swap(share)),
        "svvv",
        [],
        0,
        16,
    )
    cat = functools.partial(jnp.concatenate, axis=0)
    cos, sin = half_tables(tokens)
    inputs_came = plan.swap(after(inputs, first))
    down = after(down_weight.T[None], first)
    down_came = plan.send(down, far_second, 1)
    first = cat(after_all(plan.gather_far(first), inputs_came, second))
    first_came = plan.permute(first, plan.first)
    second = plan.gather_far(after(second, first))
    up = after(up_weight[None], first)
    up_came = plan.send(up, far_first, 1)
    first, first_came = after_all((first, first_came))
    first = cat((first, first_came))
    first_came = plan.permute(first, plan.last)
    second = cat(after_all(second, first))
    second_came = plan.permute(second, plan.first)
    up = cat(after_all((up, up_came), second))
    up_came = plan.send(up, far_first, 2)
    down = cat(after_all((down, down_came), up))
    down_came = plan.send(down, far_second, 2)
    second, second_came = after_all((second, second_came), up)
    second = cat((second, second_came))
    first, first_came = after_all((first, first_came), second)
    second_came = plan.permute(second, plan.last)
    up = cat(after_all((up, up_came), first_came))
    up_came = plan.permute(up, plan.first)
    ups = [up, up_came, plan.permute(up, plan.last)]
    down = cat(after_all((down, down_came), up))
    down_came = plan.send(down, far_second, 4)
    second, second_came = after_all((second, second_came), down)
    att_own = [first, first_came, second, second_came]
    att_other = [plan.swap(v) for v in att_own]
    (vecs,) = call(
        functools.partial(vectors_kernel, plan, piece),
        [shape((TABLE_ROWS, width), F32)],
        (table, *att_own[2:]),
        "svv",
        [
            VMEM((plan.slots, 2 * third, SHARE), BF),
            VMEM((8, 3 * width + 2 * SHARE), F32),
            VMEM((8, width + 2 * SHARE), F32),
            VMEM((narrow, 8, width + 2 * SHARE), F32),
            VMEM((8, width + 2 * SHARE), F32),
        ],
        0,
        32,
    )

    def attend(h, pieces, gate=()):
        return call(
            functools.partial(attention_kernel, plan, rows, h),
            [
                shape((tokens, 3 * half)),
                shape((half // HD, tokens, tokens)),
                shape((tokens, half)),
            ],
            (after(table, *gate), inputs, *pieces, cos, sin, vecs),
            "s" + 8 * "v",
            [VMEM((width, 3 * half), BF)],
            80 * flops,
            24,
        )

    own, p_own, context_own = attend(0, att_own, (second_came, *att_other[:2]))
    (up_came,) = after_all((ups[1],), context_own)
    ups = [ups[0], up_came, ups[2], plan.permute(up_came, plan.last)]
    down = cat(after_all((down, down_came), up_came))
    downs = [down, plan.permute(down, plan.last)]
    other, p_other, context_other = attend(1, att_other, (down,))
    unit, inv, low = call(
        functools.partial(mix_kernel, plan, rows),
        [shape((tokens, width), F32), shape((tokens, 128), F32), shape((tokens, width))],
        (table, inputs, context_own, context_other, *att_own, *att_other, vecs),
        "s" + 12 * "v",
        [VMEM((2, width, half), BF)],
        1,
        24,
    )
    hidden_scratch = [VMEM((2, width, hidden_half), BF)]
    ups = [*ups, *(plan.swap(v) for v in ups)]
    down_low_came = plan.swap(downs[0])
    context_came = plan.swap(context_own), plan.swap(context_other)
    act_own, act_other, slope_own, slope_other = call(
        functools.partial(up_kernel, plan, far_first, tile_rows, hidden),
        [shape((tokens, hidden_half))] * 4,
        (table, low, *ups, vecs),
        "s" + 10 * "v",
        hidden_scratch,
        1,
        24,
    )
    (down_high,) = after_all(downs[1:], act_own)
    downs = [downs[0], down_high, down_low_came, plan.swap(down_high)]
    low_came, act_came = plan.swap(low), plan.swap(act_other)
    half_scratch = [VMEM((width, hidden_half), BF)]
    (downward,) = call(
        functools.partial(down_own_kernel, plan, far_second, tile_rows, hidden),
        [shape((tokens, width), F32)],
        (after(table, *context_came), act_own, *downs[:2]),
        "svvv",
        half_scratch,
        80 * flops,
        24,
    )
    outputs, grad_second, grad_down, sums_second = call(
        functools.partial(down_kernel, plan, far_second, tile_rows, hidden),
        [
            shape((tokens, width)),
            shape((tokens, width), F32),
            shape((tokens, width)),
            shape((3, width), F32),
        ],
        (table, downward, act_other, *downs[2:], unit, cotangent, vecs),
        "s" + 7 * "v",
        half_scratch,
        1,
        24,
    )
    grad_down_came = plan.swap(grad_down)
    gu_own, gu_other, sums_up = call(
        functools.partial(grad_up_kernel, plan, far_second, tile_rows, hidden),
        [shape((tokens, hidden_half))] * 2 + [shape((2, hidden_half), F32)],
        (table, grad_down, *downs, slope_own, slope_other),
        "s" + 7 * "v",
        hidden_scratch,
        1,
        24,
    )
    gu_came = plan.swap(gu_other)

    def hidden_grad(route, left, left_came, right, right_came, cost, gate):
        return call(
            functools.partial(hidden_grad_kernel, plan, route, tile_rows, hidden),
            [shape((half_slots, tile_rows, hidden))] * 2,
            (after(table, *gate), left, left_came, right, right_came),
            "svvvv",
            [VMEM((wide, narrow // 2, tile_rows, hidden), BF)],
            cost,
            24,
        )

    down_low, down_high = hidden_grad(
        far_second, grad_down, grad_down_came, act_own, act_came, 80 * flops, (sums_up,)
    )
    down_came = plan.permute(down_high, plan.last)
    up_low, up_high = hidden_grad(far_first, low, low_came, gu_own, gu_came, 1, (down_low,))
    up_came = plan.permute(up_high, plan.last)
    grad_middle, branch_mine, branch_theirs, grad_context, sums_first = call(
        functools.partial(first_grad_kernel, plan, far_first, tile_rows, hidden, rows),
        [
            shape((tokens, width), F32),
            shape((tokens, half)),
            shape((tokens, half)),
            shape((tokens, width)),
            shape((3, width), F32),
        ],
        (
            after(table, up_low),
            gu_own,
            gu_other,
            *ups,
            *att_own,
            *att_other,
            grad_second,
            unit,
            inv,
            vecs,
        ),
        "s" + 22 * "v",
        hidden_scratch
        + [VMEM((2, width, half), BF), VMEM((tokens, width), BF)],
        1,
        24,
    )
    branch_came = plan.swap(branch_theirs)

    def attention_grad(h, keep, probs, gate=()):
        return call(
            functools.partial(attention_grad_kernel, plan, h),
            [shape((tokens, 3 * half)), shape((1, 3 * half), F32)],
            (after(table, *gate), keep, probs, grad_context, cos, sin),
            "svvvvv",
            [],
            1,
            24,
        )

    gt_other, bias_other = attention_grad(1, other, p_other, (act_came,))
    gt_came = plan.swap(gt_other)
    down_stay, down_away = halves(*after_all((down_low, down_came), bias_other))
    down_came = plan.send(down_away, far_second, 4)
    gt_own, bias_own = attention_grad(0, own, p_own, (down_away,))
    up_stay, up_away = halves(*after_all((up_low, up_came), bias_own))
    up_came = plan.permute(up_away, plan.first)
    height = rows + third
    packed_low, packed_high = call(
        functools.partial(attention_weight_kernel, plan, rows),
        [shape((half_slots * height + TABLE_ROWS, 3 * half))] * 2,
        (
            after(table, up_away),
            inputs,
            inputs_came,
            gt_own,
            gt_came,
            context_own,
            context_other,
            *context_came,
            branch_mine,
            branch_came,
            bias_own,
            bias_other,
            sums_first,
            sums_second,
            sums_up,
        ),
        "s" + 15 * "v",
        [
            VMEM((plan.slots, rows, 3 * half), BF),
            VMEM((plan.slots, 3, third, half), BF),
            VMEM((TABLE_ROWS, 3 * half), F32),
        ],
        80 * flops,
        24,
    )
    packed_came = plan.permute(packed_high, plan.last)
    down_stay, down_away = halves(*after_all((down_stay, down_came), packed_low))
    down_came = plan.send(down_away, far_second, 2)
    up_stay, up_away = halves(*after_all((up_stay, up_came), down_away))
    up_came = plan.send(up_away, far_first, 2)
    (input_grad,) = call(
        functools.partial(input_grad_kernel, plan, rows),
        [shape((tokens, width))],
        (after(table, up_away), grad_middle, gt_own, gt_other, *att_own, *att_other),
        "s" + 11 * "v",
        [VMEM((2, width, 3 * half), BF)],
        80 * flops,
        24,
    )
    packed_low, packed_came = after_all((packed_low, packed_came), input_grad)
    cut, end = half_slots // 2 * height, half_slots * height
    sums = added(packed_low[end:], packed_came[end:])
    packed_stay = added(packed_low[:cut], packed_came[:cut])
    packed_away = cat([added(packed_low[cut:end], packed_came[cut:end]), sums])
    packed_came = plan.permute(packed_away, plan.first)
    down_stay, down_came, up_stay, up_came = after_all(
        (down_stay, down_came, up_stay, up_came), packed_away
    )
    down_stay, down_away = halves(down_stay, down_came)
    down_came = plan.send(down_away, far_second, 1)
    up_stay, up_away = halves(up_stay, up_came)
    up_came = plan.send(up_away, far_first, 1)
    (packed_came,) = after_all((packed_came,), down_came, up_came)
    sums = added(sums, packed_came[cut:])
    parts = [
        cat(
            [
                added(packed_stay[k * height :][:height], packed_came[k * height :][:height]),
                sums,
            ]
        )
        for k in range(plan.far)
    ]
    down_stay, down_came, up_stay, up_came = after_all(
        (down_stay, down_came, up_stay, up_came), parts[1]
    )
    down_total = down_stay[0].astype(F32) + down_came[0].astype(F32)
    up_total = up_stay[0].astype(F32) + up_came[0].astype(F32)
    mine, theirs = call(
        functools.partial(total_kernel, plan, rows),
        [shape((piece + TABLE_ROWS, 4 * half), F32)] * 2,
        (table, parts[0], *plan.send_far(parts)),
        "svvvv",
        [VMEM((rows, 4 * half), F32)],
        1,
        16,
    )
    one = [3 * piece, piece, piece, piece, hidden, down_bias.shape[0], piece, piece]
    triple_grad, mix_grad, *vectors = call(
        functools.partial(share_kernel, plan),
        [shape((piece, 3 * width), F32), shape((piece, width), F32)]
        + [shape((1, n), F32) for n in one],
        (table, place, mine, plan.swap(theirs)),
        "ssvv",
        [],
        1,
        16,
    )
    vectors = [v.reshape(-1) for v in vectors]
    return (
        outputs,
        input_grad,
        triple_grad,
        vectors[0],
        mix_grad,
        *vectors[1:4],
        up_total,
        vectors[4],
        down_total.T,
        *vectors[5:],
    )


def fits(plan_shape, width, hidden):
    wide, narrow = plan_shape
    powers = all(n >= 4 and n & (n - 1) == 0 for n in (wide, narrow)) and narrow == 4
    return (
        powers
        and width % (wide * 16) == 0
        and width % (wide * narrow // 2 * 48) == 0
        and hidden % (narrow * 128) == 0
        and width % 768 == 0
    )


def solution(mesh):
    placed = (
        P(("wide", "narrow"), None),
        P(("wide", "narrow")),
        P(("wide", "narrow"), None),
        P(("wide", "narrow")),
        P(("wide", "narrow"), None),
        P(("wide", "narrow")),
        P(("wide", "narrow")),
        P(("wide", "narrow")),
        P("wide", "narrow"),
        P("narrow"),
        P("narrow", "wide"),
        P("wide"),
        P(("wide", "narrow")),
        P(("wide", "narrow")),
        P(("wide", "narrow"), None),
    )
    wide, narrow = mesh.shape["wide"], mesh.shape["narrow"]

    def layer(*arrays):
        rows, hidden = arrays[8].shape
        if fits((wide, narrow), rows * wide, hidden * narrow):
            return fast_body(Plan(wide, narrow), *arrays)
        return body(*arrays)

    return jax.shard_map(
        layer,
        mesh=mesh,
        in_specs=placed,
        out_specs=(
            P(("wide", "narrow"), None),
            P(("wide", "narrow"), None),
            P(("wide", "narrow"), None),
            P(("wide", "narrow")),
            P(("wide", "narrow"), None),
            P(("wide", "narrow")),
            P(("wide", "narrow")),
            P(("wide", "narrow")),
            P("wide", "narrow"),
            P("narrow"),
            P("narrow", "wide"),
            P("wide"),
            P(("wide", "narrow")),
            P(("wide", "narrow")),
        ),
        check_vma=False,
    )
```

```python
import functools
import math

import jax
import jax.numpy as jnp
import numpy as np
from jax import lax
from jax.experimental import pallas as pl
from jax.experimental.pallas import tpu as pltpu
from jax.sharding import PartitionSpec as P

H = 12
HD = 64


EPSILON = 1e-06


def tables(token_rows, width, head):
    position = jnp.arange(token_rows, dtype=jnp.float32)
    column = jnp.arange(width, dtype=jnp.int32)
    pair_index = (column % head // 2).astype(jnp.float32)
    frequency = jnp.exp(pair_index * (-2.0 / head) * math.log(10000.0))
    angle = position[:, None] * frequency[None, :]
    parity = (column % 2).astype(jnp.float32) * 2.0 - 1.0
    return (jnp.cos(angle), jnp.sin(angle) * parity[None, :])


def swapped(values):
    shape = values.shape
    paired = values.reshape(shape[:-1] + (shape[-1] // 2, 2))
    return paired[..., ::-1].reshape(shape)


def rotate(values, cosine, sine):
    return values * cosine + swapped(values) * sine


def unrotate(grad, cosine, sine):
    return grad * cosine + swapped(grad * sine)


def normalize_forward(values, gain, shift):
    mean_row = jnp.mean(values, -1, keepdims=True)
    centred = values - mean_row
    inverse = lax.rsqrt(jnp.mean(centred * centred, -1, keepdims=True) + EPSILON)
    unit = centred * inverse
    return (unit * gain + shift, unit, inverse)


def normalize_backward(grad, unit, inverse, gain):
    scaled = grad * gain
    inner = (
        scaled
        - jnp.mean(scaled, -1, keepdims=True)
        - unit * jnp.mean(scaled * unit, -1, keepdims=True)
    )
    return (inner * inverse, jnp.sum(grad * unit, 0), jnp.sum(grad, 0))


def gelu_exact(values):
    return jax.nn.gelu(values, approximate=False)


def gelu_backward(upward, grad_active):
    unused, pull_back = jax.vjp(gelu_exact, upward)
    return pull_back(grad_active)[0]


def softmax_block(query_block, key, valid, scale):
    scores = (
        jnp.einsum("qhd,khd->hqk", query_block, key, preferred_element_type=jnp.float32) * scale
    )
    scores = jnp.where(valid[None, None, :], scores, -1e30)
    return jax.nn.softmax(scores, axis=-1)


def attention_forward(query, key, value, valid, scale):
    token_rows = query.shape[0]
    block = min(512, token_rows)
    weights_block = softmax_block(query, key, valid, scale)
    context = jnp.einsum(
        "hqk,khd->qhd",
        weights_block.astype(jnp.bfloat16),
        value,
        preferred_element_type=jnp.float32,
    )
    pieces = context.reshape(block, -1).astype(jnp.bfloat16)
    return pieces


def attention_backward(query, key, value, grad_context, valid, scale):
    weights_block = softmax_block(query, key, valid, scale)
    grad_weights = jnp.einsum(
        "qhd,khd->hqk", grad_context, value, preferred_element_type=jnp.float32
    )
    inner = weights_block * (
        grad_weights - jnp.sum(weights_block * grad_weights, -1, keepdims=True)
    )
    inner_low = inner.astype(jnp.bfloat16)
    query_pieces = (
        jnp.einsum("hqk,khd->qhd", inner_low, key, preferred_element_type=jnp.float32) * scale
    )
    grad_key = (
        jnp.einsum("hqk,qhd->khd", inner_low, query, preferred_element_type=jnp.float32) * scale
    )
    grad_value = jnp.einsum(
        "hqk,qhd->khd",
        weights_block.astype(jnp.bfloat16),
        grad_context,
        preferred_element_type=jnp.float32,
    )
    return (query_pieces, grad_key, grad_value)


def body(
    inputs,
    lengths,
    triple_weight,
    triple_bias,
    mix_weight,
    mix_bias,
    first_gain,
    first_shift,
    up_weight,
    up_bias,
    down_weight,
    down_bias,
    second_gain,
    second_shift,
    cotangent,
):
    token_rows, width = inputs.shape
    scale = 1.0 / math.sqrt(HD)
    head_shape = (token_rows, H, HD)
    (
        triple_full,
        mix_full,
        triple_bias_full,
        mix_bias_full,
        gain_one,
        shift_one,
        gain_two,
        shift_two,
    ) = (
        lax.all_gather(triple_weight, ("wide", "narrow"), axis=0, tiled=True),
        lax.all_gather(mix_weight, ("wide", "narrow"), axis=0, tiled=True),
        lax.all_gather(triple_bias, ("wide", "narrow"), axis=0, tiled=True),
        lax.all_gather(mix_bias, ("wide", "narrow"), axis=0, tiled=True),
        lax.all_gather(first_gain, ("wide", "narrow"), axis=0, tiled=True),
        lax.all_gather(first_shift, ("wide", "narrow"), axis=0, tiled=True),
        lax.all_gather(second_gain, ("wide", "narrow"), axis=0, tiled=True),
        lax.all_gather(second_shift, ("wide", "narrow"), axis=0, tiled=True),
    )
    up_rows, down_columns, down_bias_full = (
        lax.all_gather(up_weight, "wide", axis=0, tiled=True),
        lax.all_gather(down_weight, "wide", axis=1, tiled=True),
        lax.all_gather(down_bias, "wide", axis=0, tiled=True),
    )
    gain_one = gain_one.astype(jnp.float32)
    gain_two = gain_two.astype(jnp.float32)
    cosine, sine = tables(token_rows, width, HD)
    valid = jnp.arange(token_rows, dtype=jnp.int32) < lengths[0]
    triple = jnp.dot(
        inputs, triple_full, preferred_element_type=jnp.float32
    ) + triple_bias_full.astype(jnp.float32)
    query = rotate(triple[:, :width], cosine, sine).astype(jnp.bfloat16).reshape(head_shape)
    key = (
        rotate(triple[:, width : 2 * width], cosine, sine).astype(jnp.bfloat16).reshape(head_shape)
    )
    value = triple[:, 2 * width :].astype(jnp.bfloat16).reshape(head_shape)
    context = attention_forward(query, key, value, valid, scale)
    branch = jnp.dot(context, mix_full, preferred_element_type=jnp.float32) + mix_bias_full.astype(
        jnp.float32
    )
    first, first_unit, first_inverse = normalize_forward(
        inputs.astype(jnp.float32) + branch, gain_one, shift_one.astype(jnp.float32)
    )
    first_low = first.astype(jnp.bfloat16)
    gathered = lax.all_gather(first_low, "narrow", axis=0, tiled=True)
    upward = jnp.dot(gathered, up_rows, preferred_element_type=jnp.float32) + up_bias.astype(
        jnp.float32
    )
    active = gelu_exact(upward).astype(jnp.bfloat16)
    downward = lax.psum_scatter(
        jnp.dot(active, down_columns, preferred_element_type=jnp.float32).astype(jnp.bfloat16),
        "narrow",
        scatter_dimension=0,
        tiled=True,
    ).astype(jnp.float32)
    downward = downward + down_bias_full.astype(jnp.float32)
    result, second_unit, second_inverse = normalize_forward(
        first + downward, gain_two, shift_two.astype(jnp.float32)
    )
    outputs = result.astype(jnp.bfloat16)
    grad_second, second_gain_grad, second_shift_grad = normalize_backward(
        cotangent.astype(jnp.float32), second_unit, second_inverse, gain_two
    )
    grad_down = grad_second.astype(jnp.bfloat16)
    grad_gathered = lax.all_gather(grad_down, "narrow", axis=0, tiled=True)
    grad_active = jnp.dot(grad_gathered, down_columns.T, preferred_element_type=jnp.float32)
    grad_up = gelu_backward(upward, grad_active).astype(jnp.bfloat16)
    grad_feed = lax.psum_scatter(
        jnp.dot(grad_up, up_rows.T, preferred_element_type=jnp.float32).astype(jnp.bfloat16),
        "narrow",
        scatter_dimension=0,
        tiled=True,
    ).astype(jnp.float32)
    up_part = jnp.dot(gathered.T, grad_up, preferred_element_type=jnp.float32)
    down_part = jnp.dot(active.T, grad_gathered, preferred_element_type=jnp.float32)
    down_bias_part = jnp.sum(grad_gathered, 0, dtype=jnp.float32)
    up_weight_grad, down_weight_grad, down_bias_grad = (
        lax.psum_scatter(
            up_part.astype(jnp.bfloat16), "wide", scatter_dimension=0, tiled=True
        ).astype(jnp.float32),
        lax.psum_scatter(
            down_part.astype(jnp.bfloat16), "wide", scatter_dimension=1, tiled=True
        ).astype(jnp.float32),
        lax.psum_scatter(
            down_bias_part.astype(jnp.bfloat16), "wide", scatter_dimension=0, tiled=True
        ).astype(jnp.float32),
    )
    up_bias_grad = lax.psum(jnp.sum(grad_up, 0, dtype=jnp.float32), "wide")
    grad_first = grad_second + grad_feed
    grad_middle, first_gain_grad, first_shift_grad = normalize_backward(
        grad_first, first_unit, first_inverse, gain_one
    )
    grad_branch = grad_middle.astype(jnp.bfloat16)
    mix_weight_grad = jnp.dot(context.T, grad_branch, preferred_element_type=jnp.float32)
    mix_bias_grad = jnp.sum(grad_branch, 0, dtype=jnp.float32)
    triple_back, mix_back = (
        lax.all_gather(triple_weight, ("wide", "narrow"), axis=0, tiled=True),
        lax.all_gather(mix_weight, ("wide", "narrow"), axis=0, tiled=True),
    )
    grad_context = (
        jnp.dot(grad_branch, mix_back.T, preferred_element_type=jnp.float32)
        .astype(jnp.bfloat16)
        .reshape(head_shape)
    )
    grad_query, grad_key, grad_value = attention_backward(
        query, key, value, grad_context, valid, scale
    )
    grad_triple = jnp.concatenate(
        [
            unrotate(grad_query.reshape(token_rows, width), cosine, sine),
            unrotate(grad_key.reshape(token_rows, width), cosine, sine),
            grad_value.reshape(token_rows, width),
        ],
        1,
    ).astype(jnp.bfloat16)
    triple_local = jnp.dot(inputs.T, grad_triple, preferred_element_type=jnp.float32)
    triple_bias_local = jnp.sum(grad_triple, 0, dtype=jnp.float32)
    grad_inputs = grad_middle + jnp.dot(
        grad_triple, triple_back.T, preferred_element_type=jnp.float32
    )
    summed = (
        lax.psum_scatter(triple_local, ("wide", "narrow"), scatter_dimension=0, tiled=True),
        lax.psum_scatter(mix_weight_grad, ("wide", "narrow"), scatter_dimension=0, tiled=True),
        lax.psum_scatter(triple_bias_local, ("wide", "narrow"), scatter_dimension=0, tiled=True),
        lax.psum_scatter(mix_bias_grad, ("wide", "narrow"), scatter_dimension=0, tiled=True),
        lax.psum_scatter(first_gain_grad, ("wide", "narrow"), scatter_dimension=0, tiled=True),
        lax.psum_scatter(first_shift_grad, ("wide", "narrow"), scatter_dimension=0, tiled=True),
        lax.psum_scatter(second_gain_grad, ("wide", "narrow"), scatter_dimension=0, tiled=True),
        lax.psum_scatter(second_shift_grad, ("wide", "narrow"), scatter_dimension=0, tiled=True),
    )
    return (
        outputs,
        grad_inputs.astype(jnp.bfloat16),
        summed[0],
        summed[2],
        summed[1],
        summed[3],
        summed[4],
        summed[5],
        up_weight_grad,
        up_bias_grad,
        down_weight_grad,
        down_bias_grad,
        summed[6],
        summed[7],
    )


VMEM = pltpu.VMEM
SMEM = pltpu.SMEM
BF = jnp.bfloat16
F32 = jnp.float32
AXES = ("wide", "narrow")
WHOLE = pl.BlockSpec(memory_space=VMEM)
SCALARS = pl.BlockSpec(memory_space=SMEM)
LEFT = pl.BlockSpec(memory_space=pltpu.HBM)


def nn(a, b):
    return lax.dot_general(a, b, (((1,), (0,)), ((), ())), preferred_element_type=F32)


def nt(a, b):
    return lax.dot_general(a, b, (((1,), (1,)), ((), ())), preferred_element_type=F32)


def tn(a, b):
    return lax.dot_general(a, b, (((0,), (0,)), ((), ())), preferred_element_type=F32)


def shape(dims, dtype=BF):
    return jax.ShapeDtypeStruct(dims, dtype)


class Load:
    def __init__(self, source, held, sem):
        self.copy = pltpu.make_async_copy(source, held, sem)
        self.held, self.waited = held, False
        self.shape = held.shape
        self.copy.start()

    def __call__(self):
        if not self.waited:
            self.copy.wait()
            self.waited = True
        return self.held


def call(kernel, outs, operands, kinds, scratch, flops, megabytes, out_specs=None):
    specs = {"s": SCALARS, "v": WHOLE, "h": LEFT, "l": LEFT}
    loads = [k for k, kind in enumerate(kinds) if kind == "l"]
    held = [VMEM(operands[k].shape, operands[k].dtype) for k in loads]
    assert len(kinds) == len(operands)

    def whole(*refs):
        refs = list(refs)
        count = len(loads)
        if count:
            sems = refs.pop()
            buffers, refs = refs[-count:], refs[:-count]
            for n, k in enumerate(loads):
                refs[k] = Load(refs[k], buffers[n], sems.at[n])
        kernel(*refs)
        for k in loads:
            refs[k]()

    return pl.pallas_call(
        whole,
        out_shape=outs,
        in_specs=[specs[kind] for kind in kinds],
        out_specs=[WHOLE] * len(outs) if out_specs is None else out_specs,
        scratch_shapes=list(scratch)
        + held
        + ([pltpu.SemaphoreType.DMA((len(loads),))] if loads else []),
        compiler_params=pltpu.CompilerParams(vmem_limit_bytes=megabytes << 20),
        cost_estimate=pl.CostEstimate(
            flops=int(flops), bytes_accessed=1, transcendentals=0
        ),
    )(*operands)


def drain(ref, sem):
    pltpu.make_async_copy(ref, ref, sem).wait()


class Plan:
    def __init__(self, wide, narrow):
        self.wide, self.narrow = wide, narrow
        self.devices = wide * narrow
        x, y = narrow, narrow // 2
        self.first, self.last = (x, y), (y, x)
        self.far = wide // 2
        line = self.devices // self.far
        along = [(line << k, line << k) for k in reversed(range(self.far.bit_length() - 1))]
        self.far_first = (*along, self.first, self.last)
        self.far_second = (self.first, *along, self.last)
        self.routes = (self.far_first, self.far_second)
        self.slots = 1 << len(self.far_first)

    def lead(self, route, slot):
        masks = [0, 0]
        for k, pair in enumerate(route):
            if slot >> k & 1:
                masks = [mask ^ bit for mask, bit in zip(masks, pair)]
        return masks

    def chips(self, device):
        core = device & 1
        return [
            (device ^ self.lead(route, r)[c]) >> 1
            for route in self.routes
            for c in (core, core ^ 1)
            for r in range(self.slots)
        ]

    def table(self, index, live):
        chips = np.array([self.chips(i) for i in range(self.devices)], np.int32)
        mine = lax.dynamic_slice(jnp.asarray(chips), (index, 0), (1, chips.shape[1]))[0]
        return jnp.concatenate([mine, (index & 1)[None].astype(jnp.int32), live])

    def chip(self, table, route, h, slot):
        return table[(2 * self.routes.index(route) + h) * self.slots + slot]

    def core(self, table):
        return table[2 * len(self.routes) * self.slots]

    def live(self, table):
        return table[2 * len(self.routes) * self.slots + 1]

    def permute(self, value, masks):
        return lax.ppermute(value, AXES, [(i, i ^ masks[i & 1]) for i in range(self.devices)])

    def swap(self, value):
        return self.permute(value, (1, 1))

    def send(self, value, route, slot):
        return self.permute(value, self.lead(route, slot))

    def gather_far(self, value):
        return [value] + [self.send(value, self.far_first, m) for m in range(1, self.far)]

    def send_far(self, parts):
        return [self.send(v, self.far_first, m) for m, v in enumerate(parts) if m]


def added(*values):
    return sum([v.astype(F32) for v in values[1:]], values[0].astype(F32)).astype(BF)


def halves(*values):
    count = values[0].shape[0] // 2
    return added(*(v[:count] for v in values)), added(*(v[count:] for v in values))


def together(*lists):
    flat = list(lax.optimization_barrier(tuple(v for values in lists for v in values)))
    return [[flat.pop(0) for _ in values] for values in lists]


def after_all(values, *others):
    return lax.optimization_barrier(tuple(values) + others)[: len(values)]


def after(value, *others):
    return lax.optimization_barrier((value,) + others)[0] if others else value


def mean(v):
    return jnp.mean(v, -1, keepdims=True)


def swap_lanes(v):
    lane = lax.broadcasted_iota(jnp.int32, v.shape, 1)
    return jnp.where(lane % 2 == 0, pltpu.roll(v, v.shape[1] - 1, 1), pltpu.roll(v, 1, 1))


def first_half(rows):
    return lax.broadcasted_iota(jnp.int32, (rows, 2 * HD), 1) < HD


def place_attention(plan, table, h, pieces, triple, mix, rows):
    core = plan.core(table)
    half_slots = plan.slots // 2
    third = rows // 3
    columns = pieces[0].shape[2]
    width = columns // 3
    for r in range(plan.slots):
        chip = plan.chip(table, plan.far_first, h, r)
        side, at = divmod(r, half_slots)
        first, second = pieces[side], pieces[2 + side]
        if triple is not None:
            top = pl.ds(pl.multiple_of(chip * rows, 16), 2 * third)
            triple[top, :] = first[at]
            rest = pl.ds(pl.multiple_of(chip * rows + 2 * third, 16), third)
            triple[rest, :] = second[at, :third, :columns]
        if mix is not None:
            for b in range(3):
                here = pl.ds(pl.multiple_of(chip * rows + b * third, 16), third)
                mix[core ^ h, here, :] = second[at, third:, b * width : (b + 1) * width]


def place_hidden(plan, route, table, h, pieces, weight, rows, columns):
    across = plan.narrow // 2
    slots = [(piece, k) for piece in pieces for k in range(piece.shape[0])]
    for r, (piece, k) in enumerate(slots):
        chip = plan.chip(table, route, h, r)
        down = pl.ds(pl.multiple_of(chip // across * rows, 16), rows)
        over = pl.ds(pl.multiple_of(chip % across * columns, 128), columns)
        weight[down, over] = piece[k]


TRIPLE, MIX, GAIN1, SHIFT1, GAIN2, SHIFT2, UP = 0, 3, 4, 5, 6, 7, 8
TABLE_ROWS = 16
SHARE = 128


def split_kernel(index_ref, triple_ref, mix_ref, mine_ref, theirs_ref):
    core = index_ref[0] % 2
    width = mix_ref.shape[1]
    half = width // 2
    for out, h in ((mine_ref, core), (theirs_ref, core ^ 1)):
        for g in range(3):
            at = pl.multiple_of(g * width + h * half, 128)
            out[:, g * half : (g + 1) * half] = triple_ref[:, pl.ds(at, half)]
        out[:, 3 * half :] = mix_ref[:, pl.ds(pl.multiple_of(h * half, 128), half)]


def join_kernel(index_ref, mine_ref, came_ref, first_ref, rest_ref):
    core = index_ref[0] % 2
    half = mine_ref.shape[1] // 4
    mine, came = mine_ref[...].astype(F32), came_ref[...].astype(F32)
    both = jnp.concatenate(
        [jnp.where(core == 0, mine, came), jnp.where(core == 0, came, mine)], 0
    ).astype(BF)
    third = both.shape[0] // 3
    first_ref[0] = both[: 2 * third, : 3 * half]
    rest_ref[:third, :] = both[2 * third :, : 3 * half]
    for b in range(3):
        rest_ref[third:, b * half : (b + 1) * half] = both[b * third : (b + 1) * third, 3 * half :]


def spread_kernel(plan, index_ref, tb_ref, mb_ref, g1_ref, s1_ref, g2_ref, s2_ref, ub_ref, db_ref,
                  share_ref, spread):
    of_narrow = index_ref[0] % plan.narrow
    spread[...] = jnp.zeros_like(spread)
    for row, ref in ((TRIPLE, tb_ref), (MIX, mb_ref), (GAIN1, g1_ref), (SHIFT1, s1_ref),
                     (GAIN2, g2_ref), (SHIFT2, s2_ref), (UP, ub_ref)):
        spread[row : row + 1, : ref.shape[1]] = ref()[...].astype(F32)
    count = db_ref.shape[1] // plan.narrow
    values = db_ref()[...].astype(F32)
    mine = values[:, :count]
    for k in range(1, plan.narrow):
        mine = jnp.where(of_narrow == k, values[:, k * count : (k + 1) * count], mine)
    spread[UP + plan.narrow : UP + plan.narrow + 1, :count] = mine
    share_ref[...] = spread[...].astype(BF)


def beside_kernel(index_ref, rest_ref, share_ref, came_ref, out_ref):
    core = index_ref[0] % 2
    columns = rest_ref.shape[1]
    share, came = share_ref[...], came_ref[...]
    out_ref[0, :, :columns] = rest_ref[...]
    out_ref[0, :TABLE_ROWS, columns:] = jnp.where(core == 0, share, came)
    out_ref[0, TABLE_ROWS:, columns:] = jnp.where(core == 0, came, share)


def vectors_kernel(plan, share, table, low_ref, high_ref, out_ref, held, triple, plain, up, down):
    half_slots = plan.slots // 2
    columns = low_ref.shape[2] - SHARE
    for r in range(plan.slots):
        piece = (low_ref, high_ref)[r // half_slots]
        held[plan.chip(table, plan.far_first, 0, r)] = piece[r % half_slots, :, columns:]
    for ref in (triple, plain, up, down):
        ref[...] = jnp.zeros_like(ref)
    width = out_ref.shape[1]
    part = width // plan.wide

    def put(ref, rows, at):
        block, lane = divmod(at, SHARE)
        s = slice(block * SHARE, (block + 2) * SHARE)
        ref[..., s] = ref[..., s] + (pltpu.roll(rows, lane, 1) if lane else rows)

    for device in range(plan.devices):
        of_wide, of_narrow = divmod(device, plan.narrow)
        rows = held[device // 2].astype(F32)[device % 2 * TABLE_ROWS :][:TABLE_ROWS]
        rows = jnp.concatenate([rows, jnp.zeros_like(rows)], 1)
        put(triple, rows[:8], 3 * share * device)
        put(plain, rows[:8], share * device)
        put(up.at[of_narrow], rows[8:], part * of_wide)
        put(down, rows[8:], share * device)
    out_ref[...] = jnp.zeros_like(out_ref)
    for g in range(3):
        out_ref[TRIPLE + g : TRIPLE + g + 1, :] = triple[0:1, g * width : (g + 1) * width]
    out_ref[MIX:UP, :] = plain[MIX:UP, :width]
    for n in range(plan.narrow):
        out_ref[UP + n : UP + n + 1, :] = up[n, 0:1, :width]
    row = UP + plan.narrow
    out_ref[row : row + 1, :] = down[row - 8 : row - 7, :width]


def pack_vectors(plan, core, width, bias_own, bias_other, first_ref, second_ref, cot_ref, up_own,
                 up_other, out_ref):
    out_ref[...] = jnp.zeros_like(out_ref)
    half = width // 2
    for h, ref in ((0, bias_own), (1, bias_other)):
        at = pl.ds(pl.multiple_of((core ^ h) * half, 128), half)
        for g in range(3):
            out_ref[TRIPLE + g : TRIPLE + g + 1, at] = ref[:, g * half : (g + 1) * half]
    out_ref[MIX : MIX + 1, :width] = first_ref[2:3, :]
    out_ref[GAIN1 : GAIN1 + 2, :width] = first_ref[0:2, :]
    out_ref[GAIN2 : GAIN2 + 1, :width] = second_ref[0:1, :]
    out_ref[SHIFT2 : SHIFT2 + 1, :width] = cot_ref[...]
    for h, up_ref in ((0, up_own), (1, up_other)):
        for y in range(plan.narrow // 2):
            row = up_ref[:, y * width : (y + 1) * width]
            out_ref[pl.ds(UP + 2 * y + (core ^ h), 1), :width] = row
    out_ref[UP + plan.narrow : UP + plan.narrow + 1, :width] = second_ref[1:2, :]


def attention_kernel(plan, rows, h, table, x_ref, a, b, c, d, cos_ref, sin_ref, vec_ref,
                     keep_ref, probs_ref, context_ref, triple):
    core, live = plan.core(table), plan.live(table)
    tokens, width = x_ref.shape
    half = width // 2
    place_attention(plan, table, h, (a, b, c, d), triple, None, rows)
    x = x_ref[...]
    cos, sin = cos_ref[...], sin_ref[...]
    left = first_half(tokens)
    valid = lax.broadcasted_iota(jnp.int32, (1, tokens), 1) < live
    scale = jnp.asarray(1.0 / math.sqrt(HD), BF)
    for q in range(half // 128):
        at = [slice(g * half + 128 * q, g * half + 128 * q + 128) for g in range(3)]
        here = pl.ds(pl.multiple_of((core ^ h) * half + 128 * q, 128), 128)
        out = [
            nn(x, triple[:, s]) + vec_ref[TRIPLE + g : TRIPLE + g + 1, here]
            for g, s in enumerate(at)
        ]
        query, key = [(v * cos + swap_lanes(v) * sin).astype(BF) for v in out[:2]]
        value = out[2].astype(BF)
        for s, v in zip(at, (query, key, value)):
            keep_ref[:, s] = v
        context = []
        for e in (0, 1):
            mine = left if e == 0 else ~left
            masked = jnp.where(mine, query, jnp.zeros_like(query)) * scale
            score = jnp.where(valid, nt(masked, key), -1e30)
            power = jnp.exp(score - jnp.max(score, -1, keepdims=True))
            prob = power * (1.0 / jnp.sum(power, -1, keepdims=True))
            prob = prob.astype(BF)
            probs_ref[2 * q + e] = prob
            context.append(nn(prob, value))
        context_ref[:, 128 * q : 128 * q + 128] = (
            jnp.where(left, context[0], context[1]).astype(BF)
        )


def mix_kernel(plan, rows, table, x_ref, context_own, context_other, a, b, c, d, e, f, g, k,
               vec_ref, unit_ref, inv_ref, low_ref, mix):
    core = plan.core(table)
    half = context_own.shape[1]
    for h, pieces in ((0, (a, b, c, d)), (1, (e, f, g, k))):
        place_attention(plan, table, h, pieces, None, mix, rows)
    sides = []
    for side in (0, 1):
        total = 0.0
        for h, context in ((0, context_own), (1, context_other)):
            at = pl.ds(pl.multiple_of((core ^ h) * half, 128), half)
            total = total + nn(context[...], mix[side, at, :])
        sides.append(total)
    branch = jnp.concatenate(sides, 1)
    summed = x_ref[...].astype(F32) + (branch + vec_ref[MIX : MIX + 1, :])
    centred = summed - mean(summed)
    inverse = lax.rsqrt(mean(centred * centred) + EPSILON)
    unit = centred * inverse
    unit_ref[...] = unit
    inv_ref[...] = jnp.broadcast_to(inverse, inv_ref.shape)
    low_ref[...] = (
        unit * vec_ref[GAIN1 : GAIN1 + 1, :] + vec_ref[SHIFT1 : SHIFT1 + 1, :]
    ).astype(BF)


def up_kernel(plan, route, rows, columns, table, low_ref, a, b, c, d, e, f, g, k, vec_ref,
              own_ref, other_ref, slope_own_ref, slope_other_ref, weight):
    core = plan.core(table)
    low = low_ref[...]
    step = 256
    for h, (out, slope) in enumerate(((own_ref, slope_own_ref), (other_ref, slope_other_ref))):
        place_hidden(plan, route, table, h, ((a, b, c, d), (e, f, g, k))[h], weight.at[h], rows, columns)
        for n in range(out.shape[1] // step):
            s = slice(n * step, (n + 1) * step)
            y, at = divmod(n * step, columns)
            row = vec_ref[pl.ds(UP + 2 * y + (core ^ h), 1), at : at + step]
            up = nn(low, weight[h, :, s]) + row
            share = 0.5 * (1.0 + lax.erf(up * math.sqrt(0.5)))
            out[:, s] = (up * share).astype(BF)
            slope[:, s] = (
                share + up * jnp.exp(-0.5 * up * up) * (1.0 / math.sqrt(2.0 * math.pi))
            ).astype(BF)


def down_own_kernel(plan, route, rows, columns, table, act, a, b, unit_ref, cot_ref, vec_ref,
                    out_ref, mean_ref, sum_ref, weight):
    place_hidden(plan, route, table, 0, (a, b), weight, rows, columns)
    first = unit_ref[...] * vec_ref[GAIN1 : GAIN1 + 1, :] + vec_ref[SHIFT1 : SHIFT1 + 1, :]
    bias = vec_ref[UP + plan.narrow : UP + plan.narrow + 1, :]
    out_ref[...] = first + (nt(act[...], weight[...]) + bias)
    cot = cot_ref[...].astype(F32)
    sum_ref[...] = jnp.sum(cot, 0, keepdims=True)
    scaled_mean = mean(cot * vec_ref[GAIN2 : GAIN2 + 1, :])
    mean_ref[...] = jnp.broadcast_to(scaled_mean, mean_ref.shape)


def down_kernel(plan, route, rows, columns, table, part_ref, act, a, b, mean_ref,
                cot_ref, vec_ref, out_ref, grad_ref, grad_low_ref, sums_ref, weight):
    place_hidden(plan, route, table, 1, (a, b), weight, rows, columns)
    summed = part_ref[...] + nt(act[...], weight[...])
    cot = cot_ref[...].astype(F32)
    scaled = cot * vec_ref[GAIN2 : GAIN2 + 1, :]
    centred = summed - mean(summed)
    inverse = lax.rsqrt(mean(centred * centred) + EPSILON)
    unit = centred * inverse
    grad = inverse * (scaled - mean_ref[:, 0:1] - unit * mean(scaled * unit))
    grad_ref[...] = grad
    low = grad.astype(BF)
    grad_low_ref[...] = low
    sums_ref[0:1, :] = jnp.sum(cot * unit, 0, keepdims=True)
    sums_ref[1:2, :] = jnp.sum(low.astype(F32), 0, keepdims=True)
    out_ref[...] = (
        unit * vec_ref[GAIN2 : GAIN2 + 1, :] + vec_ref[SHIFT2 : SHIFT2 + 1, :]
    ).astype(BF)


def grad_up_kernel(plan, route, h, rows, columns, table, low_ref, a, b, slope, out, sums_ref,
                   weight):
    place_hidden(plan, route, table, h, (a, b), weight, rows, columns)
    low = low_ref[...]
    step = 256
    for n in range(out.shape[1] // step):
        s = slice(n * step, (n + 1) * step)
        grad = (nn(low, weight[:, s]) * slope[:, s].astype(F32)).astype(BF)
        out[:, s] = grad
        sums_ref[:, s] = jnp.sum(grad.astype(F32), 0, keepdims=True)


def hidden_grad_kernel(plan, route, rows, columns, table, left_own, left_other, right_own,
                       right_other, low_ref, high_ref, block):
    across, half_slots = plan.narrow // 2, plan.slots // 2
    a, b = left_own[...], left_other[...]
    for y in range(across):
        s = slice(y * columns, (y + 1) * columns)
        tile = tn(a, right_own[:, s]) + tn(b, right_other[:, s])
        block[:, y] = tile.astype(BF).reshape(plan.wide, rows, columns)
    for r in reversed(range(plan.slots)):
        chip = plan.chip(table, route, 0, r)
        out = (low_ref, high_ref)[r // half_slots]
        out[r % half_slots] = block[chip // across, chip % across]


def hidden_part_kernel(plan, route, part, rows, columns, table, left_own, left_other, right_own,
                       right_other, out_ref, block, lefts, some):
    across, half_slots = plan.narrow // 2, plan.slots // 2
    core = plan.core(table)
    here = plan.chip(table, route, 0, 0)
    lefts[0] = left_own[...].T
    lefts[1] = left_other[...].T

    @pl.when(core == 0)
    def _():
        y = (here % across) ^ part
        s = pl.ds(pl.multiple_of(y * columns, 128), columns)
        tile = nn(lefts[0], right_own[:, s]) + nn(lefts[1], right_other[:, s])
        block[:, pl.ds(y, 1)] = tile.astype(BF).reshape(plan.wide, 1, rows, columns)

    @pl.when(core == 1)
    def _():
        x = (here // across % 2) ^ part
        for z in range(plan.far):
            at = pl.ds(pl.multiple_of((2 * z + x) * rows, 16), rows)
            for k in (0, 1):
                some[k, z * rows : (z + 1) * rows, :] = lefts[k, at, :]
        tile = nn(some[0], right_own[...]) + nn(some[1], right_other[...])
        for z in range(plan.far):
            for y in range(across):
                block[2 * z + x, y] = tile[
                    z * rows : (z + 1) * rows, y * columns : (y + 1) * columns
                ].astype(BF)

    for r in range(half_slots):
        chip = plan.chip(table, route, 0, part * half_slots + r)
        out_ref[r] = block[chip // across, chip % across]


def first_grad_kernel(plan, route, rows, columns, arows, table, gu_own, gu_other, a, b, c, d,
                      e, f, g, k, p, q, r, s, l, m, n, o, grad_ref, unit_ref, inv_ref, vec_ref, middle_ref,
                      mine_ref, theirs_ref, context_ref, sums_ref, weight, mix, low_ref):
    for h in (0, 1):
        place_hidden(plan, route, table, h, ((a, b, c, d), (e, f, g, k))[h], weight.at[h], rows, columns)
    width = unit_ref.shape[1]
    half = width // 2
    for h, pieces in ((0, (p, q, r, s)), (1, (l, m, n, o))):
        place_attention(plan, table, h, pieces, None, mix, arows)
    core = plan.core(table)
    total = nt(gu_own[...], weight[0])
    total = total + nt(gu_other[...], weight[1])
    grad = grad_ref[...] + total
    unit = unit_ref[...]
    scaled = grad * vec_ref[GAIN1 : GAIN1 + 1, :]
    middle = inv_ref[:, 0:1] * (scaled - mean(scaled) - unit * mean(scaled * unit))
    low = middle.astype(BF)
    middle_ref[...] = middle
    low_ref[...] = low
    mine_ref[...] = low_ref[:, pl.ds(pl.multiple_of(core * half, 128), half)]
    theirs_ref[...] = low_ref[:, pl.ds(pl.multiple_of((core ^ 1) * half, 128), half)]
    sums_ref[0:1, :] = jnp.sum(grad * unit, 0, keepdims=True)
    sums_ref[1:2, :] = jnp.sum(grad, 0, keepdims=True)
    sums_ref[2:3, :] = jnp.sum(low.astype(F32), 0, keepdims=True)
    context_ref[...] = (nt(low[:, :half], mix[0]) + nt(low[:, half:], mix[1])).astype(BF)


def attention_grad_kernel(plan, h, table, keep_ref, probs_ref, grad_ref, cos_ref, sin_ref,
                          out_ref, sums_ref):
    core = plan.core(table)
    tokens, width = grad_ref.shape
    half = width // 2
    cos, sin = cos_ref[...], sin_ref[...]
    left = first_half(tokens)
    scale = 1.0 / math.sqrt(HD)
    keep, grads_in, probs = keep_ref, grad_ref, probs_ref
    for q in range(half // 128):
        at = [slice(g * half + 128 * q, g * half + 128 * q + 128) for g in range(3)]
        query, key, value = [keep[:, s] for s in at]
        came = grads_in[:, pl.ds(pl.multiple_of((core ^ h) * half + 128 * q, 128), 128)]
        parts = []
        for e in (0, 1):
            mine = left if e == 0 else ~left
            low = probs[2 * q + e]
            prob = low.astype(F32)
            grad = nt(jnp.where(mine, came, jnp.zeros_like(came)), value)
            score = prob * (grad - jnp.sum(prob * grad, -1, keepdims=True))
            score = score.astype(BF)
            parts.append((nn(score, key), tn(score, query), tn(low, came)))
        grads = [jnp.where(left, u, v) for u, v in zip(*parts)]
        grads = [(g * scale) * cos + swap_lanes((g * scale) * sin) for g in grads[:2]] + grads[2:]
        for s, g in zip(at, grads):
            g = g.astype(BF)
            out_ref[:, s] = g
            sums_ref[:, s] = jnp.sum(g.astype(F32), 0, keepdims=True)


def attention_weight_kernel(plan, rows, table, x_own, x_other, g_own, g_other, c_own, c_other,
                            c_came_own, c_came_other, b_own, b_other, bias_own, bias_other,
                            first_ref, second_ref, cot_ref, up_own, up_other, low_ref, high_ref,
                            block, mixed, sums):
    core = plan.core(table)
    half_slots = plan.slots // 2
    tokens, columns = g_own.shape
    third = columns // 3
    height = rows + rows // 3
    pack_vectors(plan, core, x_own.shape[1], bias_own, bias_other, first_ref, second_ref, cot_ref,
                 up_own, up_other, sums)
    for ref in (high_ref, low_ref):
        ref[half_slots * height :, :] = sums[...].astype(BF)
    block[...] = (
        (tn(x_own[...], g_own[...]) + tn(x_other[...], g_other[...]))
        .astype(BF)
        .reshape(block.shape)
    )
    for h, mine, came in ((0, c_own, c_came_other), (1, c_other, c_came_own)):
        mixed[pl.ds((core ^ h) * half_slots, half_slots)] = (
            (tn(mine[...], b_own[...]) + tn(came[...], b_other[...]))
            .astype(BF)
            .reshape((half_slots,) + mixed.shape[1:])
        )
    for r in reversed(range(plan.slots)):
        chip = plan.chip(table, plan.far_first, 0, r)
        out, at = (low_ref, high_ref)[r // half_slots], r % half_slots * height
        out[at : at + rows, :] = block[chip]
        for b in range(3):
            out[at + rows : at + height, b * third : (b + 1) * third] = mixed[chip, b]


def input_grad_kernel(plan, rows, table, middle_ref, g_own, g_other, a, b, c, d, e, f, g, k,
                      out_ref, triple):
    for h, pieces in ((0, (a, b, c, d)), (1, (e, f, g, k))):
        place_attention(plan, table, h, pieces, triple.at[h], None, rows)
    total = nt(g_own[...], triple[0])
    total = total + nt(g_other[...], triple[1])
    out_ref[...] = (middle_ref[...] + total).astype(BF)


def total_kernel(plan, rows, table, a, b, c, d, mine_ref, theirs_ref, both):
    core = plan.core(table)
    total = sum([ref[...].astype(F32) for ref in (b, c, d)], a[...].astype(F32))
    third, half = rows // 3, total.shape[1] // 3
    width = 2 * half
    both[:, : 3 * half] = total[:rows]
    for k in range(3):
        both[k * third : (k + 1) * third, 3 * half :] = (
            total[rows : rows + third, k * half : (k + 1) * half]
        )
    piece = rows // 2
    mine_ref[:piece, :] = both[pl.ds(pl.multiple_of(core * piece, 8), piece), :]
    theirs_ref[:piece, :] = both[pl.ds(pl.multiple_of((core ^ 1) * piece, 8), piece), :]
    for ref in (mine_ref, theirs_ref):
        ref[piece:, :width] = total[rows + third :, :width]


def share_kernel(plan, table, index_ref, mine_ref, came_ref, triple_ref, mix_ref, tb_ref, mb_ref,
                 g1_ref, s1_ref, ub_ref, db_ref, g2_ref, s2_ref):
    core, index = plan.core(table), index_ref[0]
    piece, width = mix_ref.shape
    half = width // 2
    for ref, h in ((mine_ref, core), (came_ref, core ^ 1)):
        for g in range(3):
            at = pl.ds(pl.multiple_of(g * width + h * half, 128), half)
            triple_ref[:, at] = ref[:piece, g * half : (g + 1) * half]
        mix_ref[:, pl.ds(pl.multiple_of(h * half, 128), half)] = ref[:piece, 3 * half : 4 * half]
    sums = mine_ref[piece:, :width] + came_ref[piece:, :width]
    biases = jnp.concatenate([sums[g : g + 1, :] for g in range(3)], 1)
    biases = jnp.broadcast_to(biases, (8, 3 * width))
    tb_ref[...] = pltpu.roll(biases, (3 * width - index * 3 * piece) % (3 * width), 1)[
        0:1, : 3 * piece
    ]
    rolled = pltpu.roll(sums[:8], (width - index * piece) % width, 1)
    for row, ref in ((MIX, mb_ref), (GAIN1, g1_ref), (SHIFT1, s1_ref), (GAIN2, g2_ref),
                     (SHIFT2, s2_ref)):
        ref[...] = rolled[row : row + 1, :piece]
    of_wide, of_narrow = index // plan.narrow, index % plan.narrow
    mine = sums[UP : UP + 1, :]
    for n in range(1, plan.narrow):
        mine = jnp.where(of_narrow == n, sums[UP + n : UP + n + 1, :], mine)
    ub_ref[...] = mine
    count = db_ref.shape[1]
    rolled = pltpu.roll(sums[8:], (width - of_wide * count) % width, 1)
    row = UP + plan.narrow - 8
    db_ref[...] = rolled[row : row + 1, :count]


def half_tables(tokens):
    position = jnp.arange(tokens, dtype=F32)
    column = jnp.arange(2 * HD, dtype=jnp.int32)
    pair = (column % HD // 2).astype(F32)
    angle = position[:, None] * jnp.exp(pair * (-2.0 / HD) * math.log(10000.0))[None, :]
    parity = (column % 2).astype(F32) * 2.0 - 1.0
    return jnp.cos(angle), jnp.sin(angle) * parity[None, :]


def fast_body(
    plan,
    inputs,
    lengths,
    triple_weight,
    triple_bias,
    mix_weight,
    mix_bias,
    first_gain,
    first_shift,
    up_weight,
    up_bias,
    down_weight,
    down_bias,
    second_gain,
    second_shift,
    cotangent,
):
    tokens, width = inputs.shape
    half = width // 2
    wide, narrow = plan.wide, plan.narrow
    index = lax.axis_index(AXES)
    core = index & 1
    of_wide = lax.axis_index("wide")
    table = plan.table(index, lengths)
    hidden = up_weight.shape[1]
    tile_rows = up_weight.shape[0]
    piece = triple_weight.shape[0]
    rows = 2 * piece
    third = rows // 3
    half_slots = plan.slots // 2
    far_first, far_second = plan.far_first, plan.far_second
    flops = 2.0 * tokens * width * width
    hidden_half = hidden * narrow // 2

    place = index.astype(jnp.int32)[None]
    mine, theirs = call(
        split_kernel,
        [shape((piece, 4 * half))] * 2,
        (place, triple_weight, mix_weight),
        "svv",
        [],
        0,
        16,
    )
    first, rest = call(
        join_kernel,
        [shape((1, 2 * third, 3 * half)), shape((2 * third, 3 * half))],
        (place, mine, plan.swap(theirs)),
        "svv",
        [],
        0,
        16,
    )
    row = functools.partial(jnp.reshape, shape=(1, -1))
    up_share = lax.dynamic_slice(up_bias, (of_wide * (hidden // wide),), (hidden // wide,))
    (share,) = call(
        functools.partial(spread_kernel, plan),
        [shape((TABLE_ROWS, SHARE))],
        (
            after(place, first),
            row(triple_bias),
            row(mix_bias),
            row(first_gain),
            row(first_shift),
            row(second_gain),
            row(second_shift),
            row(up_share),
            row(down_bias),
        ),
        "s" + 8 * "l",
        [VMEM((TABLE_ROWS, SHARE), F32)],
        0,
        60,
    )
    (second,) = call(
        beside_kernel,
        [shape((1, 2 * third, 3 * half + SHARE))],
        (place, rest, share, plan.swap(share)),
        "svvv",
        [],
        0,
        16,
    )
    cat = functools.partial(jnp.concatenate, axis=0)
    cos, sin = half_tables(tokens)
    inputs_came = plan.swap(after(inputs, first))
    down = after(down_weight.T[None], first)
    down_came = plan.send(down, far_second, 1)
    first = cat(after_all(plan.gather_far(first), inputs_came, second))
    first_came = plan.permute(first, plan.first)
    second = plan.gather_far(after(second, first))
    up = after(up_weight[None], first)
    up_came = plan.send(up, far_first, 1)
    first, first_came = after_all((first, first_came))
    first = cat((first, first_came))
    first_came = plan.permute(first, plan.last)
    second = cat(after_all(second, first))
    second_came = plan.permute(second, plan.first)
    down = cat(after_all((down, down_came), first))
    down_came = plan.send(down, far_second, 2)
    up = cat(after_all((up, up_came), down))
    up_came = plan.send(up, far_first, 2)
    second, second_came = after_all((second, second_came), up)
    second = cat((second, second_came))
    first, first_came = after_all((first, first_came), second)
    second_came = plan.permute(second, plan.last)
    up = cat(after_all((up, up_came), first_came))
    up_came = plan.permute(up, plan.first)
    ups = [up, up_came, plan.permute(up, plan.last)]
    down = cat(after_all((down, down_came), up))
    down_came = plan.send(down, far_second, 4)
    second, second_came = after_all((second, second_came), down)
    att_own = [first, first_came, second, second_came]
    att_other = [plan.swap(v) for v in att_own]
    (vecs,) = call(
        functools.partial(vectors_kernel, plan, piece),
        [shape((TABLE_ROWS, width), F32)],
        (table, *att_own[2:]),
        "svv",
        [
            VMEM((plan.slots, 2 * third, SHARE), BF),
            VMEM((8, 3 * width + 2 * SHARE), F32),
            VMEM((8, width + 2 * SHARE), F32),
            VMEM((narrow, 8, width + 2 * SHARE), F32),
            VMEM((8, width + 2 * SHARE), F32),
        ],
        0,
        32,
    )

    def attend(h, pieces, gate=()):
        return call(
            functools.partial(attention_kernel, plan, rows, h),
            [
                shape((tokens, 3 * half)),
                shape((half // HD, tokens, tokens)),
                shape((tokens, half)),
            ],
            (after(table, *gate), inputs, *pieces, cos, sin, vecs),
            "s" + 8 * "v",
            [VMEM((width, 3 * half), BF)],
            80 * flops,
            24,
        )

    own, p_own, context_own = attend(0, att_own, (second_came, *att_other[:2]))
    (up_came,) = after_all((ups[1],), context_own)
    ups = [ups[0], up_came, ups[2], plan.permute(up_came, plan.last)]
    down = cat(after_all((down, down_came), up_came))
    downs = [down, plan.permute(down, plan.last)]
    other, p_other, context_other = attend(1, att_other, (down,))
    unit, inv, low = call(
        functools.partial(mix_kernel, plan, rows),
        [shape((tokens, width), F32), shape((tokens, 128), F32), shape((tokens, width))],
        (table, inputs, context_own, context_other, *att_own, *att_other, vecs),
        "s" + 12 * "v",
        [VMEM((2, width, half), BF)],
        1,
        24,
    )
    hidden_scratch = [VMEM((2, width, hidden_half), BF)]
    ups = [*ups, *(plan.swap(v) for v in ups)]
    down_low_came = plan.swap(downs[0])
    context_came = plan.swap(context_own), plan.swap(context_other)
    act_own, act_other, slope_own, slope_other = call(
        functools.partial(up_kernel, plan, far_first, tile_rows, hidden),
        [shape((tokens, hidden_half))] * 4,
        (table, low, *ups, vecs),
        "s" + 10 * "v",
        hidden_scratch,
        1,
        24,
    )
    (down_high,) = after_all(downs[1:], act_own)
    downs = [downs[0], down_high, down_low_came, plan.swap(down_high)]
    low_came, act_came = plan.swap(low), plan.swap(act_other)
    half_scratch = [VMEM((width, hidden_half), BF)]
    downward, scaled_mean, cot_sum = call(
        functools.partial(down_own_kernel, plan, far_second, tile_rows, hidden),
        [shape((tokens, width), F32), shape((tokens, 128), F32), shape((1, width), F32)],
        (after(table, *context_came), act_own, *downs[:2], unit, cotangent, vecs),
        "s" + 6 * "v",
        half_scratch,
        80 * flops,
        24,
    )
    outputs, grad_second, grad_down, sums_second = call(
        functools.partial(down_kernel, plan, far_second, tile_rows, hidden),
        [
            shape((tokens, width)),
            shape((tokens, width), F32),
            shape((tokens, width)),
            shape((2, width), F32),
        ],
        (table, downward, act_other, *downs[2:], scaled_mean, cotangent, vecs),
        "s" + 7 * "v",
        half_scratch,
        1,
        24,
    )
    grad_down_came = plan.swap(grad_down)

    def grad_up(h, pieces, slope, gate=()):
        return call(
            functools.partial(grad_up_kernel, plan, far_second, h, tile_rows, hidden),
            [shape((tokens, hidden_half)), shape((1, hidden_half), F32)],
            (after(table, *gate), grad_down, *pieces, slope),
            "s" + 4 * "v",
            half_scratch,
            1,
            24,
        )

    gu_other, sums_up_other = grad_up(1, downs[2:], slope_other)
    gu_came = plan.swap(gu_other)

    def hidden_grad(route, left, left_came, right, right_came, cost, gate):
        return call(
            functools.partial(hidden_grad_kernel, plan, route, tile_rows, hidden),
            [shape((half_slots, tile_rows, hidden))] * 2,
            (after(table, *gate), left, left_came, right, right_came),
            "svvvv",
            [VMEM((wide, narrow // 2, tile_rows, hidden), BF)],
            cost,
            24,
        )

    def down_grad(part, gate):
        (tiles,) = call(
            functools.partial(hidden_part_kernel, plan, far_second, part, tile_rows, hidden),
            [shape((half_slots, tile_rows, hidden))],
            (after(table, *gate), grad_down, grad_down_came, act_own, act_came),
            "svvvv",
            [
                VMEM((wide, narrow // 2, tile_rows, hidden), BF),
                VMEM((2, width, tokens), BF),
                VMEM((2, width // 2, tokens), BF),
            ],
            80 * flops if part else 1,
            24,
        )
        return tiles

    down_high = down_grad(1, (sums_up_other,))
    down_came = plan.permute(down_high, plan.last)
    gu_own, sums_up_own = grad_up(0, downs[:2], slope_own, (down_high,))
    down_low = down_grad(0, (sums_up_own,))
    up_low, up_high = hidden_grad(far_first, low, low_came, gu_own, gu_came, 1, (down_low,))
    up_came = plan.permute(up_high, plan.last)
    grad_middle, branch_mine, branch_theirs, grad_context, sums_first = call(
        functools.partial(first_grad_kernel, plan, far_first, tile_rows, hidden, rows),
        [
            shape((tokens, width), F32),
            shape((tokens, half)),
            shape((tokens, half)),
            shape((tokens, width)),
            shape((3, width), F32),
        ],
        (
            after(table, up_low),
            gu_own,
            gu_other,
            *ups,
            *att_own,
            *att_other,
            grad_second,
            unit,
            inv,
            vecs,
        ),
        "s" + 22 * "v",
        hidden_scratch
        + [VMEM((2, width, half), BF), VMEM((tokens, width), BF)],
        1,
        24,
    )
    branch_came = plan.swap(branch_theirs)

    def attention_grad(h, keep, probs, gate=()):
        return call(
            functools.partial(attention_grad_kernel, plan, h),
            [shape((tokens, 3 * half)), shape((1, 3 * half), F32)],
            (after(table, *gate), keep, probs, grad_context, cos, sin),
            "svvvvv",
            [],
            1,
            24,
        )

    gt_other, bias_other = attention_grad(1, other, p_other, (act_came,))
    gt_came = plan.swap(gt_other)
    down_stay, down_away = halves(*after_all((down_low, down_came), bias_other))
    down_came = plan.send(down_away, far_second, 4)
    gt_own, bias_own = attention_grad(0, own, p_own, (down_away,))
    up_stay, up_away = halves(*after_all((up_low, up_came), bias_own))
    up_came = plan.permute(up_away, plan.first)
    height = rows + third
    packed_low, packed_high = call(
        functools.partial(attention_weight_kernel, plan, rows),
        [shape((half_slots * height + TABLE_ROWS, 3 * half))] * 2,
        (
            after(table, up_away),
            inputs,
            inputs_came,
            gt_own,
            gt_came,
            context_own,
            context_other,
            *context_came,
            branch_mine,
            branch_came,
            bias_own,
            bias_other,
            sums_first,
            sums_second,
            cot_sum,
            sums_up_own,
            sums_up_other,
        ),
        "s" + 17 * "v",
        [
            VMEM((plan.slots, rows, 3 * half), BF),
            VMEM((plan.slots, 3, third, half), BF),
            VMEM((TABLE_ROWS, 3 * half), F32),
        ],
        80 * flops,
        24,
    )
    packed_came = plan.permute(packed_high, plan.last)
    down_stay, down_away = halves(*after_all((down_stay, down_came), packed_low))
    down_came = plan.send(down_away, far_second, 2)
    up_stay, up_away = halves(*after_all((up_stay, up_came), down_away))
    up_came = plan.send(up_away, far_first, 2)
    (input_grad,) = call(
        functools.partial(input_grad_kernel, plan, rows),
        [shape((tokens, width))],
        (after(table, up_away), grad_middle, gt_own, gt_other, *att_own, *att_other),
        "s" + 11 * "v",
        [VMEM((2, width, 3 * half), BF)],
        80 * flops,
        24,
    )
    packed_low, packed_came = after_all((packed_low, packed_came), input_grad)
    cut, end = half_slots // 2 * height, half_slots * height
    sums = added(packed_low[end:], packed_came[end:])
    packed_stay = added(packed_low[:cut], packed_came[:cut])
    packed_away = cat([added(packed_low[cut:end], packed_came[cut:end]), sums])
    packed_came = plan.permute(packed_away, plan.first)
    down_stay, down_came, up_stay, up_came = after_all(
        (down_stay, down_came, up_stay, up_came), packed_away
    )
    down_stay, down_away = halves(down_stay, down_came)
    down_came = plan.send(down_away, far_second, 1)
    up_stay, up_away = halves(up_stay, up_came)
    up_came = plan.send(up_away, far_first, 1)
    (packed_came,) = after_all((packed_came,), down_away, up_away)
    sums = added(sums, packed_came[cut:])
    parts = [
        cat(
            [
                added(packed_stay[k * height :][:height], packed_came[k * height :][:height]),
                sums,
            ]
        )
        for k in range(plan.far)
    ]
    down_stay, down_came, up_stay, up_came = after_all(
        (down_stay, down_came, up_stay, up_came), parts[1]
    )
    down_total = down_stay[0].astype(F32) + down_came[0].astype(F32)
    up_total = up_stay[0].astype(F32) + up_came[0].astype(F32)
    mine, theirs = call(
        functools.partial(total_kernel, plan, rows),
        [shape((piece + TABLE_ROWS, 4 * half), F32)] * 2,
        (after(table, down_total, up_total), parts[0], *plan.send_far(parts)),
        "svvvv",
        [VMEM((rows, 4 * half), F32)],
        1,
        16,
    )
    one = [3 * piece, piece, piece, piece, hidden, down_bias.shape[0], piece, piece]
    triple_grad, mix_grad, *vectors = call(
        functools.partial(share_kernel, plan),
        [shape((piece, 3 * width), F32), shape((piece, width), F32)]
        + [shape((1, n), F32) for n in one],
        (table, place, mine, plan.swap(theirs)),
        "ssvv",
        [],
        1,
        16,
    )
    vectors = [v.reshape(-1) for v in vectors]
    return (
        outputs,
        input_grad,
        triple_grad,
        vectors[0],
        mix_grad,
        *vectors[1:4],
        up_total,
        vectors[4],
        down_total.T,
        *vectors[5:],
    )


def fits(plan_shape, width, hidden):
    wide, narrow = plan_shape
    powers = all(n >= 4 and n & (n - 1) == 0 for n in (wide, narrow)) and narrow == 4
    return (
        powers
        and width % (wide * 16) == 0
        and width % (wide * narrow // 2 * 48) == 0
        and hidden % (narrow * 128) == 0
        and width % 768 == 0
    )


def solution(mesh):
    placed = (
        P(("wide", "narrow"), None),
        P(("wide", "narrow")),
        P(("wide", "narrow"), None),
        P(("wide", "narrow")),
        P(("wide", "narrow"), None),
        P(("wide", "narrow")),
        P(("wide", "narrow")),
        P(("wide", "narrow")),
        P("wide", "narrow"),
        P("narrow"),
        P("narrow", "wide"),
        P("wide"),
        P(("wide", "narrow")),
        P(("wide", "narrow")),
        P(("wide", "narrow"), None),
    )
    wide, narrow = mesh.shape["wide"], mesh.shape["narrow"]

    def layer(*arrays):
        rows, hidden = arrays[8].shape
        if fits((wide, narrow), rows * wide, hidden * narrow):
            return fast_body(Plan(wide, narrow), *arrays)
        return body(*arrays)

    return jax.shard_map(
        layer,
        mesh=mesh,
        in_specs=placed,
        out_specs=(
            P(("wide", "narrow"), None),
            P(("wide", "narrow"), None),
            P(("wide", "narrow"), None),
            P(("wide", "narrow")),
            P(("wide", "narrow"), None),
            P(("wide", "narrow")),
            P(("wide", "narrow")),
            P(("wide", "narrow")),
            P("wide", "narrow"),
            P("narrow"),
            P("narrow", "wide"),
            P("wide"),
            P(("wide", "narrow")),
            P(("wide", "narrow")),
        ),
        check_vma=False,
    )
```

```python
import functools
import math

import jax
import jax.numpy as jnp
import numpy as np
from jax import lax
from jax.experimental import pallas as pl
from jax.experimental.pallas import tpu as pltpu
from jax.sharding import PartitionSpec as P

H = 12
HD = 64


EPSILON = 1e-06


def tables(token_rows, width, head):
    position = jnp.arange(token_rows, dtype=jnp.float32)
    column = jnp.arange(width, dtype=jnp.int32)
    pair_index = (column % head // 2).astype(jnp.float32)
    frequency = jnp.exp(pair_index * (-2.0 / head) * math.log(10000.0))
    angle = position[:, None] * frequency[None, :]
    parity = (column % 2).astype(jnp.float32) * 2.0 - 1.0
    return (jnp.cos(angle), jnp.sin(angle) * parity[None, :])


def swapped(values):
    shape = values.shape
    paired = values.reshape(shape[:-1] + (shape[-1] // 2, 2))
    return paired[..., ::-1].reshape(shape)


def rotate(values, cosine, sine):
    return values * cosine + swapped(values) * sine


def unrotate(grad, cosine, sine):
    return grad * cosine + swapped(grad * sine)


def normalize_forward(values, gain, shift):
    mean_row = jnp.mean(values, -1, keepdims=True)
    centred = values - mean_row
    inverse = lax.rsqrt(jnp.mean(centred * centred, -1, keepdims=True) + EPSILON)
    unit = centred * inverse
    return (unit * gain + shift, unit, inverse)


def normalize_backward(grad, unit, inverse, gain):
    scaled = grad * gain
    inner = (
        scaled
        - jnp.mean(scaled, -1, keepdims=True)
        - unit * jnp.mean(scaled * unit, -1, keepdims=True)
    )
    return (inner * inverse, jnp.sum(grad * unit, 0), jnp.sum(grad, 0))


def gelu_exact(values):
    return jax.nn.gelu(values, approximate=False)


def gelu_backward(upward, grad_active):
    unused, pull_back = jax.vjp(gelu_exact, upward)
    return pull_back(grad_active)[0]


def softmax_block(query_block, key, valid, scale):
    scores = (
        jnp.einsum("qhd,khd->hqk", query_block, key, preferred_element_type=jnp.float32) * scale
    )
    scores = jnp.where(valid[None, None, :], scores, -1e30)
    return jax.nn.softmax(scores, axis=-1)


def attention_forward(query, key, value, valid, scale):
    token_rows = query.shape[0]
    block = min(512, token_rows)
    weights_block = softmax_block(query, key, valid, scale)
    context = jnp.einsum(
        "hqk,khd->qhd",
        weights_block.astype(jnp.bfloat16),
        value,
        preferred_element_type=jnp.float32,
    )
    pieces = context.reshape(block, -1).astype(jnp.bfloat16)
    return pieces


def attention_backward(query, key, value, grad_context, valid, scale):
    weights_block = softmax_block(query, key, valid, scale)
    grad_weights = jnp.einsum(
        "qhd,khd->hqk", grad_context, value, preferred_element_type=jnp.float32
    )
    inner = weights_block * (
        grad_weights - jnp.sum(weights_block * grad_weights, -1, keepdims=True)
    )
    inner_low = inner.astype(jnp.bfloat16)
    query_pieces = (
        jnp.einsum("hqk,khd->qhd", inner_low, key, preferred_element_type=jnp.float32) * scale
    )
    grad_key = (
        jnp.einsum("hqk,qhd->khd", inner_low, query, preferred_element_type=jnp.float32) * scale
    )
    grad_value = jnp.einsum(
        "hqk,qhd->khd",
        weights_block.astype(jnp.bfloat16),
        grad_context,
        preferred_element_type=jnp.float32,
    )
    return (query_pieces, grad_key, grad_value)


def body(
    inputs,
    lengths,
    triple_weight,
    triple_bias,
    mix_weight,
    mix_bias,
    first_gain,
    first_shift,
    up_weight,
    up_bias,
    down_weight,
    down_bias,
    second_gain,
    second_shift,
    cotangent,
):
    token_rows, width = inputs.shape
    scale = 1.0 / math.sqrt(HD)
    head_shape = (token_rows, H, HD)
    (
        triple_full,
        mix_full,
        triple_bias_full,
        mix_bias_full,
        gain_one,
        shift_one,
        gain_two,
        shift_two,
    ) = (
        lax.all_gather(triple_weight, ("wide", "narrow"), axis=0, tiled=True),
        lax.all_gather(mix_weight, ("wide", "narrow"), axis=0, tiled=True),
        lax.all_gather(triple_bias, ("wide", "narrow"), axis=0, tiled=True),
        lax.all_gather(mix_bias, ("wide", "narrow"), axis=0, tiled=True),
        lax.all_gather(first_gain, ("wide", "narrow"), axis=0, tiled=True),
        lax.all_gather(first_shift, ("wide", "narrow"), axis=0, tiled=True),
        lax.all_gather(second_gain, ("wide", "narrow"), axis=0, tiled=True),
        lax.all_gather(second_shift, ("wide", "narrow"), axis=0, tiled=True),
    )
    up_rows, down_columns, down_bias_full = (
        lax.all_gather(up_weight, "wide", axis=0, tiled=True),
        lax.all_gather(down_weight, "wide", axis=1, tiled=True),
        lax.all_gather(down_bias, "wide", axis=0, tiled=True),
    )
    gain_one = gain_one.astype(jnp.float32)
    gain_two = gain_two.astype(jnp.float32)
    cosine, sine = tables(token_rows, width, HD)
    valid = jnp.arange(token_rows, dtype=jnp.int32) < lengths[0]
    triple = jnp.dot(
        inputs, triple_full, preferred_element_type=jnp.float32
    ) + triple_bias_full.astype(jnp.float32)
    query = rotate(triple[:, :width], cosine, sine).astype(jnp.bfloat16).reshape(head_shape)
    key = (
        rotate(triple[:, width : 2 * width], cosine, sine).astype(jnp.bfloat16).reshape(head_shape)
    )
    value = triple[:, 2 * width :].astype(jnp.bfloat16).reshape(head_shape)
    context = attention_forward(query, key, value, valid, scale)
    branch = jnp.dot(context, mix_full, preferred_element_type=jnp.float32) + mix_bias_full.astype(
        jnp.float32
    )
    first, first_unit, first_inverse = normalize_forward(
        inputs.astype(jnp.float32) + branch, gain_one, shift_one.astype(jnp.float32)
    )
    first_low = first.astype(jnp.bfloat16)
    gathered = lax.all_gather(first_low, "narrow", axis=0, tiled=True)
    upward = jnp.dot(gathered, up_rows, preferred_element_type=jnp.float32) + up_bias.astype(
        jnp.float32
    )
    active = gelu_exact(upward).astype(jnp.bfloat16)
    downward = lax.psum_scatter(
        jnp.dot(active, down_columns, preferred_element_type=jnp.float32).astype(jnp.bfloat16),
        "narrow",
        scatter_dimension=0,
        tiled=True,
    ).astype(jnp.float32)
    downward = downward + down_bias_full.astype(jnp.float32)
    result, second_unit, second_inverse = normalize_forward(
        first + downward, gain_two, shift_two.astype(jnp.float32)
    )
    outputs = result.astype(jnp.bfloat16)
    grad_second, second_gain_grad, second_shift_grad = normalize_backward(
        cotangent.astype(jnp.float32), second_unit, second_inverse, gain_two
    )
    grad_down = grad_second.astype(jnp.bfloat16)
    grad_gathered = lax.all_gather(grad_down, "narrow", axis=0, tiled=True)
    grad_active = jnp.dot(grad_gathered, down_columns.T, preferred_element_type=jnp.float32)
    grad_up = gelu_backward(upward, grad_active).astype(jnp.bfloat16)
    grad_feed = lax.psum_scatter(
        jnp.dot(grad_up, up_rows.T, preferred_element_type=jnp.float32).astype(jnp.bfloat16),
        "narrow",
        scatter_dimension=0,
        tiled=True,
    ).astype(jnp.float32)
    up_part = jnp.dot(gathered.T, grad_up, preferred_element_type=jnp.float32)
    down_part = jnp.dot(active.T, grad_gathered, preferred_element_type=jnp.float32)
    down_bias_part = jnp.sum(grad_gathered, 0, dtype=jnp.float32)
    up_weight_grad, down_weight_grad, down_bias_grad = (
        lax.psum_scatter(
            up_part.astype(jnp.bfloat16), "wide", scatter_dimension=0, tiled=True
        ).astype(jnp.float32),
        lax.psum_scatter(
            down_part.astype(jnp.bfloat16), "wide", scatter_dimension=1, tiled=True
        ).astype(jnp.float32),
        lax.psum_scatter(
            down_bias_part.astype(jnp.bfloat16), "wide", scatter_dimension=0, tiled=True
        ).astype(jnp.float32),
    )
    up_bias_grad = lax.psum(jnp.sum(grad_up, 0, dtype=jnp.float32), "wide")
    grad_first = grad_second + grad_feed
    grad_middle, first_gain_grad, first_shift_grad = normalize_backward(
        grad_first, first_unit, first_inverse, gain_one
    )
    grad_branch = grad_middle.astype(jnp.bfloat16)
    mix_weight_grad = jnp.dot(context.T, grad_branch, preferred_element_type=jnp.float32)
    mix_bias_grad = jnp.sum(grad_branch, 0, dtype=jnp.float32)
    triple_back, mix_back = (
        lax.all_gather(triple_weight, ("wide", "narrow"), axis=0, tiled=True),
        lax.all_gather(mix_weight, ("wide", "narrow"), axis=0, tiled=True),
    )
    grad_context = (
        jnp.dot(grad_branch, mix_back.T, preferred_element_type=jnp.float32)
        .astype(jnp.bfloat16)
        .reshape(head_shape)
    )
    grad_query, grad_key, grad_value = attention_backward(
        query, key, value, grad_context, valid, scale
    )
    grad_triple = jnp.concatenate(
        [
            unrotate(grad_query.reshape(token_rows, width), cosine, sine),
            unrotate(grad_key.reshape(token_rows, width), cosine, sine),
            grad_value.reshape(token_rows, width),
        ],
        1,
    ).astype(jnp.bfloat16)
    triple_local = jnp.dot(inputs.T, grad_triple, preferred_element_type=jnp.float32)
    triple_bias_local = jnp.sum(grad_triple, 0, dtype=jnp.float32)
    grad_inputs = grad_middle + jnp.dot(
        grad_triple, triple_back.T, preferred_element_type=jnp.float32
    )
    summed = (
        lax.psum_scatter(triple_local, ("wide", "narrow"), scatter_dimension=0, tiled=True),
        lax.psum_scatter(mix_weight_grad, ("wide", "narrow"), scatter_dimension=0, tiled=True),
        lax.psum_scatter(triple_bias_local, ("wide", "narrow"), scatter_dimension=0, tiled=True),
        lax.psum_scatter(mix_bias_grad, ("wide", "narrow"), scatter_dimension=0, tiled=True),
        lax.psum_scatter(first_gain_grad, ("wide", "narrow"), scatter_dimension=0, tiled=True),
        lax.psum_scatter(first_shift_grad, ("wide", "narrow"), scatter_dimension=0, tiled=True),
        lax.psum_scatter(second_gain_grad, ("wide", "narrow"), scatter_dimension=0, tiled=True),
        lax.psum_scatter(second_shift_grad, ("wide", "narrow"), scatter_dimension=0, tiled=True),
    )
    return (
        outputs,
        grad_inputs.astype(jnp.bfloat16),
        summed[0],
        summed[2],
        summed[1],
        summed[3],
        summed[4],
        summed[5],
        up_weight_grad,
        up_bias_grad,
        down_weight_grad,
        down_bias_grad,
        summed[6],
        summed[7],
    )


VMEM = pltpu.VMEM
SMEM = pltpu.SMEM
BF = jnp.bfloat16
F32 = jnp.float32
AXES = ("wide", "narrow")
WHOLE = pl.BlockSpec(memory_space=VMEM)
SCALARS = pl.BlockSpec(memory_space=SMEM)
LEFT = pl.BlockSpec(memory_space=pltpu.HBM)


def nn(a, b):
    return lax.dot_general(a, b, (((1,), (0,)), ((), ())), preferred_element_type=F32)


def nt(a, b):
    return lax.dot_general(a, b, (((1,), (1,)), ((), ())), preferred_element_type=F32)


def tn(a, b):
    return lax.dot_general(a, b, (((0,), (0,)), ((), ())), preferred_element_type=F32)


def shape(dims, dtype=BF):
    return jax.ShapeDtypeStruct(dims, dtype)


class Load:
    def __init__(self, source, held, sem):
        self.copy = pltpu.make_async_copy(source, held, sem)
        self.held, self.waited = held, False
        self.shape = held.shape
        self.copy.start()

    def __call__(self):
        if not self.waited:
            self.copy.wait()
            self.waited = True
        return self.held


def call(kernel, outs, operands, kinds, scratch, flops, megabytes, out_specs=None):
    specs = {"s": SCALARS, "v": WHOLE, "h": LEFT, "l": LEFT}
    loads = [k for k, kind in enumerate(kinds) if kind == "l"]
    held = [VMEM(operands[k].shape, operands[k].dtype) for k in loads]
    assert len(kinds) == len(operands)

    def whole(*refs):
        refs = list(refs)
        count = len(loads)
        if count:
            sems = refs.pop()
            buffers, refs = refs[-count:], refs[:-count]
            for n, k in enumerate(loads):
                refs[k] = Load(refs[k], buffers[n], sems.at[n])
        kernel(*refs)
        for k in loads:
            refs[k]()

    return pl.pallas_call(
        whole,
        out_shape=outs,
        in_specs=[specs[kind] for kind in kinds],
        out_specs=[WHOLE] * len(outs) if out_specs is None else out_specs,
        scratch_shapes=list(scratch)
        + held
        + ([pltpu.SemaphoreType.DMA((len(loads),))] if loads else []),
        compiler_params=pltpu.CompilerParams(vmem_limit_bytes=megabytes << 20),
        cost_estimate=pl.CostEstimate(
            flops=int(flops), bytes_accessed=1, transcendentals=0
        ),
    )(*operands)


def drain(ref, sem):
    pltpu.make_async_copy(ref, ref, sem).wait()


class Plan:
    def __init__(self, wide, narrow):
        self.wide, self.narrow = wide, narrow
        self.devices = wide * narrow
        x, y = narrow, narrow // 2
        self.first, self.last = (x, y), (y, x)
        self.far = wide // 2
        line = self.devices // self.far
        along = [(line << k, line << k) for k in reversed(range(self.far.bit_length() - 1))]
        self.far_first = (*along, self.first, self.last)
        self.far_second = (self.first, *along, self.last)
        self.routes = (self.far_first, self.far_second)
        self.slots = 1 << len(self.far_first)

    def lead(self, route, slot):
        masks = [0, 0]
        for k, pair in enumerate(route):
            if slot >> k & 1:
                masks = [mask ^ bit for mask, bit in zip(masks, pair)]
        return masks

    def chips(self, device):
        core = device & 1
        return [
            (device ^ self.lead(route, r)[c]) >> 1
            for route in self.routes
            for c in (core, core ^ 1)
            for r in range(self.slots)
        ]

    def table(self, index, live):
        chips = np.array([self.chips(i) for i in range(self.devices)], np.int32)
        mine = lax.dynamic_slice(jnp.asarray(chips), (index, 0), (1, chips.shape[1]))[0]
        return jnp.concatenate([mine, (index & 1)[None].astype(jnp.int32), live])

    def chip(self, table, route, h, slot):
        return table[(2 * self.routes.index(route) + h) * self.slots + slot]

    def core(self, table):
        return table[2 * len(self.routes) * self.slots]

    def live(self, table):
        return table[2 * len(self.routes) * self.slots + 1]

    def permute(self, value, masks):
        return lax.ppermute(value, AXES, [(i, i ^ masks[i & 1]) for i in range(self.devices)])

    def swap(self, value):
        return self.permute(value, (1, 1))

    def send(self, value, route, slot):
        return self.permute(value, self.lead(route, slot))

    def gather_far(self, value):
        return [value] + [self.send(value, self.far_first, m) for m in range(1, self.far)]

    def send_far(self, parts):
        return [self.send(v, self.far_first, m) for m, v in enumerate(parts) if m]


def added(*values):
    return sum([v.astype(F32) for v in values[1:]], values[0].astype(F32)).astype(BF)


def halves(*values):
    count = values[0].shape[0] // 2
    return added(*(v[:count] for v in values)), added(*(v[count:] for v in values))


def together(*lists):
    flat = list(lax.optimization_barrier(tuple(v for values in lists for v in values)))
    return [[flat.pop(0) for _ in values] for values in lists]


def after_all(values, *others):
    return lax.optimization_barrier(tuple(values) + others)[: len(values)]


def after(value, *others):
    return lax.optimization_barrier((value,) + others)[0] if others else value


def mean(v):
    return jnp.mean(v, -1, keepdims=True)


def swap_lanes(v):
    lane = lax.broadcasted_iota(jnp.int32, v.shape, 1)
    return jnp.where(lane % 2 == 0, pltpu.roll(v, v.shape[1] - 1, 1), pltpu.roll(v, 1, 1))


def first_half(rows):
    return lax.broadcasted_iota(jnp.int32, (rows, 2 * HD), 1) < HD


def place_attention(plan, table, h, pieces, triple, mix, rows):
    core = plan.core(table)
    half_slots = plan.slots // 2
    third = rows // 3
    columns = pieces[0].shape[2]
    width = columns // 3
    for r in range(plan.slots):
        chip = plan.chip(table, plan.far_first, h, r)
        side, at = divmod(r, half_slots)
        first, second = pieces[side], pieces[2 + side]
        if triple is not None:
            top = pl.ds(pl.multiple_of(chip * rows, 16), 2 * third)
            triple[top, :] = first[at]
            rest = pl.ds(pl.multiple_of(chip * rows + 2 * third, 16), third)
            triple[rest, :] = second[at, :third, :columns]
        if mix is not None:
            for b in range(3):
                here = pl.ds(pl.multiple_of(chip * rows + b * third, 16), third)
                mix[core ^ h, here, :] = second[at, third:, b * width : (b + 1) * width]


def place_hidden(plan, route, table, h, pieces, weight, rows, columns):
    across = plan.narrow // 2
    slots = [(piece, k) for piece in pieces for k in range(piece.shape[0])]
    for r, (piece, k) in enumerate(slots):
        chip = plan.chip(table, route, h, r)
        down = pl.ds(pl.multiple_of(chip // across * rows, 16), rows)
        over = pl.ds(pl.multiple_of(chip % across * columns, 128), columns)
        weight[down, over] = piece[k]


TRIPLE, MIX, GAIN1, SHIFT1, GAIN2, SHIFT2, UP = 0, 3, 4, 5, 6, 7, 8
TABLE_ROWS = 16
SHARE = 128


def split_kernel(index_ref, triple_ref, mix_ref, mine_ref, theirs_ref):
    core = index_ref[0] % 2
    width = mix_ref.shape[1]
    half = width // 2
    for out, h in ((mine_ref, core), (theirs_ref, core ^ 1)):
        for g in range(3):
            at = pl.multiple_of(g * width + h * half, 128)
            out[:, g * half : (g + 1) * half] = triple_ref[:, pl.ds(at, half)]
        out[:, 3 * half :] = mix_ref[:, pl.ds(pl.multiple_of(h * half, 128), half)]


def join_kernel(index_ref, mine_ref, came_ref, first_ref, rest_ref):
    core = index_ref[0] % 2
    half = mine_ref.shape[1] // 4
    mine, came = mine_ref[...].astype(F32), came_ref[...].astype(F32)
    both = jnp.concatenate(
        [jnp.where(core == 0, mine, came), jnp.where(core == 0, came, mine)], 0
    ).astype(BF)
    third = both.shape[0] // 3
    first_ref[0] = both[: 2 * third, : 3 * half]
    rest_ref[:third, :] = both[2 * third :, : 3 * half]
    for b in range(3):
        rest_ref[third:, b * half : (b + 1) * half] = both[b * third : (b + 1) * third, 3 * half :]


def spread_kernel(plan, index_ref, tb_ref, mb_ref, g1_ref, s1_ref, g2_ref, s2_ref, ub_ref, db_ref,
                  share_ref, spread):
    of_narrow = index_ref[0] % plan.narrow
    spread[...] = jnp.zeros_like(spread)
    for row, ref in ((TRIPLE, tb_ref), (MIX, mb_ref), (GAIN1, g1_ref), (SHIFT1, s1_ref),
                     (GAIN2, g2_ref), (SHIFT2, s2_ref), (UP, ub_ref)):
        spread[row : row + 1, : ref.shape[1]] = ref()[...].astype(F32)
    count = db_ref.shape[1] // plan.narrow
    values = db_ref()[...].astype(F32)
    mine = values[:, :count]
    for k in range(1, plan.narrow):
        mine = jnp.where(of_narrow == k, values[:, k * count : (k + 1) * count], mine)
    spread[UP + plan.narrow : UP + plan.narrow + 1, :count] = mine
    share_ref[...] = spread[...].astype(BF)


def beside_kernel(index_ref, rest_ref, share_ref, came_ref, out_ref):
    core = index_ref[0] % 2
    columns = rest_ref.shape[1]
    share, came = share_ref[...], came_ref[...]
    out_ref[0, :, :columns] = rest_ref[...]
    out_ref[0, :TABLE_ROWS, columns:] = jnp.where(core == 0, share, came)
    out_ref[0, TABLE_ROWS:, columns:] = jnp.where(core == 0, came, share)


def vectors_kernel(plan, share, table, low_ref, high_ref, out_ref, held, triple, plain, up, down):
    half_slots = plan.slots // 2
    columns = low_ref.shape[2] - SHARE
    for r in range(plan.slots):
        piece = (low_ref, high_ref)[r // half_slots]
        held[plan.chip(table, plan.far_first, 0, r)] = piece[r % half_slots, :, columns:]
    for ref in (triple, plain, up, down):
        ref[...] = jnp.zeros_like(ref)
    width = out_ref.shape[1]
    part = width // plan.wide

    def put(ref, rows, at):
        block, lane = divmod(at, SHARE)
        s = slice(block * SHARE, (block + 2) * SHARE)
        ref[..., s] = ref[..., s] + (pltpu.roll(rows, lane, 1) if lane else rows)

    for device in range(plan.devices):
        of_wide, of_narrow = divmod(device, plan.narrow)
        rows = held[device // 2].astype(F32)[device % 2 * TABLE_ROWS :][:TABLE_ROWS]
        rows = jnp.concatenate([rows, jnp.zeros_like(rows)], 1)
        put(triple, rows[:8], 3 * share * device)
        put(plain, rows[:8], share * device)
        put(up.at[of_narrow], rows[8:], part * of_wide)
        put(down, rows[8:], share * device)
    out_ref[...] = jnp.zeros_like(out_ref)
    for g in range(3):
        out_ref[TRIPLE + g : TRIPLE + g + 1, :] = triple[0:1, g * width : (g + 1) * width]
    out_ref[MIX:UP, :] = plain[MIX:UP, :width]
    for n in range(plan.narrow):
        out_ref[UP + n : UP + n + 1, :] = up[n, 0:1, :width]
    row = UP + plan.narrow
    out_ref[row : row + 1, :] = down[row - 8 : row - 7, :width]


def pack_vectors(plan, core, width, bias_own, bias_other, first_ref, second_ref, cot_ref, up_own,
                 up_other, out_ref):
    out_ref[...] = jnp.zeros_like(out_ref)
    half = width // 2
    for h, ref in ((0, bias_own), (1, bias_other)):
        at = pl.ds(pl.multiple_of((core ^ h) * half, 128), half)
        for g in range(3):
            out_ref[TRIPLE + g : TRIPLE + g + 1, at] = ref[:, g * half : (g + 1) * half]
    out_ref[MIX : MIX + 1, :width] = first_ref[2:3, :]
    out_ref[GAIN1 : GAIN1 + 2, :width] = first_ref[0:2, :]
    out_ref[GAIN2 : GAIN2 + 1, :width] = second_ref[0:1, :]
    out_ref[SHIFT2 : SHIFT2 + 1, :width] = cot_ref[...]
    for h, up_ref in ((0, up_own), (1, up_other)):
        for y in range(plan.narrow // 2):
            row = up_ref[:, y * width : (y + 1) * width]
            out_ref[pl.ds(UP + 2 * y + (core ^ h), 1), :width] = row
    out_ref[UP + plan.narrow : UP + plan.narrow + 1, :width] = second_ref[1:2, :]


def attention_kernel(plan, rows, h, table, x_ref, a, b, c, d, cos_ref, sin_ref, vec_ref,
                     keep_ref, probs_ref, context_ref, triple):
    core, live = plan.core(table), plan.live(table)
    tokens, width = x_ref.shape
    half = width // 2
    place_attention(plan, table, h, (a, b, c, d), triple, None, rows)
    x = x_ref[...]
    cos, sin = cos_ref[...], sin_ref[...]
    left = first_half(tokens)
    valid = lax.broadcasted_iota(jnp.int32, (1, tokens), 1) < live
    scale = jnp.asarray(1.0 / math.sqrt(HD), BF)
    for q in range(half // 128):
        at = [slice(g * half + 128 * q, g * half + 128 * q + 128) for g in range(3)]
        here = pl.ds(pl.multiple_of((core ^ h) * half + 128 * q, 128), 128)
        out = [
            nn(x, triple[:, s]) + vec_ref[TRIPLE + g : TRIPLE + g + 1, here]
            for g, s in enumerate(at)
        ]
        query, key = [(v * cos + swap_lanes(v) * sin).astype(BF) for v in out[:2]]
        value = out[2].astype(BF)
        for s, v in zip(at, (query, key, value)):
            keep_ref[:, s] = v
        context = []
        for e in (0, 1):
            mine = left if e == 0 else ~left
            masked = jnp.where(mine, query, jnp.zeros_like(query)) * scale
            score = jnp.where(valid, nt(masked, key), -1e30)
            power = jnp.exp(score - jnp.max(score, -1, keepdims=True))
            prob = power * (1.0 / jnp.sum(power, -1, keepdims=True))
            prob = prob.astype(BF)
            probs_ref[2 * q + e] = prob
            context.append(nn(prob, value))
        context_ref[:, 128 * q : 128 * q + 128] = (
            jnp.where(left, context[0], context[1]).astype(BF)
        )


def mix_kernel(plan, rows, table, x_ref, context_own, context_other, a, b, c, d, e, f, g, k,
               vec_ref, unit_ref, inv_ref, low_ref, mix):
    core = plan.core(table)
    half = context_own.shape[1]
    for h, pieces in ((0, (a, b, c, d)), (1, (e, f, g, k))):
        place_attention(plan, table, h, pieces, None, mix, rows)
    sides = []
    for side in (0, 1):
        total = 0.0
        for h, context in ((0, context_own), (1, context_other)):
            at = pl.ds(pl.multiple_of((core ^ h) * half, 128), half)
            total = total + nn(context[...], mix[side, at, :])
        sides.append(total)
    branch = jnp.concatenate(sides, 1)
    summed = x_ref[...].astype(F32) + (branch + vec_ref[MIX : MIX + 1, :])
    centred = summed - mean(summed)
    inverse = lax.rsqrt(mean(centred * centred) + EPSILON)
    unit = centred * inverse
    unit_ref[...] = unit
    inv_ref[...] = jnp.broadcast_to(inverse, inv_ref.shape)
    low_ref[...] = (
        unit * vec_ref[GAIN1 : GAIN1 + 1, :] + vec_ref[SHIFT1 : SHIFT1 + 1, :]
    ).astype(BF)


def up_kernel(plan, route, rows, columns, table, low_ref, a, b, c, d, e, f, g, k, vec_ref,
              own_ref, other_ref, slope_own_ref, slope_other_ref, weight):
    core = plan.core(table)
    low = low_ref[...]
    step = 256
    for h, (out, slope) in enumerate(((own_ref, slope_own_ref), (other_ref, slope_other_ref))):
        place_hidden(plan, route, table, h, ((a, b, c, d), (e, f, g, k))[h], weight.at[h], rows, columns)
        for n in range(out.shape[1] // step):
            s = slice(n * step, (n + 1) * step)
            y, at = divmod(n * step, columns)
            row = vec_ref[pl.ds(UP + 2 * y + (core ^ h), 1), at : at + step]
            up = nn(low, weight[h, :, s]) + row
            share = 0.5 * (1.0 + lax.erf(up * math.sqrt(0.5)))
            out[:, s] = (up * share).astype(BF)
            slope[:, s] = (
                share + up * jnp.exp(-0.5 * up * up) * (1.0 / math.sqrt(2.0 * math.pi))
            ).astype(BF)


def down_own_kernel(plan, route, rows, columns, table, act, a, b, unit_ref, cot_ref, vec_ref,
                    out_ref, mean_ref, sum_ref, weight):
    place_hidden(plan, route, table, 0, (a, b), weight, rows, columns)
    first = unit_ref[...] * vec_ref[GAIN1 : GAIN1 + 1, :] + vec_ref[SHIFT1 : SHIFT1 + 1, :]
    bias = vec_ref[UP + plan.narrow : UP + plan.narrow + 1, :]
    out_ref[...] = first + (nt(act[...], weight[...]) + bias)
    cot = cot_ref[...].astype(F32)
    sum_ref[...] = jnp.sum(cot, 0, keepdims=True)
    scaled_mean = mean(cot * vec_ref[GAIN2 : GAIN2 + 1, :])
    mean_ref[...] = jnp.broadcast_to(scaled_mean, mean_ref.shape)


def down_kernel(plan, route, rows, columns, table, part_ref, act, a, b, mean_ref,
                cot_ref, vec_ref, out_ref, grad_ref, grad_low_ref, sums_ref, weight):
    place_hidden(plan, route, table, 1, (a, b), weight, rows, columns)
    summed = part_ref[...] + nt(act[...], weight[...])
    cot = cot_ref[...].astype(F32)
    scaled = cot * vec_ref[GAIN2 : GAIN2 + 1, :]
    centred = summed - mean(summed)
    inverse = lax.rsqrt(mean(centred * centred) + EPSILON)
    unit = centred * inverse
    grad = inverse * (scaled - mean_ref[:, 0:1] - unit * mean(scaled * unit))
    grad_ref[...] = grad
    low = grad.astype(BF)
    grad_low_ref[...] = low
    sums_ref[0:1, :] = jnp.sum(cot * unit, 0, keepdims=True)
    sums_ref[1:2, :] = jnp.sum(low.astype(F32), 0, keepdims=True)
    out_ref[...] = (
        unit * vec_ref[GAIN2 : GAIN2 + 1, :] + vec_ref[SHIFT2 : SHIFT2 + 1, :]
    ).astype(BF)


def grad_up_kernel(plan, route, h, rows, columns, table, low_ref, a, b, slope, out, sums_ref,
                   weight):
    place_hidden(plan, route, table, h, (a, b), weight, rows, columns)
    low = low_ref[...]
    step = 256
    for n in range(out.shape[1] // step):
        s = slice(n * step, (n + 1) * step)
        grad = (nn(low, weight[:, s]) * slope[:, s].astype(F32)).astype(BF)
        out[:, s] = grad
        sums_ref[:, s] = jnp.sum(grad.astype(F32), 0, keepdims=True)


def hidden_grad_kernel(plan, route, rows, columns, table, left_own, left_other, right_own,
                       right_other, low_ref, high_ref, block):
    across, half_slots = plan.narrow // 2, plan.slots // 2
    a, b = left_own[...], left_other[...]
    for y in range(across):
        s = slice(y * columns, (y + 1) * columns)
        tile = tn(a, right_own[:, s]) + tn(b, right_other[:, s])
        block[:, y] = tile.astype(BF).reshape(plan.wide, rows, columns)
    for r in reversed(range(plan.slots)):
        chip = plan.chip(table, route, 0, r)
        out = (low_ref, high_ref)[r // half_slots]
        out[r % half_slots] = block[chip // across, chip % across]


def hidden_part_kernel(plan, route, part, rows, columns, table, left_own, left_other, right_own,
                       right_other, out_ref, block, lefts, some):
    across, half_slots = plan.narrow // 2, plan.slots // 2
    core = plan.core(table)
    here = plan.chip(table, route, 0, 0)
    lefts[0] = left_own[...].T
    lefts[1] = left_other[...].T

    @pl.when(core == 0)
    def _():
        y = (here % across) ^ part
        s = pl.ds(pl.multiple_of(y * columns, 128), columns)
        tile = nn(lefts[0], right_own[:, s]) + nn(lefts[1], right_other[:, s])
        block[:, pl.ds(y, 1)] = tile.astype(BF).reshape(plan.wide, 1, rows, columns)

    @pl.when(core == 1)
    def _():
        x = (here // across % 2) ^ part
        for z in range(plan.far):
            at = pl.ds(pl.multiple_of((2 * z + x) * rows, 16), rows)
            for k in (0, 1):
                some[k, z * rows : (z + 1) * rows, :] = lefts[k, at, :]
        tile = nn(some[0], right_own[...]) + nn(some[1], right_other[...])
        for z in range(plan.far):
            for y in range(across):
                block[2 * z + x, y] = tile[
                    z * rows : (z + 1) * rows, y * columns : (y + 1) * columns
                ].astype(BF)

    for r in range(half_slots):
        chip = plan.chip(table, route, 0, part * half_slots + r)
        out_ref[r] = block[chip // across, chip % across]


def first_grad_kernel(plan, route, rows, columns, arows, table, gu_own, gu_other, a, b, c, d,
                      e, f, g, k, p, q, r, s, l, m, n, o, grad_ref, unit_ref, inv_ref, vec_ref, middle_ref,
                      mine_ref, theirs_ref, context_ref, sums_ref, weight, mix, low_ref):
    for h in (0, 1):
        place_hidden(plan, route, table, h, ((a, b, c, d), (e, f, g, k))[h], weight.at[h], rows, columns)
    width = unit_ref.shape[1]
    half = width // 2
    for h, pieces in ((0, (p, q, r, s)), (1, (l, m, n, o))):
        place_attention(plan, table, h, pieces, None, mix, arows)
    core = plan.core(table)
    total = nt(gu_own[...], weight[0])
    total = total + nt(gu_other[...], weight[1])
    grad = grad_ref[...] + total
    unit = unit_ref[...]
    scaled = grad * vec_ref[GAIN1 : GAIN1 + 1, :]
    middle = inv_ref[:, 0:1] * (scaled - mean(scaled) - unit * mean(scaled * unit))
    low = middle.astype(BF)
    middle_ref[...] = middle
    low_ref[...] = low
    mine_ref[...] = low_ref[:, pl.ds(pl.multiple_of(core * half, 128), half)]
    theirs_ref[...] = low_ref[:, pl.ds(pl.multiple_of((core ^ 1) * half, 128), half)]
    sums_ref[0:1, :] = jnp.sum(grad * unit, 0, keepdims=True)
    sums_ref[1:2, :] = jnp.sum(grad, 0, keepdims=True)
    sums_ref[2:3, :] = jnp.sum(low.astype(F32), 0, keepdims=True)
    context_ref[...] = (nt(low[:, :half], mix[0]) + nt(low[:, half:], mix[1])).astype(BF)


def attention_grad_kernel(plan, h, table, keep_ref, probs_ref, grad_ref, cos_ref, sin_ref,
                          out_ref, sums_ref):
    core = plan.core(table)
    tokens, width = grad_ref.shape
    half = width // 2
    cos, sin = cos_ref[...], sin_ref[...]
    left = first_half(tokens)
    scale = 1.0 / math.sqrt(HD)
    keep, grads_in, probs = keep_ref, grad_ref, probs_ref
    for q in range(half // 128):
        at = [slice(g * half + 128 * q, g * half + 128 * q + 128) for g in range(3)]
        query, key, value = [keep[:, s] for s in at]
        came = grads_in[:, pl.ds(pl.multiple_of((core ^ h) * half + 128 * q, 128), 128)]
        parts = []
        for e in (0, 1):
            mine = left if e == 0 else ~left
            low = probs[2 * q + e]
            prob = low.astype(F32)
            grad = nt(jnp.where(mine, came, jnp.zeros_like(came)), value)
            score = prob * (grad - jnp.sum(prob * grad, -1, keepdims=True))
            score = score.astype(BF)
            parts.append((nn(score, key), tn(score, query), tn(low, came)))
        grads = [jnp.where(left, u, v) for u, v in zip(*parts)]
        grads = [(g * scale) * cos + swap_lanes((g * scale) * sin) for g in grads[:2]] + grads[2:]
        for s, g in zip(at, grads):
            g = g.astype(BF)
            out_ref[:, s] = g
            sums_ref[:, s] = jnp.sum(g.astype(F32), 0, keepdims=True)


def attention_weight_kernel(plan, rows, table, x_own, x_other, g_own, g_other, c_own, c_other,
                            c_came_own, c_came_other, b_own, b_other, bias_own, bias_other,
                            first_ref, second_ref, cot_ref, up_own, up_other, low_one, low_rest,
                            low_away, high_one, high_rest, high_away, block, mixed, sums):
    core = plan.core(table)
    half_slots = plan.slots // 2
    tokens, columns = g_own.shape
    third = columns // 3
    height = rows + rows // 3
    pack_vectors(plan, core, x_own.shape[1], bias_own, bias_other, first_ref, second_ref, cot_ref,
                 up_own, up_other, sums)
    far = plan.far
    for ref in (low_away, high_away):
        ref[far * height :, :] = sums[...].astype(BF)
    high_rest[(far - 1) * height :, :] = jnp.zeros_like(high_rest[(far - 1) * height :, :])
    block[...] = (
        (tn(x_own[...], g_own[...]) + tn(x_other[...], g_other[...]))
        .astype(BF)
        .reshape(block.shape)
    )
    for h, mine, came in ((0, c_own, c_came_other), (1, c_other, c_came_own)):
        mixed[pl.ds((core ^ h) * half_slots, half_slots)] = (
            (tn(mine[...], b_own[...]) + tn(came[...], b_other[...]))
            .astype(BF)
            .reshape((half_slots,) + mixed.shape[1:])
        )
    for r in reversed(range(plan.slots)):
        chip = plan.chip(table, plan.far_first, 0, r)
        side, slot = divmod(r, half_slots)
        one, rest, away = ((low_one, low_rest, low_away), (high_one, high_rest, high_away))[side]
        if slot == 0:
            out, at = one, 0
        elif slot < far:
            out, at = rest, (slot - 1) * height
        else:
            out, at = away, (slot - far) * height
        out[at : at + rows, :] = block[chip]
        for b in range(3):
            out[at + rows : at + height, b * third : (b + 1) * third] = mixed[chip, b]


def input_grad_kernel(plan, rows, table, middle_ref, g_own, g_other, a, b, c, d, e, f, g, k,
                      out_ref, triple):
    for h, pieces in ((0, (a, b, c, d)), (1, (e, f, g, k))):
        place_attention(plan, table, h, pieces, triple.at[h], None, rows)
    total = nt(g_own[...], triple[0])
    total = total + nt(g_other[...], triple[1])
    out_ref[...] = (middle_ref[...] + total).astype(BF)


def total_kernel(plan, rows, table, one, sums, a, b, c, mine_ref, theirs_ref, both):
    core = plan.core(table)
    total = jnp.concatenate([one[...], sums[...].astype(F32)], 0)
    for ref in (a, b, c):
        total = total + ref[...].astype(F32)
    third, half = rows // 3, total.shape[1] // 3
    width = 2 * half
    both[:, : 3 * half] = total[:rows]
    for k in range(3):
        both[k * third : (k + 1) * third, 3 * half :] = (
            total[rows : rows + third, k * half : (k + 1) * half]
        )
    piece = rows // 2
    mine_ref[:piece, :] = both[pl.ds(pl.multiple_of(core * piece, 8), piece), :]
    theirs_ref[:piece, :] = both[pl.ds(pl.multiple_of((core ^ 1) * piece, 8), piece), :]
    for ref in (mine_ref, theirs_ref):
        ref[piece:, :width] = total[rows + third :, :width]


def share_kernel(plan, table, index_ref, mine_ref, came_ref, triple_ref, mix_ref, tb_ref, mb_ref,
                 g1_ref, s1_ref, ub_ref, db_ref, g2_ref, s2_ref):
    core, index = plan.core(table), index_ref[0]
    piece, width = mix_ref.shape
    half = width // 2
    for ref, h in ((mine_ref, core), (came_ref, core ^ 1)):
        for g in range(3):
            at = pl.ds(pl.multiple_of(g * width + h * half, 128), half)
            triple_ref[:, at] = ref[:piece, g * half : (g + 1) * half]
        mix_ref[:, pl.ds(pl.multiple_of(h * half, 128), half)] = ref[:piece, 3 * half : 4 * half]
    sums = mine_ref[piece:, :width] + came_ref[piece:, :width]
    biases = jnp.concatenate([sums[g : g + 1, :] for g in range(3)], 1)
    biases = jnp.broadcast_to(biases, (8, 3 * width))
    tb_ref[...] = pltpu.roll(biases, (3 * width - index * 3 * piece) % (3 * width), 1)[
        0:1, : 3 * piece
    ]
    rolled = pltpu.roll(sums[:8], (width - index * piece) % width, 1)
    for row, ref in ((MIX, mb_ref), (GAIN1, g1_ref), (SHIFT1, s1_ref), (GAIN2, g2_ref),
                     (SHIFT2, s2_ref)):
        ref[...] = rolled[row : row + 1, :piece]
    of_wide, of_narrow = index // plan.narrow, index % plan.narrow
    mine = sums[UP : UP + 1, :]
    for n in range(1, plan.narrow):
        mine = jnp.where(of_narrow == n, sums[UP + n : UP + n + 1, :], mine)
    ub_ref[...] = mine
    count = db_ref.shape[1]
    rolled = pltpu.roll(sums[8:], (width - of_wide * count) % width, 1)
    row = UP + plan.narrow - 8
    db_ref[...] = rolled[row : row + 1, :count]


def half_tables(tokens):
    position = jnp.arange(tokens, dtype=F32)
    column = jnp.arange(2 * HD, dtype=jnp.int32)
    pair = (column % HD // 2).astype(F32)
    angle = position[:, None] * jnp.exp(pair * (-2.0 / HD) * math.log(10000.0))[None, :]
    parity = (column % 2).astype(F32) * 2.0 - 1.0
    return jnp.cos(angle), jnp.sin(angle) * parity[None, :]


def fast_body(
    plan,
    inputs,
    lengths,
    triple_weight,
    triple_bias,
    mix_weight,
    mix_bias,
    first_gain,
    first_shift,
    up_weight,
    up_bias,
    down_weight,
    down_bias,
    second_gain,
    second_shift,
    cotangent,
):
    tokens, width = inputs.shape
    half = width // 2
    wide, narrow = plan.wide, plan.narrow
    index = lax.axis_index(AXES)
    core = index & 1
    of_wide = lax.axis_index("wide")
    table = plan.table(index, lengths)
    hidden = up_weight.shape[1]
    tile_rows = up_weight.shape[0]
    piece = triple_weight.shape[0]
    rows = 2 * piece
    third = rows // 3
    half_slots = plan.slots // 2
    far_first, far_second = plan.far_first, plan.far_second
    flops = 2.0 * tokens * width * width
    hidden_half = hidden * narrow // 2

    place = index.astype(jnp.int32)[None]
    mine, theirs = call(
        split_kernel,
        [shape((piece, 4 * half))] * 2,
        (place, triple_weight, mix_weight),
        "svv",
        [],
        0,
        16,
    )
    first, rest = call(
        join_kernel,
        [shape((1, 2 * third, 3 * half)), shape((2 * third, 3 * half))],
        (place, mine, plan.swap(theirs)),
        "svv",
        [],
        0,
        16,
    )
    row = functools.partial(jnp.reshape, shape=(1, -1))
    up_share = lax.dynamic_slice(up_bias, (of_wide * (hidden // wide),), (hidden // wide,))
    (share,) = call(
        functools.partial(spread_kernel, plan),
        [shape((TABLE_ROWS, SHARE))],
        (
            after(place, first),
            row(triple_bias),
            row(mix_bias),
            row(first_gain),
            row(first_shift),
            row(second_gain),
            row(second_shift),
            row(up_share),
            row(down_bias),
        ),
        "s" + 8 * "l",
        [VMEM((TABLE_ROWS, SHARE), F32)],
        0,
        60,
    )
    (second,) = call(
        beside_kernel,
        [shape((1, 2 * third, 3 * half + SHARE))],
        (place, rest, share, plan.swap(share)),
        "svvv",
        [],
        0,
        16,
    )
    cat = functools.partial(jnp.concatenate, axis=0)
    cos, sin = half_tables(tokens)
    inputs_came = plan.swap(after(inputs, first))
    down = after(down_weight.T[None], first)
    down_came = plan.send(down, far_second, 1)
    first = cat(after_all(plan.gather_far(first), inputs_came, second))
    first_came = plan.permute(first, plan.first)
    second = plan.gather_far(after(second, first))
    up = after(up_weight[None], first)
    up_came = plan.send(up, far_first, 1)
    first, first_came = after_all((first, first_came))
    first = cat((first, first_came))
    first_came = plan.permute(first, plan.last)
    second = cat(after_all(second, first))
    second_came = plan.permute(second, plan.first)
    down = cat(after_all((down, down_came), first))
    down_came = plan.send(down, far_second, 2)
    up = cat(after_all((up, up_came), down))
    up_came = plan.send(up, far_first, 2)
    second, second_came = after_all((second, second_came), up)
    second = cat((second, second_came))
    first, first_came = after_all((first, first_came), second)
    second_came = plan.permute(second, plan.last)
    up = cat(after_all((up, up_came), first_came))
    up_came = plan.permute(up, plan.first)
    ups = [up, up_came, plan.permute(up, plan.last)]
    down = cat(after_all((down, down_came), up))
    down_came = plan.send(down, far_second, 4)
    second, second_came = after_all((second, second_came), down)
    att_own = [first, first_came, second, second_came]
    att_other = [plan.swap(v) for v in att_own]
    (vecs,) = call(
        functools.partial(vectors_kernel, plan, piece),
        [shape((TABLE_ROWS, width), F32)],
        (table, *att_own[2:]),
        "svv",
        [
            VMEM((plan.slots, 2 * third, SHARE), BF),
            VMEM((8, 3 * width + 2 * SHARE), F32),
            VMEM((8, width + 2 * SHARE), F32),
            VMEM((narrow, 8, width + 2 * SHARE), F32),
            VMEM((8, width + 2 * SHARE), F32),
        ],
        0,
        32,
    )

    def attend(h, pieces, gate=()):
        return call(
            functools.partial(attention_kernel, plan, rows, h),
            [
                shape((tokens, 3 * half)),
                shape((half // HD, tokens, tokens)),
                shape((tokens, half)),
            ],
            (after(table, *gate), inputs, *pieces, cos, sin, vecs),
            "s" + 8 * "v",
            [VMEM((width, 3 * half), BF)],
            80 * flops,
            24,
        )

    own, p_own, context_own = attend(0, att_own, (second_came, *att_other[:2]))
    (up_came,) = after_all((ups[1],), context_own)
    ups = [ups[0], up_came, ups[2], plan.permute(up_came, plan.last)]
    down = cat(after_all((down, down_came), up_came))
    downs = [down, plan.permute(down, plan.last)]
    other, p_other, context_other = attend(1, att_other, (down,))
    unit, inv, low = call(
        functools.partial(mix_kernel, plan, rows),
        [shape((tokens, width), F32), shape((tokens, 128), F32), shape((tokens, width))],
        (table, inputs, context_own, context_other, *att_own, *att_other, vecs),
        "s" + 12 * "v",
        [VMEM((2, width, half), BF)],
        1,
        24,
    )
    hidden_scratch = [VMEM((2, width, hidden_half), BF)]
    ups = [*ups, *(plan.swap(v) for v in ups)]
    down_low_came = plan.swap(downs[0])
    context_came = plan.swap(context_own), plan.swap(context_other)
    act_own, act_other, slope_own, slope_other = call(
        functools.partial(up_kernel, plan, far_first, tile_rows, hidden),
        [shape((tokens, hidden_half))] * 4,
        (table, low, *ups, vecs),
        "s" + 10 * "v",
        hidden_scratch,
        1,
        24,
    )
    (down_high,) = after_all(downs[1:], act_own)
    downs = [downs[0], down_high, down_low_came, plan.swap(down_high)]
    low_came, act_came = plan.swap(low), plan.swap(act_other)
    half_scratch = [VMEM((width, hidden_half), BF)]
    downward, scaled_mean, cot_sum = call(
        functools.partial(down_own_kernel, plan, far_second, tile_rows, hidden),
        [shape((tokens, width), F32), shape((tokens, 128), F32), shape((1, width), F32)],
        (after(table, *context_came), act_own, *downs[:2], unit, cotangent, vecs),
        "s" + 6 * "v",
        half_scratch,
        80 * flops,
        24,
    )
    outputs, grad_second, grad_down, sums_second = call(
        functools.partial(down_kernel, plan, far_second, tile_rows, hidden),
        [
            shape((tokens, width)),
            shape((tokens, width), F32),
            shape((tokens, width)),
            shape((2, width), F32),
        ],
        (table, downward, act_other, *downs[2:], scaled_mean, cotangent, vecs),
        "s" + 7 * "v",
        half_scratch,
        1,
        24,
    )
    grad_down_came = plan.swap(grad_down)

    def grad_up(h, pieces, slope, gate=()):
        return call(
            functools.partial(grad_up_kernel, plan, far_second, h, tile_rows, hidden),
            [shape((tokens, hidden_half)), shape((1, hidden_half), F32)],
            (after(table, *gate), grad_down, *pieces, slope),
            "s" + 4 * "v",
            half_scratch,
            1,
            24,
        )

    gu_other, sums_up_other = grad_up(1, downs[2:], slope_other)
    gu_came = plan.swap(gu_other)

    def hidden_grad(route, left, left_came, right, right_came, cost, gate):
        return call(
            functools.partial(hidden_grad_kernel, plan, route, tile_rows, hidden),
            [shape((half_slots, tile_rows, hidden))] * 2,
            (after(table, *gate), left, left_came, right, right_came),
            "svvvv",
            [VMEM((wide, narrow // 2, tile_rows, hidden), BF)],
            cost,
            24,
        )

    def down_grad(part, gate):
        (tiles,) = call(
            functools.partial(hidden_part_kernel, plan, far_second, part, tile_rows, hidden),
            [shape((half_slots, tile_rows, hidden))],
            (after(table, *gate), grad_down, grad_down_came, act_own, act_came),
            "svvvv",
            [
                VMEM((wide, narrow // 2, tile_rows, hidden), BF),
                VMEM((2, width, tokens), BF),
                VMEM((2, width // 2, tokens), BF),
            ],
            80 * flops if part else 1,
            24,
        )
        return tiles

    down_high = down_grad(1, (sums_up_other,))
    down_came = plan.permute(down_high, plan.last)
    gu_own, sums_up_own = grad_up(0, downs[:2], slope_own, (down_high,))
    down_low = down_grad(0, (sums_up_own,))
    up_low, up_high = hidden_grad(far_first, low, low_came, gu_own, gu_came, 1, (down_low,))
    up_came = plan.permute(up_high, plan.last)
    grad_middle, branch_mine, branch_theirs, grad_context, sums_first = call(
        functools.partial(first_grad_kernel, plan, far_first, tile_rows, hidden, rows),
        [
            shape((tokens, width), F32),
            shape((tokens, half)),
            shape((tokens, half)),
            shape((tokens, width)),
            shape((3, width), F32),
        ],
        (
            after(table, up_low),
            gu_own,
            gu_other,
            *ups,
            *att_own,
            *att_other,
            grad_second,
            unit,
            inv,
            vecs,
        ),
        "s" + 22 * "v",
        hidden_scratch
        + [VMEM((2, width, half), BF), VMEM((tokens, width), BF)],
        1,
        24,
    )
    branch_came = plan.swap(branch_theirs)

    def attention_grad(h, keep, probs, gate=()):
        return call(
            functools.partial(attention_grad_kernel, plan, h),
            [shape((tokens, 3 * half)), shape((1, 3 * half), F32)],
            (after(table, *gate), keep, probs, grad_context, cos, sin),
            "svvvvv",
            [],
            1,
            24,
        )

    gt_other, bias_other = attention_grad(1, other, p_other, (act_came,))
    gt_came = plan.swap(gt_other)
    down_stay, down_away = halves(*after_all((down_low, down_came), bias_other))
    down_came = plan.send(down_away, far_second, 4)
    gt_own, bias_own = attention_grad(0, own, p_own, (down_away,))
    up_stay, up_away = halves(*after_all((up_low, up_came), bias_own))
    up_came = plan.permute(up_away, plan.first)
    height = rows + third
    far = plan.far
    kinds = [shape((k * height + more, 3 * half)) for k, more in ((1, 0), (far - 1, 0), (far, TABLE_ROWS))]
    longer = shape(((far - 1) * height + 2 * TABLE_ROWS, 3 * half))
    low_one, low_rest, low_away, high_one, high_rest, high_away = call(
        functools.partial(attention_weight_kernel, plan, rows),
        kinds + [kinds[0], longer, kinds[2]],
        (
            after(table, up_away),
            inputs,
            inputs_came,
            gt_own,
            gt_came,
            context_own,
            context_other,
            *context_came,
            branch_mine,
            branch_came,
            bias_own,
            bias_other,
            sums_first,
            sums_second,
            cot_sum,
            sums_up_own,
            sums_up_other,
        ),
        "s" + 17 * "v",
        [
            VMEM((plan.slots, rows, 3 * half), BF),
            VMEM((plan.slots, 3, third, half), BF),
            VMEM((TABLE_ROWS, 3 * half), F32),
        ],
        80 * flops,
        24,
    )
    came_away = plan.permute(high_away, plan.last)
    came_rest = plan.permute(high_rest, plan.last)
    came_one = plan.permute(high_one, plan.last)
    down_stay, down_away = halves(*after_all((down_stay, down_came), low_away))
    down_came = plan.send(down_away, far_second, 2)
    up_stay, up_away = halves(*after_all((up_stay, up_came), down_away))
    up_came = plan.send(up_away, far_first, 2)
    (input_grad,) = call(
        functools.partial(input_grad_kernel, plan, rows),
        [shape((tokens, width))],
        (after(table, up_away), grad_middle, gt_own, gt_other, *att_own, *att_other),
        "s" + 11 * "v",
        [VMEM((2, width, 3 * half), BF)],
        80 * flops,
        24,
    )
    low_away, came_away = after_all((low_away, came_away), input_grad)
    away = added(low_away[height:], came_away[height:])
    next_rest = plan.permute(away, plan.first)
    next_one = plan.permute(added(low_away[:height], came_away[:height]), plan.first)
    down_stay, down_came, up_stay, up_came = after_all(
        (down_stay, down_came, up_stay, up_came), away
    )
    down_stay, down_away = halves(down_stay, down_came)
    down_came = plan.send(down_away, far_second, 1)
    up_stay, up_away = halves(up_stay, up_came)
    up_came = plan.send(up_away, far_first, 1)
    end = (far - 1) * height
    (next_rest,) = after_all((next_rest,), down_away, up_away)
    came_one, next_one = after_all((came_one, next_one), next_rest)
    one = low_one.astype(F32) + came_one.astype(F32) + next_one.astype(F32)
    (next_rest,) = after_all((next_rest,), one)
    sums = added(away[end:], next_rest[end:])
    parts = [None]
    for k in range(far - 1):
        part = slice(k * height, (k + 1) * height)
        parts.append(cat([added(low_rest[part], came_rest[part], next_rest[part]), sums]))
    down_stay, down_came, up_stay, up_came = after_all(
        (down_stay, down_came, up_stay, up_came), parts[1]
    )
    down_total = down_stay[0].astype(F32) + down_came[0].astype(F32)
    up_total = up_stay[0].astype(F32) + up_came[0].astype(F32)
    mine, theirs = call(
        functools.partial(total_kernel, plan, rows),
        [shape((piece + TABLE_ROWS, 4 * half), F32)] * 2,
        (
            after(table, down_total, up_total),
            one,
            sums,
            *plan.send_far(parts),
        ),
        "s" + 5 * "v",
        [VMEM((rows, 4 * half), F32)],
        1,
        16,
    )
    one = [3 * piece, piece, piece, piece, hidden, down_bias.shape[0], piece, piece]
    triple_grad, mix_grad, *vectors = call(
        functools.partial(share_kernel, plan),
        [shape((piece, 3 * width), F32), shape((piece, width), F32)]
        + [shape((1, n), F32) for n in one],
        (table, place, mine, plan.swap(theirs)),
        "ssvv",
        [],
        1,
        16,
    )
    vectors = [v.reshape(-1) for v in vectors]
    return (
        outputs,
        input_grad,
        triple_grad,
        vectors[0],
        mix_grad,
        *vectors[1:4],
        up_total,
        vectors[4],
        down_total.T,
        *vectors[5:],
    )


def fits(plan_shape, width, hidden):
    wide, narrow = plan_shape
    powers = all(n >= 4 and n & (n - 1) == 0 for n in (wide, narrow)) and narrow == 4
    return (
        powers
        and width % (wide * 16) == 0
        and width % (wide * narrow // 2 * 48) == 0
        and hidden % (narrow * 128) == 0
        and width % 768 == 0
    )


def solution(mesh):
    placed = (
        P(("wide", "narrow"), None),
        P(("wide", "narrow")),
        P(("wide", "narrow"), None),
        P(("wide", "narrow")),
        P(("wide", "narrow"), None),
        P(("wide", "narrow")),
        P(("wide", "narrow")),
        P(("wide", "narrow")),
        P("wide", "narrow"),
        P("narrow"),
        P("narrow", "wide"),
        P("wide"),
        P(("wide", "narrow")),
        P(("wide", "narrow")),
        P(("wide", "narrow"), None),
    )
    wide, narrow = mesh.shape["wide"], mesh.shape["narrow"]

    def layer(*arrays):
        rows, hidden = arrays[8].shape
        if fits((wide, narrow), rows * wide, hidden * narrow):
            return fast_body(Plan(wide, narrow), *arrays)
        return body(*arrays)

    return jax.shard_map(
        layer,
        mesh=mesh,
        in_specs=placed,
        out_specs=(
            P(("wide", "narrow"), None),
            P(("wide", "narrow"), None),
            P(("wide", "narrow"), None),
            P(("wide", "narrow")),
            P(("wide", "narrow"), None),
            P(("wide", "narrow")),
            P(("wide", "narrow")),
            P(("wide", "narrow")),
            P("wide", "narrow"),
            P("narrow"),
            P("narrow", "wide"),
            P("wide"),
            P(("wide", "narrow")),
            P(("wide", "narrow")),
        ),
        check_vma=False,
    )
```

```python
import functools
import math

import jax
import jax.numpy as jnp
import numpy as np
from jax import lax
from jax.experimental import pallas as pl
from jax.experimental.pallas import tpu as pltpu
from jax.sharding import PartitionSpec as P

H = 12
HD = 64


EPSILON = 1e-06


def tables(token_rows, width, head):
    position = jnp.arange(token_rows, dtype=jnp.float32)
    column = jnp.arange(width, dtype=jnp.int32)
    pair_index = (column % head // 2).astype(jnp.float32)
    frequency = jnp.exp(pair_index * (-2.0 / head) * math.log(10000.0))
    angle = position[:, None] * frequency[None, :]
    parity = (column % 2).astype(jnp.float32) * 2.0 - 1.0
    return (jnp.cos(angle), jnp.sin(angle) * parity[None, :])


def swapped(values):
    shape = values.shape
    paired = values.reshape(shape[:-1] + (shape[-1] // 2, 2))
    return paired[..., ::-1].reshape(shape)


def rotate(values, cosine, sine):
    return values * cosine + swapped(values) * sine


def unrotate(grad, cosine, sine):
    return grad * cosine + swapped(grad * sine)


def normalize_forward(values, gain, shift):
    mean_row = jnp.mean(values, -1, keepdims=True)
    centred = values - mean_row
    inverse = lax.rsqrt(jnp.mean(centred * centred, -1, keepdims=True) + EPSILON)
    unit = centred * inverse
    return (unit * gain + shift, unit, inverse)


def normalize_backward(grad, unit, inverse, gain):
    scaled = grad * gain
    inner = (
        scaled
        - jnp.mean(scaled, -1, keepdims=True)
        - unit * jnp.mean(scaled * unit, -1, keepdims=True)
    )
    return (inner * inverse, jnp.sum(grad * unit, 0), jnp.sum(grad, 0))


def gelu_exact(values):
    return jax.nn.gelu(values, approximate=False)


def gelu_backward(upward, grad_active):
    unused, pull_back = jax.vjp(gelu_exact, upward)
    return pull_back(grad_active)[0]


def softmax_block(query_block, key, valid, scale):
    scores = (
        jnp.einsum("qhd,khd->hqk", query_block, key, preferred_element_type=jnp.float32) * scale
    )
    scores = jnp.where(valid[None, None, :], scores, -1e30)
    return jax.nn.softmax(scores, axis=-1)


def attention_forward(query, key, value, valid, scale):
    token_rows = query.shape[0]
    block = min(512, token_rows)
    weights_block = softmax_block(query, key, valid, scale)
    context = jnp.einsum(
        "hqk,khd->qhd",
        weights_block.astype(jnp.bfloat16),
        value,
        preferred_element_type=jnp.float32,
    )
    pieces = context.reshape(block, -1).astype(jnp.bfloat16)
    return pieces


def attention_backward(query, key, value, grad_context, valid, scale):
    weights_block = softmax_block(query, key, valid, scale)
    grad_weights = jnp.einsum(
        "qhd,khd->hqk", grad_context, value, preferred_element_type=jnp.float32
    )
    inner = weights_block * (
        grad_weights - jnp.sum(weights_block * grad_weights, -1, keepdims=True)
    )
    inner_low = inner.astype(jnp.bfloat16)
    query_pieces = (
        jnp.einsum("hqk,khd->qhd", inner_low, key, preferred_element_type=jnp.float32) * scale
    )
    grad_key = (
        jnp.einsum("hqk,qhd->khd", inner_low, query, preferred_element_type=jnp.float32) * scale
    )
    grad_value = jnp.einsum(
        "hqk,qhd->khd",
        weights_block.astype(jnp.bfloat16),
        grad_context,
        preferred_element_type=jnp.float32,
    )
    return (query_pieces, grad_key, grad_value)


def body(
    inputs,
    lengths,
    triple_weight,
    triple_bias,
    mix_weight,
    mix_bias,
    first_gain,
    first_shift,
    up_weight,
    up_bias,
    down_weight,
    down_bias,
    second_gain,
    second_shift,
    cotangent,
):
    token_rows, width = inputs.shape
    scale = 1.0 / math.sqrt(HD)
    head_shape = (token_rows, H, HD)
    (
        triple_full,
        mix_full,
        triple_bias_full,
        mix_bias_full,
        gain_one,
        shift_one,
        gain_two,
        shift_two,
    ) = (
        lax.all_gather(triple_weight, ("wide", "narrow"), axis=0, tiled=True),
        lax.all_gather(mix_weight, ("wide", "narrow"), axis=0, tiled=True),
        lax.all_gather(triple_bias, ("wide", "narrow"), axis=0, tiled=True),
        lax.all_gather(mix_bias, ("wide", "narrow"), axis=0, tiled=True),
        lax.all_gather(first_gain, ("wide", "narrow"), axis=0, tiled=True),
        lax.all_gather(first_shift, ("wide", "narrow"), axis=0, tiled=True),
        lax.all_gather(second_gain, ("wide", "narrow"), axis=0, tiled=True),
        lax.all_gather(second_shift, ("wide", "narrow"), axis=0, tiled=True),
    )
    up_rows, down_columns, down_bias_full = (
        lax.all_gather(up_weight, "wide", axis=0, tiled=True),
        lax.all_gather(down_weight, "wide", axis=1, tiled=True),
        lax.all_gather(down_bias, "wide", axis=0, tiled=True),
    )
    gain_one = gain_one.astype(jnp.float32)
    gain_two = gain_two.astype(jnp.float32)
    cosine, sine = tables(token_rows, width, HD)
    valid = jnp.arange(token_rows, dtype=jnp.int32) < lengths[0]
    triple = jnp.dot(
        inputs, triple_full, preferred_element_type=jnp.float32
    ) + triple_bias_full.astype(jnp.float32)
    query = rotate(triple[:, :width], cosine, sine).astype(jnp.bfloat16).reshape(head_shape)
    key = (
        rotate(triple[:, width : 2 * width], cosine, sine).astype(jnp.bfloat16).reshape(head_shape)
    )
    value = triple[:, 2 * width :].astype(jnp.bfloat16).reshape(head_shape)
    context = attention_forward(query, key, value, valid, scale)
    branch = jnp.dot(context, mix_full, preferred_element_type=jnp.float32) + mix_bias_full.astype(
        jnp.float32
    )
    first, first_unit, first_inverse = normalize_forward(
        inputs.astype(jnp.float32) + branch, gain_one, shift_one.astype(jnp.float32)
    )
    first_low = first.astype(jnp.bfloat16)
    gathered = lax.all_gather(first_low, "narrow", axis=0, tiled=True)
    upward = jnp.dot(gathered, up_rows, preferred_element_type=jnp.float32) + up_bias.astype(
        jnp.float32
    )
    active = gelu_exact(upward).astype(jnp.bfloat16)
    downward = lax.psum_scatter(
        jnp.dot(active, down_columns, preferred_element_type=jnp.float32).astype(jnp.bfloat16),
        "narrow",
        scatter_dimension=0,
        tiled=True,
    ).astype(jnp.float32)
    downward = downward + down_bias_full.astype(jnp.float32)
    result, second_unit, second_inverse = normalize_forward(
        first + downward, gain_two, shift_two.astype(jnp.float32)
    )
    outputs = result.astype(jnp.bfloat16)
    grad_second, second_gain_grad, second_shift_grad = normalize_backward(
        cotangent.astype(jnp.float32), second_unit, second_inverse, gain_two
    )
    grad_down = grad_second.astype(jnp.bfloat16)
    grad_gathered = lax.all_gather(grad_down, "narrow", axis=0, tiled=True)
    grad_active = jnp.dot(grad_gathered, down_columns.T, preferred_element_type=jnp.float32)
    grad_up = gelu_backward(upward, grad_active).astype(jnp.bfloat16)
    grad_feed = lax.psum_scatter(
        jnp.dot(grad_up, up_rows.T, preferred_element_type=jnp.float32).astype(jnp.bfloat16),
        "narrow",
        scatter_dimension=0,
        tiled=True,
    ).astype(jnp.float32)
    up_part = jnp.dot(gathered.T, grad_up, preferred_element_type=jnp.float32)
    down_part = jnp.dot(active.T, grad_gathered, preferred_element_type=jnp.float32)
    down_bias_part = jnp.sum(grad_gathered, 0, dtype=jnp.float32)
    up_weight_grad, down_weight_grad, down_bias_grad = (
        lax.psum_scatter(
            up_part.astype(jnp.bfloat16), "wide", scatter_dimension=0, tiled=True
        ).astype(jnp.float32),
        lax.psum_scatter(
            down_part.astype(jnp.bfloat16), "wide", scatter_dimension=1, tiled=True
        ).astype(jnp.float32),
        lax.psum_scatter(
            down_bias_part.astype(jnp.bfloat16), "wide", scatter_dimension=0, tiled=True
        ).astype(jnp.float32),
    )
    up_bias_grad = lax.psum(jnp.sum(grad_up, 0, dtype=jnp.float32), "wide")
    grad_first = grad_second + grad_feed
    grad_middle, first_gain_grad, first_shift_grad = normalize_backward(
        grad_first, first_unit, first_inverse, gain_one
    )
    grad_branch = grad_middle.astype(jnp.bfloat16)
    mix_weight_grad = jnp.dot(context.T, grad_branch, preferred_element_type=jnp.float32)
    mix_bias_grad = jnp.sum(grad_branch, 0, dtype=jnp.float32)
    triple_back, mix_back = (
        lax.all_gather(triple_weight, ("wide", "narrow"), axis=0, tiled=True),
        lax.all_gather(mix_weight, ("wide", "narrow"), axis=0, tiled=True),
    )
    grad_context = (
        jnp.dot(grad_branch, mix_back.T, preferred_element_type=jnp.float32)
        .astype(jnp.bfloat16)
        .reshape(head_shape)
    )
    grad_query, grad_key, grad_value = attention_backward(
        query, key, value, grad_context, valid, scale
    )
    grad_triple = jnp.concatenate(
        [
            unrotate(grad_query.reshape(token_rows, width), cosine, sine),
            unrotate(grad_key.reshape(token_rows, width), cosine, sine),
            grad_value.reshape(token_rows, width),
        ],
        1,
    ).astype(jnp.bfloat16)
    triple_local = jnp.dot(inputs.T, grad_triple, preferred_element_type=jnp.float32)
    triple_bias_local = jnp.sum(grad_triple, 0, dtype=jnp.float32)
    grad_inputs = grad_middle + jnp.dot(
        grad_triple, triple_back.T, preferred_element_type=jnp.float32
    )
    summed = (
        lax.psum_scatter(triple_local, ("wide", "narrow"), scatter_dimension=0, tiled=True),
        lax.psum_scatter(mix_weight_grad, ("wide", "narrow"), scatter_dimension=0, tiled=True),
        lax.psum_scatter(triple_bias_local, ("wide", "narrow"), scatter_dimension=0, tiled=True),
        lax.psum_scatter(mix_bias_grad, ("wide", "narrow"), scatter_dimension=0, tiled=True),
        lax.psum_scatter(first_gain_grad, ("wide", "narrow"), scatter_dimension=0, tiled=True),
        lax.psum_scatter(first_shift_grad, ("wide", "narrow"), scatter_dimension=0, tiled=True),
        lax.psum_scatter(second_gain_grad, ("wide", "narrow"), scatter_dimension=0, tiled=True),
        lax.psum_scatter(second_shift_grad, ("wide", "narrow"), scatter_dimension=0, tiled=True),
    )
    return (
        outputs,
        grad_inputs.astype(jnp.bfloat16),
        summed[0],
        summed[2],
        summed[1],
        summed[3],
        summed[4],
        summed[5],
        up_weight_grad,
        up_bias_grad,
        down_weight_grad,
        down_bias_grad,
        summed[6],
        summed[7],
    )


VMEM = pltpu.VMEM
SMEM = pltpu.SMEM
BF = jnp.bfloat16
F32 = jnp.float32
AXES = ("wide", "narrow")
WHOLE = pl.BlockSpec(memory_space=VMEM)
SCALARS = pl.BlockSpec(memory_space=SMEM)
LEFT = pl.BlockSpec(memory_space=pltpu.HBM)


def nn(a, b):
    return lax.dot_general(a, b, (((1,), (0,)), ((), ())), preferred_element_type=F32)


def nt(a, b):
    return lax.dot_general(a, b, (((1,), (1,)), ((), ())), preferred_element_type=F32)


def tn(a, b):
    return lax.dot_general(a, b, (((0,), (0,)), ((), ())), preferred_element_type=F32)


def shape(dims, dtype=BF):
    return jax.ShapeDtypeStruct(dims, dtype)


class Load:
    def __init__(self, source, held, sem):
        self.copy = pltpu.make_async_copy(source, held, sem)
        self.held, self.waited = held, False
        self.shape = held.shape
        self.copy.start()

    def __call__(self):
        if not self.waited:
            self.copy.wait()
            self.waited = True
        return self.held


def call(kernel, outs, operands, kinds, scratch, flops, megabytes, out_specs=None):
    specs = {"s": SCALARS, "v": WHOLE, "h": LEFT, "l": LEFT}
    loads = [k for k, kind in enumerate(kinds) if kind == "l"]
    held = [VMEM(operands[k].shape, operands[k].dtype) for k in loads]
    assert len(kinds) == len(operands)

    def whole(*refs):
        refs = list(refs)
        count = len(loads)
        if count:
            sems = refs.pop()
            buffers, refs = refs[-count:], refs[:-count]
            for n, k in enumerate(loads):
                refs[k] = Load(refs[k], buffers[n], sems.at[n])
        kernel(*refs)
        for k in loads:
            refs[k]()

    return pl.pallas_call(
        whole,
        out_shape=outs,
        in_specs=[specs[kind] for kind in kinds],
        out_specs=[WHOLE] * len(outs) if out_specs is None else out_specs,
        scratch_shapes=list(scratch)
        + held
        + ([pltpu.SemaphoreType.DMA((len(loads),))] if loads else []),
        compiler_params=pltpu.CompilerParams(vmem_limit_bytes=megabytes << 20),
        cost_estimate=pl.CostEstimate(
            flops=int(flops), bytes_accessed=1, transcendentals=0
        ),
    )(*operands)


def drain(ref, sem):
    pltpu.make_async_copy(ref, ref, sem).wait()


class Plan:
    def __init__(self, wide, narrow):
        self.wide, self.narrow = wide, narrow
        self.devices = wide * narrow
        x, y = narrow, narrow // 2
        self.first, self.last = (x, y), (y, x)
        self.far = wide // 2
        line = self.devices // self.far
        along = [(line << k, line << k) for k in reversed(range(self.far.bit_length() - 1))]
        self.far_first = (*along, self.first, self.last)
        self.far_second = (self.first, *along, self.last)
        self.routes = (self.far_first, self.far_second)
        self.slots = 1 << len(self.far_first)

    def lead(self, route, slot):
        masks = [0, 0]
        for k, pair in enumerate(route):
            if slot >> k & 1:
                masks = [mask ^ bit for mask, bit in zip(masks, pair)]
        return masks

    def chips(self, device):
        core = device & 1
        return [
            (device ^ self.lead(route, r)[c]) >> 1
            for route in self.routes
            for c in (core, core ^ 1)
            for r in range(self.slots)
        ]

    def table(self, index, live):
        chips = np.array([self.chips(i) for i in range(self.devices)], np.int32)
        mine = lax.dynamic_slice(jnp.asarray(chips), (index, 0), (1, chips.shape[1]))[0]
        return jnp.concatenate([mine, (index & 1)[None].astype(jnp.int32), live])

    def chip(self, table, route, h, slot):
        return table[(2 * self.routes.index(route) + h) * self.slots + slot]

    def core(self, table):
        return table[2 * len(self.routes) * self.slots]

    def live(self, table):
        return table[2 * len(self.routes) * self.slots + 1]

    def permute(self, value, masks):
        return lax.ppermute(value, AXES, [(i, i ^ masks[i & 1]) for i in range(self.devices)])

    def swap(self, value):
        return self.permute(value, (1, 1))

    def send(self, value, route, slot):
        return self.permute(value, self.lead(route, slot))

    def gather_far(self, value):
        return [value] + [self.send(value, self.far_first, m) for m in range(1, self.far)]

    def send_far(self, parts):
        return [self.send(v, self.far_first, m) for m, v in enumerate(parts) if m]


def added(*values):
    return sum([v.astype(F32) for v in values[1:]], values[0].astype(F32)).astype(BF)


def halves(*values):
    count = values[0].shape[0] // 2
    return added(*(v[:count] for v in values)), added(*(v[count:] for v in values))


def together(*lists):
    flat = list(lax.optimization_barrier(tuple(v for values in lists for v in values)))
    return [[flat.pop(0) for _ in values] for values in lists]


def after_all(values, *others):
    return lax.optimization_barrier(tuple(values) + others)[: len(values)]


def after(value, *others):
    return lax.optimization_barrier((value,) + others)[0] if others else value


def mean(v):
    return jnp.mean(v, -1, keepdims=True)


def swap_lanes(v):
    lane = lax.broadcasted_iota(jnp.int32, v.shape, 1)
    return jnp.where(lane % 2 == 0, pltpu.roll(v, v.shape[1] - 1, 1), pltpu.roll(v, 1, 1))


def first_half(rows):
    return lax.broadcasted_iota(jnp.int32, (rows, 2 * HD), 1) < HD


def place_attention(plan, table, h, pieces, triple, mix, rows):
    core = plan.core(table)
    half_slots = plan.slots // 2
    third = rows // 3
    columns = pieces[0].shape[2]
    width = columns // 3
    for r in range(plan.slots):
        chip = plan.chip(table, plan.far_first, h, r)
        side, at = divmod(r, half_slots)
        first, second = pieces[side], pieces[2 + side]
        if triple is not None:
            top = pl.ds(pl.multiple_of(chip * rows, 16), 2 * third)
            triple[top, :] = first[at]
            rest = pl.ds(pl.multiple_of(chip * rows + 2 * third, 16), third)
            triple[rest, :] = second[at, :third, :columns]
        if mix is not None:
            for b in range(3):
                here = pl.ds(pl.multiple_of(chip * rows + b * third, 16), third)
                mix[core ^ h, here, :] = second[at, third:, b * width : (b + 1) * width]


def place_hidden(plan, route, table, h, pieces, weight, rows, columns):
    across = plan.narrow // 2
    slots = [(piece, k) for piece in pieces for k in range(piece.shape[0])]
    for r, (piece, k) in enumerate(slots):
        chip = plan.chip(table, route, h, r)
        down = pl.ds(pl.multiple_of(chip // across * rows, 16), rows)
        over = pl.ds(pl.multiple_of(chip % across * columns, 128), columns)
        weight[down, over] = piece[k]


TRIPLE, MIX, GAIN1, SHIFT1, GAIN2, SHIFT2, UP = 0, 3, 4, 5, 6, 7, 8
TABLE_ROWS = 16
SHARE = 128


def split_kernel(index_ref, triple_ref, mix_ref, mine_ref, theirs_ref):
    core = index_ref[0] % 2
    width = mix_ref.shape[1]
    half = width // 2
    for out, h in ((mine_ref, core), (theirs_ref, core ^ 1)):
        for g in range(3):
            at = pl.multiple_of(g * width + h * half, 128)
            out[:, g * half : (g + 1) * half] = triple_ref[:, pl.ds(at, half)]
        out[:, 3 * half :] = mix_ref[:, pl.ds(pl.multiple_of(h * half, 128), half)]


def join_kernel(index_ref, mine_ref, came_ref, first_ref, rest_ref):
    core = index_ref[0] % 2
    half = mine_ref.shape[1] // 4
    mine, came = mine_ref[...].astype(F32), came_ref[...].astype(F32)
    both = jnp.concatenate(
        [jnp.where(core == 0, mine, came), jnp.where(core == 0, came, mine)], 0
    ).astype(BF)
    third = both.shape[0] // 3
    first_ref[0] = both[: 2 * third, : 3 * half]
    rest_ref[:third, :] = both[2 * third :, : 3 * half]
    for b in range(3):
        rest_ref[third:, b * half : (b + 1) * half] = both[b * third : (b + 1) * third, 3 * half :]


def spread_kernel(plan, index_ref, tb_ref, mb_ref, g1_ref, s1_ref, g2_ref, s2_ref, ub_ref, db_ref,
                  share_ref, spread):
    of_narrow = index_ref[0] % plan.narrow
    spread[...] = jnp.zeros_like(spread)
    for row, ref in ((TRIPLE, tb_ref), (MIX, mb_ref), (GAIN1, g1_ref), (SHIFT1, s1_ref),
                     (GAIN2, g2_ref), (SHIFT2, s2_ref), (UP, ub_ref)):
        spread[row : row + 1, : ref.shape[1]] = ref()[...].astype(F32)
    count = db_ref.shape[1] // plan.narrow
    values = db_ref()[...].astype(F32)
    mine = values[:, :count]
    for k in range(1, plan.narrow):
        mine = jnp.where(of_narrow == k, values[:, k * count : (k + 1) * count], mine)
    spread[UP + plan.narrow : UP + plan.narrow + 1, :count] = mine
    share_ref[...] = spread[...].astype(BF)


def beside_kernel(index_ref, rest_ref, share_ref, came_ref, out_ref):
    core = index_ref[0] % 2
    columns = rest_ref.shape[1]
    share, came = share_ref[...], came_ref[...]
    out_ref[0, :, :columns] = rest_ref[...]
    out_ref[0, :TABLE_ROWS, columns:] = jnp.where(core == 0, share, came)
    out_ref[0, TABLE_ROWS:, columns:] = jnp.where(core == 0, came, share)


def vectors_kernel(plan, share, table, low_ref, high_ref, out_ref, held, triple, plain, up, down):
    half_slots = plan.slots // 2
    columns = low_ref.shape[2] - SHARE
    for r in range(plan.slots):
        piece = (low_ref, high_ref)[r // half_slots]
        held[plan.chip(table, plan.far_first, 0, r)] = piece[r % half_slots, :, columns:]
    for ref in (triple, plain, up, down):
        ref[...] = jnp.zeros_like(ref)
    width = out_ref.shape[1]
    part = width // plan.wide

    def put(ref, rows, at):
        block, lane = divmod(at, SHARE)
        s = slice(block * SHARE, (block + 2) * SHARE)
        ref[..., s] = ref[..., s] + (pltpu.roll(rows, lane, 1) if lane else rows)

    for device in range(plan.devices):
        of_wide, of_narrow = divmod(device, plan.narrow)
        rows = held[device // 2].astype(F32)[device % 2 * TABLE_ROWS :][:TABLE_ROWS]
        rows = jnp.concatenate([rows, jnp.zeros_like(rows)], 1)
        put(triple, rows[:8], 3 * share * device)
        put(plain, rows[:8], share * device)
        put(up.at[of_narrow], rows[8:], part * of_wide)
        put(down, rows[8:], share * device)
    out_ref[...] = jnp.zeros_like(out_ref)
    for g in range(3):
        out_ref[TRIPLE + g : TRIPLE + g + 1, :] = triple[0:1, g * width : (g + 1) * width]
    out_ref[MIX:UP, :] = plain[MIX:UP, :width]
    for n in range(plan.narrow):
        out_ref[UP + n : UP + n + 1, :] = up[n, 0:1, :width]
    row = UP + plan.narrow
    out_ref[row : row + 1, :] = down[row - 8 : row - 7, :width]


def pack_vectors(plan, core, width, bias_own, bias_other, first_ref, second_ref, cot_ref, up_own,
                 up_other, out_ref):
    out_ref[...] = jnp.zeros_like(out_ref)
    half = width // 2
    for h, ref in ((0, bias_own), (1, bias_other)):
        at = pl.ds(pl.multiple_of((core ^ h) * half, 128), half)
        for g in range(3):
            out_ref[TRIPLE + g : TRIPLE + g + 1, at] = ref[:, g * half : (g + 1) * half]
    out_ref[MIX : MIX + 1, :width] = first_ref[2:3, :]
    out_ref[GAIN1 : GAIN1 + 2, :width] = first_ref[0:2, :]
    out_ref[GAIN2 : GAIN2 + 1, :width] = second_ref[0:1, :]
    out_ref[SHIFT2 : SHIFT2 + 1, :width] = cot_ref[...]
    for h, up_ref in ((0, up_own), (1, up_other)):
        for y in range(plan.narrow // 2):
            row = up_ref[:, y * width : (y + 1) * width]
            out_ref[pl.ds(UP + 2 * y + (core ^ h), 1), :width] = row
    out_ref[UP + plan.narrow : UP + plan.narrow + 1, :width] = second_ref[1:2, :]


def attention_kernel(plan, rows, h, table, x_ref, a, b, c, d, cos_ref, sin_ref, vec_ref,
                     keep_ref, probs_ref, context_ref, triple):
    core, live = plan.core(table), plan.live(table)
    tokens, width = x_ref.shape
    half = width // 2
    place_attention(plan, table, h, (a, b, c, d), triple, None, rows)
    x = x_ref[...]
    cos, sin = cos_ref[...], sin_ref[...]
    left = first_half(tokens)
    valid = lax.broadcasted_iota(jnp.int32, (1, tokens), 1) < live
    scale = jnp.asarray(1.0 / math.sqrt(HD), BF)
    for q in range(half // 128):
        at = [slice(g * half + 128 * q, g * half + 128 * q + 128) for g in range(3)]
        here = pl.ds(pl.multiple_of((core ^ h) * half + 128 * q, 128), 128)
        out = [
            nn(x, triple[:, s]) + vec_ref[TRIPLE + g : TRIPLE + g + 1, here]
            for g, s in enumerate(at)
        ]
        query, key = [(v * cos + swap_lanes(v) * sin).astype(BF) for v in out[:2]]
        value = out[2].astype(BF)
        for s, v in zip(at, (query, key, value)):
            keep_ref[:, s] = v
        context = []
        for e in (0, 1):
            mine = left if e == 0 else ~left
            masked = jnp.where(mine, query, jnp.zeros_like(query)) * scale
            score = jnp.where(valid, nt(masked, key), -1e30)
            power = jnp.exp(score - jnp.max(score, -1, keepdims=True))
            prob = power * (1.0 / jnp.sum(power, -1, keepdims=True))
            prob = prob.astype(BF)
            probs_ref[2 * q + e] = prob
            context.append(nn(prob, value))
        context_ref[:, 128 * q : 128 * q + 128] = (
            jnp.where(left, context[0], context[1]).astype(BF)
        )


def mix_kernel(plan, rows, table, x_ref, context_own, context_other, a, b, c, d, e, f, g, k,
               vec_ref, unit_ref, inv_ref, low_ref, mix):
    core = plan.core(table)
    half = context_own.shape[1]
    for h, pieces in ((0, (a, b, c, d)), (1, (e, f, g, k))):
        place_attention(plan, table, h, pieces, None, mix, rows)
    sides = []
    for side in (0, 1):
        total = 0.0
        for h, context in ((0, context_own), (1, context_other)):
            at = pl.ds(pl.multiple_of((core ^ h) * half, 128), half)
            total = total + nn(context[...], mix[side, at, :])
        sides.append(total)
    branch = jnp.concatenate(sides, 1)
    summed = x_ref[...].astype(F32) + (branch + vec_ref[MIX : MIX + 1, :])
    centred = summed - mean(summed)
    inverse = lax.rsqrt(mean(centred * centred) + EPSILON)
    unit = centred * inverse
    unit_ref[...] = unit
    inv_ref[...] = jnp.broadcast_to(inverse, inv_ref.shape)
    low_ref[...] = (
        unit * vec_ref[GAIN1 : GAIN1 + 1, :] + vec_ref[SHIFT1 : SHIFT1 + 1, :]
    ).astype(BF)


def up_kernel(plan, route, rows, columns, table, low_ref, a, b, c, d, e, f, g, k, vec_ref,
              own_ref, other_ref, slope_own_ref, slope_other_ref, weight):
    core = plan.core(table)
    low = low_ref[...]
    step = 256
    for h, (out, slope) in enumerate(((own_ref, slope_own_ref), (other_ref, slope_other_ref))):
        place_hidden(plan, route, table, h, ((a, b, c, d), (e, f, g, k))[h], weight.at[h], rows, columns)
        for n in range(out.shape[1] // step):
            s = slice(n * step, (n + 1) * step)
            y, at = divmod(n * step, columns)
            row = vec_ref[pl.ds(UP + 2 * y + (core ^ h), 1), at : at + step]
            up = nn(low, weight[h, :, s]) + row
            share = 0.5 * (1.0 + lax.erf(up * math.sqrt(0.5)))
            out[:, s] = (up * share).astype(BF)
            slope[:, s] = (
                share + up * jnp.exp(-0.5 * up * up) * (1.0 / math.sqrt(2.0 * math.pi))
            ).astype(BF)


def down_own_kernel(plan, route, rows, columns, table, act, a, b, unit_ref, cot_ref, vec_ref,
                    out_ref, mean_ref, sum_ref, weight):
    place_hidden(plan, route, table, 0, (a, b), weight, rows, columns)
    first = unit_ref[...] * vec_ref[GAIN1 : GAIN1 + 1, :] + vec_ref[SHIFT1 : SHIFT1 + 1, :]
    bias = vec_ref[UP + plan.narrow : UP + plan.narrow + 1, :]
    out_ref[...] = first + (nt(act[...], weight[...]) + bias)
    cot = cot_ref[...].astype(F32)
    sum_ref[...] = jnp.sum(cot, 0, keepdims=True)
    scaled_mean = mean(cot * vec_ref[GAIN2 : GAIN2 + 1, :])
    mean_ref[...] = jnp.broadcast_to(scaled_mean, mean_ref.shape)


def down_kernel(plan, route, rows, columns, table, part_ref, act, a, b, mean_ref,
                cot_ref, vec_ref, out_ref, grad_ref, grad_low_ref, sums_ref, weight):
    place_hidden(plan, route, table, 1, (a, b), weight, rows, columns)
    summed = part_ref[...] + nt(act[...], weight[...])
    cot = cot_ref[...].astype(F32)
    scaled = cot * vec_ref[GAIN2 : GAIN2 + 1, :]
    centred = summed - mean(summed)
    inverse = lax.rsqrt(mean(centred * centred) + EPSILON)
    unit = centred * inverse
    grad = inverse * (scaled - mean_ref[:, 0:1] - unit * mean(scaled * unit))
    grad_ref[...] = grad
    low = grad.astype(BF)
    grad_low_ref[...] = low
    sums_ref[0:1, :] = jnp.sum(cot * unit, 0, keepdims=True)
    sums_ref[1:2, :] = jnp.sum(low.astype(F32), 0, keepdims=True)
    out_ref[...] = (
        unit * vec_ref[GAIN2 : GAIN2 + 1, :] + vec_ref[SHIFT2 : SHIFT2 + 1, :]
    ).astype(BF)


def grad_up_kernel(plan, route, h, rows, columns, table, low_ref, a, b, slope, out, sums_ref,
                   weight):
    place_hidden(plan, route, table, h, (a, b), weight, rows, columns)
    low = low_ref[...]
    step = 256
    for n in range(out.shape[1] // step):
        s = slice(n * step, (n + 1) * step)
        grad = (nn(low, weight[:, s]) * slope[:, s].astype(F32)).astype(BF)
        out[:, s] = grad
        sums_ref[:, s] = jnp.sum(grad.astype(F32), 0, keepdims=True)


def hidden_grad_kernel(plan, route, rows, columns, table, left_own, left_other, right_own,
                       right_other, low_ref, high_ref, block):
    across, half_slots = plan.narrow // 2, plan.slots // 2
    a, b = left_own[...], left_other[...]
    for y in range(across):
        s = slice(y * columns, (y + 1) * columns)
        tile = tn(a, right_own[:, s]) + tn(b, right_other[:, s])
        block[:, y] = tile.astype(BF).reshape(plan.wide, rows, columns)
    for r in reversed(range(plan.slots)):
        chip = plan.chip(table, route, 0, r)
        out = (low_ref, high_ref)[r // half_slots]
        out[r % half_slots] = block[chip // across, chip % across]


def hidden_part_kernel(plan, route, part, rows, columns, table, left_own, left_other, right_own,
                       right_other, out_ref, block, lefts, some):
    across, half_slots = plan.narrow // 2, plan.slots // 2
    core = plan.core(table)
    here = plan.chip(table, route, 0, 0)
    lefts[0] = left_own[...].T
    lefts[1] = left_other[...].T

    @pl.when(core == 0)
    def _():
        y = (here % across) ^ part
        s = pl.ds(pl.multiple_of(y * columns, 128), columns)
        tile = nn(lefts[0], right_own[:, s]) + nn(lefts[1], right_other[:, s])
        block[:, pl.ds(y, 1)] = tile.astype(BF).reshape(plan.wide, 1, rows, columns)

    @pl.when(core == 1)
    def _():
        x = (here // across % 2) ^ part
        for z in range(plan.far):
            at = pl.ds(pl.multiple_of((2 * z + x) * rows, 16), rows)
            for k in (0, 1):
                some[k, z * rows : (z + 1) * rows, :] = lefts[k, at, :]
        tile = nn(some[0], right_own[...]) + nn(some[1], right_other[...])
        for z in range(plan.far):
            for y in range(across):
                block[2 * z + x, y] = tile[
                    z * rows : (z + 1) * rows, y * columns : (y + 1) * columns
                ].astype(BF)

    for r in range(half_slots):
        chip = plan.chip(table, route, 0, part * half_slots + r)
        out_ref[r] = block[chip // across, chip % across]


def first_grad_kernel(plan, route, rows, columns, arows, table, gu_own, gu_other, a, b, c, d,
                      e, f, g, k, p, q, r, s, l, m, n, o, grad_ref, unit_ref, inv_ref, vec_ref, middle_ref,
                      mine_ref, theirs_ref, context_ref, sums_ref, weight, mix, low_ref):
    for h in (0, 1):
        place_hidden(plan, route, table, h, ((a, b, c, d), (e, f, g, k))[h], weight.at[h], rows, columns)
    width = unit_ref.shape[1]
    half = width // 2
    for h, pieces in ((0, (p, q, r, s)), (1, (l, m, n, o))):
        place_attention(plan, table, h, pieces, None, mix, arows)
    core = plan.core(table)
    total = nt(gu_own[...], weight[0])
    total = total + nt(gu_other[...], weight[1])
    grad = grad_ref[...] + total
    unit = unit_ref[...]
    scaled = grad * vec_ref[GAIN1 : GAIN1 + 1, :]
    middle = inv_ref[:, 0:1] * (scaled - mean(scaled) - unit * mean(scaled * unit))
    low = middle.astype(BF)
    middle_ref[...] = middle
    low_ref[...] = low
    mine_ref[...] = low_ref[:, pl.ds(pl.multiple_of(core * half, 128), half)]
    theirs_ref[...] = low_ref[:, pl.ds(pl.multiple_of((core ^ 1) * half, 128), half)]
    sums_ref[0:1, :] = jnp.sum(grad * unit, 0, keepdims=True)
    sums_ref[1:2, :] = jnp.sum(grad, 0, keepdims=True)
    sums_ref[2:3, :] = jnp.sum(low.astype(F32), 0, keepdims=True)
    context_ref[...] = (nt(low[:, :half], mix[0]) + nt(low[:, half:], mix[1])).astype(BF)


def attention_grad_kernel(plan, h, table, keep_ref, probs_ref, grad_ref, cos_ref, sin_ref,
                          out_ref, sums_ref):
    core = plan.core(table)
    tokens, width = grad_ref.shape
    half = width // 2
    cos, sin = cos_ref[...], sin_ref[...]
    left = first_half(tokens)
    scale = 1.0 / math.sqrt(HD)
    keep, grads_in, probs = keep_ref, grad_ref, probs_ref
    for q in range(half // 128):
        at = [slice(g * half + 128 * q, g * half + 128 * q + 128) for g in range(3)]
        query, key, value = [keep[:, s] for s in at]
        came = grads_in[:, pl.ds(pl.multiple_of((core ^ h) * half + 128 * q, 128), 128)]
        parts = []
        for e in (0, 1):
            mine = left if e == 0 else ~left
            low = probs[2 * q + e]
            prob = low.astype(F32)
            grad = nt(jnp.where(mine, came, jnp.zeros_like(came)), value)
            score = prob * (grad - jnp.sum(prob * grad, -1, keepdims=True))
            score = score.astype(BF)
            parts.append((nn(score, key), tn(score, query), tn(low, came)))
        grads = [jnp.where(left, u, v) for u, v in zip(*parts)]
        grads = [(g * scale) * cos + swap_lanes((g * scale) * sin) for g in grads[:2]] + grads[2:]
        for s, g in zip(at, grads):
            g = g.astype(BF)
            out_ref[:, s] = g
            sums_ref[:, s] = jnp.sum(g.astype(F32), 0, keepdims=True)


def attention_weight_kernel(plan, rows, table, x_own, x_other, g_own, g_other, c_own, c_other,
                            c_came_own, c_came_other, b_own, b_other, bias_own, bias_other,
                            first_ref, second_ref, cot_ref, up_own, up_other, low_one, low_rest,
                            low_away, high_one, high_rest, high_away, block, mixed, sums):
    core = plan.core(table)
    half_slots = plan.slots // 2
    tokens, columns = g_own.shape
    third = columns // 3
    height = rows + rows // 3
    pack_vectors(plan, core, x_own.shape[1], bias_own, bias_other, first_ref, second_ref, cot_ref,
                 up_own, up_other, sums)
    far = plan.far
    for ref in (low_away, high_away):
        ref[far * height :, :] = sums[...].astype(BF)
    block[...] = (
        (tn(x_own[...], g_own[...]) + tn(x_other[...], g_other[...]))
        .astype(BF)
        .reshape(block.shape)
    )
    for h, mine, came in ((0, c_own, c_came_other), (1, c_other, c_came_own)):
        mixed[pl.ds((core ^ h) * half_slots, half_slots)] = (
            (tn(mine[...], b_own[...]) + tn(came[...], b_other[...]))
            .astype(BF)
            .reshape((half_slots,) + mixed.shape[1:])
        )
    for r in reversed(range(plan.slots)):
        chip = plan.chip(table, plan.far_first, 0, r)
        side, slot = divmod(r, half_slots)
        one, rest, away = ((low_one, low_rest, low_away), (high_one, high_rest, high_away))[side]
        if slot == 0:
            out, at = one, 0
        elif slot < far:
            out, at = rest, (slot - 1) * height
        else:
            out, at = away, (slot - far) * height
        out[at : at + rows, :] = block[chip]
        for b in range(3):
            out[at + rows : at + height, b * third : (b + 1) * third] = mixed[chip, b]


def input_grad_kernel(plan, rows, table, middle_ref, g_own, g_other, a, b, c, d, e, f, g, k,
                      out_ref, triple):
    for h, pieces in ((0, (a, b, c, d)), (1, (e, f, g, k))):
        place_attention(plan, table, h, pieces, triple.at[h], None, rows)
    total = nt(g_own[...], triple[0])
    total = total + nt(g_other[...], triple[1])
    out_ref[...] = (middle_ref[...] + total).astype(BF)


def total_kernel(plan, rows, table, one, sums, a, b, c, mine_ref, theirs_ref, both):
    core = plan.core(table)
    total = jnp.concatenate([one[...], sums[...].astype(F32)], 0)
    for ref in (a, b, c):
        total = total + ref[...].astype(F32)
    third, half = rows // 3, total.shape[1] // 3
    width = 2 * half
    both[:, : 3 * half] = total[:rows]
    for k in range(3):
        both[k * third : (k + 1) * third, 3 * half :] = (
            total[rows : rows + third, k * half : (k + 1) * half]
        )
    piece = rows // 2
    mine_ref[:piece, :] = both[pl.ds(pl.multiple_of(core * piece, 8), piece), :]
    theirs_ref[:piece, :] = both[pl.ds(pl.multiple_of((core ^ 1) * piece, 8), piece), :]
    for ref in (mine_ref, theirs_ref):
        ref[piece:, :width] = total[rows + third :, :width]


def share_kernel(plan, table, index_ref, mine_ref, came_ref, triple_ref, mix_ref, tb_ref, mb_ref,
                 g1_ref, s1_ref, ub_ref, db_ref, g2_ref, s2_ref):
    core, index = plan.core(table), index_ref[0]
    piece, width = mix_ref.shape
    half = width // 2
    for ref, h in ((mine_ref, core), (came_ref, core ^ 1)):
        for g in range(3):
            at = pl.ds(pl.multiple_of(g * width + h * half, 128), half)
            triple_ref[:, at] = ref[:piece, g * half : (g + 1) * half]
        mix_ref[:, pl.ds(pl.multiple_of(h * half, 128), half)] = ref[:piece, 3 * half : 4 * half]
    sums = mine_ref[piece:, :width] + came_ref[piece:, :width]
    biases = jnp.concatenate([sums[g : g + 1, :] for g in range(3)], 1)
    biases = jnp.broadcast_to(biases, (8, 3 * width))
    tb_ref[...] = pltpu.roll(biases, (3 * width - index * 3 * piece) % (3 * width), 1)[
        0:1, : 3 * piece
    ]
    rolled = pltpu.roll(sums[:8], (width - index * piece) % width, 1)
    for row, ref in ((MIX, mb_ref), (GAIN1, g1_ref), (SHIFT1, s1_ref), (GAIN2, g2_ref),
                     (SHIFT2, s2_ref)):
        ref[...] = rolled[row : row + 1, :piece]
    of_wide, of_narrow = index // plan.narrow, index % plan.narrow
    mine = sums[UP : UP + 1, :]
    for n in range(1, plan.narrow):
        mine = jnp.where(of_narrow == n, sums[UP + n : UP + n + 1, :], mine)
    ub_ref[...] = mine
    count = db_ref.shape[1]
    rolled = pltpu.roll(sums[8:], (width - of_wide * count) % width, 1)
    row = UP + plan.narrow - 8
    db_ref[...] = rolled[row : row + 1, :count]


def half_tables(tokens):
    position = jnp.arange(tokens, dtype=F32)
    column = jnp.arange(2 * HD, dtype=jnp.int32)
    pair = (column % HD // 2).astype(F32)
    angle = position[:, None] * jnp.exp(pair * (-2.0 / HD) * math.log(10000.0))[None, :]
    parity = (column % 2).astype(F32) * 2.0 - 1.0
    return jnp.cos(angle), jnp.sin(angle) * parity[None, :]


def fast_body(
    plan,
    inputs,
    lengths,
    triple_weight,
    triple_bias,
    mix_weight,
    mix_bias,
    first_gain,
    first_shift,
    up_weight,
    up_bias,
    down_weight,
    down_bias,
    second_gain,
    second_shift,
    cotangent,
):
    tokens, width = inputs.shape
    half = width // 2
    wide, narrow = plan.wide, plan.narrow
    index = lax.axis_index(AXES)
    core = index & 1
    of_wide = lax.axis_index("wide")
    table = plan.table(index, lengths)
    hidden = up_weight.shape[1]
    tile_rows = up_weight.shape[0]
    piece = triple_weight.shape[0]
    rows = 2 * piece
    third = rows // 3
    half_slots = plan.slots // 2
    far_first, far_second = plan.far_first, plan.far_second
    flops = 2.0 * tokens * width * width
    hidden_half = hidden * narrow // 2

    place = index.astype(jnp.int32)[None]
    mine, theirs = call(
        split_kernel,
        [shape((piece, 4 * half))] * 2,
        (place, triple_weight, mix_weight),
        "svv",
        [],
        0,
        16,
    )
    first, rest = call(
        join_kernel,
        [shape((1, 2 * third, 3 * half)), shape((2 * third, 3 * half))],
        (place, mine, plan.swap(theirs)),
        "svv",
        [],
        0,
        16,
    )
    row = functools.partial(jnp.reshape, shape=(1, -1))
    up_share = lax.dynamic_slice(up_bias, (of_wide * (hidden // wide),), (hidden // wide,))
    (share,) = call(
        functools.partial(spread_kernel, plan),
        [shape((TABLE_ROWS, SHARE))],
        (
            after(place, first),
            row(triple_bias),
            row(mix_bias),
            row(first_gain),
            row(first_shift),
            row(second_gain),
            row(second_shift),
            row(up_share),
            row(down_bias),
        ),
        "s" + 8 * "l",
        [VMEM((TABLE_ROWS, SHARE), F32)],
        0,
        60,
    )
    (second,) = call(
        beside_kernel,
        [shape((1, 2 * third, 3 * half + SHARE))],
        (place, rest, share, plan.swap(share)),
        "svvv",
        [],
        0,
        16,
    )
    cat = functools.partial(jnp.concatenate, axis=0)
    cos, sin = half_tables(tokens)
    inputs_came = plan.swap(after(inputs, first))
    down = after(down_weight.T[None], first)
    down_came = plan.send(down, far_second, 1)
    first = cat(after_all(plan.gather_far(first), inputs_came, second))
    first_came = plan.permute(first, plan.first)
    second = plan.gather_far(after(second, first))
    up = after(up_weight[None], first)
    up_came = plan.send(up, far_first, 1)
    first, first_came = after_all((first, first_came))
    first = cat((first, first_came))
    first_came = plan.permute(first, plan.last)
    second = cat(after_all(second, first))
    second_came = plan.permute(second, plan.first)
    down = cat(after_all((down, down_came), first))
    down_came = plan.send(down, far_second, 2)
    up = cat(after_all((up, up_came), down))
    up_came = plan.send(up, far_first, 2)
    second, second_came = after_all((second, second_came), up)
    second = cat((second, second_came))
    first, first_came = after_all((first, first_came), second)
    second_came = plan.permute(second, plan.last)
    up = cat(after_all((up, up_came), first_came))
    up_came = plan.permute(up, plan.first)
    ups = [up, up_came, plan.permute(up, plan.last)]
    down = cat(after_all((down, down_came), up))
    down_came = plan.send(down, far_second, 4)
    second, second_came = after_all((second, second_came), down)
    att_own = [first, first_came, second, second_came]
    att_other = [plan.swap(v) for v in att_own]
    (vecs,) = call(
        functools.partial(vectors_kernel, plan, piece),
        [shape((TABLE_ROWS, width), F32)],
        (table, *att_own[2:]),
        "svv",
        [
            VMEM((plan.slots, 2 * third, SHARE), BF),
            VMEM((8, 3 * width + 2 * SHARE), F32),
            VMEM((8, width + 2 * SHARE), F32),
            VMEM((narrow, 8, width + 2 * SHARE), F32),
            VMEM((8, width + 2 * SHARE), F32),
        ],
        0,
        32,
    )

    def attend(h, pieces, gate=()):
        return call(
            functools.partial(attention_kernel, plan, rows, h),
            [
                shape((tokens, 3 * half)),
                shape((half // HD, tokens, tokens)),
                shape((tokens, half)),
            ],
            (after(table, *gate), inputs, *pieces, cos, sin, vecs),
            "s" + 8 * "v",
            [VMEM((width, 3 * half), BF)],
            80 * flops,
            24,
        )

    own, p_own, context_own = attend(0, att_own, (second_came, *att_other[:2]))
    (up_came,) = after_all((ups[1],), context_own)
    ups = [ups[0], up_came, ups[2], plan.permute(up_came, plan.last)]
    down = cat(after_all((down, down_came), up_came))
    downs = [down, plan.permute(down, plan.last)]
    other, p_other, context_other = attend(1, att_other, (down,))
    unit, inv, low = call(
        functools.partial(mix_kernel, plan, rows),
        [shape((tokens, width), F32), shape((tokens, 128), F32), shape((tokens, width))],
        (table, inputs, context_own, context_other, *att_own, *att_other, vecs),
        "s" + 12 * "v",
        [VMEM((2, width, half), BF)],
        1,
        24,
    )
    hidden_scratch = [VMEM((2, width, hidden_half), BF)]
    ups = [*ups, *(plan.swap(v) for v in ups)]
    down_low_came = plan.swap(downs[0])
    context_came = plan.swap(context_own), plan.swap(context_other)
    act_own, act_other, slope_own, slope_other = call(
        functools.partial(up_kernel, plan, far_first, tile_rows, hidden),
        [shape((tokens, hidden_half))] * 4,
        (table, low, *ups, vecs),
        "s" + 10 * "v",
        hidden_scratch,
        1,
        24,
    )
    (down_high,) = after_all(downs[1:], act_own)
    downs = [downs[0], down_high, down_low_came, plan.swap(down_high)]
    low_came, act_came = plan.swap(low), plan.swap(act_other)
    half_scratch = [VMEM((width, hidden_half), BF)]
    downward, scaled_mean, cot_sum = call(
        functools.partial(down_own_kernel, plan, far_second, tile_rows, hidden),
        [shape((tokens, width), F32), shape((tokens, 128), F32), shape((1, width), F32)],
        (after(table, *context_came), act_own, *downs[:2], unit, cotangent, vecs),
        "s" + 6 * "v",
        half_scratch,
        80 * flops,
        24,
    )
    outputs, grad_second, grad_down, sums_second = call(
        functools.partial(down_kernel, plan, far_second, tile_rows, hidden),
        [
            shape((tokens, width)),
            shape((tokens, width), F32),
            shape((tokens, width)),
            shape((2, width), F32),
        ],
        (table, downward, act_other, *downs[2:], scaled_mean, cotangent, vecs),
        "s" + 7 * "v",
        half_scratch,
        1,
        24,
    )
    grad_down_came = plan.swap(grad_down)

    def grad_up(h, pieces, slope, gate=()):
        return call(
            functools.partial(grad_up_kernel, plan, far_second, h, tile_rows, hidden),
            [shape((tokens, hidden_half)), shape((1, hidden_half), F32)],
            (after(table, *gate), grad_down, *pieces, slope),
            "s" + 4 * "v",
            half_scratch,
            1,
            24,
        )

    gu_other, sums_up_other = grad_up(1, downs[2:], slope_other)
    gu_came = plan.swap(gu_other)

    def hidden_grad(route, left, left_came, right, right_came, cost, gate):
        return call(
            functools.partial(hidden_grad_kernel, plan, route, tile_rows, hidden),
            [shape((half_slots, tile_rows, hidden))] * 2,
            (after(table, *gate), left, left_came, right, right_came),
            "svvvv",
            [VMEM((wide, narrow // 2, tile_rows, hidden), BF)],
            cost,
            24,
        )

    def down_grad(part, gate):
        (tiles,) = call(
            functools.partial(hidden_part_kernel, plan, far_second, part, tile_rows, hidden),
            [shape((half_slots, tile_rows, hidden))],
            (after(table, *gate), grad_down, grad_down_came, act_own, act_came),
            "svvvv",
            [
                VMEM((wide, narrow // 2, tile_rows, hidden), BF),
                VMEM((2, width, tokens), BF),
                VMEM((2, width // 2, tokens), BF),
            ],
            80 * flops if part else 1,
            24,
        )
        return tiles

    down_high = down_grad(1, (sums_up_other,))
    down_came = plan.permute(down_high, plan.last)
    gu_own, sums_up_own = grad_up(0, downs[:2], slope_own, (down_high,))
    down_low = down_grad(0, (sums_up_own,))
    up_low, up_high = hidden_grad(far_first, low, low_came, gu_own, gu_came, 1, (down_low,))
    up_came = plan.permute(up_high, plan.last)
    grad_middle, branch_mine, branch_theirs, grad_context, sums_first = call(
        functools.partial(first_grad_kernel, plan, far_first, tile_rows, hidden, rows),
        [
            shape((tokens, width), F32),
            shape((tokens, half)),
            shape((tokens, half)),
            shape((tokens, width)),
            shape((3, width), F32),
        ],
        (
            after(table, up_low),
            gu_own,
            gu_other,
            *ups,
            *att_own,
            *att_other,
            grad_second,
            unit,
            inv,
            vecs,
        ),
        "s" + 22 * "v",
        hidden_scratch
        + [VMEM((2, width, half), BF), VMEM((tokens, width), BF)],
        1,
        24,
    )
    branch_came = plan.swap(branch_theirs)

    def attention_grad(h, keep, probs, gate=()):
        return call(
            functools.partial(attention_grad_kernel, plan, h),
            [shape((tokens, 3 * half)), shape((1, 3 * half), F32)],
            (after(table, *gate), keep, probs, grad_context, cos, sin),
            "svvvvv",
            [],
            1,
            24,
        )

    gt_other, bias_other = attention_grad(1, other, p_other, (act_came,))
    gt_came = plan.swap(gt_other)
    down_stay, down_away = halves(*after_all((down_low, down_came), bias_other))
    down_came = plan.send(down_away, far_second, 4)
    gt_own, bias_own = attention_grad(0, own, p_own, (down_away,))
    up_stay, up_away = halves(*after_all((up_low, up_came), bias_own))
    up_came = plan.permute(up_away, plan.first)
    height = rows + third
    far = plan.far
    kinds = [shape((k * height + more, 3 * half)) for k, more in ((1, 0), (far - 1, 0), (far, TABLE_ROWS))]
    low_one, low_rest, low_away, high_one, high_rest, high_away = call(
        functools.partial(attention_weight_kernel, plan, rows),
        kinds + kinds,
        (
            after(table, up_away),
            inputs,
            inputs_came,
            gt_own,
            gt_came,
            context_own,
            context_other,
            *context_came,
            branch_mine,
            branch_came,
            bias_own,
            bias_other,
            sums_first,
            sums_second,
            cot_sum,
            sums_up_own,
            sums_up_other,
        ),
        "s" + 17 * "v",
        [
            VMEM((plan.slots, rows, 3 * half), BF),
            VMEM((plan.slots, 3, third, half), BF),
            VMEM((TABLE_ROWS, 3 * half), F32),
        ],
        80 * flops,
        24,
    )
    came_away = plan.permute(high_away, plan.last)
    came_rest = plan.permute(high_rest, plan.last)
    came_one = plan.permute(high_one, plan.last)
    down_stay, down_away = halves(*after_all((down_stay, down_came), low_away))
    down_came = plan.send(down_away, far_second, 2)
    up_stay, up_away = halves(*after_all((up_stay, up_came), down_away))
    up_came = plan.send(up_away, far_first, 2)
    (input_grad,) = call(
        functools.partial(input_grad_kernel, plan, rows),
        [shape((tokens, width))],
        (after(table, up_away), grad_middle, gt_own, gt_other, *att_own, *att_other),
        "s" + 11 * "v",
        [VMEM((2, width, 3 * half), BF)],
        80 * flops,
        24,
    )
    low_away, came_away = after_all((low_away, came_away), input_grad)
    away = added(low_away[height:], came_away[height:])
    next_rest = plan.permute(away, plan.first)
    next_one = plan.permute(added(low_away[:height], came_away[:height]), plan.first)
    down_stay, down_came, up_stay, up_came = after_all(
        (down_stay, down_came, up_stay, up_came), away
    )
    down_stay, down_away = halves(down_stay, down_came)
    down_came = plan.send(down_away, far_second, 1)
    up_stay, up_away = halves(up_stay, up_came)
    up_came = plan.send(up_away, far_first, 1)
    end = (far - 1) * height
    (next_rest,) = after_all((next_rest,), down_away, up_away)
    came_one, next_one = after_all((came_one, next_one), next_rest)
    one = low_one.astype(F32) + came_one.astype(F32) + next_one.astype(F32)
    (next_rest,) = after_all((next_rest,), one)
    sums = added(away[end:], next_rest[end:])
    parts = [None]
    for k in range(far - 1):
        part = slice(k * height, (k + 1) * height)
        parts.append(cat([added(low_rest[part], came_rest[part], next_rest[part]), sums]))
    down_stay, down_came, up_stay, up_came = after_all(
        (down_stay, down_came, up_stay, up_came), parts[1]
    )
    down_total = down_stay[0].astype(F32) + down_came[0].astype(F32)
    up_total = up_stay[0].astype(F32) + up_came[0].astype(F32)
    mine, theirs = call(
        functools.partial(total_kernel, plan, rows),
        [shape((piece + TABLE_ROWS, 4 * half), F32)] * 2,
        (
            after(table, down_total, up_total),
            one,
            sums,
            *plan.send_far(parts),
        ),
        "s" + 5 * "v",
        [VMEM((rows, 4 * half), F32)],
        1,
        16,
    )
    one = [3 * piece, piece, piece, piece, hidden, down_bias.shape[0], piece, piece]
    triple_grad, mix_grad, *vectors = call(
        functools.partial(share_kernel, plan),
        [shape((piece, 3 * width), F32), shape((piece, width), F32)]
        + [shape((1, n), F32) for n in one],
        (table, place, mine, plan.swap(theirs)),
        "ssvv",
        [],
        1,
        16,
    )
    vectors = [v.reshape(-1) for v in vectors]
    return (
        outputs,
        input_grad,
        triple_grad,
        vectors[0],
        mix_grad,
        *vectors[1:4],
        up_total,
        vectors[4],
        down_total.T,
        *vectors[5:],
    )


def fits(plan_shape, width, hidden):
    wide, narrow = plan_shape
    powers = all(n >= 4 and n & (n - 1) == 0 for n in (wide, narrow)) and narrow == 4
    return (
        powers
        and width % (wide * 16) == 0
        and width % (wide * narrow // 2 * 48) == 0
        and hidden % (narrow * 128) == 0
        and width % 768 == 0
    )


def solution(mesh):
    placed = (
        P(("wide", "narrow"), None),
        P(("wide", "narrow")),
        P(("wide", "narrow"), None),
        P(("wide", "narrow")),
        P(("wide", "narrow"), None),
        P(("wide", "narrow")),
        P(("wide", "narrow")),
        P(("wide", "narrow")),
        P("wide", "narrow"),
        P("narrow"),
        P("narrow", "wide"),
        P("wide"),
        P(("wide", "narrow")),
        P(("wide", "narrow")),
        P(("wide", "narrow"), None),
    )
    wide, narrow = mesh.shape["wide"], mesh.shape["narrow"]

    def layer(*arrays):
        rows, hidden = arrays[8].shape
        if fits((wide, narrow), rows * wide, hidden * narrow):
            return fast_body(Plan(wide, narrow), *arrays)
        return body(*arrays)

    return jax.shard_map(
        layer,
        mesh=mesh,
        in_specs=placed,
        out_specs=(
            P(("wide", "narrow"), None),
            P(("wide", "narrow"), None),
            P(("wide", "narrow"), None),
            P(("wide", "narrow")),
            P(("wide", "narrow"), None),
            P(("wide", "narrow")),
            P(("wide", "narrow")),
            P(("wide", "narrow")),
            P("wide", "narrow"),
            P("narrow"),
            P("narrow", "wide"),
            P("wide"),
            P(("wide", "narrow")),
            P(("wide", "narrow")),
        ),
        check_vma=False,
    )
```

```python
import functools
import math

import jax
import jax.numpy as jnp
import numpy as np
from jax import lax
from jax.experimental import pallas as pl
from jax.experimental.pallas import tpu as pltpu
from jax.sharding import PartitionSpec as P

H = 12
HD = 64


EPSILON = 1e-06


def tables(token_rows, width, head):
    position = jnp.arange(token_rows, dtype=jnp.float32)
    column = jnp.arange(width, dtype=jnp.int32)
    pair_index = (column % head // 2).astype(jnp.float32)
    frequency = jnp.exp(pair_index * (-2.0 / head) * math.log(10000.0))
    angle = position[:, None] * frequency[None, :]
    parity = (column % 2).astype(jnp.float32) * 2.0 - 1.0
    return (jnp.cos(angle), jnp.sin(angle) * parity[None, :])


def swapped(values):
    shape = values.shape
    paired = values.reshape(shape[:-1] + (shape[-1] // 2, 2))
    return paired[..., ::-1].reshape(shape)


def rotate(values, cosine, sine):
    return values * cosine + swapped(values) * sine


def unrotate(grad, cosine, sine):
    return grad * cosine + swapped(grad * sine)


def normalize_forward(values, gain, shift):
    mean_row = jnp.mean(values, -1, keepdims=True)
    centred = values - mean_row
    inverse = lax.rsqrt(jnp.mean(centred * centred, -1, keepdims=True) + EPSILON)
    unit = centred * inverse
    return (unit * gain + shift, unit, inverse)


def normalize_backward(grad, unit, inverse, gain):
    scaled = grad * gain
    inner = (
        scaled
        - jnp.mean(scaled, -1, keepdims=True)
        - unit * jnp.mean(scaled * unit, -1, keepdims=True)
    )
    return (inner * inverse, jnp.sum(grad * unit, 0), jnp.sum(grad, 0))


def gelu_exact(values):
    return jax.nn.gelu(values, approximate=False)


def gelu_backward(upward, grad_active):
    unused, pull_back = jax.vjp(gelu_exact, upward)
    return pull_back(grad_active)[0]


def softmax_block(query_block, key, valid, scale):
    scores = (
        jnp.einsum("qhd,khd->hqk", query_block, key, preferred_element_type=jnp.float32) * scale
    )
    scores = jnp.where(valid[None, None, :], scores, -1e30)
    return jax.nn.softmax(scores, axis=-1)


def attention_forward(query, key, value, valid, scale):
    token_rows = query.shape[0]
    block = min(512, token_rows)
    weights_block = softmax_block(query, key, valid, scale)
    context = jnp.einsum(
        "hqk,khd->qhd",
        weights_block.astype(jnp.bfloat16),
        value,
        preferred_element_type=jnp.float32,
    )
    pieces = context.reshape(block, -1).astype(jnp.bfloat16)
    return pieces


def attention_backward(query, key, value, grad_context, valid, scale):
    weights_block = softmax_block(query, key, valid, scale)
    grad_weights = jnp.einsum(
        "qhd,khd->hqk", grad_context, value, preferred_element_type=jnp.float32
    )
    inner = weights_block * (
        grad_weights - jnp.sum(weights_block * grad_weights, -1, keepdims=True)
    )
    inner_low = inner.astype(jnp.bfloat16)
    query_pieces = (
        jnp.einsum("hqk,khd->qhd", inner_low, key, preferred_element_type=jnp.float32) * scale
    )
    grad_key = (
        jnp.einsum("hqk,qhd->khd", inner_low, query, preferred_element_type=jnp.float32) * scale
    )
    grad_value = jnp.einsum(
        "hqk,qhd->khd",
        weights_block.astype(jnp.bfloat16),
        grad_context,
        preferred_element_type=jnp.float32,
    )
    return (query_pieces, grad_key, grad_value)


def body(
    inputs,
    lengths,
    triple_weight,
    triple_bias,
    mix_weight,
    mix_bias,
    first_gain,
    first_shift,
    up_weight,
    up_bias,
    down_weight,
    down_bias,
    second_gain,
    second_shift,
    cotangent,
):
    token_rows, width = inputs.shape
    scale = 1.0 / math.sqrt(HD)
    head_shape = (token_rows, H, HD)
    (
        triple_full,
        mix_full,
        triple_bias_full,
        mix_bias_full,
        gain_one,
        shift_one,
        gain_two,
        shift_two,
    ) = (
        lax.all_gather(triple_weight, ("wide", "narrow"), axis=0, tiled=True),
        lax.all_gather(mix_weight, ("wide", "narrow"), axis=0, tiled=True),
        lax.all_gather(triple_bias, ("wide", "narrow"), axis=0, tiled=True),
        lax.all_gather(mix_bias, ("wide", "narrow"), axis=0, tiled=True),
        lax.all_gather(first_gain, ("wide", "narrow"), axis=0, tiled=True),
        lax.all_gather(first_shift, ("wide", "narrow"), axis=0, tiled=True),
        lax.all_gather(second_gain, ("wide", "narrow"), axis=0, tiled=True),
        lax.all_gather(second_shift, ("wide", "narrow"), axis=0, tiled=True),
    )
    up_rows, down_columns, down_bias_full = (
        lax.all_gather(up_weight, "wide", axis=0, tiled=True),
        lax.all_gather(down_weight, "wide", axis=1, tiled=True),
        lax.all_gather(down_bias, "wide", axis=0, tiled=True),
    )
    gain_one = gain_one.astype(jnp.float32)
    gain_two = gain_two.astype(jnp.float32)
    cosine, sine = tables(token_rows, width, HD)
    valid = jnp.arange(token_rows, dtype=jnp.int32) < lengths[0]
    triple = jnp.dot(
        inputs, triple_full, preferred_element_type=jnp.float32
    ) + triple_bias_full.astype(jnp.float32)
    query = rotate(triple[:, :width], cosine, sine).astype(jnp.bfloat16).reshape(head_shape)
    key = (
        rotate(triple[:, width : 2 * width], cosine, sine).astype(jnp.bfloat16).reshape(head_shape)
    )
    value = triple[:, 2 * width :].astype(jnp.bfloat16).reshape(head_shape)
    context = attention_forward(query, key, value, valid, scale)
    branch = jnp.dot(context, mix_full, preferred_element_type=jnp.float32) + mix_bias_full.astype(
        jnp.float32
    )
    first, first_unit, first_inverse = normalize_forward(
        inputs.astype(jnp.float32) + branch, gain_one, shift_one.astype(jnp.float32)
    )
    first_low = first.astype(jnp.bfloat16)
    gathered = lax.all_gather(first_low, "narrow", axis=0, tiled=True)
    upward = jnp.dot(gathered, up_rows, preferred_element_type=jnp.float32) + up_bias.astype(
        jnp.float32
    )
    active = gelu_exact(upward).astype(jnp.bfloat16)
    downward = lax.psum_scatter(
        jnp.dot(active, down_columns, preferred_element_type=jnp.float32).astype(jnp.bfloat16),
        "narrow",
        scatter_dimension=0,
        tiled=True,
    ).astype(jnp.float32)
    downward = downward + down_bias_full.astype(jnp.float32)
    result, second_unit, second_inverse = normalize_forward(
        first + downward, gain_two, shift_two.astype(jnp.float32)
    )
    outputs = result.astype(jnp.bfloat16)
    grad_second, second_gain_grad, second_shift_grad = normalize_backward(
        cotangent.astype(jnp.float32), second_unit, second_inverse, gain_two
    )
    grad_down = grad_second.astype(jnp.bfloat16)
    grad_gathered = lax.all_gather(grad_down, "narrow", axis=0, tiled=True)
    grad_active = jnp.dot(grad_gathered, down_columns.T, preferred_element_type=jnp.float32)
    grad_up = gelu_backward(upward, grad_active).astype(jnp.bfloat16)
    grad_feed = lax.psum_scatter(
        jnp.dot(grad_up, up_rows.T, preferred_element_type=jnp.float32).astype(jnp.bfloat16),
        "narrow",
        scatter_dimension=0,
        tiled=True,
    ).astype(jnp.float32)
    up_part = jnp.dot(gathered.T, grad_up, preferred_element_type=jnp.float32)
    down_part = jnp.dot(active.T, grad_gathered, preferred_element_type=jnp.float32)
    down_bias_part = jnp.sum(grad_gathered, 0, dtype=jnp.float32)
    up_weight_grad, down_weight_grad, down_bias_grad = (
        lax.psum_scatter(
            up_part.astype(jnp.bfloat16), "wide", scatter_dimension=0, tiled=True
        ).astype(jnp.float32),
        lax.psum_scatter(
            down_part.astype(jnp.bfloat16), "wide", scatter_dimension=1, tiled=True
        ).astype(jnp.float32),
        lax.psum_scatter(
            down_bias_part.astype(jnp.bfloat16), "wide", scatter_dimension=0, tiled=True
        ).astype(jnp.float32),
    )
    up_bias_grad = lax.psum(jnp.sum(grad_up, 0, dtype=jnp.float32), "wide")
    grad_first = grad_second + grad_feed
    grad_middle, first_gain_grad, first_shift_grad = normalize_backward(
        grad_first, first_unit, first_inverse, gain_one
    )
    grad_branch = grad_middle.astype(jnp.bfloat16)
    mix_weight_grad = jnp.dot(context.T, grad_branch, preferred_element_type=jnp.float32)
    mix_bias_grad = jnp.sum(grad_branch, 0, dtype=jnp.float32)
    triple_back, mix_back = (
        lax.all_gather(triple_weight, ("wide", "narrow"), axis=0, tiled=True),
        lax.all_gather(mix_weight, ("wide", "narrow"), axis=0, tiled=True),
    )
    grad_context = (
        jnp.dot(grad_branch, mix_back.T, preferred_element_type=jnp.float32)
        .astype(jnp.bfloat16)
        .reshape(head_shape)
    )
    grad_query, grad_key, grad_value = attention_backward(
        query, key, value, grad_context, valid, scale
    )
    grad_triple = jnp.concatenate(
        [
            unrotate(grad_query.reshape(token_rows, width), cosine, sine),
            unrotate(grad_key.reshape(token_rows, width), cosine, sine),
            grad_value.reshape(token_rows, width),
        ],
        1,
    ).astype(jnp.bfloat16)
    triple_local = jnp.dot(inputs.T, grad_triple, preferred_element_type=jnp.float32)
    triple_bias_local = jnp.sum(grad_triple, 0, dtype=jnp.float32)
    grad_inputs = grad_middle + jnp.dot(
        grad_triple, triple_back.T, preferred_element_type=jnp.float32
    )
    summed = (
        lax.psum_scatter(triple_local, ("wide", "narrow"), scatter_dimension=0, tiled=True),
        lax.psum_scatter(mix_weight_grad, ("wide", "narrow"), scatter_dimension=0, tiled=True),
        lax.psum_scatter(triple_bias_local, ("wide", "narrow"), scatter_dimension=0, tiled=True),
        lax.psum_scatter(mix_bias_grad, ("wide", "narrow"), scatter_dimension=0, tiled=True),
        lax.psum_scatter(first_gain_grad, ("wide", "narrow"), scatter_dimension=0, tiled=True),
        lax.psum_scatter(first_shift_grad, ("wide", "narrow"), scatter_dimension=0, tiled=True),
        lax.psum_scatter(second_gain_grad, ("wide", "narrow"), scatter_dimension=0, tiled=True),
        lax.psum_scatter(second_shift_grad, ("wide", "narrow"), scatter_dimension=0, tiled=True),
    )
    return (
        outputs,
        grad_inputs.astype(jnp.bfloat16),
        summed[0],
        summed[2],
        summed[1],
        summed[3],
        summed[4],
        summed[5],
        up_weight_grad,
        up_bias_grad,
        down_weight_grad,
        down_bias_grad,
        summed[6],
        summed[7],
    )


VMEM = pltpu.VMEM
SMEM = pltpu.SMEM
BF = jnp.bfloat16
F32 = jnp.float32
AXES = ("wide", "narrow")
WHOLE = pl.BlockSpec(memory_space=VMEM)
SCALARS = pl.BlockSpec(memory_space=SMEM)
LEFT = pl.BlockSpec(memory_space=pltpu.HBM)


def nn(a, b):
    return lax.dot_general(a, b, (((1,), (0,)), ((), ())), preferred_element_type=F32)


def nt(a, b):
    return lax.dot_general(a, b, (((1,), (1,)), ((), ())), preferred_element_type=F32)


def tn(a, b):
    return lax.dot_general(a, b, (((0,), (0,)), ((), ())), preferred_element_type=F32)


def shape(dims, dtype=BF):
    return jax.ShapeDtypeStruct(dims, dtype)


class Load:
    def __init__(self, source, held, sem):
        self.copy = pltpu.make_async_copy(source, held, sem)
        self.held, self.waited = held, False
        self.shape = held.shape
        self.copy.start()

    def __call__(self):
        if not self.waited:
            self.copy.wait()
            self.waited = True
        return self.held


def call(kernel, outs, operands, kinds, scratch, flops, megabytes, out_specs=None):
    specs = {"s": SCALARS, "v": WHOLE, "h": LEFT, "l": LEFT}
    loads = [k for k, kind in enumerate(kinds) if kind == "l"]
    held = [VMEM(operands[k].shape, operands[k].dtype) for k in loads]
    assert len(kinds) == len(operands)

    def whole(*refs):
        refs = list(refs)
        count = len(loads)
        if count:
            sems = refs.pop()
            buffers, refs = refs[-count:], refs[:-count]
            for n, k in enumerate(loads):
                refs[k] = Load(refs[k], buffers[n], sems.at[n])
        kernel(*refs)
        for k in loads:
            refs[k]()

    return pl.pallas_call(
        whole,
        out_shape=outs,
        in_specs=[specs[kind] for kind in kinds],
        out_specs=[WHOLE] * len(outs) if out_specs is None else out_specs,
        scratch_shapes=list(scratch)
        + held
        + ([pltpu.SemaphoreType.DMA((len(loads),))] if loads else []),
        compiler_params=pltpu.CompilerParams(vmem_limit_bytes=megabytes << 20),
        cost_estimate=pl.CostEstimate(
            flops=int(flops), bytes_accessed=1, transcendentals=0
        ),
    )(*operands)


def drain(ref, sem):
    pltpu.make_async_copy(ref, ref, sem).wait()


class Plan:
    def __init__(self, wide, narrow):
        self.wide, self.narrow = wide, narrow
        self.devices = wide * narrow
        x, y = narrow, narrow // 2
        self.first, self.last = (x, y), (y, x)
        self.far = wide // 2
        line = self.devices // self.far
        along = [(line << k, line << k) for k in reversed(range(self.far.bit_length() - 1))]
        self.far_first = (*along, self.first, self.last)
        self.far_second = (self.first, *along, self.last)
        self.routes = (self.far_first, self.far_second)
        self.slots = 1 << len(self.far_first)

    def lead(self, route, slot):
        masks = [0, 0]
        for k, pair in enumerate(route):
            if slot >> k & 1:
                masks = [mask ^ bit for mask, bit in zip(masks, pair)]
        return masks

    def chips(self, device):
        core = device & 1
        return [
            (device ^ self.lead(route, r)[c]) >> 1
            for route in self.routes
            for c in (core, core ^ 1)
            for r in range(self.slots)
        ]

    def table(self, index, live):
        chips = np.array([self.chips(i) for i in range(self.devices)], np.int32)
        mine = lax.dynamic_slice(jnp.asarray(chips), (index, 0), (1, chips.shape[1]))[0]
        return jnp.concatenate([mine, (index & 1)[None].astype(jnp.int32), live])

    def chip(self, table, route, h, slot):
        return table[(2 * self.routes.index(route) + h) * self.slots + slot]

    def core(self, table):
        return table[2 * len(self.routes) * self.slots]

    def live(self, table):
        return table[2 * len(self.routes) * self.slots + 1]

    def permute(self, value, masks):
        return lax.ppermute(value, AXES, [(i, i ^ masks[i & 1]) for i in range(self.devices)])

    def swap(self, value):
        return self.permute(value, (1, 1))

    def send(self, value, route, slot):
        return self.permute(value, self.lead(route, slot))

    def gather_far(self, value):
        return [value] + [self.send(value, self.far_first, m) for m in range(1, self.far)]

    def send_far(self, parts):
        return [self.send(v, self.far_first, m) for m, v in enumerate(parts) if m]


def added(*values):
    return sum([v.astype(F32) for v in values[1:]], values[0].astype(F32)).astype(BF)


def halves(*values):
    count = values[0].shape[0] // 2
    return added(*(v[:count] for v in values)), added(*(v[count:] for v in values))


def together(*lists):
    flat = list(lax.optimization_barrier(tuple(v for values in lists for v in values)))
    return [[flat.pop(0) for _ in values] for values in lists]


def after_all(values, *others):
    return lax.optimization_barrier(tuple(values) + others)[: len(values)]


def after(value, *others):
    return lax.optimization_barrier((value,) + others)[0] if others else value


def mean(v):
    return jnp.mean(v, -1, keepdims=True)


def swap_lanes(v):
    lane = lax.broadcasted_iota(jnp.int32, v.shape, 1)
    return jnp.where(lane % 2 == 0, pltpu.roll(v, v.shape[1] - 1, 1), pltpu.roll(v, 1, 1))


def first_half(rows):
    return lax.broadcasted_iota(jnp.int32, (rows, 2 * HD), 1) < HD


def place_attention(plan, table, h, pieces, triple, mix, rows):
    core = plan.core(table)
    half_slots = plan.slots // 2
    third = rows // 3
    columns = pieces[0].shape[2]
    width = columns // 3
    for r in range(plan.slots):
        chip = plan.chip(table, plan.far_first, h, r)
        side, at = divmod(r, half_slots)
        first, second = pieces[side], pieces[2 + side]
        if triple is not None:
            top = pl.ds(pl.multiple_of(chip * rows, 16), 2 * third)
            triple[top, :] = first[at]
            rest = pl.ds(pl.multiple_of(chip * rows + 2 * third, 16), third)
            triple[rest, :] = second[at, :third, :columns]
        if mix is not None:
            for b in range(3):
                here = pl.ds(pl.multiple_of(chip * rows + b * third, 16), third)
                mix[core ^ h, here, :] = second[at, third:, b * width : (b + 1) * width]


def place_hidden(plan, route, table, h, pieces, weight, rows, columns):
    across = plan.narrow // 2
    slots = [(piece, k) for piece in pieces for k in range(piece.shape[0])]
    for r, (piece, k) in enumerate(slots):
        chip = plan.chip(table, route, h, r)
        down = pl.ds(pl.multiple_of(chip // across * rows, 16), rows)
        over = pl.ds(pl.multiple_of(chip % across * columns, 128), columns)
        weight[down, over] = piece[k]


TRIPLE, MIX, GAIN1, SHIFT1, GAIN2, SHIFT2, UP = 0, 3, 4, 5, 6, 7, 8
TABLE_ROWS = 16
SHARE = 128


def split_kernel(index_ref, triple_ref, mix_ref, mine_ref, theirs_ref):
    core = index_ref[0] % 2
    width = mix_ref.shape[1]
    half = width // 2
    for out, h in ((mine_ref, core), (theirs_ref, core ^ 1)):
        for g in range(3):
            at = pl.multiple_of(g * width + h * half, 128)
            out[:, g * half : (g + 1) * half] = triple_ref[:, pl.ds(at, half)]
        out[:, 3 * half :] = mix_ref[:, pl.ds(pl.multiple_of(h * half, 128), half)]


def join_kernel(index_ref, mine_ref, came_ref, first_ref, rest_ref):
    core = index_ref[0] % 2
    half = mine_ref.shape[1] // 4
    mine, came = mine_ref[...].astype(F32), came_ref[...].astype(F32)
    both = jnp.concatenate(
        [jnp.where(core == 0, mine, came), jnp.where(core == 0, came, mine)], 0
    ).astype(BF)
    third = both.shape[0] // 3
    first_ref[0] = both[: 2 * third, : 3 * half]
    rest_ref[:third, :] = both[2 * third :, : 3 * half]
    for b in range(3):
        rest_ref[third:, b * half : (b + 1) * half] = both[b * third : (b + 1) * third, 3 * half :]


def spread_kernel(plan, index_ref, tb_ref, mb_ref, g1_ref, s1_ref, g2_ref, s2_ref, ub_ref, db_ref,
                  share_ref, spread):
    of_narrow = index_ref[0] % plan.narrow
    spread[...] = jnp.zeros_like(spread)
    for row, ref in ((TRIPLE, tb_ref), (MIX, mb_ref), (GAIN1, g1_ref), (SHIFT1, s1_ref),
                     (GAIN2, g2_ref), (SHIFT2, s2_ref), (UP, ub_ref)):
        spread[row : row + 1, : ref.shape[1]] = ref()[...].astype(F32)
    count = db_ref.shape[1] // plan.narrow
    values = db_ref()[...].astype(F32)
    mine = values[:, :count]
    for k in range(1, plan.narrow):
        mine = jnp.where(of_narrow == k, values[:, k * count : (k + 1) * count], mine)
    spread[UP + plan.narrow : UP + plan.narrow + 1, :count] = mine
    share_ref[...] = spread[...].astype(BF)


def beside_kernel(index_ref, rest_ref, share_ref, came_ref, out_ref):
    core = index_ref[0] % 2
    columns = rest_ref.shape[1]
    share, came = share_ref[...], came_ref[...]
    out_ref[0, :, :columns] = rest_ref[...]
    out_ref[0, :TABLE_ROWS, columns:] = jnp.where(core == 0, share, came)
    out_ref[0, TABLE_ROWS:, columns:] = jnp.where(core == 0, came, share)


def vectors_kernel(plan, share, table, low_ref, high_ref, out_ref, held, triple, plain, up, down):
    half_slots = plan.slots // 2
    columns = low_ref.shape[2] - SHARE
    for r in range(plan.slots):
        piece = (low_ref, high_ref)[r // half_slots]
        held[plan.chip(table, plan.far_first, 0, r)] = piece[r % half_slots, :, columns:]
    for ref in (triple, plain, up, down):
        ref[...] = jnp.zeros_like(ref)
    width = out_ref.shape[1]
    part = width // plan.wide

    def put(ref, rows, at):
        block, lane = divmod(at, SHARE)
        s = slice(block * SHARE, (block + 2) * SHARE)
        ref[..., s] = ref[..., s] + (pltpu.roll(rows, lane, 1) if lane else rows)

    for device in range(plan.devices):
        of_wide, of_narrow = divmod(device, plan.narrow)
        rows = held[device // 2].astype(F32)[device % 2 * TABLE_ROWS :][:TABLE_ROWS]
        rows = jnp.concatenate([rows, jnp.zeros_like(rows)], 1)
        put(triple, rows[:8], 3 * share * device)
        put(plain, rows[:8], share * device)
        put(up.at[of_narrow], rows[8:], part * of_wide)
        put(down, rows[8:], share * device)
    out_ref[...] = jnp.zeros_like(out_ref)
    for g in range(3):
        out_ref[TRIPLE + g : TRIPLE + g + 1, :] = triple[0:1, g * width : (g + 1) * width]
    out_ref[MIX:UP, :] = plain[MIX:UP, :width]
    for n in range(plan.narrow):
        out_ref[UP + n : UP + n + 1, :] = up[n, 0:1, :width]
    row = UP + plan.narrow
    out_ref[row : row + 1, :] = down[row - 8 : row - 7, :width]


def pack_vectors(plan, core, width, bias_own, bias_other, first_ref, second_ref, cot_ref, up_own,
                 up_other, out_ref):
    out_ref[...] = jnp.zeros_like(out_ref)
    half = width // 2
    for h, ref in ((0, bias_own), (1, bias_other)):
        at = pl.ds(pl.multiple_of((core ^ h) * half, 128), half)
        for g in range(3):
            out_ref[TRIPLE + g : TRIPLE + g + 1, at] = ref[:, g * half : (g + 1) * half]
    out_ref[MIX : MIX + 1, :width] = first_ref[2:3, :]
    out_ref[GAIN1 : GAIN1 + 2, :width] = first_ref[0:2, :]
    out_ref[GAIN2 : GAIN2 + 1, :width] = second_ref[0:1, :]
    out_ref[SHIFT2 : SHIFT2 + 1, :width] = cot_ref[...]
    for h, up_ref in ((0, up_own), (1, up_other)):
        for y in range(plan.narrow // 2):
            row = up_ref[:, y * width : (y + 1) * width]
            out_ref[pl.ds(UP + 2 * y + (core ^ h), 1), :width] = row
    out_ref[UP + plan.narrow : UP + plan.narrow + 1, :width] = second_ref[1:2, :]


def attention_kernel(plan, rows, h, table, x_ref, a, b, c, d, cos_ref, sin_ref, vec_ref,
                     keep_ref, probs_ref, context_ref, triple):
    core, live = plan.core(table), plan.live(table)
    tokens, width = x_ref.shape
    half = width // 2
    place_attention(plan, table, h, (a, b, c, d), triple, None, rows)
    x = x_ref[...]
    cos, sin = cos_ref[...], sin_ref[...]
    left = first_half(tokens)
    valid = lax.broadcasted_iota(jnp.int32, (1, tokens), 1) < live
    scale = jnp.asarray(1.0 / math.sqrt(HD), BF)
    for q in range(half // 128):
        at = [slice(g * half + 128 * q, g * half + 128 * q + 128) for g in range(3)]
        here = pl.ds(pl.multiple_of((core ^ h) * half + 128 * q, 128), 128)
        out = [
            nn(x, triple[:, s]) + vec_ref[TRIPLE + g : TRIPLE + g + 1, here]
            for g, s in enumerate(at)
        ]
        query, key = [(v * cos + swap_lanes(v) * sin).astype(BF) for v in out[:2]]
        value = out[2].astype(BF)
        for s, v in zip(at, (query, key, value)):
            keep_ref[:, s] = v
        context = []
        for e in (0, 1):
            mine = left if e == 0 else ~left
            masked = jnp.where(mine, query, jnp.zeros_like(query)) * scale
            score = jnp.where(valid, nt(masked, key), -1e30)
            power = jnp.exp(score - jnp.max(score, -1, keepdims=True))
            prob = power * (1.0 / jnp.sum(power, -1, keepdims=True))
            prob = prob.astype(BF)
            probs_ref[2 * q + e] = prob
            context.append(nn(prob, value))
        context_ref[:, 128 * q : 128 * q + 128] = (
            jnp.where(left, context[0], context[1]).astype(BF)
        )


def mix_kernel(plan, rows, table, x_ref, context_own, context_other, a, b, c, d, e, f, g, k,
               vec_ref, unit_ref, inv_ref, low_ref, mix):
    core = plan.core(table)
    half = context_own.shape[1]
    for h, pieces in ((0, (a, b, c, d)), (1, (e, f, g, k))):
        place_attention(plan, table, h, pieces, None, mix, rows)
    sides = []
    for side in (0, 1):
        total = 0.0
        for h, context in ((0, context_own), (1, context_other)):
            at = pl.ds(pl.multiple_of((core ^ h) * half, 128), half)
            total = total + nn(context[...], mix[side, at, :])
        sides.append(total)
    branch = jnp.concatenate(sides, 1)
    summed = x_ref[...].astype(F32) + (branch + vec_ref[MIX : MIX + 1, :])
    centred = summed - mean(summed)
    inverse = lax.rsqrt(mean(centred * centred) + EPSILON)
    unit = centred * inverse
    unit_ref[...] = unit
    inv_ref[...] = jnp.broadcast_to(inverse, inv_ref.shape)
    low_ref[...] = (
        unit * vec_ref[GAIN1 : GAIN1 + 1, :] + vec_ref[SHIFT1 : SHIFT1 + 1, :]
    ).astype(BF)


def up_kernel(plan, route, rows, columns, table, low_ref, a, b, c, d, e, f, g, k, vec_ref,
              own_ref, other_ref, slope_own_ref, slope_other_ref, weight):
    core = plan.core(table)
    low = low_ref[...]
    step = 256
    for h, (out, slope) in enumerate(((own_ref, slope_own_ref), (other_ref, slope_other_ref))):
        place_hidden(plan, route, table, h, ((a, b, c, d), (e, f, g, k))[h], weight.at[h], rows, columns)
        for n in range(out.shape[1] // step):
            s = slice(n * step, (n + 1) * step)
            y, at = divmod(n * step, columns)
            row = vec_ref[pl.ds(UP + 2 * y + (core ^ h), 1), at : at + step]
            up = nn(low, weight[h, :, s]) + row
            share = 0.5 * (1.0 + lax.erf(up * math.sqrt(0.5)))
            out[:, s] = (up * share).astype(BF)
            slope[:, s] = (
                share + up * jnp.exp(-0.5 * up * up) * (1.0 / math.sqrt(2.0 * math.pi))
            ).astype(BF)


def down_own_kernel(plan, route, rows, columns, table, act, a, b, unit_ref, cot_ref, vec_ref,
                    out_ref, mean_ref, sum_ref, weight):
    place_hidden(plan, route, table, 0, (a, b), weight, rows, columns)
    first = unit_ref[...] * vec_ref[GAIN1 : GAIN1 + 1, :] + vec_ref[SHIFT1 : SHIFT1 + 1, :]
    bias = vec_ref[UP + plan.narrow : UP + plan.narrow + 1, :]
    out_ref[...] = first + (nt(act[...], weight[...]) + bias)
    cot = cot_ref[...].astype(F32)
    sum_ref[...] = jnp.sum(cot, 0, keepdims=True)
    scaled_mean = mean(cot * vec_ref[GAIN2 : GAIN2 + 1, :])
    mean_ref[...] = jnp.broadcast_to(scaled_mean, mean_ref.shape)


def down_kernel(plan, route, rows, columns, table, part_ref, act, a, b, mean_ref,
                cot_ref, vec_ref, out_ref, grad_ref, grad_low_ref, turned_ref, sums_ref, weight):
    place_hidden(plan, route, table, 1, (a, b), weight, rows, columns)
    summed = part_ref[...] + nt(act[...], weight[...])
    cot = cot_ref[...].astype(F32)
    scaled = cot * vec_ref[GAIN2 : GAIN2 + 1, :]
    centred = summed - mean(summed)
    inverse = lax.rsqrt(mean(centred * centred) + EPSILON)
    unit = centred * inverse
    grad = inverse * (scaled - mean_ref[:, 0:1] - unit * mean(scaled * unit))
    grad_ref[...] = grad
    low = grad.astype(BF)
    grad_low_ref[...] = low
    turned_ref[...] = low.T
    sums_ref[0:1, :] = jnp.sum(cot * unit, 0, keepdims=True)
    sums_ref[1:2, :] = jnp.sum(low.astype(F32), 0, keepdims=True)
    out_ref[...] = (
        unit * vec_ref[GAIN2 : GAIN2 + 1, :] + vec_ref[SHIFT2 : SHIFT2 + 1, :]
    ).astype(BF)


def grad_up_kernel(plan, route, h, rows, columns, table, low_ref, a, b, slope, out, sums_ref,
                   weight):
    place_hidden(plan, route, table, h, (a, b), weight, rows, columns)
    low = low_ref[...]
    step = 256
    for n in range(out.shape[1] // step):
        s = slice(n * step, (n + 1) * step)
        grad = (nn(low, weight[:, s]) * slope[:, s].astype(F32)).astype(BF)
        out[:, s] = grad
        sums_ref[:, s] = jnp.sum(grad.astype(F32), 0, keepdims=True)


def hidden_grad_kernel(plan, route, rows, columns, table, left_own, left_other, right_own,
                       right_other, low_ref, high_ref, block):
    across, half_slots = plan.narrow // 2, plan.slots // 2
    a, b = left_own[...], left_other[...]
    for y in range(across):
        s = slice(y * columns, (y + 1) * columns)
        tile = tn(a, right_own[:, s]) + tn(b, right_other[:, s])
        block[:, y] = tile.astype(BF).reshape(plan.wide, rows, columns)
    for r in reversed(range(plan.slots)):
        chip = plan.chip(table, route, 0, r)
        out = (low_ref, high_ref)[r // half_slots]
        out[r % half_slots] = block[chip // across, chip % across]


def hidden_part_kernel(plan, route, part, rows, columns, table, left_own, left_other, right_own,
                       right_other, out_ref, block, some):
    across, half_slots = plan.narrow // 2, plan.slots // 2
    core = plan.core(table)
    here = plan.chip(table, route, 0, 0)

    @pl.when(core == 0)
    def _():
        y = (here % across) ^ part
        s = pl.ds(pl.multiple_of(y * columns, 128), columns)
        tile = nn(left_own[...], right_own[:, s]) + nn(left_other[...], right_other[:, s])
        block[:, pl.ds(y, 1)] = tile.astype(BF).reshape(plan.wide, 1, rows, columns)

    @pl.when(core == 1)
    def _():
        x = (here // across % 2) ^ part
        for z in range(plan.far):
            at = pl.ds(pl.multiple_of((2 * z + x) * rows, 16), rows)
            for k, left in enumerate((left_own, left_other)):
                some[k, z * rows : (z + 1) * rows, :] = left[at, :]
        tile = nn(some[0], right_own[...]) + nn(some[1], right_other[...])
        for z in range(plan.far):
            for y in range(across):
                block[2 * z + x, y] = tile[
                    z * rows : (z + 1) * rows, y * columns : (y + 1) * columns
                ].astype(BF)

    for r in range(half_slots):
        chip = plan.chip(table, route, 0, part * half_slots + r)
        out_ref[r] = block[chip // across, chip % across]


def first_grad_kernel(plan, route, rows, columns, arows, table, gu_own, gu_other, a, b, c, d,
                      e, f, g, k, p, q, r, s, l, m, n, o, grad_ref, unit_ref, inv_ref, vec_ref, middle_ref,
                      mine_ref, theirs_ref, context_ref, sums_ref, weight, mix, low_ref):
    for h in (0, 1):
        place_hidden(plan, route, table, h, ((a, b, c, d), (e, f, g, k))[h], weight.at[h], rows, columns)
    width = unit_ref.shape[1]
    half = width // 2
    for h, pieces in ((0, (p, q, r, s)), (1, (l, m, n, o))):
        place_attention(plan, table, h, pieces, None, mix, arows)
    core = plan.core(table)
    total = nt(gu_own[...], weight[0])
    total = total + nt(gu_other[...], weight[1])
    grad = grad_ref[...] + total
    unit = unit_ref[...]
    scaled = grad * vec_ref[GAIN1 : GAIN1 + 1, :]
    middle = inv_ref[:, 0:1] * (scaled - mean(scaled) - unit * mean(scaled * unit))
    low = middle.astype(BF)
    middle_ref[...] = middle
    low_ref[...] = low
    mine_ref[...] = low_ref[:, pl.ds(pl.multiple_of(core * half, 128), half)]
    theirs_ref[...] = low_ref[:, pl.ds(pl.multiple_of((core ^ 1) * half, 128), half)]
    sums_ref[0:1, :] = jnp.sum(grad * unit, 0, keepdims=True)
    sums_ref[1:2, :] = jnp.sum(grad, 0, keepdims=True)
    sums_ref[2:3, :] = jnp.sum(low.astype(F32), 0, keepdims=True)
    context_ref[...] = (nt(low[:, :half], mix[0]) + nt(low[:, half:], mix[1])).astype(BF)


def attention_grad_kernel(plan, h, table, keep_ref, probs_ref, grad_ref, cos_ref, sin_ref,
                          out_ref, sums_ref):
    core = plan.core(table)
    tokens, width = grad_ref.shape
    half = width // 2
    cos, sin = cos_ref[...], sin_ref[...]
    left = first_half(tokens)
    scale = 1.0 / math.sqrt(HD)
    keep, grads_in, probs = keep_ref, grad_ref, probs_ref
    for q in range(half // 128):
        at = [slice(g * half + 128 * q, g * half + 128 * q + 128) for g in range(3)]
        query, key, value = [keep[:, s] for s in at]
        came = grads_in[:, pl.ds(pl.multiple_of((core ^ h) * half + 128 * q, 128), 128)]
        parts = []
        for e in (0, 1):
            mine = left if e == 0 else ~left
            low = probs[2 * q + e]
            prob = low.astype(F32)
            grad = nt(jnp.where(mine, came, jnp.zeros_like(came)), value)
            score = prob * (grad - jnp.sum(prob * grad, -1, keepdims=True))
            score = score.astype(BF)
            parts.append((nn(score, key), tn(score, query), tn(low, came)))
        grads = [jnp.where(left, u, v) for u, v in zip(*parts)]
        grads = [(g * scale) * cos + swap_lanes((g * scale) * sin) for g in grads[:2]] + grads[2:]
        for s, g in zip(at, grads):
            g = g.astype(BF)
            out_ref[:, s] = g
            sums_ref[:, s] = jnp.sum(g.astype(F32), 0, keepdims=True)


def attention_weight_kernel(plan, rows, table, x_own, x_other, g_own, g_other, c_own, c_other,
                            c_came_own, c_came_other, b_own, b_other, bias_own, bias_other,
                            first_ref, second_ref, cot_ref, up_own, up_other, low_one, low_rest,
                            low_away, high_one, high_rest, high_away, block, mixed, sums):
    core = plan.core(table)
    half_slots = plan.slots // 2
    tokens, columns = g_own.shape
    third = columns // 3
    height = rows + rows // 3
    pack_vectors(plan, core, x_own.shape[1], bias_own, bias_other, first_ref, second_ref, cot_ref,
                 up_own, up_other, sums)
    far = plan.far
    for ref in (low_away, high_away):
        ref[far * height :, :] = sums[...].astype(BF)
    block[...] = (
        (tn(x_own[...], g_own[...]) + tn(x_other[...], g_other[...]))
        .astype(BF)
        .reshape(block.shape)
    )
    for h, mine, came in ((0, c_own, c_came_other), (1, c_other, c_came_own)):
        mixed[pl.ds((core ^ h) * half_slots, half_slots)] = (
            (tn(mine[...], b_own[...]) + tn(came[...], b_other[...]))
            .astype(BF)
            .reshape((half_slots,) + mixed.shape[1:])
        )
    for r in reversed(range(plan.slots)):
        chip = plan.chip(table, plan.far_first, 0, r)
        side, slot = divmod(r, half_slots)
        one, rest, away = ((low_one, low_rest, low_away), (high_one, high_rest, high_away))[side]
        if slot == 0:
            out, at = one, 0
        elif slot < far:
            out, at = rest, (slot - 1) * height
        else:
            out, at = away, (slot - far) * height
        out[at : at + rows, :] = block[chip]
        for b in range(3):
            out[at + rows : at + height, b * third : (b + 1) * third] = mixed[chip, b]


def input_grad_kernel(plan, rows, table, middle_ref, g_own, g_other, a, b, c, d, e, f, g, k,
                      out_ref, triple):
    for h, pieces in ((0, (a, b, c, d)), (1, (e, f, g, k))):
        place_attention(plan, table, h, pieces, triple.at[h], None, rows)
    total = nt(g_own[...], triple[0])
    total = total + nt(g_other[...], triple[1])
    out_ref[...] = (middle_ref[...] + total).astype(BF)


def total_kernel(plan, rows, table, one, sums, a, b, c, mine_ref, theirs_ref, both):
    core = plan.core(table)
    total = jnp.concatenate([one[...], sums[...].astype(F32)], 0)
    for ref in (a, b, c):
        total = total + ref[...].astype(F32)
    third, half = rows // 3, total.shape[1] // 3
    width = 2 * half
    both[:, : 3 * half] = total[:rows]
    for k in range(3):
        both[k * third : (k + 1) * third, 3 * half :] = (
            total[rows : rows + third, k * half : (k + 1) * half]
        )
    piece = rows // 2
    mine_ref[:piece, :] = both[pl.ds(pl.multiple_of(core * piece, 8), piece), :]
    theirs_ref[:piece, :] = both[pl.ds(pl.multiple_of((core ^ 1) * piece, 8), piece), :]
    for ref in (mine_ref, theirs_ref):
        ref[piece:, :width] = total[rows + third :, :width]


def share_kernel(plan, table, index_ref, mine_ref, came_ref, triple_ref, mix_ref, tb_ref, mb_ref,
                 g1_ref, s1_ref, ub_ref, db_ref, g2_ref, s2_ref):
    core, index = plan.core(table), index_ref[0]
    piece, width = mix_ref.shape
    half = width // 2
    for ref, h in ((mine_ref, core), (came_ref, core ^ 1)):
        for g in range(3):
            at = pl.ds(pl.multiple_of(g * width + h * half, 128), half)
            triple_ref[:, at] = ref[:piece, g * half : (g + 1) * half]
        mix_ref[:, pl.ds(pl.multiple_of(h * half, 128), half)] = ref[:piece, 3 * half : 4 * half]
    sums = mine_ref[piece:, :width] + came_ref[piece:, :width]
    biases = jnp.concatenate([sums[g : g + 1, :] for g in range(3)], 1)
    biases = jnp.broadcast_to(biases, (8, 3 * width))
    tb_ref[...] = pltpu.roll(biases, (3 * width - index * 3 * piece) % (3 * width), 1)[
        0:1, : 3 * piece
    ]
    rolled = pltpu.roll(sums[:8], (width - index * piece) % width, 1)
    for row, ref in ((MIX, mb_ref), (GAIN1, g1_ref), (SHIFT1, s1_ref), (GAIN2, g2_ref),
                     (SHIFT2, s2_ref)):
        ref[...] = rolled[row : row + 1, :piece]
    of_wide, of_narrow = index // plan.narrow, index % plan.narrow
    mine = sums[UP : UP + 1, :]
    for n in range(1, plan.narrow):
        mine = jnp.where(of_narrow == n, sums[UP + n : UP + n + 1, :], mine)
    ub_ref[...] = mine
    count = db_ref.shape[1]
    rolled = pltpu.roll(sums[8:], (width - of_wide * count) % width, 1)
    row = UP + plan.narrow - 8
    db_ref[...] = rolled[row : row + 1, :count]


def half_tables(tokens):
    position = jnp.arange(tokens, dtype=F32)
    column = jnp.arange(2 * HD, dtype=jnp.int32)
    pair = (column % HD // 2).astype(F32)
    angle = position[:, None] * jnp.exp(pair * (-2.0 / HD) * math.log(10000.0))[None, :]
    parity = (column % 2).astype(F32) * 2.0 - 1.0
    return jnp.cos(angle), jnp.sin(angle) * parity[None, :]


def fast_body(
    plan,
    inputs,
    lengths,
    triple_weight,
    triple_bias,
    mix_weight,
    mix_bias,
    first_gain,
    first_shift,
    up_weight,
    up_bias,
    down_weight,
    down_bias,
    second_gain,
    second_shift,
    cotangent,
):
    tokens, width = inputs.shape
    half = width // 2
    wide, narrow = plan.wide, plan.narrow
    index = lax.axis_index(AXES)
    core = index & 1
    of_wide = lax.axis_index("wide")
    table = plan.table(index, lengths)
    hidden = up_weight.shape[1]
    tile_rows = up_weight.shape[0]
    piece = triple_weight.shape[0]
    rows = 2 * piece
    third = rows // 3
    half_slots = plan.slots // 2
    far_first, far_second = plan.far_first, plan.far_second
    flops = 2.0 * tokens * width * width
    hidden_half = hidden * narrow // 2

    place = index.astype(jnp.int32)[None]
    mine, theirs = call(
        split_kernel,
        [shape((piece, 4 * half))] * 2,
        (place, triple_weight, mix_weight),
        "svv",
        [],
        0,
        16,
    )
    first, rest = call(
        join_kernel,
        [shape((1, 2 * third, 3 * half)), shape((2 * third, 3 * half))],
        (place, mine, plan.swap(theirs)),
        "svv",
        [],
        0,
        16,
    )
    row = functools.partial(jnp.reshape, shape=(1, -1))
    up_share = lax.dynamic_slice(up_bias, (of_wide * (hidden // wide),), (hidden // wide,))
    (share,) = call(
        functools.partial(spread_kernel, plan),
        [shape((TABLE_ROWS, SHARE))],
        (
            after(place, first),
            row(triple_bias),
            row(mix_bias),
            row(first_gain),
            row(first_shift),
            row(second_gain),
            row(second_shift),
            row(up_share),
            row(down_bias),
        ),
        "s" + 8 * "l",
        [VMEM((TABLE_ROWS, SHARE), F32)],
        0,
        60,
    )
    (second,) = call(
        beside_kernel,
        [shape((1, 2 * third, 3 * half + SHARE))],
        (place, rest, share, plan.swap(share)),
        "svvv",
        [],
        0,
        16,
    )
    cat = functools.partial(jnp.concatenate, axis=0)
    cos, sin = half_tables(tokens)
    inputs_came = plan.swap(after(inputs, first))
    down = after(down_weight.T[None], first)
    down_came = plan.send(down, far_second, 1)
    first = cat(after_all(plan.gather_far(first), inputs_came, second))
    first_came = plan.permute(first, plan.first)
    second = plan.gather_far(after(second, first))
    up = after(up_weight[None], first)
    up_came = plan.send(up, far_first, 1)
    first, first_came = after_all((first, first_came))
    first = cat((first, first_came))
    first_came = plan.permute(first, plan.last)
    second = cat(after_all(second, first))
    second_came = plan.permute(second, plan.first)
    down = cat(after_all((down, down_came), first))
    down_came = plan.send(down, far_second, 2)
    up = cat(after_all((up, up_came), down))
    up_came = plan.send(up, far_first, 2)
    second, second_came = after_all((second, second_came), up)
    second = cat((second, second_came))
    first, first_came = after_all((first, first_came), second)
    second_came = plan.permute(second, plan.last)
    up = cat(after_all((up, up_came), first_came))
    up_came = plan.permute(up, plan.first)
    ups = [up, up_came, plan.permute(up, plan.last)]
    down = cat(after_all((down, down_came), up))
    down_came = plan.send(down, far_second, 4)
    second, second_came = after_all((second, second_came), down)
    att_own = [first, first_came, second, second_came]
    att_other = [plan.swap(v) for v in att_own]
    (vecs,) = call(
        functools.partial(vectors_kernel, plan, piece),
        [shape((TABLE_ROWS, width), F32)],
        (table, *att_own[2:]),
        "svv",
        [
            VMEM((plan.slots, 2 * third, SHARE), BF),
            VMEM((8, 3 * width + 2 * SHARE), F32),
            VMEM((8, width + 2 * SHARE), F32),
            VMEM((narrow, 8, width + 2 * SHARE), F32),
            VMEM((8, width + 2 * SHARE), F32),
        ],
        0,
        32,
    )

    def attend(h, pieces, gate=()):
        return call(
            functools.partial(attention_kernel, plan, rows, h),
            [
                shape((tokens, 3 * half)),
                shape((half // HD, tokens, tokens)),
                shape((tokens, half)),
            ],
            (after(table, *gate), inputs, *pieces, cos, sin, vecs),
            "s" + 8 * "v",
            [VMEM((width, 3 * half), BF)],
            80 * flops,
            24,
        )

    own, p_own, context_own = attend(0, att_own, (second_came, *att_other[:2]))
    (up_came,) = after_all((ups[1],), context_own)
    ups = [ups[0], up_came, ups[2], plan.permute(up_came, plan.last)]
    down = cat(after_all((down, down_came), up_came))
    downs = [down, plan.permute(down, plan.last)]
    other, p_other, context_other = attend(1, att_other, (down,))
    unit, inv, low = call(
        functools.partial(mix_kernel, plan, rows),
        [shape((tokens, width), F32), shape((tokens, 128), F32), shape((tokens, width))],
        (table, inputs, context_own, context_other, *att_own, *att_other, vecs),
        "s" + 12 * "v",
        [VMEM((2, width, half), BF)],
        1,
        24,
    )
    hidden_scratch = [VMEM((2, width, hidden_half), BF)]
    ups = [*ups, *(plan.swap(v) for v in ups)]
    down_low_came = plan.swap(downs[0])
    context_came = plan.swap(context_own), plan.swap(context_other)
    act_own, act_other, slope_own, slope_other = call(
        functools.partial(up_kernel, plan, far_first, tile_rows, hidden),
        [shape((tokens, hidden_half))] * 4,
        (table, low, *ups, vecs),
        "s" + 10 * "v",
        hidden_scratch,
        1,
        24,
    )
    (down_high,) = after_all(downs[1:], act_own)
    downs = [downs[0], down_high, down_low_came, plan.swap(down_high)]
    low_came, act_came = plan.swap(low), plan.swap(act_other)
    half_scratch = [VMEM((width, hidden_half), BF)]
    downward, scaled_mean, cot_sum = call(
        functools.partial(down_own_kernel, plan, far_second, tile_rows, hidden),
        [shape((tokens, width), F32), shape((tokens, 128), F32), shape((1, width), F32)],
        (after(table, *context_came), act_own, *downs[:2], unit, cotangent, vecs),
        "s" + 6 * "v",
        half_scratch,
        80 * flops,
        24,
    )
    outputs, grad_second, grad_down, grad_turned, sums_second = call(
        functools.partial(down_kernel, plan, far_second, tile_rows, hidden),
        [
            shape((tokens, width)),
            shape((tokens, width), F32),
            shape((tokens, width)),
            shape((width, tokens)),
            shape((2, width), F32),
        ],
        (table, downward, act_other, *downs[2:], scaled_mean, cotangent, vecs),
        "s" + 7 * "v",
        half_scratch,
        1,
        24,
    )
    grad_turned_came = plan.swap(grad_turned)

    def grad_up(h, pieces, slope, gate=()):
        return call(
            functools.partial(grad_up_kernel, plan, far_second, h, tile_rows, hidden),
            [shape((tokens, hidden_half)), shape((1, hidden_half), F32)],
            (after(table, *gate), grad_down, *pieces, slope),
            "s" + 4 * "v",
            half_scratch,
            1,
            24,
        )

    gu_other, sums_up_other = grad_up(1, downs[2:], slope_other)
    gu_came = plan.swap(gu_other)

    def hidden_grad(route, left, left_came, right, right_came, cost, gate):
        return call(
            functools.partial(hidden_grad_kernel, plan, route, tile_rows, hidden),
            [shape((half_slots, tile_rows, hidden))] * 2,
            (after(table, *gate), left, left_came, right, right_came),
            "svvvv",
            [VMEM((wide, narrow // 2, tile_rows, hidden), BF)],
            cost,
            24,
        )

    def down_grad(part, gate):
        (tiles,) = call(
            functools.partial(hidden_part_kernel, plan, far_second, part, tile_rows, hidden),
            [shape((half_slots, tile_rows, hidden))],
            (after(table, *gate), grad_turned, grad_turned_came, act_own, act_came),
            "svvvv",
            [
                VMEM((wide, narrow // 2, tile_rows, hidden), BF),
                VMEM((2, width // 2, tokens), BF),
            ],
            80 * flops if part else 1,
            24,
        )
        return tiles

    down_high = down_grad(1, (sums_up_other,))
    down_came = plan.permute(down_high, plan.last)
    gu_own, sums_up_own = grad_up(0, downs[:2], slope_own, (down_high,))
    down_low = down_grad(0, (sums_up_own,))
    up_low, up_high = hidden_grad(far_first, low, low_came, gu_own, gu_came, 1, (down_low,))
    up_came = plan.permute(up_high, plan.last)
    grad_middle, branch_mine, branch_theirs, grad_context, sums_first = call(
        functools.partial(first_grad_kernel, plan, far_first, tile_rows, hidden, rows),
        [
            shape((tokens, width), F32),
            shape((tokens, half)),
            shape((tokens, half)),
            shape((tokens, width)),
            shape((3, width), F32),
        ],
        (
            after(table, up_low),
            gu_own,
            gu_other,
            *ups,
            *att_own,
            *att_other,
            grad_second,
            unit,
            inv,
            vecs,
        ),
        "s" + 22 * "v",
        hidden_scratch
        + [VMEM((2, width, half), BF), VMEM((tokens, width), BF)],
        1,
        24,
    )
    branch_came = plan.swap(branch_theirs)

    def attention_grad(h, keep, probs, gate=()):
        return call(
            functools.partial(attention_grad_kernel, plan, h),
            [shape((tokens, 3 * half)), shape((1, 3 * half), F32)],
            (after(table, *gate), keep, probs, grad_context, cos, sin),
            "svvvvv",
            [],
            1,
            24,
        )

    gt_other, bias_other = attention_grad(1, other, p_other, (act_came,))
    gt_came = plan.swap(gt_other)
    down_stay, down_away = halves(*after_all((down_low, down_came), bias_other))
    down_came = plan.send(down_away, far_second, 4)
    gt_own, bias_own = attention_grad(0, own, p_own, (down_away,))
    up_stay, up_away = halves(*after_all((up_low, up_came), bias_own))
    up_came = plan.permute(up_away, plan.first)
    height = rows + third
    far = plan.far
    kinds = [shape((k * height + more, 3 * half)) for k, more in ((1, 0), (far - 1, 0), (far, TABLE_ROWS))]
    low_one, low_rest, low_away, high_one, high_rest, high_away = call(
        functools.partial(attention_weight_kernel, plan, rows),
        kinds + kinds,
        (
            after(table, up_away),
            inputs,
            inputs_came,
            gt_own,
            gt_came,
            context_own,
            context_other,
            *context_came,
            branch_mine,
            branch_came,
            bias_own,
            bias_other,
            sums_first,
            sums_second,
            cot_sum,
            sums_up_own,
            sums_up_other,
        ),
        "s" + 17 * "v",
        [
            VMEM((plan.slots, rows, 3 * half), BF),
            VMEM((plan.slots, 3, third, half), BF),
            VMEM((TABLE_ROWS, 3 * half), F32),
        ],
        80 * flops,
        24,
    )
    came_away = plan.permute(high_away, plan.last)
    came_rest = plan.permute(high_rest, plan.last)
    came_one = plan.permute(high_one, plan.last)
    down_stay, down_away = halves(*after_all((down_stay, down_came), low_away))
    down_came = plan.send(down_away, far_second, 2)
    up_stay, up_away = halves(*after_all((up_stay, up_came), down_away))
    up_came = plan.send(up_away, far_first, 2)
    (input_grad,) = call(
        functools.partial(input_grad_kernel, plan, rows),
        [shape((tokens, width))],
        (after(table, up_away), grad_middle, gt_own, gt_other, *att_own, *att_other),
        "s" + 11 * "v",
        [VMEM((2, width, 3 * half), BF)],
        80 * flops,
        24,
    )
    low_away, came_away = after_all((low_away, came_away), input_grad)
    away = added(low_away[height:], came_away[height:])
    next_rest = plan.permute(away, plan.first)
    next_one = plan.permute(added(low_away[:height], came_away[:height]), plan.first)
    down_stay, down_came, up_stay, up_came = after_all(
        (down_stay, down_came, up_stay, up_came), away
    )
    down_stay, down_away = halves(down_stay, down_came)
    down_came = plan.send(down_away, far_second, 1)
    up_stay, up_away = halves(up_stay, up_came)
    up_came = plan.send(up_away, far_first, 1)
    end = (far - 1) * height
    (next_rest,) = after_all((next_rest,), down_away, up_away)
    came_one, next_one = after_all((came_one, next_one), next_rest)
    one = low_one.astype(F32) + came_one.astype(F32) + next_one.astype(F32)
    (next_rest,) = after_all((next_rest,), one)
    sums = added(away[end:], next_rest[end:])
    parts = [None]
    for k in range(far - 1):
        part = slice(k * height, (k + 1) * height)
        parts.append(cat([added(low_rest[part], came_rest[part], next_rest[part]), sums]))
    down_stay, down_came, up_stay, up_came = after_all(
        (down_stay, down_came, up_stay, up_came), parts[1]
    )
    down_total = down_stay[0].astype(F32) + down_came[0].astype(F32)
    up_total = up_stay[0].astype(F32) + up_came[0].astype(F32)
    mine, theirs = call(
        functools.partial(total_kernel, plan, rows),
        [shape((piece + TABLE_ROWS, 4 * half), F32)] * 2,
        (
            after(table, down_total, up_total),
            one,
            sums,
            *plan.send_far(parts),
        ),
        "s" + 5 * "v",
        [VMEM((rows, 4 * half), F32)],
        1,
        16,
    )
    one = [3 * piece, piece, piece, piece, hidden, down_bias.shape[0], piece, piece]
    triple_grad, mix_grad, *vectors = call(
        functools.partial(share_kernel, plan),
        [shape((piece, 3 * width), F32), shape((piece, width), F32)]
        + [shape((1, n), F32) for n in one],
        (table, place, mine, plan.swap(theirs)),
        "ssvv",
        [],
        1,
        16,
    )
    vectors = [v.reshape(-1) for v in vectors]
    return (
        outputs,
        input_grad,
        triple_grad,
        vectors[0],
        mix_grad,
        *vectors[1:4],
        up_total,
        vectors[4],
        down_total.T,
        *vectors[5:],
    )


def fits(plan_shape, width, hidden):
    wide, narrow = plan_shape
    powers = all(n >= 4 and n & (n - 1) == 0 for n in (wide, narrow)) and narrow == 4
    return (
        powers
        and width % (wide * 16) == 0
        and width % (wide * narrow // 2 * 48) == 0
        and hidden % (narrow * 128) == 0
        and width % 768 == 0
    )


def solution(mesh):
    placed = (
        P(("wide", "narrow"), None),
        P(("wide", "narrow")),
        P(("wide", "narrow"), None),
        P(("wide", "narrow")),
        P(("wide", "narrow"), None),
        P(("wide", "narrow")),
        P(("wide", "narrow")),
        P(("wide", "narrow")),
        P("wide", "narrow"),
        P("narrow"),
        P("narrow", "wide"),
        P("wide"),
        P(("wide", "narrow")),
        P(("wide", "narrow")),
        P(("wide", "narrow"), None),
    )
    wide, narrow = mesh.shape["wide"], mesh.shape["narrow"]

    def layer(*arrays):
        rows, hidden = arrays[8].shape
        if fits((wide, narrow), rows * wide, hidden * narrow):
            return fast_body(Plan(wide, narrow), *arrays)
        return body(*arrays)

    return jax.shard_map(
        layer,
        mesh=mesh,
        in_specs=placed,
        out_specs=(
            P(("wide", "narrow"), None),
            P(("wide", "narrow"), None),
            P(("wide", "narrow"), None),
            P(("wide", "narrow")),
            P(("wide", "narrow"), None),
            P(("wide", "narrow")),
            P(("wide", "narrow")),
            P(("wide", "narrow")),
            P("wide", "narrow"),
            P("narrow"),
            P("narrow", "wide"),
            P("wide"),
            P(("wide", "narrow")),
            P(("wide", "narrow")),
        ),
        check_vma=False,
    )
```
